32 devices in a mesh: utt: 4 (over y, core), seq: 8 (over z, x).
Axes of the slice: x: 2, y: 2, z: 4, core: 2. Of those that a mesh axis runs over, the one named last changes fastest.
Arguments:
- frames: float32 [8, 1024, 512], P('utt', 'seq'), may hold values from -6 to 6
- lengths: int32 [8], P('utt'), may hold values from 256 to 1024, as said below
- out_grad: float32 [8, 1024, 512], P('utt', 'seq'), may hold values from -6 to 6
- norm_gain: bfloat16 [5, 512], replicated, may hold values from 0.5 to 1.5
- norm_bias: bfloat16 [5, 512], replicated, may hold values from -1 to 1
- feed_in: bfloat16 [2, 512, 2048], replicated, may hold values from -0.25 to 0.25
- feed_in_bias: bfloat16 [2, 2048], replicated, may hold values from -1 to 1
- feed_out: bfloat16 [2, 2048, 512], replicated, may hold values from -0.125 to 0.125
- feed_out_bias: bfloat16 [2, 512], replicated, may hold values from -1 to 1
- attend_in: bfloat16 [4, 512, 512], replicated, may hold values from -0.25 to 0.25
- attend_vectors: bfloat16 [5, 512], replicated, may hold values from -1.5 to 1.5
- attend_out: bfloat16 [512, 512], replicated, may hold values from -1 to 1
- mixer_in: bfloat16 [512, 1024], replicated, may hold values from -0.25 to 0.25
- mixer_in_bias: bfloat16 [1024], replicated, may hold values from -1 to 1
- depthwise: bfloat16 [512, 9], replicated, may hold values from -2 to 2
- mixer_vectors: bfloat16 [2, 512], replicated, may hold values from -1 to 1
- mixer_out: bfloat16 [512, 512], replicated, may hold values from -0.25 to 0.25
- batch_gain: bfloat16 [512], replicated, may hold values from 0.5 to 1.5
- batch_shift: bfloat16 [512], replicated, may hold values from -1 to 1
- running_mean: float32 [512], replicated, may hold values from -0.08 to 0.08
- running_variance: float32 [512], replicated, may hold values from 0.004 to 0.04
Outputs:
- layer_output: float32 [8, 1024, 512], P('utt', 'seq')
- frames_grad: float32 [8, 1024, 512], P('utt', 'seq')
- norm_gain_grad: float32 [5, 512], replicated
- norm_bias_grad: float32 [5, 512], replicated
- feed_in_grad: float32 [2, 512, 2048], replicated
- feed_in_bias_grad: float32 [2, 2048], replicated
- feed_out_grad: float32 [2, 2048, 512], replicated
- feed_out_bias_grad: float32 [2, 512], replicated
- attend_in_grad: float32 [4, 512, 512], replicated
- attend_vectors_grad: float32 [5, 512], replicated
- attend_out_grad: float32 [512, 512], replicated
- mixer_in_grad: float32 [512, 1024], replicated
- mixer_in_bias_grad: float32 [1024], replicated
- depthwise_grad: float32 [512, 9], replicated
- mixer_vectors_grad: float32 [2, 512], replicated
- mixer_out_grad: float32 [512, 512], replicated
- batch_gain_grad: float32 [512], replicated
- batch_shift_grad: float32 [512], replicated
- new_mean: float32 [512], replicated
- new_variance: float32 [512], replicated
The draws below stay inside these ranges and needn't reach their ends.
Inputs may be any that keep to these rules, and one draw needn't show every extreme that they name: `lengths`: in each aligned block of 2 utterances (those of one index of utt) at least one has exactly 1024 frames.
All inputs are finite; a program needn't handle non-finite values.
Results may differ from the reference program's by a relative error of at most 0.025.
Values may be sent and summed in bfloat16 or wider, within the bound.
No kernel may reach another device: no remote copies, remote signals or barrier semaphores. Data moves between devices by JAX's collectives and lax.ppermute only.
A program may use at most 320 MiB of HBM per device.

```python
import math
import jax
import jax.numpy as jnp
from jax import lax

D = 512
FF = 2048
HEADS = 8
KERNEL = 9
UB = 2
HEAD_DIM = 64
FRAMES = 1024
UTTS = 8


def draw_lengths(key, part):
    key = jax.random.fold_in(key, 11)
    base_key, chosen_key = jax.random.split(key)
    groups = UTTS // UB
    drawn = jax.random.randint(base_key, (groups, UB), FRAMES // 4, FRAMES + 1)
    chosen = jax.random.randint(chosen_key, (groups, 1), 0, UB)
    longest = jnp.arange(UB)[None, :] == chosen
    return jnp.where(longest, FRAMES, drawn).reshape(UTTS).astype(jnp.int32)


def block_scale(key, extent, cuts, smallest, top_value):
    def one(dim, blocks):
        heights = jax.random.uniform(jax.random.fold_in(jax.random.fold_in(key, 6), dim), (blocks,), jnp.float32, smallest / len(cuts), top_value / len(cuts))
        return jnp.repeat(jnp.exp(heights), extent[dim] // blocks).reshape((-1,) + (1,) * (len(extent) - dim - 1))

    gain = one(*cuts[0])
    for cut in cuts[1:]:
        gain = gain * one(*cut)
    return gain


def normal_values(rng, shape, scale, reach, cuts=(), held_as=jnp.bfloat16):
    values = scale * jax.random.normal(rng, shape, jnp.float32)
    if cuts:
        values = values * block_scale(rng, shape, cuts, -0.22, 0.18)
    return jnp.clip(values, -reach, reach).astype(held_as)


def setup_inputs(seed: int = 0) -> dict:
    key_of = jax.random.split(jax.random.key(seed), 22)
    return {
        "frames": normal_values(key_of[0], (UTTS, FRAMES, D), 1.0, 6.0, ((0, 4), (1, 8)), jnp.float32),
        "lengths": draw_lengths(jax.random.fold_in(key_of[21], 71), 0),
        "out_grad": normal_values(key_of[2], (UTTS, FRAMES, D), 1.0, 6.0, ((0, 4), (1, 8)), jnp.float32),
        "norm_gain": jnp.clip(1.0 + 0.1 * jax.random.normal(key_of[3], (5, D), jnp.float32), 0.5, 1.5).astype(jnp.bfloat16),
        "norm_bias": normal_values(key_of[4], (5, D), 0.2, 1.0),
        "feed_in": normal_values(key_of[5], (2, D, FF), D ** -0.5, 0.25),
        "feed_in_bias": normal_values(key_of[6], (2, FF), 0.2, 1.0),
        "feed_out": normal_values(key_of[7], (2, FF, D), FF ** -0.5, 0.125),
        "feed_out_bias": normal_values(key_of[8], (2, D), 0.2, 1.0),
        "attend_in": normal_values(key_of[9], (4, D, D), D ** -0.5, 0.25),
        "attend_vectors": normal_values(key_of[10], (5, D), 0.3, 1.5),
        "attend_out": normal_values(key_of[11], (D, D), (D // 16) ** -0.5, 1.0),
        "mixer_in": normal_values(key_of[12], (D, 2 * D), D ** -0.5, 0.25),
        "mixer_in_bias": normal_values(key_of[13], (2 * D,), 0.2, 1.0),
        "depthwise": normal_values(key_of[14], (D, KERNEL), KERNEL ** -0.5, 2.0),
        "mixer_vectors": normal_values(key_of[15], (2, D), 0.2, 1.0),
        "mixer_out": normal_values(key_of[16], (D, D), D ** -0.5, 0.25),
        "batch_gain": jnp.clip(1.0 + 0.1 * jax.random.normal(key_of[17], (D,), jnp.float32), 0.5, 1.5).astype(jnp.bfloat16),
        "batch_shift": normal_values(key_of[18], (D,), 0.2, 1.0),
        "running_mean": normal_values(key_of[19], (D,), 0.02, 0.08, (), jnp.float32),
        "running_variance": jnp.clip(jnp.exp(jax.random.uniform(key_of[20], (D,), jnp.float32, math.log(0.004), math.log(0.04))), 0.004, 0.04),
    }


@jax.custom_vjp
def low(v):
    return lax.optimization_barrier(v.astype(jnp.bfloat16)).astype(jnp.float32)

@jax.custom_vjp
def low_back(v):
    return v

def low_keep(v):
    return (low(v), None)

def low_pass(kept, grad):
    return (grad,)

def back_keep(v):
    return (v, None)

def back_low(kept, grad):
    return (low(grad),)
low.defvjp(low_keep, low_pass)
low_back.defvjp(back_keep, back_low)
TOP_PRECISION = lax.Precision.HIGHEST

def product(first_operand, second_operand):
    return jnp.dot(first_operand, second_operand, precision=TOP_PRECISION, preferred_element_type=jnp.float32)

def layer_norm(values, gain_vector, shift_vector):
    average = lax.optimization_barrier(jnp.mean(values, axis=-1, keepdims=True))
    centered = values - average
    spread = lax.optimization_barrier(jnp.mean(centered * centered, axis=-1, keepdims=True))
    return centered * lax.rsqrt(spread + 1e-05) * gain_vector + shift_vector

def feed_forward(values, gain_vector, shift_vector, weight_in, bias_in, weight_out, bias_out):
    hidden = low(layer_norm(values, gain_vector, shift_vector))
    preact = low_back(product(hidden, weight_in) + bias_in)
    active = low(jax.nn.silu(preact))
    return low_back(product(active, weight_out) + bias_out)

def position_table(row_total, top_offset, feature_count):
    offsets = (top_offset - jnp.arange(row_total, dtype=jnp.int32)).astype(jnp.float32)
    halves = jnp.arange(feature_count // 2, dtype=jnp.int32).astype(jnp.float32)
    frequencies = jnp.exp(halves * (-2.0 * math.log(10000.0) / feature_count))
    angles = offsets[:, None] * frequencies[None, :]
    return jnp.stack([jnp.sin(angles), jnp.cos(angles)], axis=-1).reshape(row_total, feature_count)

def skew(before_skewing, length):
    leading = before_skewing.shape[:-2]
    row_count, col_count = (before_skewing.shape[-2], before_skewing.shape[-1])
    flattened = before_skewing.reshape(leading + (row_count * col_count,))
    flattened = jnp.pad(flattened, [(0, 0)] * len(leading) + [(0, row_count)])
    return flattened.reshape(leading + (row_count, col_count + 1))[..., :length]

def attend_group(query_content, query_offset_scores, key_rows, value_rows, lengths, relative_offsets):
    groups = query_content.shape[0]
    features = query_content.shape[-1]
    layout = (groups, FRAMES, HEADS, HEAD_DIM)
    query_content = query_content.reshape(layout)
    query_offset_scores = query_offset_scores.reshape(layout)
    key_rows = key_rows.reshape(layout)
    value_rows = value_rows.reshape(layout)
    head_offset_table = relative_offsets.reshape(2 * FRAMES - 1, HEADS, HEAD_DIM)
    direct = jnp.einsum('uqhd,ukhd->uhqk', query_content, key_rows, precision=TOP_PRECISION)
    before_skewing = jnp.einsum('zywj,bwj->zwyb', query_offset_scores[:, ::-1], head_offset_table, precision=TOP_PRECISION)
    placed = skew(before_skewing, FRAMES)[:, :, ::-1]
    scores = low_back(direct + placed) * HEAD_DIM ** (-0.5)
    allowed = jnp.arange(FRAMES, dtype=jnp.int32)[None, None, None, :] < lengths[:, None, None, None]
    scores = jnp.where(allowed, scores, -1000000000.0)
    highest = lax.optimization_barrier(jnp.max(scores, axis=-1, keepdims=True))
    weights = jnp.exp(scores - highest)
    weights = weights / lax.optimization_barrier(jnp.sum(weights, axis=-1, keepdims=True))
    attended = jnp.einsum('uhqk,ukhd->uqhd', low(weights), value_rows, precision=TOP_PRECISION)
    return attended.reshape(groups, FRAMES, features)

def forward(frames, lengths, norm_gain, norm_bias, feed_in, feed_in_bias, feed_out, feed_out_bias, attend_in, attend_vectors, attend_out, mixer_in, mixer_in_bias, depthwise, mixer_vectors, mixer_out, batch_gain, batch_shift):
    frame_mask = (jnp.arange(FRAMES, dtype=jnp.int32)[None, :] < lengths[:, None]).astype(jnp.float32)
    current = frames + 0.5 * feed_forward(frames, norm_gain[0], norm_bias[0], feed_in[0], feed_in_bias[0], feed_out[0], feed_out_bias[0])
    hidden = low(layer_norm(current, norm_gain[1], norm_bias[1]))
    queries = low_back(product(hidden, attend_in[0]) + attend_vectors[0])
    key_rows = low(low_back(product(hidden, attend_in[1])))
    value_rows = low(low_back(product(hidden, attend_in[2]) + attend_vectors[1]))
    query_content = low(queries + attend_vectors[3])
    query_offset_scores = low(queries + attend_vectors[4])
    relative_offsets = low(product(low(position_table(2 * FRAMES - 1, FRAMES - 1, D)), attend_in[3]))
    per_group = math.gcd(UTTS, max(1, 4096 // FRAMES))

    def regroup(source):
        return source.reshape((UTTS // per_group, per_group) + source.shape[1:])
    checkpointed = jax.checkpoint(attend_group)
    attended = lax.map(lambda pieces: checkpointed(pieces[0], pieces[1], pieces[2], pieces[3], pieces[4], relative_offsets), (regroup(query_content), regroup(query_offset_scores), regroup(key_rows), regroup(value_rows), regroup(lengths)))
    attended = low(low_back(attended.reshape(UTTS, FRAMES, D)))
    current = current + low_back(product(attended, attend_out) + attend_vectors[2])
    hidden = low(layer_norm(current, norm_gain[2], norm_bias[2]))
    conv_gates = low_back(product(hidden, mixer_in) + mixer_in_bias)
    gated_units = low(conv_gates[..., :D] * jax.nn.sigmoid(conv_gates[..., D:]) * frame_mask[..., None])
    margin = KERNEL // 2
    padded = jnp.pad(gated_units, ((0, 0), (margin, margin), (0, 0)))
    convolved = mixer_vectors[0] + sum((depthwise[:, offset] * padded[:, offset:offset + FRAMES] for offset in range(KERNEL)))
    convolved = low_back(convolved)
    valid_count = jnp.sum(frame_mask)
    average = lax.optimization_barrier(jnp.sum(convolved * frame_mask[..., None], axis=(0, 1))) / valid_count
    centered = convolved - average
    variance = lax.optimization_barrier(jnp.sum(centered * centered * frame_mask[..., None], axis=(0, 1))) / valid_count
    batch_out = centered * lax.rsqrt(variance + 1e-05) * batch_gain + batch_shift
    active = low(jax.nn.silu(batch_out))
    current = current + low_back(product(active, mixer_out) + mixer_vectors[1])
    current = current + 0.5 * feed_forward(current, norm_gain[3], norm_bias[3], feed_in[1], feed_in_bias[1], feed_out[1], feed_out_bias[1])
    result = layer_norm(current, norm_gain[4], norm_bias[4])
    return (result, (average, variance, valid_count))

def reference(frames, lengths, out_grad, norm_gain, norm_bias, feed_in, feed_in_bias, feed_out, feed_out_bias, attend_in, attend_vectors, attend_out, mixer_in, mixer_in_bias, depthwise, mixer_vectors, mixer_out, batch_gain, batch_shift, running_mean, running_variance):
    parameters = [source.astype(jnp.float32) for source in (norm_gain, norm_bias, feed_in, feed_in_bias, feed_out, feed_out_bias, attend_in, attend_vectors, attend_out, mixer_in, mixer_in_bias, depthwise, mixer_vectors, mixer_out, batch_gain, batch_shift)]

    def wrapped(frames_in, *weights_in):
        return forward(frames_in, lengths, *weights_in)
    result, pullback, statistics = jax.vjp(wrapped, frames, *parameters, has_aux=True)
    average, variance, valid_count = statistics
    gradients = pullback(out_grad)
    new_mean = 0.9 * running_mean + 0.1 * average
    new_variance = 0.9 * running_variance + 0.1 * variance * valid_count / (valid_count - 1.0)
    return (result, gradients[0], gradients[1], gradients[2], gradients[3], gradients[4], gradients[5], gradients[6], gradients[7], gradients[8], gradients[9], gradients[10], gradients[11], gradients[12], gradients[13], gradients[14], gradients[15], gradients[16], new_mean, new_variance)
```

```python
import math

import jax
import jax.numpy as jnp
from jax import lax
from jax.sharding import PartitionSpec as P

HEADS = 8
KERNEL = 9
HEAD_DIM = 64


TOP_PRECISION = lax.Precision.HIGHEST
EPSILON = 1e-05


def with_halo(cells, sides, width):
    for axis, dim in sides:
        count = lax.axis_size(axis)
        ends = count - 1
        head = lax.slice_in_dim(cells, 0, width, axis=dim)
        tail = lax.slice_in_dim(cells, cells.shape[dim] - width, cells.shape[dim], axis=dim)
        cells = jnp.concatenate(
            [
                lax.ppermute(tail, axis, [(i, (i + 1) % count) for i in range(ends)]),
                cells,
                lax.ppermute(head, axis, [((i + 1) % count, i) for i in range(ends)]),
            ],
            axis=dim,
        )
    return cells


def project(first_operand, second_operand):
    return jnp.dot(first_operand, second_operand, preferred_element_type=jnp.float32)


def outer_sum(first_operand, second_operand):
    return jnp.einsum(
        "ufd,ufe->de", first_operand, second_operand, preferred_element_type=jnp.float32
    )


def project_back(grad_rows, weight):
    return jnp.einsum("ufe,de->ufd", grad_rows, weight, preferred_element_type=jnp.float32)


def column_sum(grad_rows):
    return jnp.sum(grad_rows.astype(jnp.float32), axis=(0, 1))


def flatten_grads(members):
    flattened = jnp.concatenate([member.reshape(-1) for member in members])
    return flattened


def restore_grads(flattened, members):
    restored = []
    offset = 0
    for member in members:
        element_count = member.size
        restored.append(flattened[offset : offset + element_count].reshape(member.shape))
        offset = offset + element_count
    return tuple(restored)


def norm_forward(values, gain_vector, shift_vector):
    average = jnp.mean(values, axis=-1, keepdims=True)
    centered = values - average
    spread = jnp.mean(centered * centered, axis=-1, keepdims=True)
    inverse = lax.rsqrt(spread + EPSILON)
    normed = centered * inverse
    return (
        normed * gain_vector.astype(jnp.float32) + shift_vector.astype(jnp.float32),
        normed,
        inverse,
    )


def norm_backward(grad_rows, normed, inverse, gain_vector):
    scaled = grad_rows * gain_vector.astype(jnp.float32)
    row_inner = (
        scaled
        - jnp.mean(scaled, axis=-1, keepdims=True)
        - normed * jnp.mean(scaled * normed, axis=-1, keepdims=True)
    )
    return (
        row_inner * inverse,
        jnp.sum(grad_rows * normed, axis=(0, 1)),
        jnp.sum(grad_rows, axis=(0, 1)),
    )


def silu_slope(preact):
    logistic = jax.nn.sigmoid(preact)
    return logistic * (1.0 + preact * (1.0 - logistic))


def feed_forward(values, gain_vector, shift_vector, weight_in, bias_in, weight_out, bias_out):
    normed_out, normed, inverse = norm_forward(values, gain_vector, shift_vector)
    hidden = normed_out.astype(jnp.bfloat16)
    preact = project(hidden, weight_in) + bias_in.astype(jnp.float32)
    active = jax.nn.silu(preact).astype(jnp.bfloat16)
    return (
        project(active, weight_out) + bias_out.astype(jnp.float32),
        (normed, inverse, hidden, preact, active),
    )


def feed_backward(grad_rows, stored, gain_vector, weight_in, weight_out):
    normed, inverse, hidden, preact, active = stored
    grad_low = grad_rows.astype(jnp.bfloat16)
    grad_weight_out = outer_sum(active, grad_low)
    grad_bias_out = column_sum(grad_low)
    grad_pre = (project_back(grad_low, weight_out) * silu_slope(preact)).astype(jnp.bfloat16)
    grad_weight_in = outer_sum(hidden, grad_pre)
    grad_bias_in = column_sum(grad_pre)
    grad_values, grad_gain, grad_shift = norm_backward(
        project_back(grad_pre, weight_in), normed, inverse, gain_vector
    )
    return (
        grad_values,
        grad_gain,
        grad_shift,
        grad_weight_in,
        grad_bias_in,
        grad_weight_out,
        grad_bias_out,
    )


def axis_bits(axis):
    return [(axis, 1 << bit) for bit in range(lax.axis_size(axis).bit_length() - 1)]


def swap(values, step):
    axis, mask = step
    return lax.ppermute(values, axis, [(i, i ^ mask) for i in range(lax.axis_size(axis))])


def side(step):
    axis, mask = step
    return (lax.axis_index(axis) // mask) % 2


def scatter_rows(rows, steps):
    for step in steps:
        half = rows.shape[0] // 2
        mine = side(step)
        sent = lax.dynamic_slice_in_dim(rows, (1 - mine) * half, half, 0)
        kept = lax.dynamic_slice_in_dim(rows, mine * half, half, 0)
        rows = (kept.astype(jnp.float32) + swap(sent, step).astype(jnp.float32)).astype(
            jnp.bfloat16
        )
    return rows


def gather_rows(rows, steps):
    for step in reversed(steps):
        other = swap(rows, step)
        first = side(step) == 0
        rows = jnp.concatenate(
            [jnp.where(first, rows, other), jnp.where(first, other, rows)], axis=0
        )
    return rows


def step_orders():
    utt, seq = axis_bits("utt"), axis_bits("seq")
    near, across, line = utt[:1], utt[1:], seq[:1]
    rest = seq[1:]
    return (
        near + line + across + rest,
        near + across + line + rest,
        near + rest + line + across,
    )


def all_shared(rows):
    count = lax.axis_size("utt") * lax.axis_size("seq")
    copies = jnp.broadcast_to(rows[None], (count,) + rows.shape)
    return lax.all_to_all(copies, ("utt", "seq"), 0, 0, tiled=True)


def as_rows(members):
    pieces = []
    for member in members:
        for start in range(0, member.shape[1], 512):
            pieces.append(member[:, start : start + 512].astype(jnp.bfloat16))
    return jnp.concatenate(pieces, axis=0)


def from_rows(rows, shapes):
    restored = []
    offset = 0
    for height, width in shapes:
        columns = []
        for _ in range(width // 512):
            columns.append(rows[offset : offset + height])
            offset += height
        restored.append(jnp.concatenate(columns, axis=1).astype(jnp.float32))
    return restored


def angle_tables(frame_count, features):
    halves = jnp.arange(features // 2, dtype=jnp.int32).astype(jnp.float32)
    frequencies = jnp.exp(halves * (-2.0 * math.log(10000.0) / features))
    fine = 32
    low_angles = jnp.arange(fine, dtype=jnp.int32).astype(jnp.float32)[:, None] * frequencies
    high_angles = (fine * jnp.arange(frame_count // fine, dtype=jnp.int32)).astype(jnp.float32)[
        :, None
    ] * frequencies
    low_sin, low_cos = jnp.sin(low_angles)[None], jnp.cos(low_angles)[None]
    high_sin, high_cos = jnp.sin(high_angles)[:, None], jnp.cos(high_angles)[:, None]
    sines = high_sin * low_cos + high_cos * low_sin
    cosines = high_cos * low_cos - high_sin * low_sin
    shape = (frame_count, features // 2)
    return sines.reshape(shape), cosines.reshape(shape)


def heads_out(blocks, groups):
    return lax.all_to_all(jnp.tile(blocks, (groups, 1, 1)), "seq", 0, 0, tiled=True)


def shards(
    frames,
    lengths,
    out_grad,
    norm_gain,
    norm_bias,
    feed_in,
    feed_in_bias,
    feed_out,
    feed_out_bias,
    attend_in,
    attend_vectors,
    attend_out,
    mixer_in,
    mixer_in_bias,
    depthwise,
    mixer_vectors,
    mixer_out,
    batch_gain,
    batch_shift,
    running_mean,
    running_variance,
):
    utt_rows, block_frames, features = frames.shape
    seq_count = lax.axis_size("seq")
    seq_index = lax.axis_index("seq")
    count = lax.axis_size("utt") * seq_count
    frames_all = block_frames * seq_count
    groups = seq_count // HEADS
    head, group = seq_index % HEADS, seq_index // HEADS
    query_frames = frames_all // groups
    first_frame = seq_index * block_frames
    frame_mask = (
        (first_frame + jnp.arange(block_frames, dtype=jnp.int32))[None, :] < lengths[:, None]
    ).astype(jnp.float32)
    mask_cols = frame_mask[..., None]
    first_out, first_stored = feed_forward(
        frames,
        norm_gain[0],
        norm_bias[0],
        feed_in[0],
        feed_in_bias[0],
        feed_out[0],
        feed_out_bias[0],
    )
    after_first = frames + 0.5 * first_out
    attend_normed, normed_two, inverse_two = norm_forward(after_first, norm_gain[1], norm_bias[1])
    hidden_two = attend_normed.astype(jnp.bfloat16)
    queries = project(hidden_two, attend_in[0]) + attend_vectors[0].astype(jnp.float32)
    key_rows = project(hidden_two, attend_in[1]).astype(jnp.bfloat16)
    value_rows = (project(hidden_two, attend_in[2]) + attend_vectors[1].astype(jnp.float32)).astype(
        jnp.bfloat16
    )
    content = (queries + attend_vectors[3].astype(jnp.float32)).astype(jnp.bfloat16)
    sent = jnp.stack([content, key_rows, value_rows], axis=2).reshape(
        utt_rows, block_frames, 3, HEADS, HEAD_DIM
    )
    sent = jnp.transpose(sent, (3, 1, 0, 2, 4)).reshape(
        HEADS, block_frames, utt_rows * 3 * HEAD_DIM
    )
    arrived = heads_out(sent, groups).reshape(frames_all, utt_rows, 3, HEAD_DIM)
    start_query = group * query_frames
    head_content = lax.dynamic_slice_in_dim(arrived[:, :, 0], start_query, query_frames, 0)
    head_keys, head_values = arrived[:, :, 1], arrived[:, :, 2]
    head_vectors = lax.dynamic_slice_in_dim(
        attend_vectors.astype(jnp.float32), head * HEAD_DIM, HEAD_DIM, 1
    )
    head_offset = (
        head_content.astype(jnp.float32) + (head_vectors[4] - head_vectors[3])
    ).astype(jnp.bfloat16)
    head_weight = lax.dynamic_slice_in_dim(attend_in[3], head * HEAD_DIM, HEAD_DIM, 1).reshape(
        features // 2, 2, HEAD_DIM
    )
    sin_weight, cos_weight = head_weight[:, 0], head_weight[:, 1]
    sines, cosines = angle_tables(frames_all, features)
    key_table = jnp.concatenate([cosines, sines], axis=1).astype(jnp.bfloat16)
    query_sin = lax.dynamic_slice_in_dim(sines, start_query, query_frames, 0)[:, None]
    query_cos = lax.dynamic_slice_in_dim(cosines, start_query, query_frames, 0)[:, None]

    def turn(sin_part, cos_part):
        return jnp.concatenate(
            [
                sin_part * query_sin + cos_part * query_cos,
                cos_part * query_sin - sin_part * query_cos,
            ],
            axis=-1,
        ).astype(jnp.bfloat16)

    def contract(spec, first_operand, second_operand):
        return jnp.einsum(spec, first_operand, second_operand, preferred_element_type=jnp.float32)

    turned = turn(
        contract("qud,id->qui", head_offset, sin_weight),
        contract("qud,id->qui", head_offset, cos_weight),
    )
    scores = (
        contract("qud,kud->uqk", head_content, head_keys)
        + contract("qui,ki->uqk", turned, key_table)
    ) * HEAD_DIM ** (-0.5)
    allowed = jnp.arange(frames_all, dtype=jnp.int32)[None, None, :] < lengths[:, None, None]
    scores = jnp.where(allowed, scores, -1000000000.0)
    shifted = jnp.exp(scores - jnp.max(scores, axis=-1, keepdims=True))
    weights = (shifted / jnp.sum(shifted, axis=-1, keepdims=True)).astype(jnp.bfloat16)
    head_attended = contract("uqk,kud->qud", weights, head_values).astype(jnp.bfloat16)

    def frames_back(rows):
        width = rows.shape[-1]
        rows = rows.reshape(1, HEADS, block_frames, width)
        if groups > 1:
            rows = lax.dynamic_update_slice_in_dim(
                jnp.zeros((groups,) + rows.shape[1:], rows.dtype), rows, group, 0
            )
        rows = lax.all_to_all(
            rows.reshape(seq_count, block_frames, width), "seq", 0, 0, tiled=True
        ).reshape(groups, HEADS, block_frames, width)
        return lax.dynamic_slice_in_dim(rows, group, 1, 0)[0]

    def join_heads(blocks):
        blocks = blocks.reshape(HEADS, block_frames, utt_rows, HEAD_DIM)
        return jnp.transpose(blocks, (2, 1, 0, 3)).reshape(utt_rows, block_frames, features)

    attended_low = join_heads(
        frames_back(head_attended.reshape(query_frames, utt_rows * HEAD_DIM))
    )
    after_attend = (
        after_first + project(attended_low, attend_out) + attend_vectors[2].astype(jnp.float32)
    )
    mixer_normed, normed_three, inverse_three = norm_forward(
        after_attend, norm_gain[2], norm_bias[2]
    )
    hidden_three = mixer_normed.astype(jnp.bfloat16)
    mixer_pre = project(hidden_three, mixer_in) + mixer_in_bias.astype(jnp.float32)
    linear_half = mixer_pre[..., :features]
    gate_half = jax.nn.sigmoid(mixer_pre[..., features:])
    gated_units = (linear_half * gate_half * mask_cols).astype(jnp.bfloat16)
    margin = KERNEL // 2
    widened = with_halo(gated_units, (("seq", 1),), margin)
    kernel_rows = depthwise.astype(jnp.float32)
    convolved = mixer_vectors[0].astype(jnp.float32) + sum(
        (
            kernel_rows[:, offset] * widened[:, offset : offset + block_frames].astype(jnp.float32)
            for offset in range(KERNEL)
        )
    )
    mask_total = jnp.sum(frame_mask)
    local_sum = jnp.sum(convolved * mask_cols, axis=(0, 1))
    local_average = local_sum / jnp.maximum(mask_total, 1.0)
    local_centered = (convolved - local_average) * mask_cols
    local_square = jnp.sum(local_centered * local_centered, axis=(0, 1))
    shared = all_shared(
        jnp.stack([local_sum, local_square, jnp.full_like(local_sum, mask_total), local_average])
    )
    valid_count = jnp.sum(shared[:, 2], axis=0)
    average = jnp.sum(shared[:, 0], axis=0) / valid_count
    drift = shared[:, 3] - average
    variance = jnp.sum(shared[:, 1] + shared[:, 2] * drift * drift, axis=0) / valid_count
    centered = convolved - average
    inverse_batch = lax.rsqrt(variance + EPSILON)
    normed_batch = centered * inverse_batch
    batch_out = normed_batch * batch_gain.astype(jnp.float32) + batch_shift.astype(jnp.float32)
    swished = jax.nn.silu(batch_out).astype(jnp.bfloat16)
    after_mixer = after_attend + project(swished, mixer_out) + mixer_vectors[1].astype(jnp.float32)
    second_out, second_stored = feed_forward(
        after_mixer,
        norm_gain[3],
        norm_bias[3],
        feed_in[1],
        feed_in_bias[1],
        feed_out[1],
        feed_out_bias[1],
    )
    after_second = after_mixer + 0.5 * second_out
    layer_output, normed_last, inverse_last = norm_forward(after_second, norm_gain[4], norm_bias[4])
    grad_second, gain_last, shift_last = norm_backward(
        out_grad, normed_last, inverse_last, norm_gain[4]
    )
    second_back = feed_backward(
        0.5 * grad_second, second_stored, norm_gain[3], feed_in[1], feed_out[1]
    )
    second_rows = lax.psum(as_rows([second_back[3], second_back[5]]), ("utt", "seq"))
    grad_mixer = grad_second + second_back[0]
    grad_branch = grad_mixer.astype(jnp.bfloat16)
    mixer_out_grad = outer_sum(swished, grad_branch)
    out_bias_grad = column_sum(grad_branch)
    grad_batch = project_back(grad_branch, mixer_out) * silu_slope(batch_out)
    batch_shift_grad, batch_gain_grad = jnp.sum(
        all_shared(
            jnp.stack(
                [jnp.sum(grad_batch, axis=(0, 1)), jnp.sum(grad_batch * normed_batch, axis=(0, 1))]
            )
        ),
        axis=0,
    )
    grad_conv = (
        batch_gain.astype(jnp.float32)
        * inverse_batch
        * (
            grad_batch
            - mask_cols / valid_count * (batch_shift_grad + normed_batch * batch_gain_grad)
        )
    ).astype(jnp.bfloat16)
    grad_wide = with_halo(grad_conv, (("seq", 1),), margin)
    grad_gated = mask_cols * sum(
        (
            kernel_rows[:, offset]
            * grad_wide[:, 2 * margin - offset : 2 * margin - offset + block_frames].astype(
                jnp.float32
            )
            for offset in range(KERNEL)
        )
    )
    grad_conv_wide = grad_conv.astype(jnp.float32)
    depthwise_grad = jnp.stack(
        [
            jnp.sum(
                grad_conv_wide * widened[:, offset : offset + block_frames].astype(jnp.float32),
                axis=(0, 1),
            )
            for offset in range(KERNEL)
        ],
        axis=1,
    )
    kernel_bias_grad = column_sum(grad_conv)
    grad_mixer_pre = jnp.concatenate(
        [grad_gated * gate_half, grad_gated * linear_half * gate_half * (1.0 - gate_half)], axis=-1
    ).astype(jnp.bfloat16)
    mixer_in_grad = outer_sum(hidden_three, grad_mixer_pre)
    mixer_in_bias_grad = column_sum(grad_mixer_pre)
    grad_three, gain_three, shift_three = norm_backward(
        project_back(grad_mixer_pre, mixer_in), normed_three, inverse_three, norm_gain[2]
    )
    grad_attend = grad_mixer + grad_three
    mixer_vectors_grad = jnp.stack([kernel_bias_grad, out_bias_grad])
    grad_branch_two = grad_attend.astype(jnp.bfloat16)
    attend_out_grad = outer_sum(attended_low, grad_branch_two)
    out_bias_two = column_sum(grad_branch_two)
    mixer_rows = lax.psum(
        as_rows([mixer_out_grad, mixer_in_grad, attend_out_grad]), ("utt", "seq")
    )
    grad_attended = project_back(grad_branch_two, attend_out).astype(jnp.bfloat16)
    grad_blocks = grad_attended.reshape(utt_rows, block_frames, HEADS, HEAD_DIM)
    grad_blocks = jnp.transpose(grad_blocks, (2, 1, 0, 3)).reshape(
        HEADS, block_frames, utt_rows * HEAD_DIM
    )
    head_grad = lax.dynamic_slice_in_dim(
        heads_out(grad_blocks, groups).reshape(frames_all, utt_rows, HEAD_DIM),
        start_query,
        query_frames,
        0,
    )
    grad_weights = contract("qud,kud->uqk", head_grad, head_values)
    wide = weights.astype(jnp.float32)
    row_inner = jnp.sum(wide * grad_weights, axis=-1, keepdims=True)
    grad_scores = (wide * (grad_weights - row_inner) * HEAD_DIM ** (-0.5)).astype(jnp.bfloat16)
    head_grad_values = contract("uqk,qud->kud", weights, head_grad)
    head_grad_keys = contract("uqk,qud->kud", grad_scores, head_content)
    head_grad_content = contract("uqk,kud->qud", grad_scores, head_keys)
    grad_turned = contract("uqk,ki->qui", grad_scores, key_table)
    half_features = features // 2
    grad_sin = grad_turned[..., :half_features]
    grad_cos = grad_turned[..., half_features:]
    from_sin = (grad_sin * query_sin - grad_cos * query_cos).astype(jnp.bfloat16)
    from_cos = (grad_sin * query_cos + grad_cos * query_sin).astype(jnp.bfloat16)
    head_grad_position = contract("qui,id->qud", from_sin, sin_weight) + contract(
        "qui,id->qud", from_cos, cos_weight
    )
    head_weight_grad = jnp.stack(
        [
            contract("qui,qud->id", from_sin, head_offset),
            contract("qui,qud->id", from_cos, head_offset),
        ],
        axis=1,
    ).reshape(features, HEAD_DIM)
    position_weight_grad = lax.dynamic_update_slice_in_dim(
        jnp.zeros((features, features), jnp.float32), head_weight_grad, head * HEAD_DIM, 1
    )
    head_vector_grads = lax.dynamic_update_slice_in_dim(
        jnp.zeros((2, features), jnp.float32),
        jnp.stack([jnp.sum(head_grad_content, axis=(0, 1)), jnp.sum(head_grad_position, axis=(0, 1))]),
        head * HEAD_DIM,
        1,
    )
    head_grad_query = (head_grad_content + head_grad_position).astype(jnp.bfloat16)
    if groups == 1:
        returned = lax.all_to_all(
            jnp.stack(
                [
                    head_grad_query,
                    head_grad_keys.astype(jnp.bfloat16),
                    head_grad_values.astype(jnp.bfloat16),
                ],
                axis=2,
            ).reshape(seq_count, block_frames, utt_rows * 3 * HEAD_DIM),
            "seq",
            0,
            0,
            tiled=True,
        ).reshape(HEADS, block_frames, utt_rows, 3, HEAD_DIM)
        query_low, key_low, value_low = (join_heads(returned[:, :, :, i]) for i in range(3))
    else:
        query_low = join_heads(
            frames_back(head_grad_query.reshape(query_frames, utt_rows * HEAD_DIM))
        )
        returned = lax.all_to_all(
            jnp.stack([head_grad_keys, head_grad_values], axis=2)
            .astype(jnp.bfloat16)
            .reshape(seq_count, block_frames, utt_rows * 2 * HEAD_DIM),
            "seq",
            0,
            0,
            tiled=True,
        )
        returned = jnp.sum(
            returned.astype(jnp.float32).reshape(
                groups, HEADS, block_frames, utt_rows, 2, HEAD_DIM
            ),
            axis=0,
        ).astype(jnp.bfloat16)
        key_low, value_low = (join_heads(returned[:, :, :, i]) for i in range(2))
    attend_in_grads = [
        outer_sum(hidden_two, query_low),
        outer_sum(hidden_two, key_low),
        outer_sum(hidden_two, value_low),
    ]
    attend_vector_parts = [
        column_sum(query_low)[None],
        column_sum(value_low)[None],
        out_bias_two[None],
        head_vector_grads,
    ]
    grad_hidden = (
        project_back(query_low, attend_in[0])
        + project_back(key_low, attend_in[1])
        + project_back(value_low, attend_in[2])
    )
    grad_two, gain_two, shift_two = norm_backward(
        grad_hidden, normed_two, inverse_two, norm_gain[1]
    )
    grad_first = grad_attend + grad_two
    first_back = feed_backward(
        0.5 * grad_first, first_stored, norm_gain[0], feed_in[0], feed_out[0]
    )
    frames_grad = grad_first + first_back[0]
    norm_gain_grad = jnp.stack([first_back[1], gain_two, gain_three, second_back[1], gain_last])
    norm_bias_grad = jnp.stack([first_back[2], shift_two, shift_three, second_back[2], shift_last])
    feed_in_bias_grad = jnp.stack([first_back[4], second_back[4]])
    feed_out_bias_grad = jnp.stack([first_back[6], second_back[6]])
    attend_vectors_grad = jnp.concatenate(attend_vector_parts, axis=0)
    vectors = (
        norm_gain_grad,
        norm_bias_grad,
        feed_in_bias_grad,
        feed_out_bias_grad,
        attend_vectors_grad,
        mixer_in_bias_grad,
        depthwise_grad,
        mixer_vectors_grad,
    )
    flat = flatten_grads(vectors)
    vector_rows = -(-flat.shape[0] // (512 * count)) * count
    flat = jnp.pad(flat, (0, vector_rows * 512 - flat.shape[0]))
    last = as_rows([first_back[3], first_back[5]])
    middle = as_rows(attend_in_grads + [position_weight_grad])
    cuts = (3 * 512, 6 * 512)
    stripes = (
        jnp.concatenate([last[: cuts[0]], middle[:768]], axis=0),
        jnp.concatenate([last[cuts[0] : cuts[1]], middle[768:1536]], axis=0),
        jnp.concatenate(
            [last[cuts[1] :], middle[1536:], flat.astype(jnp.bfloat16).reshape(-1, 512)], axis=0
        ),
    )
    gathered = [
        gather_rows(scatter_rows(stripe, order), order)
        for stripe, order in zip(stripes, step_orders())
    ]
    last = jnp.concatenate([gathered[0][:1536], gathered[1][:1536], gathered[2][:1024]], axis=0)
    middle = jnp.concatenate(
        [gathered[0][1536:], gathered[1][1536:], gathered[2][1024:1536]], axis=0
    )
    vectors = restore_grads(
        gathered[2][1536:].astype(jnp.float32).reshape(-1), vectors
    )
    (
        norm_gain_grad,
        norm_bias_grad,
        feed_in_bias_grad,
        feed_out_bias_grad,
        attend_vectors_grad,
        mixer_in_bias_grad,
        depthwise_grad,
        mixer_vectors_grad,
    ) = vectors
    wide_in, wide_out = feed_in.shape[1:], feed_out.shape[1:]
    first_in, first_out_grad = from_rows(last, (wide_in, wide_out))
    second_in, second_out_grad = from_rows(second_rows, (wide_in, wide_out))
    feed_in_grad = jnp.stack([first_in, second_in])
    feed_out_grad = jnp.stack([first_out_grad, second_out_grad])
    attend_in_grad = middle.astype(jnp.float32).reshape(attend_in.shape)
    mixer_out_grad, mixer_in_grad, attend_out_grad = from_rows(
        mixer_rows, (mixer_out.shape, mixer_in.shape, attend_out.shape)
    )
    new_mean = 0.9 * running_mean + 0.1 * average
    new_variance = 0.9 * running_variance + 0.1 * variance * valid_count / (valid_count - 1.0)
    return (
        layer_output,
        frames_grad,
        norm_gain_grad,
        norm_bias_grad,
        feed_in_grad,
        feed_in_bias_grad,
        feed_out_grad,
        feed_out_bias_grad,
        attend_in_grad,
        attend_vectors_grad,
        attend_out_grad,
        mixer_in_grad,
        mixer_in_bias_grad,
        depthwise_grad,
        mixer_vectors_grad,
        mixer_out_grad,
        batch_gain_grad,
        batch_shift_grad,
        new_mean,
        new_variance,
    )


def solution(mesh):
    return jax.shard_map(
        shards,
        mesh=mesh,
        in_specs=(
            P("utt", "seq", None),
            P("utt"),
            P("utt", "seq", None),
            P(),
            P(),
            P(),
            P(),
            P(),
            P(),
            P(),
            P(),
            P(),
            P(),
            P(),
            P(),
            P(),
            P(),
            P(),
            P(),
            P(),
            P(),
        ),
        out_specs=(
            P("utt", "seq", None),
            P("utt", "seq", None),
            P(),
            P(),
            P(),
            P(),
            P(),
            P(),
            P(),
            P(),
            P(),
            P(),
            P(),
            P(),
            P(),
            P(),
            P(),
            P(),
            P(),
            P(),
        ),
        check_vma=False,
    )
```

```python
import functools
import math

import jax
import jax.numpy as jnp
import numpy as np
from jax import lax
from jax.experimental import pallas as pl
from jax.experimental.pallas import tpu as pltpu
from jax.sharding import PartitionSpec as P

HEADS = 8
KERNEL = 9
HEAD_DIM = 64


TOP_PRECISION = lax.Precision.HIGHEST
EPSILON = 1e-05
VMEM_LIMIT = 52 * 1024 * 1024
HALO = 8


def wide(values):
    return values.astype(jnp.float32)


def low(values):
    return values.astype(jnp.bfloat16)


def matmul(first_operand, second_operand):
    return jnp.dot(first_operand, second_operand, preferred_element_type=jnp.float32)


def column_sum(values):
    return jnp.sum(wide(values), axis=0, keepdims=True)


def normalize(values):
    average = jnp.mean(values, axis=-1, keepdims=True)
    centered = values - average
    spread = jnp.mean(centered * centered, axis=-1, keepdims=True)
    inverse = lax.rsqrt(spread + EPSILON)
    return centered * inverse, inverse


def scaled_norm(normed, gains, biases, number):
    return normed * wide(gains[number : number + 1, :]) + wide(biases[number : number + 1, :])


def norm_back(grad_rows, normed, inverse, gains, number, own=lambda values: values):
    scaled = grad_rows * wide(gains[number : number + 1, :])
    inner = (
        scaled
        - jnp.mean(scaled, axis=-1, keepdims=True)
        - normed * jnp.mean(scaled * normed, axis=-1, keepdims=True)
    )
    return inner * inverse, column_sum(own(grad_rows * normed)), column_sum(own(grad_rows))


def logistic(values):
    return 1.0 / (1.0 + jnp.exp(-values))


def silu_slope(preact, sigmoid):
    return sigmoid * (1.0 + preact * (1.0 - sigmoid))


def frame_places(info, rows, utterances, halo):
    per = rows // utterances
    row = lax.broadcasted_iota(jnp.int32, (rows, 1), 0)
    limit = jnp.full((rows, 1), info[utterances], jnp.int32)
    for utterance in range(utterances - 1):
        limit = jnp.where(row // per == utterance, info[1 + utterance], limit)
    return info[0] - halo + row % per, limit


def flags(condition):
    return jnp.where(condition, 1.0, 0.0)


def own_rows(values, utterances):
    per = values.shape[0] // utterances
    return jnp.concatenate(
        [values[u * per + HALO : (u + 1) * per - HALO] for u in range(utterances)], axis=0
    )


def with_sides(values, sides, utterances):
    per = values.shape[0] // utterances
    pieces = []
    for u in range(utterances):
        pieces.append(sides[2 * u * HALO : (2 * u + 1) * HALO])
        pieces.append(values[u * per : (u + 1) * per])
        pieces.append(sides[(2 * u + 1) * HALO : (2 * u + 2) * HALO])
    return jnp.concatenate(pieces, axis=0)


def blocks_of_heads(rows, utterances):
    per = rows.shape[0] // utterances
    first = lax.broadcasted_iota(jnp.int32, (per, 2 * HEAD_DIM), 1) < HEAD_DIM
    blocks = []
    for pair in range(HEADS // 2):
        columns = rows[:, pair * 2 * HEAD_DIM : (pair + 1) * 2 * HEAD_DIM]
        top, bottom = columns[:per], columns[per:]
        blocks.append(jnp.where(first, top, pltpu.roll(bottom, HEAD_DIM, 1)))
        blocks.append(jnp.where(first, pltpu.roll(top, HEAD_DIM, 1), bottom))
    return blocks


def rows_of_heads(blocks):
    per = blocks[0].shape[0]
    first = lax.broadcasted_iota(jnp.int32, (per, 2 * HEAD_DIM), 1) < HEAD_DIM
    columns = []
    for pair in range(HEADS // 2):
        left, right = blocks[2 * pair], blocks[2 * pair + 1]
        top = jnp.where(first, left, pltpu.roll(right, HEAD_DIM, 1))
        bottom = jnp.where(first, pltpu.roll(left, HEAD_DIM, 1), right)
        columns.append(jnp.concatenate([top, bottom], axis=0))
    return jnp.concatenate(columns, axis=1)


def vmem_call(kernel, shapes, smem, operands, scratch=(), cost=0, held=()):
    vmem = pl.BlockSpec(memory_space=pltpu.VMEM)
    return pl.pallas_call(
        kernel,
        in_specs=[pl.BlockSpec(memory_space=pltpu.SMEM)] * len(smem)
        + [vmem] * len(operands)
        + [pl.BlockSpec(memory_space=pl.ANY)] * len(held),
        out_specs=[vmem] * len(shapes),
        out_shape=[jax.ShapeDtypeStruct(shape, dtype) for shape, dtype in shapes],
        scratch_shapes=list(scratch),
        compiler_params=pltpu.CompilerParams(vmem_limit_bytes=VMEM_LIMIT),
        cost_estimate=pl.CostEstimate(flops=cost, bytes_accessed=cost // 300, transcendentals=0),
    )(*smem, *operands, *held)


def fetch(pairs, semaphores):
    copies = [
        pltpu.make_async_copy(source, target, semaphores.at[number])
        for number, (source, target) in enumerate(pairs)
    ]
    for copy in copies:
        copy.start()
    return copies


def feed_rows(values, gains, biases, copies, weight_in, bias_in, weight_out, bias_out):
    normed, _ = normalize(values)
    hidden = low(scaled_norm(normed, gains, biases, 0))
    copies[0].wait()
    preact = matmul(hidden, weight_in[...]) + wide(bias_in[0:1, :])
    sigmoid = logistic(preact)
    active = low(preact * sigmoid)
    copies[1].wait()
    branch = matmul(active, weight_out[...]) + wide(bias_out[0:1, :])
    return values + 0.5 * branch, preact, sigmoid, active


def entry_kernel(
    utterances,
    frames,
    gains,
    biases,
    bias_in,
    bias_out,
    vectors,
    feed_in,
    feed_out,
    attend_in,
    after_out,
    slope_out,
    active_out,
    sent_out,
    weight_in,
    weight_out,
    weight_attend,
    semaphores,
):
    copies = fetch(
        [
            (feed_in.at[0], weight_in),
            (feed_out.at[0], weight_out),
            (attend_in.at[pl.ds(0, 3)], weight_attend),
        ],
        semaphores,
    )
    after, preact, sigmoid, active = feed_rows(
        frames[...], gains, biases, copies, weight_in, bias_in, weight_out, bias_out
    )
    slope_out[...] = low(silu_slope(preact, sigmoid))
    active_out[...] = active
    after_out[...] = after
    normed, _ = normalize(after)
    hidden = low(scaled_norm(normed, gains, biases, 1))
    copies[2].wait()
    queries = matmul(hidden, weight_attend[0]) + wide(vectors[0:1, :])
    parts = (
        queries + wide(vectors[3:4, :]),
        matmul(hidden, weight_attend[1]),
        matmul(hidden, weight_attend[2]) + wide(vectors[1:2, :]),
    )
    lanes = 2 * HEAD_DIM
    for number, part in enumerate(parts):
        for head, block in enumerate(blocks_of_heads(part, utterances)):
            sent_out[head, :, number * lanes : (number + 1) * lanes] = low(block)


def sides_kernel(
    frames,
    gains,
    biases,
    bias_in,
    bias_out,
    feed_in,
    feed_out,
    after_out,
    weight_in,
    weight_out,
    semaphores,
):
    copies = fetch([(feed_in.at[0], weight_in), (feed_out.at[0], weight_out)], semaphores)
    after_out[...] = feed_rows(
        frames[...], gains, biases, copies, weight_in, bias_in, weight_out, bias_out
    )[0]


def mixer_kernel(
    utterances,
    info,
    blocks,
    after,
    after_sides,
    gains,
    biases,
    attend_out,
    vectors,
    mixer_in,
    mixer_bias,
    taps,
    mixer_vectors,
    after_out,
    attended_out,
    linear_out,
    gate_out,
    gated_out,
    convolved_out,
    sums_out,
    padded,
):
    per = after.shape[0] // utterances
    main, before, behind = [], [], []
    for head in range(HEADS):
        block = wide(blocks[head])
        main.append(block[:per])
        before.append(block[per : per + HALO])
        behind.append(block[per + HALO :])
    attended = rows_of_heads(main)
    attended_out[...] = low(attended)
    before, behind = rows_of_heads(before), rows_of_heads(behind)
    sides = []
    for u in range(utterances):
        sides += [before[u * HALO : (u + 1) * HALO], behind[u * HALO : (u + 1) * HALO]]
    attended = low(with_sides(attended, jnp.concatenate(sides, axis=0), utterances))
    values = with_sides(after[...], after_sides[...], utterances)
    values = values + matmul(attended, attend_out[...]) + wide(vectors[2:3, :])
    after_out[...] = values
    normed, _ = normalize(values)
    preact = matmul(low(scaled_norm(normed, gains, biases, 2)), mixer_in[...])
    preact = preact + wide(mixer_bias[...])
    rows, features = values.shape
    linear = preact[:, :features]
    gate = logistic(preact[:, features:])
    linear_out[...] = own_rows(linear, utterances)
    gate_out[...] = own_rows(gate, utterances)
    place, limit = frame_places(info, rows, utterances, HALO)
    mask = flags((place >= 0) & (place < limit))
    gated = low(linear * gate * mask)
    gated_out[...] = gated
    fill_padded(padded, wide(gated), utterances)
    total = None
    for offset in range(KERNEL):
        term = wide(taps[offset : offset + 1, :]) * moved(
            padded, utterances, offset - KERNEL // 2, rows // utterances
        )
        total = term if total is None else total + term
    convolved = total + wide(mixer_vectors[0:1, :])
    convolved_out[...] = convolved
    mask = own_rows(mask, utterances)
    convolved = own_rows(convolved, utterances)
    count = jnp.sum(mask, axis=0, keepdims=True)
    local_sum = jnp.sum(convolved * mask, axis=0, keepdims=True)
    average = local_sum / jnp.maximum(count, 1.0)
    centered = (convolved - average) * mask
    share(
        sums_out,
        [
            local_sum,
            jnp.sum(centered * centered, axis=0, keepdims=True),
            jnp.broadcast_to(count, local_sum.shape),
            average,
        ],
    )


def fill_padded(padded, values, utterances):
    per = values.shape[0] // utterances
    zeros = jnp.zeros((8, values.shape[1]), jnp.float32)
    for u in range(utterances):
        padded[u, 0:8, :] = zeros
        padded[u, 8 : 8 + per, :] = values[u * per : (u + 1) * per, :]
        padded[u, 8 + per : 16 + per, :] = zeros


def moved(padded, utterances, start, per, first=0):
    return jnp.concatenate(
        [
            padded[u, 8 + first + start : 8 + first + start + per, :]
            for u in range(utterances)
        ],
        axis=0,
    )


def share(sums_out, rows):
    rows = rows + [jnp.zeros_like(rows[0])] * (8 - len(rows))
    tile = jnp.concatenate(rows, axis=0)
    for copy in range(sums_out.shape[0] // 8):
        sums_out[copy * 8 : copy * 8 + 8, :] = tile


def shared_totals(values):
    return jnp.sum(values.reshape(-1, 8, values.shape[1]), axis=0)


def middle_kernel(
    utterances,
    convolved,
    shared,
    after,
    grads,
    grad_sides,
    gains,
    biases,
    batch_gain,
    batch_shift,
    running_mean,
    running_variance,
    mixer_out,
    vectors,
    bias_in,
    bias_out,
    feed_in,
    feed_out,
    layer_out,
    grad_mixer_out,
    grad_batch_out,
    normed_out,
    swished_out,
    branch_out,
    hidden_out,
    grad_pre_out,
    active_out,
    grad_low_out,
    sums_out,
    batch_out_rows,
    vector_out,
    weight_in,
    weight_out,
    semaphores,
):
    def own(values):
        return own_rows(values, utterances)

    copies = fetch([(feed_in.at[1], weight_in), (feed_out.at[1], weight_out)], semaphores)
    parts = shared[...]
    totals = shared_totals(parts)
    valid = totals[2:3]
    average = totals[0:1] / valid
    drift = parts - average
    spreads = shared_totals(drift * drift * pltpu.roll(parts, 1, 0))
    variance = (totals[1:2] + spreads[3:4]) / valid
    inverse_batch = lax.rsqrt(variance + EPSILON)
    batch_out_rows[0:1, :] = inverse_batch
    batch_out_rows[1:2, :] = valid
    batch_out_rows[2:3, :] = 0.9 * running_mean[...] + 0.1 * average
    batch_out_rows[3:4, :] = 0.9 * running_variance[...] + 0.1 * variance * valid / (valid - 1.0)
    normed_batch = (convolved[...] - average) * inverse_batch
    normed_out[...] = normed_batch
    batch = normed_batch * wide(batch_gain[...]) + wide(batch_shift[...])
    batch_sigmoid = logistic(batch)
    swished = low(batch * batch_sigmoid)
    swished_out[...] = low(own(batch * batch_sigmoid))
    values = after[...] + matmul(swished, mixer_out[...]) + wide(vectors[1:2, :])
    normed, inverse = normalize(values)
    scaled = scaled_norm(normed, gains, biases, 3)
    hidden_out[...] = low(own(scaled))
    copies[0].wait()
    preact = matmul(low(scaled), weight_in[...]) + wide(bias_in[1:2, :])
    sigmoid = logistic(preact)
    activated = preact * sigmoid
    active = low(activated)
    active_out[...] = low(own(activated))
    copies[1].wait()
    branch = matmul(active, weight_out[...]) + wide(bias_out[1:2, :])
    normed_last, inverse_last = normalize(values + 0.5 * branch)
    layer_out[...] = own(scaled_norm(normed_last, gains, biases, 4))
    grad_second, gain_last, shift_last = norm_back(
        with_sides(grads[...], grad_sides[...], utterances),
        normed_last,
        inverse_last,
        gains,
        4,
        own,
    )
    grad_low = low(0.5 * grad_second)
    grad_low_own = low(own(0.5 * grad_second))
    grad_low_out[...] = grad_low_own
    grad_pre = rows_dot(grad_low, weight_out[...]) * silu_slope(preact, sigmoid)
    grad_pre_own = low(own(grad_pre))
    grad_pre_out[...] = grad_pre_own
    grad_values, gain_three, shift_three = norm_back(
        rows_dot(low(grad_pre), weight_in[...]), normed, inverse, gains, 3, own
    )
    grad_mixer = grad_second + grad_values
    grad_mixer_own = own(grad_mixer)
    grad_mixer_out[...] = grad_mixer_own
    branch_own = low(grad_mixer_own)
    branch_out[...] = branch_own
    grad_batch = rows_dot(low(grad_mixer), mixer_out[...]) * silu_slope(batch, batch_sigmoid)
    grad_batch_out[...] = grad_batch
    share(
        sums_out, [column_sum(own(grad_batch)), column_sum(own(grad_batch * normed_batch))]
    )
    features = grads.shape[1]
    bias_sum = column_sum(grad_pre_own)
    put_rows(
        vector_out,
        [gain_last, shift_last, gain_three, shift_three]
        + [bias_sum[:, i : i + features] for i in range(0, bias_sum.shape[1], features)]
        + [column_sum(grad_low_own), column_sum(branch_own)],
    )


def put_rows(out, rows):
    for number, row in enumerate(rows):
        out[number : number + 1, :] = row
    out[len(rows) :, :] = jnp.zeros((out.shape[0] - len(rows), out.shape[1]), jnp.float32)


def mixer_back_kernel(
    utterances,
    info,
    grad_batch,
    normed_batch,
    shared,
    batch_rows,
    batch_gain,
    gated,
    linear,
    gate,
    grad_mixer,
    after,
    gains,
    biases,
    taps,
    mixer_in,
    attend_out,
    batch_grads_out,
    grad_attend_out,
    hidden_out,
    grad_pre_out,
    branch_out,
    sent_out,
    vector_out,
    padded,
    gated_padded,
):
    totals = shared_totals(shared[...])
    shift_grad, gain_grad = totals[0:1], totals[1:2]
    batch_grads_out[...] = totals
    rows, features = grad_batch.shape
    place, limit = frame_places(info, rows, utterances, HALO)
    mask = flags((place >= 0) & (place < limit))
    inside = flags((place >= 0) & (place < info[utterances + 1]))
    inverse_batch, valid = batch_rows[0:1, :], batch_rows[1:2, :]
    grad_conv = low(
        inside
        * wide(batch_gain[...])
        * inverse_batch
        * (grad_batch[...] - mask / valid * (shift_grad + normed_batch[...] * gain_grad))
    )
    conv_wide = wide(grad_conv)
    fill_padded(padded, conv_wide, utterances)
    fill_padded(gated_padded, wide(gated[...]), utterances)
    conv_own = own_rows(conv_wide, utterances)
    per = rows // utterances - 2 * HALO
    margin = KERNEL // 2
    total = None
    tap_rows = []
    for offset in range(KERNEL):
        term = wide(taps[offset : offset + 1, :]) * moved(
            padded, utterances, margin - offset, per, HALO
        )
        total = term if total is None else total + term
        near = moved(gated_padded, utterances, offset - margin, per, HALO)
        tap_rows.append(jnp.sum(conv_own * near, axis=0, keepdims=True))
    grad_gated = own_rows(mask, utterances) * total
    gate_half = gate[...]
    grad_pre = low(
        jnp.concatenate(
            [
                grad_gated * gate_half,
                grad_gated * linear[...] * gate_half * (1.0 - gate_half),
            ],
            axis=1,
        )
    )
    grad_pre_out[...] = grad_pre
    normed, inverse = normalize(own_rows(after[...], utterances))
    hidden_out[...] = low(scaled_norm(normed, gains, biases, 2))
    grad_values, gain_two, shift_two = norm_back(
        rows_dot(grad_pre, mixer_in[...]), normed, inverse, gains, 2
    )
    grad_attend = grad_mixer[...] + grad_values
    grad_attend_out[...] = grad_attend
    branch = low(grad_attend)
    branch_out[...] = branch
    grad_attended = rows_dot(branch, attend_out[...])
    for head, block in enumerate(blocks_of_heads(grad_attended, utterances)):
        sent_out[head] = low(block)
    bias_sum = column_sum(grad_pre)
    put_rows(
        vector_out,
        [gain_two, shift_two, column_sum(conv_own), column_sum(branch)]
        + [bias_sum[:, :features], bias_sum[:, features:]]
        + tap_rows,
    )


def entry_back_kernel(
    returned,
    grad_attend,
    frames,
    after,
    slope,
    gains,
    biases,
    feed_in,
    feed_out,
    attend_in,
    frames_out,
    hidden_out,
    hidden_two_out,
    query_out,
    key_out,
    value_out,
    grad_pre_out,
    grad_low_out,
    vector_out,
    weight_in,
    weight_out,
    weight_attend,
    semaphores,
):
    copies = fetch(
        [
            (attend_in.at[pl.ds(0, 3)], weight_attend),
            (feed_out.at[0], weight_out),
            (feed_in.at[0], weight_in),
        ],
        semaphores,
    )
    lanes = 2 * HEAD_DIM
    grad_hidden = None
    low_rows = []
    for number, out in enumerate((query_out, key_out, value_out)):
        rows = low(
            rows_of_heads(
                [
                    wide(returned[head, :, number * lanes : (number + 1) * lanes])
                    for head in range(HEADS)
                ]
            )
        )
        out[...] = rows
        low_rows.append(rows)
        if number == 0:
            copies[0].wait()
        term = rows_dot(rows, weight_attend[number])
        grad_hidden = term if grad_hidden is None else grad_hidden + term
    normed, inverse = normalize(after[...])
    hidden_two_out[...] = low(scaled_norm(normed, gains, biases, 1))
    grad_values, gain_one, shift_one = norm_back(grad_hidden, normed, inverse, gains, 1)
    grad_first = grad_attend[...] + grad_values
    grad_low = low(0.5 * grad_first)
    grad_low_out[...] = grad_low
    copies[1].wait()
    grad_pre = low(rows_dot(grad_low, weight_out[...]) * wide(slope[...]))
    grad_pre_out[...] = grad_pre
    normed, inverse = normalize(frames[...])
    hidden_out[...] = low(scaled_norm(normed, gains, biases, 0))
    copies[2].wait()
    grad_values, gain_zero, shift_zero = norm_back(
        rows_dot(grad_pre, weight_in[...]), normed, inverse, gains, 0
    )
    frames_out[...] = grad_first + grad_values
    features = frames.shape[1]
    bias_sum = column_sum(grad_pre)
    put_rows(
        vector_out,
        [gain_zero, shift_zero, gain_one, shift_one]
        + [bias_sum[:, i : i + features] for i in range(0, bias_sum.shape[1], features)]
        + [column_sum(grad_low), column_sum(low_rows[0]), column_sum(low_rows[2])],
    )


def vectors_kernel(
    rows, gain_out, bias_out, in_bias_out, out_bias_out, attend_out, mixer_bias_out, mixer_out, taps_out
):
    middle, mixer, entry, heads = (0, 16, 32, 48)
    features = gain_out.shape[1]

    def take(out, target, start):
        out[target : target + 1, :] = rows[start : start + 1, :]

    for out, first in ((gain_out, 0), (bias_out, 1)):
        take(out, 0, entry + first)
        take(out, 1, entry + 2 + first)
        take(out, 2, mixer + first)
        take(out, 3, middle + 2 + first)
        take(out, 4, middle + first)
    for target, start in ((0, entry + 4), (1, middle + 4)):
        for column in range(4):
            in_bias_out[target : target + 1, column * features : (column + 1) * features] = rows[
                start + column : start + column + 1, :
            ]
    take(out_bias_out, 0, entry + 8)
    take(out_bias_out, 1, middle + 8)
    for target, start in enumerate((entry + 9, entry + 10, mixer + 3, heads, heads + 1)):
        take(attend_out, target, start)
    for column in range(2):
        mixer_bias_out[0:1, column * features : (column + 1) * features] = rows[
            mixer + 4 + column : mixer + 5 + column, :
        ]
    take(mixer_out, 0, mixer + 2)
    take(mixer_out, 1, middle + 9)
    taps_out[...] = rows[mixer + 6 : mixer + 6 + KERNEL, :]


def axis_bits(axis):
    return [(axis, 1 << bit) for bit in range(lax.axis_size(axis).bit_length() - 1)]


def swap(values, step):
    axis, mask = step
    return lax.ppermute(values, axis, [(i, i ^ mask) for i in range(lax.axis_size(axis))])


def side(step):
    axis, mask = step
    return (lax.axis_index(axis) // mask) % 2


def swap_all(stripes, steps):
    return [swap(rows, step) for rows, step in zip(stripes, steps)]


def add_low(first_operand, second_operand):
    total = first_operand.astype(jnp.float32) + second_operand.astype(jnp.float32)
    return total.astype(jnp.bfloat16)


def pieces_of(rows):
    return 4 if rows >= 512 else 2 if rows >= 256 else 1


def fold_kernel(stripes, sides, *refs):
    for number in range(2 * stripes):
        own, other = refs[2 * number], refs[2 * number + 1]
        refs[4 * stripes + number][...] = add_low(own[...], other[...])


def fold_rows(kept, arrived, steps):
    halves = [rows.shape[0] // 2 for rows in kept]
    if any(half % 16 for half in halves):
        sent, keeps = [], []
        for own, other, step, half in zip(kept, arrived, steps, halves):
            for start, results in (((1 - side(step)) * half, sent), (side(step) * half, keeps)):
                results.append(
                    add_low(
                        *(lax.dynamic_slice_in_dim(rows, start, half, 0) for rows in (own, other))
                    )
                )
        return sent, keeps
    chunks = pieces_of(max(halves))
    in_specs, out_specs, shapes, operands = [], [], [], []

    def block(half, stripe, keeping):
        def index(i, sides):
            half_index = sides[stripe] if keeping else 1 - sides[stripe]
            return (half_index * chunks + i, 0)

        return pl.BlockSpec((half // chunks, 512), index)

    for stripe, (own, other, half) in enumerate(zip(kept, arrived, halves)):
        for keeping in (False, True):
            in_specs += [block(half, stripe, keeping)] * 2
            operands += [own, other]
            out_specs.append(pl.BlockSpec((half // chunks, 512), lambda i, sides: (i, 0)))
            shapes.append(jax.ShapeDtypeStruct((half, 512), jnp.bfloat16))
    results = pl.pallas_call(
        functools.partial(fold_kernel, len(kept)),
        grid_spec=pltpu.PrefetchScalarGridSpec(
            num_scalar_prefetch=1, grid=(chunks,), in_specs=in_specs, out_specs=out_specs
        ),
        out_shape=shapes,
        compiler_params=pltpu.CompilerParams(vmem_limit_bytes=VMEM_LIMIT),
        cost_estimate=pl.CostEstimate(
            flops=0, bytes_accessed=6 * 1024 * sum(halves), transcendentals=0
        ),
    )(jnp.stack([side(step) for step in steps]), *operands)
    return list(results[::2]), list(results[1::2])


def add_kernel(stripes, *refs):
    for number in range(stripes):
        refs[2 * stripes + number][...] = add_low(refs[2 * number][...], refs[2 * number + 1][...])


def add_rows(kept, arrived):
    if any(rows.shape[0] % 16 for rows in kept):
        return [add_low(*pair) for pair in zip(kept, arrived)]
    vmem = pl.BlockSpec(memory_space=pltpu.VMEM)
    return list(
        pl.pallas_call(
            functools.partial(add_kernel, len(kept)),
            in_specs=[vmem] * (2 * len(kept)),
            out_specs=[vmem] * len(kept),
            out_shape=[jax.ShapeDtypeStruct(rows.shape, rows.dtype) for rows in kept],
        )(*(rows for pair in zip(kept, arrived) for rows in pair))
    )


def join_kernel(chunks, stripes, sides, *refs):
    place = pl.program_id(0)
    for number in range(stripes):
        own, other, out = refs[2 * number], refs[2 * number + 1], refs[2 * stripes + number]

        @pl.when(place // chunks == sides[number])
        def _():
            out[...] = own[...]

        @pl.when(place // chunks != sides[number])
        def _():
            out[...] = other[...]


def join_rows(stripes, arrived, steps):
    halves = [rows.shape[0] for rows in stripes]
    if any(half % 16 for half in halves):
        joined = []
        for rows, other, step in zip(stripes, arrived, steps):
            first = side(step) == 0
            joined.append(
                jnp.concatenate(
                    [jnp.where(first, rows, other), jnp.where(first, other, rows)], axis=0
                )
            )
        return joined
    chunks = pieces_of(max(halves))

    def block(half, stripe, ours):
        def index(i, sides):
            offset = sides[stripe] if ours else 1 - sides[stripe]
            return (jnp.clip(i - offset * chunks, 0, chunks - 1), 0)

        return pl.BlockSpec((half // chunks, 512), index)

    in_specs, out_specs, shapes, operands = [], [], [], []
    for stripe, (rows, other, half) in enumerate(zip(stripes, arrived, halves)):
        in_specs += [block(half, stripe, True), block(half, stripe, False)]
        operands += [rows, other]
        out_specs.append(pl.BlockSpec((half // chunks, 512), lambda i, sides: (i, 0)))
        shapes.append(jax.ShapeDtypeStruct((2 * half, 512), jnp.bfloat16))
    return list(
        pl.pallas_call(
            functools.partial(join_kernel, chunks, len(stripes)),
            grid_spec=pltpu.PrefetchScalarGridSpec(
                num_scalar_prefetch=1, grid=(2 * chunks,), in_specs=in_specs, out_specs=out_specs
            ),
            out_shape=shapes,
            compiler_params=pltpu.CompilerParams(vmem_limit_bytes=VMEM_LIMIT),
            cost_estimate=pl.CostEstimate(
                flops=0, bytes_accessed=4 * 1024 * sum(halves), transcendentals=0
            ),
        )(jnp.stack([side(step) for step in steps]), *operands)
    )


def tie(*groups):
    return lax.optimization_barrier(groups)


def summing(sent, kept, phases):
    arrived = swap_all(sent, phases[0])
    for steps in phases[1:]:
        arrived = yield arrived
        sent, kept = fold_rows(kept, arrived, steps)
        arrived = swap_all(sent, steps)
    arrived = yield arrived
    rows = add_rows(kept, arrived)
    for steps in phases[:0:-1]:
        arrived = yield swap_all(rows, steps)
        rows = join_rows(rows, arrived, steps)
    arrived = yield swap_all(rows, phases[0])
    return rows, arrived


class Background:
    def __init__(self, sent, kept, phases):
        self.work = summing(sent, kept, phases)
        self.pending = next(self.work)
        self.result = None

    def advance(self, arrived):
        try:
            self.pending = self.work.send(arrived)
        except StopIteration as ended:
            self.result = ended.value

    def tick(self, *others):
        others, arrived = tie(others, self.pending)
        self.advance(arrived)
        return others


def step_orders():
    utt, seq = axis_bits("utt"), axis_bits("seq")
    near, across, line = utt[:1], utt[1:], seq[:1]
    rest = seq[1:]
    return (
        near + line + across + rest,
        near + across + line + rest[::-1],
        near + rest + line + across,
    )


def all_shared(copies):
    return lax.all_to_all(copies, ("utt", "seq"), 0, 0, tiled=True)


def from_neighbours(head, tail):
    count = lax.axis_size("seq")
    before = lax.ppermute(tail, "seq", [(i, i + 1) for i in range(count - 1)])
    behind = lax.ppermute(head, "seq", [(i + 1, i) for i in range(count - 1)])
    return before, behind


def outer_kernel(plan, cuts, inputs, core, *refs):
    outs = refs[inputs:]
    turned = {}

    def store(owner, start, value):
        for stripe, (low, high) in enumerate(zip(cuts[:-1], cuts[1:])):
            first, last = max(start, low), min(start + value.shape[0], high)
            if first >= last:
                continue
            piece = value[first - start : last - start]

            @pl.when(core[0] == owner)
            def _():
                outs[2 * stripe + 1][first - low : last - low, :] = piece

            @pl.when(core[0] != owner)
            def _():
                outs[2 * stripe][first - low : last - low, :] = piece

    for owner, start, left, left_col, right, right_col in plan:
        if right is None:
            value = refs[left][left_col[0] : left_col[1], :]
        else:
            if (left, left_col) not in turned:
                turned[left, left_col] = refs[left][:, left_col * 512 : (left_col + 1) * 512].T
            value = jnp.dot(
                turned[left, left_col],
                refs[right][:, right_col * 512 : (right_col + 1) * 512],
                preferred_element_type=jnp.float32,
            ).astype(jnp.bfloat16)
        store(owner, start, value)


def outer_blocks(core, members, plan, cuts):
    members = [member.reshape(-1, member.shape[-1]) for member in members]
    shapes = [
        jax.ShapeDtypeStruct((high - low, 512), jnp.bfloat16)
        for low, high in zip(cuts[:-1], cuts[1:])
        for _ in range(2)
    ]
    vmem = pl.BlockSpec(memory_space=pltpu.VMEM)
    results = pl.pallas_call(
        functools.partial(outer_kernel, plan, cuts, len(members)),
        in_specs=[pl.BlockSpec(memory_space=pltpu.SMEM)] + [vmem] * len(members),
        out_specs=[vmem] * len(shapes),
        out_shape=shapes,
        compiler_params=pltpu.CompilerParams(vmem_limit_bytes=VMEM_LIMIT),
        cost_estimate=pl.CostEstimate(
            flops=2 * 512 * 512 * 256 * len(plan),
            bytes_accessed=2 * 512 * 512 * len(plan),
            transcendentals=0,
        ),
    )(core, *members)
    return list(results[::2]), list(results[1::2])


def spread_kernel(steps, pieces, spare, table, *refs):
    place = pl.program_id(0)
    first_out = pieces + spare
    for number, (sources, target) in enumerate(steps):

        @pl.when(place == number)
        def _():
            out = refs[first_out + target]
            value = refs[sources[0]][...]
            if len(sources) > 1:
                value = jnp.where(table[table.shape[0] - 1, 0] == 0, value, refs[sources[1]][...])
            out[...] = value.astype(jnp.float32).reshape(out.shape)


def spread_blocks(core, pieces, height, outputs, steps, bases):
    tables = []
    for bit in range(2):
        table = np.zeros((len(pieces) + len(outputs) + 1, len(steps)), np.int32)
        for row in range(len(pieces) + len(outputs)):
            known = None
            for column, (sources, block, target, *places) in enumerate(steps):
                if row in sources:
                    known = block
                elif row == len(pieces) + target:
                    known = places[bit]
                if known is not None:
                    table[row, column] = known
            used = [
                column
                for column, (sources, _, target, *_) in enumerate(steps)
                if row in sources or row == len(pieces) + target
            ]
            table[row, : used[0]] = table[row, used[0]]
        table[-1] = bit
        tables.append(table)
    table = jnp.where(core == 0, tables[0], tables[1])

    def piece_spec(row):
        return pl.BlockSpec((height, 512), lambda i, table: (table[row, i], 0))

    def out_spec(row, block, index):
        return pl.BlockSpec(block, lambda i, table: index(table[row, i]))

    spare = [base for base in bases if base is not None]
    aliases = {}
    for number, base in enumerate(bases):
        if base is not None:
            aliases[1 + len(pieces) + len(aliases)] = number
    return pl.pallas_call(
        functools.partial(
            spread_kernel, [(step[0], step[2]) for step in steps], len(pieces), len(spare)
        ),
        grid_spec=pltpu.PrefetchScalarGridSpec(
            num_scalar_prefetch=1,
            grid=(len(steps),),
            in_specs=[piece_spec(row) for row in range(len(pieces))]
            + [pl.BlockSpec(memory_space=pl.ANY)] * len(spare),
            out_specs=[
                out_spec(len(pieces) + number, block, index)
                for number, (_, block, index) in enumerate(outputs)
            ],
        ),
        out_shape=[jax.ShapeDtypeStruct(shape, jnp.float32) for shape, _, _ in outputs],
        input_output_aliases=aliases,
        compiler_params=pltpu.CompilerParams(vmem_limit_bytes=VMEM_LIMIT),
        cost_estimate=pl.CostEstimate(
            flops=0, bytes_accessed=6 * height * 512 * len(steps), transcendentals=0
        ),
    )(table, *pieces, *spare)


def angle_tables(frame_count, features):
    halves = jnp.arange(features // 2, dtype=jnp.int32).astype(jnp.float32)
    frequencies = jnp.exp(halves * (-2.0 * math.log(10000.0) / features))
    fine = 32
    low_angles = jnp.arange(fine, dtype=jnp.int32).astype(jnp.float32)[:, None] * frequencies
    high_angles = (fine * jnp.arange(frame_count // fine, dtype=jnp.int32)).astype(jnp.float32)[
        :, None
    ] * frequencies
    low_sin, low_cos = jnp.sin(low_angles)[None], jnp.cos(low_angles)[None]
    high_sin, high_cos = jnp.sin(high_angles)[:, None], jnp.cos(high_angles)[:, None]
    sines = high_sin * low_cos + high_cos * low_sin
    cosines = high_cos * low_cos - high_sin * low_sin
    shape = (frame_count, features // 2)
    return sines.reshape(shape), cosines.reshape(shape)


def heads_out(blocks, groups):
    return lax.all_to_all(jnp.tile(blocks, (groups, 1, 1)), "seq", 0, 0, tiled=True)


def rows_dot(first_operand, second_operand):
    return lax.dot_general(
        first_operand, second_operand, (((1,), (1,)), ((), ())), preferred_element_type=jnp.float32
    )


def lane_side(shape, utterance):
    return (lax.broadcasted_iota(jnp.int32, shape, 1) // HEAD_DIM) == utterance


def turned_queries(content, shift, weight, sines, cosines):
    offset = (content.astype(jnp.float32) + shift).astype(jnp.bfloat16)
    half = sines.shape[1]
    spread = jnp.dot(offset, weight, preferred_element_type=jnp.float32)
    sin_part, cos_part = spread[:, :half], spread[:, half:]
    return (
        offset,
        (sin_part * sines + cos_part * cosines).astype(jnp.bfloat16),
        (cos_part * sines - sin_part * cosines).astype(jnp.bfloat16),
    )


def attend_kernel(
    limits,
    content,
    keys,
    values,
    shift,
    weight,
    sines,
    cosines,
    table,
    weights_out,
    attended_out,
    held,
):
    scale = HEAD_DIM ** (-0.5)
    content_rows = content[...]
    key_side = jnp.concatenate([table[...], keys[...]], axis=1)
    places = lax.broadcasted_iota(jnp.int32, (1, table.shape[0]), 1)
    attended = None
    for utterance in range(limits.shape[0]):
        ours = lane_side(content_rows.shape, utterance)
        mine = jnp.where(ours, content_rows, jnp.zeros_like(content_rows))
        moved = jnp.where(ours, shift[...], 0.0)
        _, turned_cos, turned_sin = turned_queries(
            mine, moved, weight[...], sines[...], cosines[...]
        )
        query_side = jnp.concatenate([turned_cos, turned_sin, mine], axis=1) * scale
        scores = rows_dot(query_side.astype(jnp.bfloat16), key_side)
        scores = jnp.where(places < limits[utterance], scores, -1000000000.0)
        raised = jnp.exp(scores - jnp.max(scores, axis=1, keepdims=True))
        totals = jnp.sum(raised, axis=1, keepdims=True)
        weights = (raised * (1.0 / totals)).astype(jnp.bfloat16)
        weights_out[utterance] = weights
        part = jnp.dot(weights, values[...], preferred_element_type=jnp.float32)
        attended = part if attended is None else jnp.where(ours, part, attended)
    if held is None:
        attended_out[...] = attended.astype(jnp.bfloat16)
        return
    step = pl.program_id(0)
    height = attended.shape[0]
    block = attended_out.shape[1] - 2 * HALO
    held[pl.ds(pl.multiple_of(HALO + step * height, 8), height), :] = attended
    for number in range(height // block):
        attended_out[step * (height // block) + number, 0:block, :] = attended[
            number * block : (number + 1) * block
        ].astype(jnp.bfloat16)

    @pl.when(step == pl.num_programs(0) - 1)
    def _():
        edge = jnp.zeros((HALO, held.shape[1]), jnp.float32)
        held[0:HALO, :] = edge
        held[held.shape[0] - HALO :, :] = edge
        for number in range(attended_out.shape[0]):
            start = number * block
            sides = jnp.concatenate(
                [
                    held[start : start + HALO, :],
                    held[start + HALO + block : start + 2 * HALO + block, :],
                ],
                axis=0,
            )
            attended_out[number, block:, :] = sides.astype(jnp.bfloat16)


def attend_back_kernel(
    weights,
    content,
    grads,
    keys,
    values,
    shift,
    weight,
    sines,
    cosines,
    table,
    *outs,
):
    step = pl.program_id(0)
    query_out, pairs_out, weight_out, sums_out, key_sums, value_sums = (None,) * (
        6 - len(outs)
    ) + outs
    scale = HEAD_DIM ** (-0.5)

    @pl.when(step == 0)
    def _():
        key_sums[...] = jnp.zeros_like(key_sums)
        value_sums[...] = jnp.zeros_like(value_sums)
        weight_out[...] = jnp.zeros_like(weight_out)
        sums_out[...] = jnp.zeros_like(sums_out)

    content_rows, grad_rows = content[...], grads[...]
    content_cols = content_rows.T
    grad_cols = grad_rows.T
    key_side = jnp.concatenate([table[...], keys[...]], axis=1)
    half = sines.shape[1]
    grad_content = grad_position = None
    for utterance in range(weights.shape[0]):
        low, high = utterance * HEAD_DIM, (utterance + 1) * HEAD_DIM
        ours = lane_side(content_rows.shape, utterance)
        probs = weights[utterance]
        wide = probs.astype(jnp.float32)
        grad_mine = jnp.where(ours, grad_rows, jnp.zeros_like(grad_rows)) * scale
        grad_probs = rows_dot(grad_mine.astype(jnp.bfloat16), values[...])
        product = wide * grad_probs
        inner = jnp.sum(product, axis=1, keepdims=True)
        grad_scores = (product - wide * inner).astype(jnp.bfloat16)
        value_sums[low:high, :] += jnp.dot(
            grad_cols[low:high, :], probs, preferred_element_type=jnp.float32
        )
        key_sums[low:high, :] += jnp.dot(
            content_cols[low:high, :], grad_scores, preferred_element_type=jnp.float32
        )
        grad_side = jnp.dot(grad_scores, key_side, preferred_element_type=jnp.float32)
        grad_cos_table = grad_side[:, :half]
        grad_sin_table = grad_side[:, half : 2 * half]
        from_table = jnp.concatenate(
            [
                grad_cos_table * sines[...] - grad_sin_table * cosines[...],
                grad_cos_table * cosines[...] + grad_sin_table * sines[...],
            ],
            axis=1,
        ).astype(jnp.bfloat16)
        offset = (content_rows.astype(jnp.float32) + shift[...]).astype(jnp.bfloat16)
        weight_out[...] += jnp.dot(
            offset.T[low:high, :], from_table, preferred_element_type=jnp.float32
        )
        content_part = grad_side[:, 2 * half :]
        position_part = rows_dot(from_table, weight[...])
        if grad_content is None:
            grad_content, grad_position = content_part, position_part
        else:
            grad_content = jnp.where(ours, content_part, grad_content)
            grad_position = jnp.where(ours, position_part, grad_position)
    grad_query = (grad_content + grad_position).astype(jnp.bfloat16)
    height, lanes = grad_query.shape
    if query_out is None:
        pairs_out[pl.ds(pl.multiple_of(step * height, 16), height), 0:lanes] = grad_query
    else:
        query_out[...] = grad_query
    sums_out[0:1, :] += jnp.sum(grad_content, axis=0, keepdims=True)
    sums_out[1:2, :] += jnp.sum(grad_position, axis=0, keepdims=True)

    @pl.when(step == pl.num_programs(0) - 1)
    def _():
        first = pairs_out.shape[1] - 2 * lanes
        pairs_out[:, first : first + lanes] = key_sums[...].T.astype(jnp.bfloat16)
        pairs_out[:, first + lanes :] = value_sums[...].T.astype(jnp.bfloat16)


def query_block(frames_all):
    return 256 if frames_all <= 1024 else 128


def whole_block(shape):
    return pl.BlockSpec(shape, lambda i: (0,) * len(shape))


def row_block(height, width):
    return pl.BlockSpec((height, width), lambda i: (i, 0))


def attend_heads(limits, content, arrived, shift, weight, sines, cosines, table, block):
    utterances = limits.shape[0]
    query_frames, lanes = content.shape[0], arrived.shape[1] // 3
    frames_all, table_width = table.shape
    height = query_block(frames_all)
    chunked = query_frames == frames_all and height % block == 0
    chunks = (frames_all // block, block + 2 * HALO, lanes)
    kernel = attend_kernel
    if not chunked:
        kernel = functools.partial(attend_kernel, held=None)
    return pl.pallas_call(
        kernel,
        grid=(query_frames // height,),
        in_specs=[
            pl.BlockSpec(memory_space=pltpu.SMEM),
            row_block(height, lanes),
            pl.BlockSpec((frames_all, lanes), lambda i: (0, 1)),
            pl.BlockSpec((frames_all, lanes), lambda i: (0, 2)),
            whole_block(shift.shape),
            whole_block(weight.shape),
            row_block(height, sines.shape[1]),
            row_block(height, sines.shape[1]),
            whole_block(table.shape),
        ],
        out_specs=[
            pl.BlockSpec((utterances, height, frames_all), lambda i: (0, i, 0)),
            whole_block(chunks) if chunked else row_block(height, lanes),
        ],
        out_shape=[
            jax.ShapeDtypeStruct((utterances, query_frames, frames_all), jnp.bfloat16),
            jax.ShapeDtypeStruct(chunks if chunked else (query_frames, lanes), jnp.bfloat16),
        ],
        scratch_shapes=[pltpu.VMEM((frames_all + 2 * HALO, lanes), jnp.float32)] * chunked,
        compiler_params=pltpu.CompilerParams(vmem_limit_bytes=VMEM_LIMIT),
        cost_estimate=pl.CostEstimate(
            flops=2 * utterances * query_frames * frames_all * (table_width + 256),
            bytes_accessed=2 * utterances * query_frames * frames_all,
            transcendentals=utterances * query_frames * frames_all,
        ),
    )(limits, content, arrived, arrived, shift, weight, sines, cosines, table)


def attend_heads_back(
    weights, content, grads, arrived, shift, weight, sines, cosines, table
):
    utterances, query_frames, frames_all = weights.shape
    lanes = arrived.shape[1] // 3
    height = query_block(frames_all)
    joined = query_frames == frames_all
    width = (3 if joined else 2) * lanes
    return pl.pallas_call(
        attend_back_kernel,
        grid=(query_frames // height,),
        in_specs=[
            pl.BlockSpec((utterances, height, frames_all), lambda i: (0, i, 0)),
            row_block(height, lanes),
            row_block(height, lanes),
            pl.BlockSpec((frames_all, lanes), lambda i: (0, 1)),
            pl.BlockSpec((frames_all, lanes), lambda i: (0, 2)),
            whole_block(shift.shape),
            whole_block(weight.shape),
            row_block(height, sines.shape[1]),
            row_block(height, sines.shape[1]),
            whole_block(table.shape),
        ],
        out_specs=([] if joined else [row_block(height, lanes)])
        + [
            whole_block((frames_all, width)),
            whole_block((HEAD_DIM, table.shape[1])),
            whole_block((8, lanes)),
        ],
        out_shape=(
            [] if joined else [jax.ShapeDtypeStruct((query_frames, lanes), jnp.bfloat16)]
        )
        + [
            jax.ShapeDtypeStruct((frames_all, width), jnp.bfloat16),
            jax.ShapeDtypeStruct((HEAD_DIM, table.shape[1]), jnp.float32),
            jax.ShapeDtypeStruct((8, lanes), jnp.float32),
        ],
        scratch_shapes=[
            pltpu.VMEM((lanes, frames_all), jnp.float32),
            pltpu.VMEM((lanes, frames_all), jnp.float32),
        ],
        compiler_params=pltpu.CompilerParams(vmem_limit_bytes=VMEM_LIMIT),
        cost_estimate=pl.CostEstimate(
            flops=2 * utterances * query_frames * frames_all * (table.shape[1] + 512),
            bytes_accessed=2 * utterances * query_frames * frames_all,
            transcendentals=0,
        ),
    )(weights, content, grads, arrived, arrived, shift, weight, sines, cosines, table)


def shards(
    frames,
    lengths,
    out_grad,
    norm_gain,
    norm_bias,
    feed_in,
    feed_in_bias,
    feed_out,
    feed_out_bias,
    attend_in,
    attend_vectors,
    attend_out,
    mixer_in,
    mixer_in_bias,
    depthwise,
    mixer_vectors,
    mixer_out,
    batch_gain,
    batch_shift,
    running_mean,
    running_variance,
):
    utt_rows, block_frames, features = frames.shape
    rows = utt_rows * block_frames
    seq_count = lax.axis_size("seq")
    seq_index = lax.axis_index("seq")
    count = lax.axis_size("utt") * seq_count
    frames_all = block_frames * seq_count
    groups = seq_count // HEADS
    head, group = seq_index % HEADS, seq_index // HEADS
    query_frames = frames_all // groups
    lanes = utt_rows * HEAD_DIM
    info = jnp.concatenate(
        [(seq_index * block_frames).reshape(1), lengths, jnp.full((1,), frames_all, jnp.int32)]
    )
    hidden_units = feed_in.shape[2]
    f32, bf16 = jnp.float32, jnp.bfloat16
    flat_frames = frames.reshape(rows, features)
    square, broad = (rows, features), (rows, hidden_units)
    extended = (utt_rows * (block_frames + 2 * HALO), features)
    row_flops = 2 * rows * features
    bind = functools.partial
    before, behind = from_neighbours(
        jnp.concatenate([frames[:, :HALO], out_grad[:, :HALO]], axis=1),
        jnp.concatenate([frames[:, -HALO:], out_grad[:, -HALO:]], axis=1),
    )
    feed_scratch = [
        pltpu.VMEM((features, hidden_units), bf16),
        pltpu.VMEM((hidden_units, features), bf16),
    ]
    attend_scratch = pltpu.VMEM((3, features, features), bf16)
    after_first, slope_first, active_first, sent = vmem_call(
        bind(entry_kernel, utt_rows),
        [(square, f32), (broad, bf16), (broad, bf16), ((HEADS, block_frames, 3 * lanes), bf16)],
        (),
        (flat_frames, norm_gain, norm_bias, feed_in_bias, feed_out_bias, attend_vectors),
        scratch=feed_scratch + [attend_scratch, pltpu.SemaphoreType.DMA((3,))],
        cost=row_flops * (2 * hidden_units + 3 * features),
        held=(feed_in, feed_out, attend_in),
    )
    frame_sides, grad_sides = (
        jnp.stack([before[:, part], behind[:, part]], axis=1).reshape(
            2 * utt_rows * HALO, features
        )
        for part in (slice(0, HALO), slice(HALO, 2 * HALO))
    )
    (after_sides,) = vmem_call(
        sides_kernel,
        [(frame_sides.shape, f32)],
        (),
        (frame_sides, norm_gain, norm_bias, feed_in_bias, feed_out_bias),
        scratch=feed_scratch + [pltpu.SemaphoreType.DMA((2,))],
        cost=row_flops * 2 * hidden_units // 4,
        held=(feed_in, feed_out),
    )
    arrived = heads_out(sent, groups).reshape(frames_all, 3 * lanes)
    start_query = group * query_frames
    head_content = arrived
    if groups > 1:
        head_content = lax.dynamic_slice_in_dim(arrived, start_query, query_frames, 0)
    head_vectors = lax.dynamic_slice_in_dim(
        attend_vectors.astype(f32), head * HEAD_DIM, HEAD_DIM, 1
    )
    head_shift = jnp.tile((head_vectors[4] - head_vectors[3])[None], (1, utt_rows))
    head_weight = lax.dynamic_slice_in_dim(attend_in[3], head * HEAD_DIM, HEAD_DIM, 1).reshape(
        features // 2, 2, HEAD_DIM
    )
    head_weight = jnp.tile(
        jnp.transpose(head_weight, (2, 1, 0)).reshape(HEAD_DIM, features), (utt_rows, 1)
    )
    sines, cosines = angle_tables(frames_all, features)
    key_table = jnp.concatenate([cosines, sines], axis=1).astype(bf16)
    query_sin = lax.dynamic_slice_in_dim(sines, start_query, query_frames, 0)
    query_cos = lax.dynamic_slice_in_dim(cosines, start_query, query_frames, 0)
    weights, head_attended = attend_heads(
        lengths,
        head_content,
        arrived,
        head_shift,
        head_weight,
        query_sin,
        query_cos,
        key_table,
        block_frames,
    )

    def frames_back(blocks):
        width = blocks.shape[-1]
        blocks = blocks.reshape(1, HEADS, block_frames, width)
        if groups > 1:
            blocks = lax.dynamic_update_slice_in_dim(
                jnp.zeros((groups,) + blocks.shape[1:], blocks.dtype), blocks, group, 0
            )
        blocks = lax.all_to_all(
            blocks.reshape(seq_count, block_frames, width), "seq", 0, 0, tiled=True
        ).reshape(groups, HEADS, block_frames, width)
        return lax.dynamic_slice_in_dim(blocks, group, 1, 0)[0]

    if head_attended.ndim == 2:
        placed = lax.dynamic_update_slice_in_dim(
            jnp.zeros((frames_all + 2 * HALO, lanes), bf16), head_attended, HALO + start_query, 0
        )
        main, before, behind = (
            placed[start : start + frames_all].reshape(seq_count, block_frames, lanes)
            for start in (HALO, 0, 2 * HALO)
        )
        head_attended = jnp.concatenate([main, before[:, :HALO], behind[:, -HALO:]], axis=1)
    attended_blocks = lax.all_to_all(head_attended, "seq", 0, 0, tiled=True)
    if groups > 1:
        attended_blocks = jnp.sum(
            attended_blocks.reshape((groups, HEADS) + attended_blocks.shape[1:]), axis=0
        )
    taps = depthwise.T
    padded = pltpu.VMEM((utt_rows, block_frames + 2 * HALO + 16, features), f32)
    (
        after_attend,
        attended_low,
        linear_half,
        gate_half,
        gated,
        convolved,
        shared,
    ) = vmem_call(
        bind(mixer_kernel, utt_rows),
        [
            (extended, f32),
            (square, bf16),
            (square, f32),
            (square, f32),
            (extended, bf16),
            (extended, f32),
            ((8 * count, features), f32),
        ],
        (info,),
        (
            attended_blocks,
            after_first,
            after_sides,
            norm_gain,
            norm_bias,
            attend_out,
            attend_vectors,
            mixer_in,
            mixer_in_bias.reshape(1, -1),
            taps,
            mixer_vectors,
        ),
        scratch=(padded,),
        cost=row_flops * 3 * features,
    )
    (
        layer_output,
        grad_mixer,
        grad_batch,
        normed_batch,
        swished,
        grad_branch,
        hidden_second,
        grad_pre_second,
        active_second,
        grad_low_second,
        shared,
        batch_rows,
        middle_rows,
    ) = vmem_call(
        bind(middle_kernel, utt_rows),
        [
            (square, f32),
            (square, f32),
            (extended, f32),
            (extended, f32),
            (square, bf16),
            (square, bf16),
            (square, bf16),
            (broad, bf16),
            (broad, bf16),
            (square, bf16),
            ((8 * count, features), f32),
            ((8, features), f32),
            ((16, features), f32),
        ],
        (),
        (
            convolved,
            all_shared(shared),
            after_attend,
            out_grad.reshape(rows, features),
            grad_sides,
            norm_gain,
            norm_bias,
            batch_gain.reshape(1, -1),
            batch_shift.reshape(1, -1),
            running_mean.reshape(1, -1),
            running_variance.reshape(1, -1),
            mixer_out,
            mixer_vectors,
            feed_in_bias,
            feed_out_bias,
        ),
        scratch=feed_scratch + [pltpu.SemaphoreType.DMA((2,))],
        cost=row_flops * (4 * hidden_units + 2 * features),
        held=(feed_in, feed_out),
    )
    phases = list(zip(*step_orders()))
    core = side(phases[0][0]).reshape(1)
    shared = all_shared(shared)
    second_sent, second_kept = outer_blocks(
        core,
        [hidden_second, grad_pre_second, active_second, grad_low_second],
        [
            (owner, start, *source)
            for owner in range(2)
            for start, source in (
                (0, (0, 0, 1, 2 * owner)),
                (512, (0, 0, 1, 2 * owner + 1)),
                (1024, (2, 2 * owner, 3, 0)),
                (1536, (2, 2 * owner + 1, 3, 0)),
            )
        ],
        (0, 768, 1536, 2048),
    )
    second_sum = Background(second_sent, second_kept, phases)
    (grad_batch,) = second_sum.tick(grad_batch)
    (
        batch_grads,
        grad_attend,
        hidden_three,
        grad_mixer_pre,
        grad_branch_two,
        grad_blocks,
        mixer_rows,
    ) = vmem_call(
        bind(mixer_back_kernel, utt_rows),
        [
            ((8, features), f32),
            (square, f32),
            (square, bf16),
            ((rows, 2 * features), bf16),
            (square, bf16),
            ((HEADS, block_frames, lanes), bf16),
            ((16, features), f32),
        ],
        (info,),
        (
            grad_batch,
            normed_batch,
            shared,
            batch_rows,
            batch_gain.reshape(1, -1),
            gated,
            linear_half,
            gate_half,
            grad_mixer,
            after_attend,
            norm_gain,
            norm_bias,
            taps,
            mixer_in,
            attend_out,
        ),
        scratch=(padded, padded),
        cost=row_flops * 4 * features,
    )
    (grad_blocks,) = second_sum.tick(grad_blocks)
    head_grad = heads_out(grad_blocks, groups).reshape(frames_all, lanes)
    if groups > 1:
        head_grad = lax.dynamic_slice_in_dim(head_grad, start_query, query_frames, 0)
    (head_grad,) = second_sum.tick(head_grad)
    *head_grads, head_weight_grad, head_sums = attend_heads_back(
        weights,
        head_content,
        head_grad,
        arrived,
        head_shift,
        head_weight,
        query_sin,
        query_cos,
        key_table,
    )
    head_grads, head_weight_grad, head_sums = second_sum.tick(
        head_grads, head_weight_grad, head_sums
    )
    returned = lax.all_to_all(
        head_grads[-1].reshape(seq_count, block_frames, -1), "seq", 0, 0, tiled=True
    )
    if groups > 1:
        returned = jnp.sum(
            returned.astype(f32).reshape(groups, HEADS, block_frames, 2 * lanes), axis=0
        ).astype(bf16)
        returned = jnp.concatenate([frames_back(head_grads[0]), returned], axis=2)
    head_weight_grad = jnp.transpose(
        head_weight_grad.reshape(HEAD_DIM, 2, features // 2), (2, 1, 0)
    ).reshape(features, HEAD_DIM)
    position_weight_grad = lax.dynamic_update_slice_in_dim(
        jnp.zeros((features, features), f32), head_weight_grad, head * HEAD_DIM, 1
    )
    head_vector_grads = lax.dynamic_update_slice_in_dim(
        jnp.zeros((8, features), f32),
        jnp.sum(head_sums.reshape(8, utt_rows, HEAD_DIM), axis=1),
        head * HEAD_DIM,
        1,
    )
    second_sum.advance(second_sum.pending)
    (returned,) = second_sum.tick(returned)
    (
        frames_grad,
        hidden_first,
        hidden_two,
        query_low,
        key_low,
        value_low,
        grad_pre_first,
        grad_low_first,
        entry_rows,
    ) = vmem_call(
        entry_back_kernel,
        [
            (square, f32),
            (square, bf16),
            (square, bf16),
            (square, bf16),
            (square, bf16),
            (square, bf16),
            (broad, bf16),
            (square, bf16),
            ((16, features), f32),
        ],
        (),
        (
            returned,
            grad_attend,
            flat_frames,
            after_first,
            slope_first,
            norm_gain,
            norm_bias,
        ),
        scratch=feed_scratch + [attend_scratch, pltpu.SemaphoreType.DMA((3,))],
        cost=row_flops * (2 * hidden_units + 3 * features),
        held=(feed_in, feed_out, attend_in),
    )
    grad_pre_first, grad_low_first = second_sum.tick(grad_pre_first, grad_low_first)
    flat = jnp.concatenate([middle_rows, mixer_rows, entry_rows, head_vector_grads], axis=0)
    members = [
        hidden_first,
        grad_pre_first,
        active_first,
        grad_low_first,
        hidden_two,
        query_low,
        key_low,
        value_low,
        position_weight_grad.astype(jnp.bfloat16),
        hidden_three,
        grad_mixer_pre,
        swished,
        grad_branch,
        attended_low,
        grad_branch_two,
    ]
    plan = []
    for owner in range(2):
        plan += [
            (owner, 0, 0, 0, 1, 2 * owner),
            (owner, 512, 0, 0, 1, 2 * owner + 1),
            (owner, 1024, 2, 2 * owner, 3, 0),
            (owner, 1536, 2, 2 * owner + 1, 3, 0),
            (owner, 2048, 4, 0, 5 + 2 * owner, 0),
            (owner, 2560, 4, 0, 6, 0) if owner == 0 else (owner, 2560, 8, (0, 512), None, 0),
            (owner, 3072, 9, 0, 10, owner),
            (owner, 3584, 11, 0, 12, 0) if owner == 0 else (owner, 3584, 13, 0, 14, 0),
        ]
    sent, kept = outer_blocks(core, members, plan, (0, 1536, 3072, 4096))
    wide_in = (feed_in.shape, (1, 256, 512), lambda b: (1, b % 2, b // 2))
    wide_out = (feed_out.shape, (1, 256, 512), lambda b: (1, b, 0))
    second_steps = []
    for target, first in ((0, 0), (1, 4)):
        for side_of in range(2):
            for number in range(4):
                row = first + number
                piece = min(row // 3, 2)
                second_steps.append(
                    (
                        (piece + 3 * side_of,),
                        row - 3 * piece,
                        target,
                        number + 4 * side_of,
                        number + 4 * (1 - side_of),
                    )
                )
    (sent,) = second_sum.tick(sent)
    last_sum = Background(sent, kept, phases)
    spread = None
    flat_steps = [steps[0] for steps in phases]
    while last_sum.result is None:
        if second_sum.result is None:
            pending, other = tie(last_sum.pending, second_sum.pending)
            last_sum.advance(pending)
            second_sum.advance(other)
        elif spread is None:
            rows, arrived_rows = second_sum.result
            spread = spread_blocks(
                core, rows + arrived_rows, 256, (wide_in, wide_out), second_steps, (None, None)
            )
            pending, spread = tie(last_sum.pending, spread)
            last_sum.advance(pending)
        elif flat_steps:
            flat_arrived = swap(flat, flat_steps.pop(0))
            pending, flat_arrived = tie(last_sum.pending, flat_arrived)
            flat = flat + flat_arrived
            last_sum.advance(pending)
        else:
            last_sum.advance(tie(last_sum.pending)[0])
    for step in flat_steps:
        flat = flat + swap(flat, step)
    rows, arrived_rows = last_sum.result
    last_steps = []
    for target, places in ((0, ((0, 0), (0, 1))), (1, ((0, 2), (1, 0))), (2, ((1, 1), (1, 2)))):
        for side_of in range(2):
            for number, (piece, block) in enumerate(places):
                last_steps.append(
                    (
                        (piece + 3 * side_of,),
                        block,
                        target,
                        number + 2 * side_of,
                        number + 2 * (1 - side_of),
                    )
                )
    last_steps += [
        ((2,), 0, 3, 0, 1),
        ((5,), 0, 3, 1, 0),
        ((2, 5), 1, 4, 0, 0),
        ((5, 2), 1, 5, 0, 0),
    ]
    (
        feed_in_grad,
        feed_out_grad,
        attend_in_grad,
        mixer_in_grad,
        mixer_out_grad,
        attend_out_grad,
    ) = spread_blocks(
        core,
        rows + arrived_rows,
        512,
        (
            (feed_in.shape, (1, 512, 512), lambda b: (0, 0, b)),
            (feed_out.shape, (1, 512, 512), lambda b: (0, b, 0)),
            (attend_in.shape, (1, 512, 512), lambda b: (b, 0, 0)),
            (mixer_in.shape, (512, 512), lambda b: (0, b)),
            (mixer_out.shape, (512, 512), lambda b: (0, 0)),
            (attend_out.shape, (512, 512), lambda b: (0, 0)),
        ),
        last_steps,
        tuple(spread) + (None,) * 4,
    )
    (
        norm_gain_grad,
        norm_bias_grad,
        feed_in_bias_grad,
        feed_out_bias_grad,
        attend_vectors_grad,
        mixer_in_bias_grad,
        mixer_vectors_grad,
        taps_grad,
    ) = vmem_call(
        vectors_kernel,
        [
            (norm_gain.shape, f32),
            (norm_bias.shape, f32),
            (feed_in_bias.shape, f32),
            (feed_out_bias.shape, f32),
            (attend_vectors.shape, f32),
            ((1, 2 * features), f32),
            (mixer_vectors.shape, f32),
            ((KERNEL, features), f32),
        ],
        (),
        (flat,),
    )
    return (
        layer_output.reshape(frames.shape),
        frames_grad.reshape(frames.shape),
        norm_gain_grad,
        norm_bias_grad,
        feed_in_grad,
        feed_in_bias_grad,
        feed_out_grad,
        feed_out_bias_grad,
        attend_in_grad,
        attend_vectors_grad,
        attend_out_grad,
        mixer_in_grad,
        mixer_in_bias_grad.reshape(-1),
        taps_grad.T,
        mixer_vectors_grad,
        mixer_out_grad,
        batch_grads[1],
        batch_grads[0],
        batch_rows[2],
        batch_rows[3],
    )


def solution(mesh):
    return jax.shard_map(
        shards,
        mesh=mesh,
        in_specs=(
            P("utt", "seq", None),
            P("utt"),
            P("utt", "seq", None),
            P(),
            P(),
            P(),
            P(),
            P(),
            P(),
            P(),
            P(),
            P(),
            P(),
            P(),
            P(),
            P(),
            P(),
            P(),
            P(),
            P(),
            P(),
        ),
        out_specs=(
            P("utt", "seq", None),
            P("utt", "seq", None),
            P(),
            P(),
            P(),
            P(),
            P(),
            P(),
            P(),
            P(),
            P(),
            P(),
            P(),
            P(),
            P(),
            P(),
            P(),
            P(),
            P(),
            P(),
        ),
        check_vma=False,
    )
```

```python
import functools
import math

import jax
import jax.numpy as jnp
import numpy as np
from jax import lax
from jax.experimental import pallas as pl
from jax.experimental.pallas import tpu as pltpu
from jax.sharding import PartitionSpec as P

HEADS = 8
KERNEL = 9
HEAD_DIM = 64


TOP_PRECISION = lax.Precision.HIGHEST
EPSILON = 1e-05
VMEM_LIMIT = 63 * 1024 * 1024
SUM_LIMIT = 20 * 1024 * 1024
HALO = 8


def wide(values):
    return values.astype(jnp.float32)


def low(values):
    return values.astype(jnp.bfloat16)


def matmul(first_operand, second_operand):
    return jnp.dot(first_operand, second_operand, preferred_element_type=jnp.float32)


def column_sum(values):
    return jnp.sum(wide(values), axis=0, keepdims=True)


def normalize(values):
    average = jnp.mean(values, axis=-1, keepdims=True)
    centered = values - average
    spread = jnp.mean(centered * centered, axis=-1, keepdims=True)
    inverse = lax.rsqrt(spread + EPSILON)
    return centered * inverse, inverse


def scaled_norm(normed, gains, biases, number):
    return normed * wide(gains[number : number + 1, :]) + wide(biases[number : number + 1, :])


def norm_back(grad_rows, normed, inverse, gains, number, own=lambda values: values):
    scaled = grad_rows * wide(gains[number : number + 1, :])
    inner = (
        scaled
        - jnp.mean(scaled, axis=-1, keepdims=True)
        - normed * jnp.mean(scaled * normed, axis=-1, keepdims=True)
    )
    return inner * inverse, column_sum(own(grad_rows * normed)), column_sum(own(grad_rows))


def logistic(values):
    return 1.0 / (1.0 + jnp.exp(-values))


def silu_slope(preact, sigmoid):
    return sigmoid * (1.0 + preact * (1.0 - sigmoid))


def frame_places(info, rows, utterances, halo):
    per = rows // utterances
    row = lax.broadcasted_iota(jnp.int32, (rows, 1), 0)
    limit = jnp.full((rows, 1), info[utterances], jnp.int32)
    for utterance in range(utterances - 1):
        limit = jnp.where(row // per == utterance, info[1 + utterance], limit)
    return info[0] - halo + row % per, limit


def flags(condition):
    return jnp.where(condition, 1.0, 0.0)


def own_rows(values, utterances):
    per = values.shape[0] // utterances
    return jnp.concatenate(
        [values[u * per + HALO : (u + 1) * per - HALO] for u in range(utterances)], axis=0
    )


def with_sides(values, sides, utterances):
    per = values.shape[0] // utterances
    pieces = []
    for u in range(utterances):
        pieces.append(sides[2 * u * HALO : (2 * u + 1) * HALO])
        pieces.append(values[u * per : (u + 1) * per])
        pieces.append(sides[(2 * u + 1) * HALO : (2 * u + 2) * HALO])
    return jnp.concatenate(pieces, axis=0)


def blocks_of_heads(rows, utterances):
    per = rows.shape[0] // utterances
    first = lax.broadcasted_iota(jnp.int32, (per, 2 * HEAD_DIM), 1) < HEAD_DIM
    blocks = []
    for pair in range(HEADS // 2):
        columns = rows[:, pair * 2 * HEAD_DIM : (pair + 1) * 2 * HEAD_DIM]
        top, bottom = columns[:per], columns[per:]
        blocks.append(jnp.where(first, top, pltpu.roll(bottom, HEAD_DIM, 1)))
        blocks.append(jnp.where(first, pltpu.roll(top, HEAD_DIM, 1), bottom))
    return blocks


def rows_of_heads(blocks):
    per = blocks[0].shape[0]
    first = lax.broadcasted_iota(jnp.int32, (per, 2 * HEAD_DIM), 1) < HEAD_DIM
    columns = []
    for pair in range(HEADS // 2):
        left, right = blocks[2 * pair], blocks[2 * pair + 1]
        top = jnp.where(first, left, pltpu.roll(right, HEAD_DIM, 1))
        bottom = jnp.where(first, pltpu.roll(left, HEAD_DIM, 1), right)
        columns.append(jnp.concatenate([top, bottom], axis=0))
    return jnp.concatenate(columns, axis=1)


def whole_array(shape):
    return pl.BlockSpec(shape, lambda i: (0,) * len(shape))


class Part:
    def __init__(self, array, block, index):
        self.array, self.block, self.index = array, block, index

    def spec(self):
        def index(i, *numbers):
            return tuple(at(*numbers) if callable(at) else at for at in self.index)

        return pl.BlockSpec(self.block, index)


def vmem_call(kernel, shapes, smem, operands, scratch=(), cost=0, held=(), numbers=()):
    def whole(shape):
        return pl.BlockSpec(shape, lambda i, *numbers: (0,) * len(shape))

    return pl.pallas_call(
        kernel,
        grid_spec=pltpu.PrefetchScalarGridSpec(
            num_scalar_prefetch=len(numbers),
            grid=(1,),
            in_specs=[pl.BlockSpec(memory_space=pltpu.SMEM)] * len(smem)
            + [
                operand.spec() if isinstance(operand, Part) else whole(operand.shape)
                for operand in operands
            ]
            + [pl.BlockSpec(memory_space=pl.ANY)] * len(held),
            out_specs=[whole(shape) for shape, _ in shapes],
            scratch_shapes=list(scratch),
        ),
        out_shape=[jax.ShapeDtypeStruct(shape, dtype) for shape, dtype in shapes],
        compiler_params=pltpu.CompilerParams(vmem_limit_bytes=VMEM_LIMIT),
        cost_estimate=pl.CostEstimate(flops=cost, bytes_accessed=cost // 300, transcendentals=0),
    )(
        *numbers,
        *smem,
        *(operand.array if isinstance(operand, Part) else operand for operand in operands),
        *held,
    )


def fetch(pairs, semaphores):
    copies = [
        pltpu.make_async_copy(source, target, semaphores.at[number])
        for number, (source, target) in enumerate(pairs)
    ]
    for copy in copies:
        copy.start()
    return copies


def feed_rows(values, gains, biases, copies, weight_in, bias_in, weight_out, bias_out):
    normed, _ = normalize(values)
    hidden = low(scaled_norm(normed, gains, biases, 0))
    copies[0].wait()
    preact = matmul(hidden, weight_in[...]) + wide(bias_in[0:1, :])
    sigmoid = logistic(preact)
    active = low(preact * sigmoid)
    copies[1].wait()
    branch = matmul(active, weight_out[...]) + wide(bias_out[0:1, :])
    return values + 0.5 * branch, preact, sigmoid, active


def entry_kernel(
    utterances,
    frames,
    gains,
    biases,
    bias_in,
    bias_out,
    vectors,
    grads_head,
    grads_tail,
    feed_in,
    feed_out,
    attend_in,
    head_out,
    tail_out,
    after_out,
    slope_out,
    pack_out,
    sent_out,
    weight_in,
    weight_out,
    weight_attend,
    semaphores,
):
    copies = fetch(
        [
            (feed_in.at[0], weight_in),
            (feed_out.at[0], weight_out),
            (attend_in.at[pl.ds(0, 3)], weight_attend),
        ],
        semaphores,
    )
    per = frames.shape[0] // utterances
    for u in range(utterances):
        head_out[u, 0:HALO, :] = frames[u * per : u * per + HALO, :]
        head_out[u, HALO:, :] = grads_head[u]
        tail_out[u, 0:HALO, :] = frames[(u + 1) * per - HALO : (u + 1) * per, :]
        tail_out[u, HALO:, :] = grads_tail[u]
    units, features = slope_out.shape[1], frames.shape[1]
    pack_out[:, units : units + features] = low(scaled_norm(normalize(frames[...])[0], gains, biases, 0))
    after, preact, sigmoid, active = feed_rows(
        frames[...], gains, biases, copies, weight_in, bias_in, weight_out, bias_out
    )
    slope_out[...] = low(silu_slope(preact, sigmoid))
    pack_out[:, :units] = active
    after_out[...] = after
    normed, _ = normalize(after)
    hidden = low(scaled_norm(normed, gains, biases, 1))
    pack_out[:, units + features :] = hidden
    copies[2].wait()
    queries = matmul(hidden, weight_attend[0]) + wide(vectors[0:1, :])
    parts = (
        queries + wide(vectors[3:4, :]),
        matmul(hidden, weight_attend[1]),
        matmul(hidden, weight_attend[2]) + wide(vectors[1:2, :]),
    )
    lanes = 2 * HEAD_DIM
    for number, part in enumerate(parts):
        for head, block in enumerate(blocks_of_heads(part, utterances)):
            sent_out[head, :, number * lanes : (number + 1) * lanes] = low(block)


def sides_kernel(
    before,
    behind,
    gains,
    biases,
    bias_in,
    bias_out,
    feed_in,
    feed_out,
    after_out,
    grads_out,
    weight_in,
    weight_out,
    semaphores,
):
    copies = fetch([(feed_in.at[0], weight_in), (feed_out.at[0], weight_out)], semaphores)
    frames, grads = (
        jnp.concatenate(
            [
                source[u, first : first + HALO, :]
                for u in range(before.shape[0])
                for source in (before, behind)
            ],
            axis=0,
        )
        for first in (0, HALO)
    )
    grads_out[...] = grads
    after_out[...] = feed_rows(
        frames, gains, biases, copies, weight_in, bias_in, weight_out, bias_out
    )[0]


def mixer_kernel(
    utterances,
    info,
    blocks,
    after,
    after_sides,
    gains,
    biases,
    attend_out,
    vectors,
    mixer_in,
    mixer_bias,
    taps,
    mixer_vectors,
    after_out,
    pack_out,
    linear_out,
    gate_out,
    gated_out,
    convolved_out,
    sums_out,
    padded,
):
    per = after.shape[0] // utterances
    main, before, behind = [], [], []
    for head in range(HEADS):
        block = wide(blocks[head])
        main.append(block[:per])
        before.append(block[per : per + HALO])
        behind.append(block[per + HALO :])
    attended = rows_of_heads(main)
    features = after.shape[1]
    pack_out[:, :features] = low(attended)
    before, behind = rows_of_heads(before), rows_of_heads(behind)
    sides = []
    for u in range(utterances):
        sides += [before[u * HALO : (u + 1) * HALO], behind[u * HALO : (u + 1) * HALO]]
    attended = low(with_sides(attended, jnp.concatenate(sides, axis=0), utterances))
    values = with_sides(after[...], after_sides[...], utterances)
    values = values + matmul(attended, attend_out[...]) + wide(vectors[2:3, :])
    after_out[...] = values
    normed, _ = normalize(values)
    scaled = scaled_norm(normed, gains, biases, 2)
    pack_out[:, features:] = low(own_rows(scaled, utterances))
    preact = matmul(low(scaled), mixer_in[...])
    preact = preact + wide(mixer_bias[...])
    rows = values.shape[0]
    linear = preact[:, :features]
    gate = logistic(preact[:, features:])
    linear_out[...] = own_rows(linear, utterances)
    gate_out[...] = own_rows(gate, utterances)
    place, limit = frame_places(info, rows, utterances, HALO)
    mask = flags((place >= 0) & (place < limit))
    gated = low(linear * gate * mask)
    gated_out[...] = gated
    fill_padded(padded, wide(gated), utterances)
    total = None
    for offset in range(KERNEL):
        term = wide(taps[offset : offset + 1, :]) * moved(
            padded, utterances, offset - KERNEL // 2, rows // utterances
        )
        total = term if total is None else total + term
    convolved = total + wide(mixer_vectors[0:1, :])
    convolved_out[...] = convolved
    mask = own_rows(mask, utterances)
    convolved = own_rows(convolved, utterances)
    count = jnp.sum(mask, axis=0, keepdims=True)
    local_sum = jnp.sum(convolved * mask, axis=0, keepdims=True)
    centered = (convolved - local_sum / jnp.maximum(count, 1.0)) * mask
    share(sums_out, local_sum, jnp.sum(centered * centered, axis=0, keepdims=True))


def fill_padded(padded, values, utterances):
    per = values.shape[0] // utterances
    zeros = jnp.zeros((8, values.shape[1]), jnp.float32)
    for u in range(utterances):
        padded[u, 0:8, :] = zeros
        padded[u, 8 : 8 + per, :] = values[u * per : (u + 1) * per, :]
        padded[u, 8 + per : 16 + per, :] = zeros


def moved(padded, utterances, start, per, first=0):
    return jnp.concatenate(
        [
            padded[u, 8 + first + start : 8 + first + start + per, :]
            for u in range(utterances)
        ],
        axis=0,
    )


def share(sums_out, *rows):
    tile = jnp.concatenate(
        [row[:, i : i + 128] for row in rows for i in range(0, row.shape[1], 128)], axis=0
    )
    for copy in range(sums_out.shape[0] // 8):
        sums_out[copy * 8 : copy * 8 + 8, :] = tile


def as_row(tile):
    return jnp.concatenate([tile[i : i + 1] for i in range(tile.shape[0])], axis=1)


def frame_counts(limits, shape, utterances, seq_count, per):
    place = lax.broadcasted_iota(jnp.int32, shape, 0)
    owner, first = place // seq_count, place % seq_count * per
    total = jnp.zeros(shape, jnp.int32)
    for number in range(limits.shape[0]):
        inside = jnp.clip(limits[number] - first, 0, per)
        total = total + jnp.where(owner == number // utterances, inside, 0)
    return total.astype(jnp.float32)


def middle_kernel(
    utterances,
    seq_count,
    limits,
    convolved,
    shared,
    after,
    grads,
    grad_sides,
    gains,
    biases,
    batch_gain,
    batch_shift,
    running_mean,
    running_variance,
    mixer_out,
    vectors,
    bias_in,
    bias_out,
    feed_in,
    feed_out,
    layer_out,
    grad_mixer_out,
    grad_batch_out,
    normed_out,
    pack_out,
    sums_out,
    batch_out_rows,
    vector_out,
    weight_in,
    weight_out,
    semaphores,
):
    def own(values):
        return own_rows(values, utterances)

    features, units = feed_in.shape[1:]

    def pack(number, rows):
        first = 2 * units + number * features
        pack_out[:, first : first + features] = rows

    copies = fetch([(feed_in.at[1], weight_in), (feed_out.at[1], weight_out)], semaphores)
    parts = shared[...].reshape(-1, 8, 128)
    per = grads.shape[0] // utterances
    counts = frame_counts(limits, parts.shape, utterances, seq_count, per)
    totals = jnp.sum(parts, axis=0)
    valid_tile = jnp.sum(counts, axis=0)
    valid = as_row(valid_tile[:4])
    average_tile = totals / valid_tile
    drift = parts / jnp.maximum(counts, 1.0) - average_tile
    spreads = jnp.sum(counts * drift * drift, axis=0)
    average = as_row(average_tile[:4])
    variance = as_row((totals[4:] + spreads[:4]) / valid_tile[:4])
    inverse_batch = lax.rsqrt(variance + EPSILON)
    batch_out_rows[0:1, :] = inverse_batch
    batch_out_rows[1:2, :] = valid
    batch_out_rows[2:3, :] = 0.9 * running_mean[...] + 0.1 * average
    batch_out_rows[3:4, :] = 0.9 * running_variance[...] + 0.1 * variance * valid / (valid - 1.0)
    normed_batch = (convolved[...] - average) * inverse_batch
    normed_out[...] = normed_batch
    batch = normed_batch * wide(batch_gain[...]) + wide(batch_shift[...])
    batch_sigmoid = logistic(batch)
    swished = low(batch * batch_sigmoid)
    pack(2, low(own(batch * batch_sigmoid)))
    values = after[...] + matmul(swished, mixer_out[...]) + wide(vectors[1:2, :])
    normed, inverse = normalize(values)
    scaled = scaled_norm(normed, gains, biases, 3)
    pack(0, low(own(scaled)))
    copies[0].wait()
    preact = matmul(low(scaled), weight_in[...]) + wide(bias_in[1:2, :])
    sigmoid = logistic(preact)
    activated = preact * sigmoid
    active = low(activated)
    pack_out[:, units : 2 * units] = low(own(activated))
    copies[1].wait()
    branch = matmul(active, weight_out[...]) + wide(bias_out[1:2, :])
    normed_last, inverse_last = normalize(values + 0.5 * branch)
    layer_out[...] = own(scaled_norm(normed_last, gains, biases, 4))
    grad_second, gain_last, shift_last = norm_back(
        with_sides(grads[...], grad_sides[...], utterances),
        normed_last,
        inverse_last,
        gains,
        4,
        own,
    )
    grad_low = low(0.5 * grad_second)
    grad_low_own = low(own(0.5 * grad_second))
    pack(1, grad_low_own)
    grad_pre = rows_dot(grad_low, weight_out[...]) * silu_slope(preact, sigmoid)
    grad_pre_own = low(own(grad_pre))
    pack_out[:, :units] = grad_pre_own
    grad_values, gain_three, shift_three = norm_back(
        rows_dot(low(grad_pre), weight_in[...]), normed, inverse, gains, 3, own
    )
    grad_mixer = grad_second + grad_values
    grad_mixer_own = own(grad_mixer)
    grad_mixer_out[...] = grad_mixer_own
    branch_own = low(grad_mixer_own)
    pack(3, branch_own)
    grad_batch = rows_dot(low(grad_mixer), mixer_out[...]) * silu_slope(batch, batch_sigmoid)
    grad_batch_out[...] = grad_batch
    share(sums_out, column_sum(own(grad_batch)), column_sum(own(grad_batch * normed_batch)))
    bias_sum = column_sum(grad_pre_own)
    put_rows(
        vector_out,
        [gain_last, shift_last, gain_three, shift_three]
        + [bias_sum[:, i : i + features] for i in range(0, bias_sum.shape[1], features)]
        + [column_sum(grad_low_own), column_sum(branch_own)],
    )


def put_rows(out, rows):
    for number, row in enumerate(rows):
        out[number : number + 1, :] = row
    out[len(rows) :, :] = jnp.zeros((out.shape[0] - len(rows), out.shape[1]), jnp.float32)


def mixer_back_kernel(
    utterances,
    info,
    grad_batch,
    normed_batch,
    shared,
    batch_rows,
    batch_gain,
    gated,
    linear,
    gate,
    grad_mixer,
    after,
    gains,
    taps,
    mixer_in,
    attend_out,
    batch_grads_out,
    grad_attend_out,
    pack_out,
    sent_out,
    vector_out,
    padded,
    gated_padded,
):
    totals = jnp.sum(shared[...].reshape(-1, 8, 128), axis=0)
    shift_grad, gain_grad = as_row(totals[:4]), as_row(totals[4:])
    batch_grads_out[0:1, :] = shift_grad
    batch_grads_out[1:2, :] = gain_grad
    rows, features = grad_batch.shape
    place, limit = frame_places(info, rows, utterances, HALO)
    mask = flags((place >= 0) & (place < limit))
    inside = flags((place >= 0) & (place < info[utterances + 1]))
    inverse_batch, valid = batch_rows[0:1, :], batch_rows[1:2, :]
    grad_conv = low(
        inside
        * wide(batch_gain[...])
        * inverse_batch
        * (grad_batch[...] - mask / valid * (shift_grad + normed_batch[...] * gain_grad))
    )
    conv_wide = wide(grad_conv)
    fill_padded(padded, conv_wide, utterances)
    fill_padded(gated_padded, wide(gated[...]), utterances)
    conv_own = own_rows(conv_wide, utterances)
    per = rows // utterances - 2 * HALO
    margin = KERNEL // 2
    total = None
    tap_rows = []
    for offset in range(KERNEL):
        term = wide(taps[offset : offset + 1, :]) * moved(
            padded, utterances, margin - offset, per, HALO
        )
        total = term if total is None else total + term
        near = moved(gated_padded, utterances, offset - margin, per, HALO)
        tap_rows.append(jnp.sum(conv_own * near, axis=0, keepdims=True))
    grad_gated = own_rows(mask, utterances) * total
    gate_half = gate[...]
    grad_pre = low(
        jnp.concatenate(
            [
                grad_gated * gate_half,
                grad_gated * linear[...] * gate_half * (1.0 - gate_half),
            ],
            axis=1,
        )
    )
    pack_out[:, : 2 * features] = grad_pre
    normed, inverse = normalize(own_rows(after[...], utterances))
    grad_values, gain_two, shift_two = norm_back(
        rows_dot(grad_pre, mixer_in[...]), normed, inverse, gains, 2
    )
    grad_attend = grad_mixer[...] + grad_values
    grad_attend_out[...] = grad_attend
    branch = low(grad_attend)
    pack_out[:, 2 * features :] = branch
    grad_attended = rows_dot(branch, attend_out[...])
    for head, block in enumerate(blocks_of_heads(grad_attended, utterances)):
        sent_out[head] = low(block)
    bias_sum = column_sum(grad_pre)
    put_rows(
        vector_out,
        [gain_two, shift_two, column_sum(conv_own), column_sum(branch)]
        + [bias_sum[:, :features], bias_sum[:, features:]]
        + tap_rows,
    )


def entry_back_kernel(
    returned,
    grad_attend,
    frames,
    after,
    slope,
    gains,
    feed_in,
    feed_out,
    attend_in,
    frames_out,
    pack_out,
    vector_out,
    weight_in,
    weight_out,
    weight_attend,
    semaphores,
):
    copies = fetch(
        [
            (attend_in.at[pl.ds(0, 3)], weight_attend),
            (feed_out.at[0], weight_out),
            (feed_in.at[0], weight_in),
        ],
        semaphores,
    )
    lanes = 2 * HEAD_DIM
    features, units = feed_in.shape[1:]

    def pack(number, rows):
        first = units + number * features
        pack_out[:, first : first + features] = rows

    grad_hidden = None
    low_rows = []
    for number in range(3):
        rows = low(
            rows_of_heads(
                [
                    wide(returned[head, :, number * lanes : (number + 1) * lanes])
                    for head in range(HEADS)
                ]
            )
        )
        pack(number, rows)
        low_rows.append(rows)
        if number == 0:
            copies[0].wait()
        term = rows_dot(rows, weight_attend[number])
        grad_hidden = term if grad_hidden is None else grad_hidden + term
    normed, inverse = normalize(after[...])
    grad_values, gain_one, shift_one = norm_back(grad_hidden, normed, inverse, gains, 1)
    grad_first = grad_attend[...] + grad_values
    grad_low = low(0.5 * grad_first)
    pack(3, grad_low)
    copies[1].wait()
    grad_pre = low(rows_dot(grad_low, weight_out[...]) * wide(slope[...]))
    pack_out[:, :units] = grad_pre
    normed, inverse = normalize(frames[...])
    copies[2].wait()
    grad_values, gain_zero, shift_zero = norm_back(
        rows_dot(grad_pre, weight_in[...]), normed, inverse, gains, 0
    )
    frames_out[...] = grad_first + grad_values
    bias_sum = column_sum(grad_pre)
    put_rows(
        vector_out,
        [gain_zero, shift_zero, gain_one, shift_one]
        + [bias_sum[:, i : i + features] for i in range(0, bias_sum.shape[1], features)]
        + [column_sum(grad_low), column_sum(low_rows[0]), column_sum(low_rows[2])],
    )


def vectors_kernel(
    rows, gain_out, bias_out, in_bias_out, out_bias_out, attend_out, mixer_bias_out, mixer_out, taps_out
):
    middle, mixer, entry, heads = (0, 16, 32, 48)
    features = gain_out.shape[1]

    def take(out, target, start):
        out[target : target + 1, :] = rows[start : start + 1, :]

    for out, first in ((gain_out, 0), (bias_out, 1)):
        take(out, 0, entry + first)
        take(out, 1, entry + 2 + first)
        take(out, 2, mixer + first)
        take(out, 3, middle + 2 + first)
        take(out, 4, middle + first)
    for target, start in ((0, entry + 4), (1, middle + 4)):
        for column in range(4):
            in_bias_out[target : target + 1, column * features : (column + 1) * features] = rows[
                start + column : start + column + 1, :
            ]
    take(out_bias_out, 0, entry + 8)
    take(out_bias_out, 1, middle + 8)
    for target, start in enumerate((entry + 9, entry + 10, mixer + 3, heads, heads + 1)):
        take(attend_out, target, start)
    for column in range(2):
        mixer_bias_out[0:1, column * features : (column + 1) * features] = rows[
            mixer + 4 + column : mixer + 5 + column, :
        ]
    take(mixer_out, 0, mixer + 2)
    take(mixer_out, 1, middle + 9)
    taps_out[...] = rows[mixer + 6 : mixer + 6 + KERNEL, :]


def axis_bits(axis):
    return [(axis, 1 << bit) for bit in range(lax.axis_size(axis).bit_length() - 1)]


def swap(values, step):
    axis, mask = step
    return lax.ppermute(values, axis, [(i, i ^ mask) for i in range(lax.axis_size(axis))])


def side(step):
    axis, mask = step
    return (lax.axis_index(axis) // mask) % 2


def swap_all(stripes, steps):
    return [swap(rows, step) for rows, step in zip(stripes, steps)]


def add_low(first_operand, second_operand):
    total = first_operand.astype(jnp.float32) + second_operand.astype(jnp.float32)
    return total.astype(jnp.bfloat16)


def pieces_of(rows):
    return 4 if rows >= 512 else 2 if rows >= 256 else 1


def fold_kernel(stripes, sides, *refs):
    for number in range(2 * stripes):
        own, other = refs[2 * number], refs[2 * number + 1]
        refs[4 * stripes + number][...] = add_low(own[...], other[...])


def fold_rows(kept, arrived, steps):
    halves = [rows.shape[0] // 2 for rows in kept]
    if any(half % 16 for half in halves):
        sent, keeps = [], []
        for own, other, step, half in zip(kept, arrived, steps, halves):
            for start, results in (((1 - side(step)) * half, sent), (side(step) * half, keeps)):
                results.append(
                    add_low(
                        *(lax.dynamic_slice_in_dim(rows, start, half, 0) for rows in (own, other))
                    )
                )
        return sent, keeps
    chunks = pieces_of(max(halves))
    in_specs, out_specs, shapes, operands = [], [], [], []

    def block(half, stripe, keeping):
        def index(i, sides):
            half_index = sides[stripe] if keeping else 1 - sides[stripe]
            return (half_index * chunks + i, 0)

        return pl.BlockSpec((half // chunks, 512), index)

    for stripe, (own, other, half) in enumerate(zip(kept, arrived, halves)):
        for keeping in (False, True):
            in_specs += [block(half, stripe, keeping)] * 2
            operands += [own, other]
            out_specs.append(pl.BlockSpec((half // chunks, 512), lambda i, sides: (i, 0)))
            shapes.append(jax.ShapeDtypeStruct((half, 512), jnp.bfloat16))
    results = pl.pallas_call(
        functools.partial(fold_kernel, len(kept)),
        grid_spec=pltpu.PrefetchScalarGridSpec(
            num_scalar_prefetch=1, grid=(chunks,), in_specs=in_specs, out_specs=out_specs
        ),
        out_shape=shapes,
        compiler_params=pltpu.CompilerParams(
            vmem_limit_bytes=VMEM_LIMIT if max(halves) >= 256 else SUM_LIMIT
        ),
        cost_estimate=pl.CostEstimate(
            flops=0, bytes_accessed=6 * 1024 * sum(halves), transcendentals=0
        ),
    )(jnp.stack([side(step) for step in steps]), *operands)
    return list(results[::2]), list(results[1::2])


def fold_pair_kernel(stripes, sides, *refs):
    for number in range(stripes):
        pieces = refs[4 * number : 4 * number + 4]
        height = pieces[0].shape[0] // 2
        for keeping in range(2):
            place = sides[number] if keeping else 1 - sides[number]
            rows = pl.ds(pl.multiple_of(place * height, 16), height)
            out = refs[4 * stripes + 2 * number + keeping]
            out[:height, :] = add_low(pieces[0][rows, :], pieces[1][rows, :])
            out[height:, :] = add_low(pieces[2][rows, :], pieces[3][rows, :])


def fold_pairs(early, late, steps):
    operands = list(zip(*early, *late))
    height = operands[0][0].shape[0]
    if height % 32:
        sent, kept = [], []
        for four, step in zip(operands, steps):
            sums = [add_low(*four[:2]), add_low(*four[2:])]
            for place, results in ((1 - side(step), sent), (side(step), kept)):
                start = place * (height // 2)
                results.append(
                    jnp.concatenate(
                        [lax.dynamic_slice_in_dim(rows, start, height // 2, 0) for rows in sums]
                    )
                )
        return sent, kept

    def whole(rows):
        return pl.BlockSpec((rows, 512), lambda i, sides: (0, 0))

    count = 2 * len(steps)
    results = pl.pallas_call(
        functools.partial(fold_pair_kernel, len(steps)),
        grid_spec=pltpu.PrefetchScalarGridSpec(
            num_scalar_prefetch=1,
            grid=(1,),
            in_specs=[whole(height)] * (2 * count),
            out_specs=[whole(height)] * count,
        ),
        out_shape=[jax.ShapeDtypeStruct((height, 512), jnp.bfloat16)] * count,
        compiler_params=pltpu.CompilerParams(vmem_limit_bytes=SUM_LIMIT),
        cost_estimate=pl.CostEstimate(
            flops=0, bytes_accessed=6 * 1024 * height * count, transcendentals=0
        ),
    )(jnp.stack([side(step) for step in steps]), *(rows for four in operands for rows in four))
    return list(results[::2]), list(results[1::2])


def add_kernel(stripes, *refs):
    for number in range(stripes):
        refs[2 * stripes + number][...] = add_low(refs[2 * number][...], refs[2 * number + 1][...])


def add_rows(kept, arrived):
    if any(rows.shape[0] % 16 for rows in kept):
        return [add_low(*pair) for pair in zip(kept, arrived)]
    specs = [whole_array(rows.shape) for rows in kept]
    return list(
        pl.pallas_call(
            functools.partial(add_kernel, len(kept)),
            grid=(1,),
            in_specs=[spec for spec in specs for _ in range(2)],
            out_specs=specs,
            out_shape=[jax.ShapeDtypeStruct(rows.shape, rows.dtype) for rows in kept],
            compiler_params=pltpu.CompilerParams(vmem_limit_bytes=SUM_LIMIT),
        )(*(rows for pair in zip(kept, arrived) for rows in pair))
    )


def join_kernel(stripes, apart, sides, *refs):
    for number in range(stripes):
        own, other = refs[2 * number], refs[2 * number + 1]
        outs = refs[2 * stripes + number * (1 + apart) :]
        height = own.shape[0] // 2
        for part in range(2):
            out = outs[part * apart]
            first = 0 if apart else 2 * part * height
            for source, place in ((own, sides[number]), (other, 1 - sides[number])):
                start = pl.multiple_of(first + place * height, 16)
                rows = source[part * height : (part + 1) * height, :]
                out[pl.ds(start, height), :] = rows
                if apart:
                    first = (part * stripes + number) * 2 * height
                    start = pl.multiple_of(first + place * height, 16)
                    refs[-1][pl.ds(start, height), :] = rows
                    first = 0


def join_rows(stripes, arrived, steps, apart=False):
    heights = [rows.shape[0] // 2 for rows in stripes]
    if any(height % 16 for height in heights):
        joined = []
        for rows, other, step, height in zip(stripes, arrived, steps, heights):
            first = side(step) == 0
            low_rows, high_rows = jnp.where(first, rows, other), jnp.where(first, other, rows)
            parts = [
                jnp.concatenate([low_rows[part], high_rows[part]], axis=0)
                for part in (slice(0, height), slice(height, None))
            ]
            joined += parts if apart else [jnp.concatenate(parts, axis=0)]
        return joined + ([jnp.concatenate(joined[::2] + joined[1::2], axis=0)] if apart else [])

    def whole(height):
        return pl.BlockSpec((height, 512), lambda i, sides: (0, 0))

    outs = [2 * height for height in heights for _ in range(2)]
    outs.append(sum(outs))
    if not apart:
        outs = [4 * height for height in heights]
    return list(
        pl.pallas_call(
            functools.partial(join_kernel, len(stripes), apart),
            grid_spec=pltpu.PrefetchScalarGridSpec(
                num_scalar_prefetch=1,
                grid=(1,),
                in_specs=[whole(2 * height) for height in heights for _ in range(2)],
                out_specs=[whole(height) for height in outs],
            ),
            out_shape=[jax.ShapeDtypeStruct((height, 512), jnp.bfloat16) for height in outs],
            compiler_params=pltpu.CompilerParams(vmem_limit_bytes=SUM_LIMIT),
            cost_estimate=pl.CostEstimate(
                flops=0, bytes_accessed=8 * 1024 * sum(heights), transcendentals=0
            ),
        )(
            jnp.stack([side(step) for step in steps]),
            *(rows for pair in zip(stripes, arrived) for rows in pair),
        )
    )


def tie(*groups):
    return lax.optimization_barrier(groups)


def step_orders():
    utt, seq = axis_bits("utt"), axis_bits("seq")
    across, line, rest = utt[1:], seq[:1], seq[1:]
    return (
        line + across + rest,
        across + rest + line,
        rest[:1] + line + across + rest[1:],
    )


def all_shared(copies):
    return lax.all_to_all(copies, ("utt", "seq"), 0, 0, tiled=True)


def from_neighbours(head, tail):
    count = lax.axis_size("seq")
    before = lax.ppermute(tail, "seq", [(i, i + 1) for i in range(count - 1)])
    behind = lax.ppermute(head, "seq", [(i + 1, i) for i in range(count - 1)])
    return before, behind


def pair_rows(mine, theirs, start=0, width=None):
    columns = slice(start, start + (width or mine.shape[1]))
    return jnp.concatenate([mine[:, columns], theirs[:, columns]], axis=0)


def outer(left, right):
    return low(matmul(left.T, right))


def put_half(outs, side_number, half, value):
    @pl.when(side_number == half)
    def _():
        outs[1][...] = value

    @pl.when(side_number != half)
    def _():
        outs[0][...] = value


def feed_blocks(refs, outs, sides):
    hidden, grad_pre, active, grad_low = (refs[2 * i : 2 * i + 2] for i in range(4))
    hidden_cols = pair_rows(*hidden).T
    grad_rows = pair_rows(*grad_low)
    for half in range(2):
        block = low(matmul(hidden_cols, pair_rows(*grad_pre, 512 * half, 512)))
        put_half(outs[:2], sides[1], half, block)
        block = outer(pair_rows(*active, 512 * half, 512), grad_rows)
        put_half(outs[2:4], sides[2], half, block)


def second_kernel(places, *refs):
    feed_blocks(refs[:8], refs[8:], places)


def mixer_blocks_kernel(places, *refs):
    refs, outs = refs[:12], refs[12:]
    mixer = outer(pair_rows(*refs[:2]), pair_rows(*refs[2:4]))
    branch = outer(pair_rows(*refs[4:6]), pair_rows(*refs[6:8]))
    attend = outer(pair_rows(*refs[8:10]), pair_rows(*refs[10:12]))
    for half in range(2):
        pieces = (
            mixer[256 * half : 256 * half + 256],
            branch[128 * half : 128 * half + 128],
            attend[128 * half : 128 * half + 128],
        )
        put_half(outs, places[3], half, jnp.concatenate(pieces, axis=0))


def late_kernel(places, *refs):
    core = places[0]
    refs, outs = refs[:18], refs[18:]
    feed_blocks(refs[:8], outs[:4], places)
    hidden_cols = pair_rows(*refs[8:10]).T
    query, key, value = (pair_rows(*refs[10 + 2 * i : 12 + 2 * i]) for i in range(3))
    first = low(matmul(hidden_cols, jnp.where(core == 0, query, value)))
    second = low(matmul(hidden_cols, key))
    second = jnp.where(core == 0, second, add_low(refs[16][...], refs[17][...]))
    put_half(outs[4:], places[3], 0, first)
    put_half(outs[4:], places[3], 1, second)


def columns(pair, width, number, by_core=False):
    index = (lambda numbers: number + numbers[0]) if by_core else number
    return [Part(array, (array.shape[0], width), (0, index)) for array in pair]


def block_sums(kernel, places, stripes, operands):
    blocks = vmem_call(
        kernel,
        [((512, 512), jnp.bfloat16)] * (2 * stripes),
        (),
        [part for pair in operands for part in pair],
        cost=7 * 10**8 * stripes,
        numbers=(places,),
    )
    return blocks[::2], blocks[1::2]


def spread_kernel(count, places, *refs):
    for source, out in zip(refs[:count], refs[-count:]):
        out[...] = wide(source[...]).reshape(out.shape)


def spread_blocks(core, halves, stripes, firsts, early, shapes, bases):
    parts = 2
    high = 512 // parts

    def source(height, start):
        return pl.BlockSpec((height, 512), lambda i, places: (start // height + i, 0))

    def quarter(p):
        return 2 * p[0] + p[3]

    layer = 1 if early else 0
    pieces = list(stripes)
    in_specs = [source(high, first) for first in firsts]
    out_specs = [
        pl.BlockSpec((1, high, 512), lambda i, p: (layer, i, 2 * p[0] + p[1])),
        pl.BlockSpec((1, high, 512), lambda i, p: (layer, parts * (2 * p[0] + p[2]) + i, 0)),
        pl.BlockSpec((1, high, 512), lambda i, p: (quarter(p), i, 0)),
    ]
    if early:
        pieces += [stripes[2]] * 2
        thin = high // 4
        in_specs[2:] = [
            source(2 * thin, firsts[2]),
            source(thin, firsts[2] + 256),
            source(thin, firsts[2] + 384),
        ]
        out_specs[2:] = [
            pl.BlockSpec((2 * thin, 512), lambda i, p: (parts * p[3] + i, p[0]))
        ] + [pl.BlockSpec((thin, 512), lambda i, p: (parts * quarter(p) + i, 0))] * 2
    count = len(pieces)
    bases = list(bases)
    aliased = {
        1 + count + place: number
        for place, number in enumerate(i for i, base in enumerate(bases) if base is not None)
    }
    bases = [base for base in bases if base is not None]
    return list(
        pl.pallas_call(
            functools.partial(spread_kernel, count),
            grid_spec=pltpu.PrefetchScalarGridSpec(
                num_scalar_prefetch=1,
                grid=(parts,),
                in_specs=in_specs + [pl.BlockSpec(memory_space=pl.ANY)] * len(bases),
                out_specs=out_specs,
            ),
            out_shape=[jax.ShapeDtypeStruct(shape, jnp.float32) for shape in shapes],
            input_output_aliases=aliased,
            compiler_params=pltpu.CompilerParams(vmem_limit_bytes=SUM_LIMIT),
            cost_estimate=pl.CostEstimate(
                flops=0, bytes_accessed=6 * 512 * 1536, transcendentals=0
            ),
        )(jnp.concatenate([core, halves]), *pieces, *bases)
    )


def angle_tables(frame_count, features):
    halves = jnp.arange(features // 2, dtype=jnp.int32).astype(jnp.float32)
    frequencies = jnp.exp(halves * (-2.0 * math.log(10000.0) / features))
    fine = 32
    low_angles = jnp.arange(fine, dtype=jnp.int32).astype(jnp.float32)[:, None] * frequencies
    high_angles = (fine * jnp.arange(frame_count // fine, dtype=jnp.int32)).astype(jnp.float32)[
        :, None
    ] * frequencies
    low_sin, low_cos = jnp.sin(low_angles)[None], jnp.cos(low_angles)[None]
    high_sin, high_cos = jnp.sin(high_angles)[:, None], jnp.cos(high_angles)[:, None]
    sines = high_sin * low_cos + high_cos * low_sin
    cosines = high_cos * low_cos - high_sin * low_sin
    shape = (frame_count, features // 2)
    return sines.reshape(shape), cosines.reshape(shape)


def heads_out(blocks, groups):
    return lax.all_to_all(jnp.tile(blocks, (groups, 1, 1)), "seq", 0, 0, tiled=True)


def rows_dot(first_operand, second_operand):
    return lax.dot_general(
        first_operand, second_operand, (((1,), (1,)), ((), ())), preferred_element_type=jnp.float32
    )


def lane_side(shape, utterance):
    return (lax.broadcasted_iota(jnp.int32, shape, 1) // HEAD_DIM) == utterance


def turned_queries(content, shift, weight, sines, cosines):
    offset = (content.astype(jnp.float32) + shift).astype(jnp.bfloat16)
    half = sines.shape[1]
    spread = jnp.dot(offset, weight, preferred_element_type=jnp.float32)
    sin_part, cos_part = spread[:, :half], spread[:, half:]
    return (
        offset,
        (sin_part * sines + cos_part * cosines).astype(jnp.bfloat16),
        (cos_part * sines - sin_part * cosines).astype(jnp.bfloat16),
    )


def attend_kernel(
    limits,
    content,
    keys,
    values,
    shift,
    weight,
    sines,
    cosines,
    table,
    weights_out,
    attended_out,
    held,
):
    scale = HEAD_DIM ** (-0.5)
    content_rows = content[...]
    key_side = jnp.concatenate([table[...], keys[...]], axis=1)
    places = lax.broadcasted_iota(jnp.int32, (1, table.shape[0]), 1)
    attended = None
    for utterance in range(limits.shape[0]):
        ours = lane_side(content_rows.shape, utterance)
        mine = jnp.where(ours, content_rows, jnp.zeros_like(content_rows))
        moved = jnp.where(ours, shift[...], 0.0)
        _, turned_cos, turned_sin = turned_queries(
            mine, moved, weight[...], sines[...], cosines[...]
        )
        query_side = jnp.concatenate([turned_cos, turned_sin, mine], axis=1) * scale
        scores = rows_dot(query_side.astype(jnp.bfloat16), key_side)
        scores = jnp.where(places < limits[utterance], scores, -1000000000.0)
        raised = jnp.exp(scores - jnp.max(scores, axis=1, keepdims=True))
        totals = jnp.sum(raised, axis=1, keepdims=True)
        weights = (raised * (1.0 / totals)).astype(jnp.bfloat16)
        weights_out[utterance] = weights
        part = jnp.dot(weights, values[...], preferred_element_type=jnp.float32)
        attended = part if attended is None else jnp.where(ours, part, attended)
    if held is None:
        attended_out[...] = attended.astype(jnp.bfloat16)
        return
    step = pl.program_id(0)
    height = attended.shape[0]
    block = attended_out.shape[1] - 2 * HALO
    held[pl.ds(pl.multiple_of(HALO + step * height, 8), height), :] = attended
    for number in range(height // block):
        attended_out[step * (height // block) + number, 0:block, :] = attended[
            number * block : (number + 1) * block
        ].astype(jnp.bfloat16)

    @pl.when(step == pl.num_programs(0) - 1)
    def _():
        edge = jnp.zeros((HALO, held.shape[1]), jnp.float32)
        held[0:HALO, :] = edge
        held[held.shape[0] - HALO :, :] = edge
        for number in range(attended_out.shape[0]):
            start = number * block
            sides = jnp.concatenate(
                [
                    held[start : start + HALO, :],
                    held[start + HALO + block : start + 2 * HALO + block, :],
                ],
                axis=0,
            )
            attended_out[number, block:, :] = sides.astype(jnp.bfloat16)


def attend_back_kernel(
    weights,
    content,
    grads,
    keys,
    values,
    shift,
    weight,
    sines,
    cosines,
    table,
    *outs,
):
    step = pl.program_id(0)
    query_out, pairs_out, weight_out, sums_out, key_sums, value_sums = (None,) * (
        6 - len(outs)
    ) + outs
    scale = HEAD_DIM ** (-0.5)

    @pl.when(step == 0)
    def _():
        key_sums[...] = jnp.zeros_like(key_sums)
        value_sums[...] = jnp.zeros_like(value_sums)
        weight_out[...] = jnp.zeros_like(weight_out)
        sums_out[...] = jnp.zeros_like(sums_out)

    content_rows, grad_rows = content[...], grads[...]
    content_cols = content_rows.T
    grad_cols = grad_rows.T
    key_side = jnp.concatenate([table[...], keys[...]], axis=1)
    half = sines.shape[1]
    grad_content = grad_position = None
    for utterance in range(weights.shape[0]):
        low, high = utterance * HEAD_DIM, (utterance + 1) * HEAD_DIM
        ours = lane_side(content_rows.shape, utterance)
        probs = weights[utterance]
        wide = probs.astype(jnp.float32)
        grad_mine = jnp.where(ours, grad_rows, jnp.zeros_like(grad_rows)) * scale
        grad_probs = rows_dot(grad_mine.astype(jnp.bfloat16), values[...])
        product = wide * grad_probs
        inner = jnp.sum(product, axis=1, keepdims=True)
        grad_scores = (product - wide * inner).astype(jnp.bfloat16)
        value_sums[low:high, :] += jnp.dot(
            grad_cols[low:high, :], probs, preferred_element_type=jnp.float32
        )
        key_sums[low:high, :] += jnp.dot(
            content_cols[low:high, :], grad_scores, preferred_element_type=jnp.float32
        )
        grad_side = jnp.dot(grad_scores, key_side, preferred_element_type=jnp.float32)
        grad_cos_table = grad_side[:, :half]
        grad_sin_table = grad_side[:, half : 2 * half]
        from_table = jnp.concatenate(
            [
                grad_cos_table * sines[...] - grad_sin_table * cosines[...],
                grad_cos_table * cosines[...] + grad_sin_table * sines[...],
            ],
            axis=1,
        ).astype(jnp.bfloat16)
        offset = (content_rows.astype(jnp.float32) + shift[...]).astype(jnp.bfloat16)
        weight_out[...] += jnp.dot(
            offset.T[low:high, :], from_table, preferred_element_type=jnp.float32
        )
        content_part = grad_side[:, 2 * half :]
        position_part = rows_dot(from_table, weight[...])
        if grad_content is None:
            grad_content, grad_position = content_part, position_part
        else:
            grad_content = jnp.where(ours, content_part, grad_content)
            grad_position = jnp.where(ours, position_part, grad_position)
    grad_query = (grad_content + grad_position).astype(jnp.bfloat16)
    height, lanes = grad_query.shape
    if query_out is None:
        pairs_out[pl.ds(pl.multiple_of(step * height, 16), height), 0:lanes] = grad_query
    else:
        query_out[...] = grad_query
    sums_out[0:1, :] += jnp.sum(grad_content, axis=0, keepdims=True)
    sums_out[1:2, :] += jnp.sum(grad_position, axis=0, keepdims=True)

    @pl.when(step == pl.num_programs(0) - 1)
    def _():
        first = pairs_out.shape[1] - 2 * lanes
        pairs_out[:, first : first + lanes] = key_sums[...].T.astype(jnp.bfloat16)
        pairs_out[:, first + lanes :] = value_sums[...].T.astype(jnp.bfloat16)


def query_block(frames_all):
    return 256 if frames_all <= 1024 else 128


def whole_block(shape):
    return pl.BlockSpec(shape, lambda i: (0,) * len(shape))


def row_block(height, width):
    return pl.BlockSpec((height, width), lambda i: (i, 0))


def attend_heads(limits, content, arrived, shift, weight, sines, cosines, table, block):
    utterances = limits.shape[0]
    query_frames, lanes = content.shape[0], arrived.shape[1] // 3
    frames_all, table_width = table.shape
    height = query_block(frames_all)
    chunked = query_frames == frames_all and height % block == 0
    chunks = (frames_all // block, block + 2 * HALO, lanes)
    kernel = attend_kernel
    if not chunked:
        kernel = functools.partial(attend_kernel, held=None)
    return pl.pallas_call(
        kernel,
        grid=(query_frames // height,),
        in_specs=[
            pl.BlockSpec(memory_space=pltpu.SMEM),
            row_block(height, lanes),
            pl.BlockSpec((frames_all, lanes), lambda i: (0, 1)),
            pl.BlockSpec((frames_all, lanes), lambda i: (0, 2)),
            whole_block(shift.shape),
            whole_block(weight.shape),
            row_block(height, sines.shape[1]),
            row_block(height, sines.shape[1]),
            whole_block(table.shape),
        ],
        out_specs=[
            pl.BlockSpec((utterances, height, frames_all), lambda i: (0, i, 0)),
            whole_block(chunks) if chunked else row_block(height, lanes),
        ],
        out_shape=[
            jax.ShapeDtypeStruct((utterances, query_frames, frames_all), jnp.bfloat16),
            jax.ShapeDtypeStruct(chunks if chunked else (query_frames, lanes), jnp.bfloat16),
        ],
        scratch_shapes=[pltpu.VMEM((frames_all + 2 * HALO, lanes), jnp.float32)] * chunked,
        compiler_params=pltpu.CompilerParams(vmem_limit_bytes=VMEM_LIMIT),
        cost_estimate=pl.CostEstimate(
            flops=2 * utterances * query_frames * frames_all * (table_width + 256),
            bytes_accessed=2 * utterances * query_frames * frames_all,
            transcendentals=utterances * query_frames * frames_all,
        ),
    )(limits, content, arrived, arrived, shift, weight, sines, cosines, table)


def attend_heads_back(
    weights, content, grads, arrived, shift, weight, sines, cosines, table
):
    utterances, query_frames, frames_all = weights.shape
    lanes = arrived.shape[1] // 3
    height = query_block(frames_all)
    joined = query_frames == frames_all
    width = (3 if joined else 2) * lanes
    return pl.pallas_call(
        attend_back_kernel,
        grid=(query_frames // height,),
        in_specs=[
            pl.BlockSpec((utterances, height, frames_all), lambda i: (0, i, 0)),
            row_block(height, lanes),
            row_block(height, lanes),
            pl.BlockSpec((frames_all, lanes), lambda i: (0, 1)),
            pl.BlockSpec((frames_all, lanes), lambda i: (0, 2)),
            whole_block(shift.shape),
            whole_block(weight.shape),
            row_block(height, sines.shape[1]),
            row_block(height, sines.shape[1]),
            whole_block(table.shape),
        ],
        out_specs=([] if joined else [row_block(height, lanes)])
        + [
            whole_block((frames_all, width)),
            whole_block((HEAD_DIM, table.shape[1])),
            whole_block((8, lanes)),
        ],
        out_shape=(
            [] if joined else [jax.ShapeDtypeStruct((query_frames, lanes), jnp.bfloat16)]
        )
        + [
            jax.ShapeDtypeStruct((frames_all, width), jnp.bfloat16),
            jax.ShapeDtypeStruct((HEAD_DIM, table.shape[1]), jnp.float32),
            jax.ShapeDtypeStruct((8, lanes), jnp.float32),
        ],
        scratch_shapes=[
            pltpu.VMEM((lanes, frames_all), jnp.float32),
            pltpu.VMEM((lanes, frames_all), jnp.float32),
        ],
        compiler_params=pltpu.CompilerParams(vmem_limit_bytes=VMEM_LIMIT),
        cost_estimate=pl.CostEstimate(
            flops=2 * utterances * query_frames * frames_all * (table.shape[1] + 512),
            bytes_accessed=2 * utterances * query_frames * frames_all,
            transcendentals=0,
        ),
    )(weights, content, grads, arrived, arrived, shift, weight, sines, cosines, table)


def shards(
    frames,
    lengths,
    out_grad,
    norm_gain,
    norm_bias,
    feed_in,
    feed_in_bias,
    feed_out,
    feed_out_bias,
    attend_in,
    attend_vectors,
    attend_out,
    mixer_in,
    mixer_in_bias,
    depthwise,
    mixer_vectors,
    mixer_out,
    batch_gain,
    batch_shift,
    running_mean,
    running_variance,
):
    utt_rows, block_frames, features = frames.shape
    rows = utt_rows * block_frames
    seq_count = lax.axis_size("seq")
    seq_index = lax.axis_index("seq")
    count = lax.axis_size("utt") * seq_count
    frames_all = block_frames * seq_count
    groups = seq_count // HEADS
    head, group = seq_index % HEADS, seq_index // HEADS
    query_frames = frames_all // groups
    lanes = utt_rows * HEAD_DIM
    info = jnp.concatenate(
        [(seq_index * block_frames).reshape(1), lengths, jnp.full((1,), frames_all, jnp.int32)]
    )
    hidden_units = feed_in.shape[2]
    f32, bf16 = jnp.float32, jnp.bfloat16
    flat_frames = frames.reshape(rows, features)
    square, broad = (rows, features), (rows, hidden_units)
    extended = (utt_rows * (block_frames + 2 * HALO), features)
    row_flops = 2 * rows * features
    bind = functools.partial
    edge = ((utt_rows, 2 * HALO, features), f32)
    feed_scratch = [
        pltpu.VMEM((features, hidden_units), bf16),
        pltpu.VMEM((hidden_units, features), bf16),
    ]
    attend_scratch = pltpu.VMEM((3, features, features), bf16)
    (
        edge_head,
        edge_tail,
        after_first,
        slope_first,
        entry_pack,
        sent,
    ) = vmem_call(
        bind(entry_kernel, utt_rows),
        [
            edge,
            edge,
            (square, f32),
            (broad, bf16),
            ((rows, hidden_units + 2 * features), bf16),
            ((HEADS, block_frames, 3 * lanes), bf16),
        ],
        (),
        (
            flat_frames,
            norm_gain,
            norm_bias,
            feed_in_bias,
            feed_out_bias,
            attend_vectors,
            Part(out_grad, (utt_rows, HALO, features), (0, 0, 0)),
            Part(out_grad, (utt_rows, HALO, features), (0, block_frames // HALO - 1, 0)),
        ),
        scratch=feed_scratch + [attend_scratch, pltpu.SemaphoreType.DMA((3,))],
        cost=row_flops * (2 * hidden_units + 3 * features),
        held=(feed_in, feed_out, attend_in),
    )
    sent, edge_head, edge_tail = tie(sent, edge_head, edge_tail)
    before, behind = from_neighbours(edge_head, edge_tail)
    after_sides, grad_sides = vmem_call(
        sides_kernel,
        [((2 * utt_rows * HALO, features), f32)] * 2,
        (),
        (before, behind, norm_gain, norm_bias, feed_in_bias, feed_out_bias),
        scratch=feed_scratch + [pltpu.SemaphoreType.DMA((2,))],
        cost=row_flops * 2 * hidden_units // 4,
        held=(feed_in, feed_out),
    )
    arrived, after_sides, grad_sides = tie(heads_out(sent, groups), after_sides, grad_sides)
    arrived = arrived.reshape(frames_all, 3 * lanes)
    start_query = group * query_frames
    head_content = arrived
    if groups > 1:
        head_content = lax.dynamic_slice_in_dim(arrived, start_query, query_frames, 0)
    head_vectors = lax.dynamic_slice_in_dim(
        attend_vectors.astype(f32), head * HEAD_DIM, HEAD_DIM, 1
    )
    head_shift = jnp.tile((head_vectors[4] - head_vectors[3])[None], (1, utt_rows))
    head_weight = lax.dynamic_slice_in_dim(attend_in[3], head * HEAD_DIM, HEAD_DIM, 1).reshape(
        features // 2, 2, HEAD_DIM
    )
    head_weight = jnp.tile(
        jnp.transpose(head_weight, (2, 1, 0)).reshape(HEAD_DIM, features), (utt_rows, 1)
    )
    sines, cosines = angle_tables(frames_all, features)
    key_table = jnp.concatenate([cosines, sines], axis=1).astype(bf16)
    query_sin = lax.dynamic_slice_in_dim(sines, start_query, query_frames, 0)
    query_cos = lax.dynamic_slice_in_dim(cosines, start_query, query_frames, 0)
    weights, head_attended = attend_heads(
        lengths,
        head_content,
        arrived,
        head_shift,
        head_weight,
        query_sin,
        query_cos,
        key_table,
        block_frames,
    )

    def frames_back(blocks):
        width = blocks.shape[-1]
        blocks = blocks.reshape(1, HEADS, block_frames, width)
        if groups > 1:
            blocks = lax.dynamic_update_slice_in_dim(
                jnp.zeros((groups,) + blocks.shape[1:], blocks.dtype), blocks, group, 0
            )
        blocks = lax.all_to_all(
            blocks.reshape(seq_count, block_frames, width), "seq", 0, 0, tiled=True
        ).reshape(groups, HEADS, block_frames, width)
        return lax.dynamic_slice_in_dim(blocks, group, 1, 0)[0]

    head_attended, own_limits = tie(head_attended, lengths)
    all_limits = lax.all_gather(own_limits, "utt", tiled=True)
    if head_attended.ndim == 2:
        placed = lax.dynamic_update_slice_in_dim(
            jnp.zeros((frames_all + 2 * HALO, lanes), bf16), head_attended, HALO + start_query, 0
        )
        main, before, behind = (
            placed[start : start + frames_all].reshape(seq_count, block_frames, lanes)
            for start in (HALO, 0, 2 * HALO)
        )
        head_attended = jnp.concatenate([main, before[:, :HALO], behind[:, -HALO:]], axis=1)
    attended_blocks = lax.all_to_all(head_attended, "seq", 0, 0, tiled=True)
    attended_blocks, all_limits = tie(attended_blocks, all_limits)
    if groups > 1:
        attended_blocks = jnp.sum(
            attended_blocks.reshape((groups, HEADS) + attended_blocks.shape[1:]), axis=0
        )
    taps = depthwise.T
    padded = pltpu.VMEM((utt_rows, block_frames + 2 * HALO + 16, features), f32)
    (
        after_attend,
        mixer_pack,
        linear_half,
        gate_half,
        gated,
        convolved,
        shared,
    ) = vmem_call(
        bind(mixer_kernel, utt_rows),
        [
            (extended, f32),
            ((rows, 2 * features), bf16),
            (square, f32),
            (square, f32),
            (extended, bf16),
            (extended, f32),
            ((8 * count, 128), f32),
        ],
        (info,),
        (
            attended_blocks,
            after_first,
            after_sides,
            norm_gain,
            norm_bias,
            attend_out,
            attend_vectors,
            mixer_in,
            mixer_in_bias.reshape(1, -1),
            taps,
            mixer_vectors,
        ),
        scratch=(padded,),
        cost=row_flops * 3 * features,
    )
    (
        layer_output,
        grad_mixer,
        grad_batch,
        normed_batch,
        second_pack,
        shared,
        batch_rows,
        middle_rows,
    ) = vmem_call(
        bind(middle_kernel, utt_rows, seq_count),
        [
            (square, f32),
            (square, f32),
            (extended, f32),
            (extended, f32),
            ((rows, 2 * hidden_units + 4 * features), bf16),
            ((8 * count, 128), f32),
            ((8, features), f32),
            ((16, features), f32),
        ],
        (all_limits,),
        (
            convolved,
            all_shared(shared),
            after_attend,
            out_grad.reshape(rows, features),
            grad_sides,
            norm_gain,
            norm_bias,
            batch_gain.reshape(1, -1),
            batch_shift.reshape(1, -1),
            running_mean.reshape(1, -1),
            running_variance.reshape(1, -1),
            mixer_out,
            mixer_vectors,
            feed_in_bias,
            feed_out_bias,
        ),
        scratch=feed_scratch + [pltpu.SemaphoreType.DMA((2,))],
        cost=row_flops * (4 * hidden_units + 2 * features),
        held=(feed_in, feed_out),
    )
    phases = list(zip(*step_orders()))
    near = axis_bits("utt")[0]
    core = side(near).reshape(1)
    halves = jnp.stack([side(step) for step in phases[0]])
    places = jnp.concatenate([core, halves])
    half_units, half_features = hidden_units // 2, features // 2

    def with_pair(array):
        return [array, swap(array, near)]

    second_pair = with_pair(second_pack)
    second_sent, second_kept = block_sums(
        second_kernel,
        places,
        2,
        [
            columns(second_pair, features, 8),
            columns(second_pair, half_units, 0, True),
            columns(second_pair, half_units, 2, True),
            columns(second_pair, features, 9),
        ],
    )
    second_pair, second_sent, second_kept, shared = tie(
        second_pair, second_sent, second_kept, all_shared(shared)
    )
    (
        batch_grads,
        grad_attend,
        mixer_back_pack,
        grad_blocks,
        mixer_rows,
    ) = vmem_call(
        bind(mixer_back_kernel, utt_rows),
        [
            ((8, features), f32),
            (square, f32),
            ((rows, 3 * features), bf16),
            ((HEADS, block_frames, lanes), bf16),
            ((16, features), f32),
        ],
        (info,),
        (
            grad_batch,
            normed_batch,
            shared,
            batch_rows,
            batch_gain.reshape(1, -1),
            gated,
            linear_half,
            gate_half,
            grad_mixer,
            after_attend,
            norm_gain,
            taps,
            mixer_in,
            attend_out,
        ),
        scratch=(padded, padded),
        cost=row_flops * 4 * features,
    )
    mixer_pair, mixer_back_pair = with_pair(mixer_pack), with_pair(mixer_back_pack)
    third_sent, third_kept = block_sums(
        mixer_blocks_kernel,
        places,
        1,
        [
            columns(mixer_pair, features, 1),
            columns(mixer_back_pair, features, 0, True),
            columns(second_pair, half_features, 20, True),
            columns(second_pair, features, 11),
            columns(mixer_pair, half_features, 0, True),
            columns(mixer_back_pair, features, 2),
        ],
    )
    early_sent, early_kept = second_sent + third_sent, second_kept + third_kept
    early_arrived = swap_all(early_sent, phases[0])
    head_grad = heads_out(grad_blocks, groups).reshape(frames_all, lanes)
    if groups > 1:
        head_grad = lax.dynamic_slice_in_dim(head_grad, start_query, query_frames, 0)
    head_grad, early_kept = tie(head_grad, early_kept)
    *head_grads, head_weight_grad, head_sums = attend_heads_back(
        weights,
        head_content,
        head_grad,
        arrived,
        head_shift,
        head_weight,
        query_sin,
        query_cos,
        key_table,
    )
    head_grads, head_weight_grad, head_sums, early_arrived = tie(
        head_grads, head_weight_grad, head_sums, early_arrived
    )
    grad_blocks = head_grads[-1].reshape(seq_count, block_frames, -1)
    returned = lax.all_to_all(grad_blocks, "seq", 0, 0, tiled=True)
    if groups > 1:
        returned = jnp.sum(
            returned.astype(f32).reshape(groups, HEADS, block_frames, 2 * lanes), axis=0
        ).astype(bf16)
        returned = jnp.concatenate([frames_back(head_grads[0]), returned], axis=2)
    head_weight_grad = jnp.transpose(
        head_weight_grad.reshape(HEAD_DIM, 2, features // 2), (2, 1, 0)
    ).reshape(features, HEAD_DIM)
    position_weight_grad = lax.dynamic_update_slice_in_dim(
        jnp.zeros((features, features), f32), head_weight_grad, head * HEAD_DIM, 1
    )
    head_vector_grads = lax.dynamic_update_slice_in_dim(
        jnp.zeros((8, features), f32),
        jnp.sum(head_sums.reshape(8, utt_rows, HEAD_DIM), axis=1),
        head * HEAD_DIM,
        1,
    )
    def next_phase(kept, arrived_rows, steps):
        sent_rows, kept = fold_rows(kept, arrived_rows, steps)
        return kept, swap_all(tie(sent_rows)[0], steps)

    early_kept, early_arrived = next_phase(early_kept, early_arrived, phases[1])
    entry_pair = with_pair(entry_pack)
    position_pair = with_pair(position_weight_grad.astype(bf16))
    returned, early_arrived, entry_pair, position_pair = tie(
        returned, early_arrived, entry_pair, position_pair
    )
    (
        frames_grad,
        entry_back_pack,
        entry_rows,
    ) = vmem_call(
        entry_back_kernel,
        [
            (square, f32),
            ((rows, hidden_units + 4 * features), bf16),
            ((16, features), f32),
        ],
        (),
        (
            returned,
            grad_attend,
            flat_frames,
            after_first,
            slope_first,
            norm_gain,
        ),
        scratch=feed_scratch + [attend_scratch, pltpu.SemaphoreType.DMA((3,))],
        cost=row_flops * (2 * hidden_units + 3 * features),
        held=(feed_in, feed_out, attend_in),
    )
    entry_back_pack, early_kept, early_arrived = tie(entry_back_pack, early_kept, early_arrived)
    entry_back_pair = with_pair(entry_back_pack)
    for steps in phases[2:-1]:
        early_kept, early_arrived = next_phase(early_kept, early_arrived, steps)
    late_sent, late_kept = block_sums(
        late_kernel,
        places,
        3,
        [
            columns(entry_pair, features, 4),
            columns(entry_back_pair, half_units, 0, True),
            columns(entry_pair, half_units, 0, True),
            columns(entry_back_pair, features, 7),
            columns(entry_pair, features, 5),
            columns(entry_back_pair, features, 4),
            columns(entry_back_pair, features, 5),
            columns(entry_back_pair, features, 6),
            columns(position_pair, features, 0),
        ],
    )
    late_sent, early_arrived, middle_rows = tie(late_sent, early_arrived, middle_rows)
    late_arrived = swap_all(late_sent, phases[0])
    flat = jnp.concatenate([middle_rows, mixer_rows, entry_rows, head_vector_grads], axis=0)
    flat_steps = [near] + [steps[0] for steps in phases]
    late_arrived, flat = tie(late_arrived, flat)
    for steps in phases[1:]:
        if steps is phases[-1]:
            sent_rows, late_kept = fold_pairs(
                (early_kept, early_arrived), (late_kept, late_arrived), steps
            )
        else:
            sent_rows, late_kept = fold_rows(late_kept, late_arrived, steps)
        sent_rows, flat = tie(sent_rows, flat)
        late_arrived, flat_arrived = tie(swap_all(sent_rows, steps), swap(flat, flat_steps.pop()))
        flat = flat + flat_arrived
    sums = add_rows(late_kept, late_arrived)
    for steps in phases[:0:-1]:
        sums, flat = tie(sums, flat)
        flat_arrived = swap(flat, flat_steps.pop()) if flat_steps else jnp.zeros_like(flat)
        arrived_rows, flat_arrived = tie(swap_all(sums, steps), flat_arrived)
        flat = flat + flat_arrived
        sums = join_rows(sums, arrived_rows, steps, steps is phases[1])
    (sums,) = tie(sums)
    *sums, joined_rows = sums
    early_rows, late_rows = sums[::2], sums[1::2]
    vector_grads = vmem_call(
        vectors_kernel,
        [
            (norm_gain.shape, f32),
            (norm_bias.shape, f32),
            (feed_in_bias.shape, f32),
            (feed_out_bias.shape, f32),
            (attend_vectors.shape, f32),
            ((1, 2 * features), f32),
            (mixer_vectors.shape, f32),
            ((KERNEL, features), f32),
        ],
        (),
        (flat,),
    )
    vector_grads = list(vector_grads)
    vector_grads[5] = vector_grads[5].reshape(-1)
    vector_grads[7] = vector_grads[7].T
    vector_grads = [*vector_grads, batch_grads[1], batch_grads[0], batch_rows[2], batch_rows[3]]
    early_arrived = swap_all(early_rows, phases[0])
    late_arrived = swap_all(late_rows, phases[0])
    across = swap(joined_rows, near)
    early_shapes = [
        feed_in.shape, feed_out.shape, mixer_in.shape, mixer_out.shape, attend_out.shape
    ]
    late_shapes = [feed_in.shape, feed_out.shape, attend_in.shape]

    def spread_early(spread, near_core, near_halves, stripes, firsts=(0, 0, 0)):
        feeds, mixers, attends = spread
        feeds = spread_blocks(
            near_core, near_halves, stripes, firsts, True, early_shapes, feeds + mixers
        )
        return feeds[:2], feeds[2:], attends

    def spread_late(spread, near_core, near_halves, stripes, firsts=(0, 0, 0)):
        feeds, mixers, attends = spread
        feeds = spread_blocks(
            near_core, near_halves, stripes, firsts, False, late_shapes, feeds + attends
        )
        return feeds[:2], mixers, feeds[2:]

    spread = ([None] * 2, [None] * 3, [None])
    spread = spread_early(spread, core, halves, early_rows)
    spread = spread_late(spread, core, halves, late_rows)
    spread = spread_early(spread, 1 - core, halves, [across] * 3, (0, 512, 1024))
    spread = spread_late(spread, 1 - core, halves, [across] * 3, (1536, 2048, 2560))
    spread, early_arrived = tie(spread, early_arrived)
    early_across = swap_all(early_arrived, [near] * 3)
    spread = spread_early(spread, core, 1 - halves, early_arrived)
    spread = spread_early(spread, 1 - core, 1 - halves, early_across)
    spread, late_arrived, vector_grads = tie(spread, late_arrived, vector_grads)
    late_across = swap_all(late_arrived, [near] * 3)
    spread = spread_late(spread, core, 1 - halves, late_arrived)
    spread = spread_late(spread, 1 - core, 1 - halves, late_across)
    (feed_in_grad, feed_out_grad), mixers, (attend_in_grad,) = spread
    mixer_in_grad, mixer_out_grad, attend_out_grad = mixers
    (
        norm_gain_grad,
        norm_bias_grad,
        feed_in_bias_grad,
        feed_out_bias_grad,
        attend_vectors_grad,
        mixer_in_bias_grad,
        mixer_vectors_grad,
        taps_grad,
        batch_gain_grad,
        batch_shift_grad,
        new_mean,
        new_variance,
    ) = vector_grads
    return (
        layer_output.reshape(frames.shape),
        frames_grad.reshape(frames.shape),
        norm_gain_grad,
        norm_bias_grad,
        feed_in_grad,
        feed_in_bias_grad,
        feed_out_grad,
        feed_out_bias_grad,
        attend_in_grad,
        attend_vectors_grad,
        attend_out_grad,
        mixer_in_grad,
        mixer_in_bias_grad,
        taps_grad,
        mixer_vectors_grad,
        mixer_out_grad,
        batch_gain_grad,
        batch_shift_grad,
        new_mean,
        new_variance,
    )


def solution(mesh):
    return jax.shard_map(
        shards,
        mesh=mesh,
        in_specs=(
            P("utt", "seq", None),
            P("utt"),
            P("utt", "seq", None),
            P(),
            P(),
            P(),
            P(),
            P(),
            P(),
            P(),
            P(),
            P(),
            P(),
            P(),
            P(),
            P(),
            P(),
            P(),
            P(),
            P(),
            P(),
        ),
        out_specs=(
            P("utt", "seq", None),
            P("utt", "seq", None),
            P(),
            P(),
            P(),
            P(),
            P(),
            P(),
            P(),
            P(),
            P(),
            P(),
            P(),
            P(),
            P(),
            P(),
            P(),
            P(),
            P(),
            P(),
        ),
        check_vma=False,
    )
```

```python
import functools
import math

import jax
import jax.numpy as jnp
import numpy as np
from jax import lax
from jax.experimental import pallas as pl
from jax.experimental.pallas import tpu as pltpu
from jax.sharding import PartitionSpec as P

HEADS = 8
KERNEL = 9
HEAD_DIM = 64


TOP_PRECISION = lax.Precision.HIGHEST
EPSILON = 1e-05
VMEM_LIMIT = 63 * 1024 * 1024
SUM_LIMIT = 20 * 1024 * 1024
FOLD_LIMIT = SUM_LIMIT
HALO = 8


def wide(values):
    return values.astype(jnp.float32)


def low(values):
    return values.astype(jnp.bfloat16)


def matmul(first_operand, second_operand):
    return jnp.dot(first_operand, second_operand, preferred_element_type=jnp.float32)


def column_sum(values):
    return jnp.sum(wide(values), axis=0, keepdims=True)


def normalize(values):
    average = jnp.mean(values, axis=-1, keepdims=True)
    centered = values - average
    spread = jnp.mean(centered * centered, axis=-1, keepdims=True)
    inverse = lax.rsqrt(spread + EPSILON)
    return centered * inverse, inverse


def scaled_norm(normed, gains, biases, number):
    return normed * wide(gains[number : number + 1, :]) + wide(biases[number : number + 1, :])


def norm_back(grad_rows, normed, inverse, gains, number, own=lambda values: values):
    scaled = grad_rows * wide(gains[number : number + 1, :])
    inner = (
        scaled
        - jnp.mean(scaled, axis=-1, keepdims=True)
        - normed * jnp.mean(scaled * normed, axis=-1, keepdims=True)
    )
    return inner * inverse, column_sum(own(grad_rows * normed)), column_sum(own(grad_rows))


def logistic(values):
    return 1.0 / (1.0 + jnp.exp(-values))


def silu_slope(preact, sigmoid):
    return sigmoid * (1.0 + preact * (1.0 - sigmoid))


def frame_places(info, rows, utterances, halo):
    per = rows // utterances
    row = lax.broadcasted_iota(jnp.int32, (rows, 1), 0)
    limit = jnp.full((rows, 1), info[utterances], jnp.int32)
    for utterance in range(utterances - 1):
        limit = jnp.where(row // per == utterance, info[1 + utterance], limit)
    return info[0] - halo + row % per, limit


def flags(condition):
    return jnp.where(condition, 1.0, 0.0)


def own_rows(values, utterances):
    per = values.shape[0] // utterances
    return jnp.concatenate(
        [values[u * per + HALO : (u + 1) * per - HALO] for u in range(utterances)], axis=0
    )


def with_sides(values, sides, utterances):
    per = values.shape[0] // utterances
    pieces = []
    for u in range(utterances):
        pieces.append(sides[2 * u * HALO : (2 * u + 1) * HALO])
        pieces.append(values[u * per : (u + 1) * per])
        pieces.append(sides[(2 * u + 1) * HALO : (2 * u + 2) * HALO])
    return jnp.concatenate(pieces, axis=0)


def blocks_of_heads(rows, utterances):
    per = rows.shape[0] // utterances
    first = lax.broadcasted_iota(jnp.int32, (per, 2 * HEAD_DIM), 1) < HEAD_DIM
    blocks = []
    for pair in range(HEADS // 2):
        columns = rows[:, pair * 2 * HEAD_DIM : (pair + 1) * 2 * HEAD_DIM]
        top, bottom = columns[:per], columns[per:]
        blocks.append(jnp.where(first, top, pltpu.roll(bottom, HEAD_DIM, 1)))
        blocks.append(jnp.where(first, pltpu.roll(top, HEAD_DIM, 1), bottom))
    return blocks


def rows_of_heads(blocks):
    per = blocks[0].shape[0]
    first = lax.broadcasted_iota(jnp.int32, (per, 2 * HEAD_DIM), 1) < HEAD_DIM
    columns = []
    for pair in range(HEADS // 2):
        left, right = blocks[2 * pair], blocks[2 * pair + 1]
        top = jnp.where(first, left, pltpu.roll(right, HEAD_DIM, 1))
        bottom = jnp.where(first, pltpu.roll(left, HEAD_DIM, 1), right)
        columns.append(jnp.concatenate([top, bottom], axis=0))
    return jnp.concatenate(columns, axis=1)


def whole_array(shape):
    return pl.BlockSpec(shape, lambda i: (0,) * len(shape))


class Part:
    def __init__(self, array, block, index):
        self.array, self.block, self.index = array, block, index

    def spec(self):
        def index(i, *numbers):
            return tuple(at(*numbers) if callable(at) else at for at in self.index)

        return pl.BlockSpec(self.block, index)


def vmem_call(kernel, shapes, smem, operands, scratch=(), cost=0, held=(), numbers=()):
    def whole(shape):
        return pl.BlockSpec(shape, lambda i, *numbers: (0,) * len(shape))

    return pl.pallas_call(
        kernel,
        grid_spec=pltpu.PrefetchScalarGridSpec(
            num_scalar_prefetch=len(numbers),
            grid=(1,),
            in_specs=[pl.BlockSpec(memory_space=pltpu.SMEM)] * len(smem)
            + [
                operand.spec() if isinstance(operand, Part) else whole(operand.shape)
                for operand in operands
            ]
            + [pl.BlockSpec(memory_space=pl.ANY)] * len(held),
            out_specs=[whole(shape) for shape, _ in shapes],
            scratch_shapes=list(scratch),
        ),
        out_shape=[jax.ShapeDtypeStruct(shape, dtype) for shape, dtype in shapes],
        compiler_params=pltpu.CompilerParams(vmem_limit_bytes=VMEM_LIMIT),
        cost_estimate=pl.CostEstimate(flops=cost, bytes_accessed=cost // 300, transcendentals=0),
    )(
        *numbers,
        *smem,
        *(operand.array if isinstance(operand, Part) else operand for operand in operands),
        *held,
    )


def fetch(pairs, semaphores):
    copies = [
        pltpu.make_async_copy(source, target, semaphores.at[number])
        for number, (source, target) in enumerate(pairs)
    ]
    for copy in copies:
        copy.start()
    return copies


def feed_rows(values, gains, biases, copies, weight_in, bias_in, weight_out, bias_out):
    normed, _ = normalize(values)
    hidden = low(scaled_norm(normed, gains, biases, 0))
    copies[0].wait()
    preact = matmul(hidden, weight_in[...]) + wide(bias_in[0:1, :])
    sigmoid = logistic(preact)
    active = low(preact * sigmoid)
    copies[1].wait()
    branch = matmul(active, weight_out[...]) + wide(bias_out[0:1, :])
    return values + 0.5 * branch, preact, sigmoid, active


def entry_kernel(
    utterances,
    frames,
    gains,
    biases,
    bias_in,
    bias_out,
    vectors,
    grads_head,
    grads_tail,
    feed_in,
    feed_out,
    attend_in,
    head_out,
    tail_out,
    after_out,
    slope_out,
    pack_out,
    sent_out,
    weight_in,
    weight_out,
    weight_attend,
    semaphores,
):
    copies = fetch(
        [
            (feed_in.at[0], weight_in),
            (feed_out.at[0], weight_out),
            (attend_in.at[pl.ds(0, 3)], weight_attend),
        ],
        semaphores,
    )
    per = frames.shape[0] // utterances
    for u in range(utterances):
        head_out[u, 0:HALO, :] = frames[u * per : u * per + HALO, :]
        head_out[u, HALO:, :] = grads_head[u]
        tail_out[u, 0:HALO, :] = frames[(u + 1) * per - HALO : (u + 1) * per, :]
        tail_out[u, HALO:, :] = grads_tail[u]
    units, features = slope_out.shape[1], frames.shape[1]
    pack_out[:, units : units + features] = low(scaled_norm(normalize(frames[...])[0], gains, biases, 0))
    after, preact, sigmoid, active = feed_rows(
        frames[...], gains, biases, copies, weight_in, bias_in, weight_out, bias_out
    )
    slope_out[...] = low(silu_slope(preact, sigmoid))
    pack_out[:, :units] = active
    after_out[...] = after
    normed, _ = normalize(after)
    hidden = low(scaled_norm(normed, gains, biases, 1))
    pack_out[:, units + features :] = hidden
    copies[2].wait()
    queries = matmul(hidden, weight_attend[0]) + wide(vectors[0:1, :])
    parts = (
        queries + wide(vectors[3:4, :]),
        matmul(hidden, weight_attend[1]),
        matmul(hidden, weight_attend[2]) + wide(vectors[1:2, :]),
    )
    lanes = 2 * HEAD_DIM
    for number, part in enumerate(parts):
        for head, block in enumerate(blocks_of_heads(part, utterances)):
            sent_out[head, :, number * lanes : (number + 1) * lanes] = low(block)


def sides_kernel(
    before,
    behind,
    gains,
    biases,
    bias_in,
    bias_out,
    feed_in,
    feed_out,
    after_out,
    grads_out,
    weight_in,
    weight_out,
    semaphores,
):
    copies = fetch([(feed_in.at[0], weight_in), (feed_out.at[0], weight_out)], semaphores)
    frames, grads = (
        jnp.concatenate(
            [
                source[u, first : first + HALO, :]
                for u in range(before.shape[0])
                for source in (before, behind)
            ],
            axis=0,
        )
        for first in (0, HALO)
    )
    grads_out[...] = grads
    after_out[...] = feed_rows(
        frames, gains, biases, copies, weight_in, bias_in, weight_out, bias_out
    )[0]


def mixer_kernel(
    utterances,
    info,
    blocks,
    after,
    after_sides,
    gains,
    biases,
    attend_out,
    vectors,
    mixer_in,
    mixer_bias,
    taps,
    mixer_vectors,
    after_out,
    pack_out,
    linear_out,
    gate_out,
    gated_out,
    convolved_out,
    sums_out,
    padded,
):
    per = after.shape[0] // utterances
    main, before, behind = [], [], []
    for head in range(HEADS):
        block = wide(blocks[head])
        main.append(block[:per])
        before.append(block[per : per + HALO])
        behind.append(block[per + HALO :])
    attended = rows_of_heads(main)
    features = after.shape[1]
    pack_out[:, :features] = low(attended)
    before, behind = rows_of_heads(before), rows_of_heads(behind)
    sides = []
    for u in range(utterances):
        sides += [before[u * HALO : (u + 1) * HALO], behind[u * HALO : (u + 1) * HALO]]
    attended = low(with_sides(attended, jnp.concatenate(sides, axis=0), utterances))
    values = with_sides(after[...], after_sides[...], utterances)
    values = values + matmul(attended, attend_out[...]) + wide(vectors[2:3, :])
    after_out[...] = values
    normed, _ = normalize(values)
    scaled = scaled_norm(normed, gains, biases, 2)
    pack_out[:, features:] = low(own_rows(scaled, utterances))
    preact = matmul(low(scaled), mixer_in[...])
    preact = preact + wide(mixer_bias[...])
    rows = values.shape[0]
    linear = preact[:, :features]
    gate = logistic(preact[:, features:])
    linear_out[...] = own_rows(linear, utterances)
    gate_out[...] = own_rows(gate, utterances)
    place, limit = frame_places(info, rows, utterances, HALO)
    mask = flags((place >= 0) & (place < limit))
    gated = low(linear * gate * mask)
    gated_out[...] = gated
    fill_padded(padded, wide(gated), utterances)
    total = None
    for offset in range(KERNEL):
        term = wide(taps[offset : offset + 1, :]) * moved(
            padded, utterances, offset - KERNEL // 2, rows // utterances
        )
        total = term if total is None else total + term
    convolved = total + wide(mixer_vectors[0:1, :])
    convolved_out[...] = convolved
    mask = own_rows(mask, utterances)
    convolved = own_rows(convolved, utterances)
    count = jnp.sum(mask, axis=0, keepdims=True)
    local_sum = jnp.sum(convolved * mask, axis=0, keepdims=True)
    centered = (convolved - local_sum / jnp.maximum(count, 1.0)) * mask
    share(sums_out, local_sum, jnp.sum(centered * centered, axis=0, keepdims=True))


def fill_padded(padded, values, utterances):
    per = values.shape[0] // utterances
    zeros = jnp.zeros((8, values.shape[1]), jnp.float32)
    for u in range(utterances):
        padded[u, 0:8, :] = zeros
        padded[u, 8 : 8 + per, :] = values[u * per : (u + 1) * per, :]
        padded[u, 8 + per : 16 + per, :] = zeros


def moved(padded, utterances, start, per, first=0):
    return jnp.concatenate(
        [
            padded[u, 8 + first + start : 8 + first + start + per, :]
            for u in range(utterances)
        ],
        axis=0,
    )


def share(sums_out, *rows):
    tile = jnp.concatenate(
        [row[:, i : i + 128] for row in rows for i in range(0, row.shape[1], 128)], axis=0
    )
    for copy in range(sums_out.shape[0] // 8):
        sums_out[copy * 8 : copy * 8 + 8, :] = tile


def as_row(tile):
    return jnp.concatenate([tile[i : i + 1] for i in range(tile.shape[0])], axis=1)


def frame_counts(limits, shape, utterances, seq_count, per):
    place = lax.broadcasted_iota(jnp.int32, shape, 0)
    owner, first = place // seq_count, place % seq_count * per
    total = jnp.zeros(shape, jnp.int32)
    for number in range(limits.shape[0]):
        inside = jnp.clip(limits[number] - first, 0, per)
        total = total + jnp.where(owner == number // utterances, inside, 0)
    return total.astype(jnp.float32)


def middle_kernel(
    utterances,
    seq_count,
    limits,
    convolved,
    shared,
    after,
    grads,
    grad_sides,
    gains,
    biases,
    batch_gain,
    batch_shift,
    running_mean,
    running_variance,
    mixer_out,
    vectors,
    bias_in,
    bias_out,
    feed_in,
    feed_out,
    layer_out,
    grad_mixer_out,
    grad_batch_out,
    normed_out,
    pack_out,
    sums_out,
    batch_out_rows,
    vector_out,
    weight_in,
    weight_out,
    semaphores,
):
    def own(values):
        return own_rows(values, utterances)

    features, units = feed_in.shape[1:]

    def pack(number, rows):
        first = 2 * units + number * features
        pack_out[:, first : first + features] = rows

    copies = fetch([(feed_in.at[1], weight_in), (feed_out.at[1], weight_out)], semaphores)
    parts = shared[...].reshape(-1, 8, 128)
    per = grads.shape[0] // utterances
    counts = frame_counts(limits, parts.shape, utterances, seq_count, per)
    totals = jnp.sum(parts, axis=0)
    valid_tile = jnp.sum(counts, axis=0)
    valid = as_row(valid_tile[:4])
    average_tile = totals / valid_tile
    drift = parts / jnp.maximum(counts, 1.0) - average_tile
    spreads = jnp.sum(counts * drift * drift, axis=0)
    average = as_row(average_tile[:4])
    variance = as_row((totals[4:] + spreads[:4]) / valid_tile[:4])
    inverse_batch = lax.rsqrt(variance + EPSILON)
    batch_out_rows[0:1, :] = inverse_batch
    batch_out_rows[1:2, :] = valid
    batch_out_rows[2:3, :] = 0.9 * running_mean[...] + 0.1 * average
    batch_out_rows[3:4, :] = 0.9 * running_variance[...] + 0.1 * variance * valid / (valid - 1.0)
    normed_batch = (convolved[...] - average) * inverse_batch
    normed_out[...] = normed_batch
    batch = normed_batch * wide(batch_gain[...]) + wide(batch_shift[...])
    batch_sigmoid = logistic(batch)
    swished = low(batch * batch_sigmoid)
    pack(2, low(own(batch * batch_sigmoid)))
    values = after[...] + matmul(swished, mixer_out[...]) + wide(vectors[1:2, :])
    normed, inverse = normalize(values)
    scaled = scaled_norm(normed, gains, biases, 3)
    pack(0, low(own(scaled)))
    copies[0].wait()
    preact = matmul(low(scaled), weight_in[...]) + wide(bias_in[1:2, :])
    sigmoid = logistic(preact)
    activated = preact * sigmoid
    active = low(activated)
    pack_out[:, units : 2 * units] = low(own(activated))
    copies[1].wait()
    branch = matmul(active, weight_out[...]) + wide(bias_out[1:2, :])
    normed_last, inverse_last = normalize(values + 0.5 * branch)
    layer_out[...] = own(scaled_norm(normed_last, gains, biases, 4))
    grad_second, gain_last, shift_last = norm_back(
        with_sides(grads[...], grad_sides[...], utterances),
        normed_last,
        inverse_last,
        gains,
        4,
        own,
    )
    grad_low = low(0.5 * grad_second)
    grad_low_own = low(own(0.5 * grad_second))
    pack(1, grad_low_own)
    grad_pre = rows_dot(grad_low, weight_out[...]) * silu_slope(preact, sigmoid)
    grad_pre_own = low(own(grad_pre))
    pack_out[:, :units] = grad_pre_own
    grad_values, gain_three, shift_three = norm_back(
        rows_dot(low(grad_pre), weight_in[...]), normed, inverse, gains, 3, own
    )
    grad_mixer = grad_second + grad_values
    grad_mixer_own = own(grad_mixer)
    grad_mixer_out[...] = grad_mixer_own
    branch_own = low(grad_mixer_own)
    pack(3, branch_own)
    grad_batch = rows_dot(low(grad_mixer), mixer_out[...]) * silu_slope(batch, batch_sigmoid)
    grad_batch_out[...] = grad_batch
    share(sums_out, column_sum(own(grad_batch)), column_sum(own(grad_batch * normed_batch)))
    bias_sum = column_sum(grad_pre_own)
    put_rows(
        vector_out,
        [gain_last, shift_last, gain_three, shift_three]
        + [bias_sum[:, i : i + features] for i in range(0, bias_sum.shape[1], features)]
        + [column_sum(grad_low_own), column_sum(branch_own)],
    )


def put_rows(out, rows):
    for number, row in enumerate(rows):
        out[number : number + 1, :] = row
    out[len(rows) :, :] = jnp.zeros((out.shape[0] - len(rows), out.shape[1]), jnp.float32)


def mixer_back_kernel(
    utterances,
    info,
    grad_batch,
    normed_batch,
    shared,
    batch_rows,
    batch_gain,
    gated,
    linear,
    gate,
    grad_mixer,
    after,
    gains,
    taps,
    mixer_in,
    attend_out,
    batch_grads_out,
    grad_attend_out,
    pack_out,
    sent_out,
    vector_out,
    padded,
    gated_padded,
):
    totals = jnp.sum(shared[...].reshape(-1, 8, 128), axis=0)
    shift_grad, gain_grad = as_row(totals[:4]), as_row(totals[4:])
    batch_grads_out[0:1, :] = shift_grad
    batch_grads_out[1:2, :] = gain_grad
    rows, features = grad_batch.shape
    place, limit = frame_places(info, rows, utterances, HALO)
    mask = flags((place >= 0) & (place < limit))
    inside = flags((place >= 0) & (place < info[utterances + 1]))
    inverse_batch, valid = batch_rows[0:1, :], batch_rows[1:2, :]
    grad_conv = low(
        inside
        * wide(batch_gain[...])
        * inverse_batch
        * (grad_batch[...] - mask / valid * (shift_grad + normed_batch[...] * gain_grad))
    )
    conv_wide = wide(grad_conv)
    fill_padded(padded, conv_wide, utterances)
    fill_padded(gated_padded, wide(gated[...]), utterances)
    conv_own = own_rows(conv_wide, utterances)
    per = rows // utterances - 2 * HALO
    margin = KERNEL // 2
    total = None
    tap_rows = []
    for offset in range(KERNEL):
        term = wide(taps[offset : offset + 1, :]) * moved(
            padded, utterances, margin - offset, per, HALO
        )
        total = term if total is None else total + term
        near = moved(gated_padded, utterances, offset - margin, per, HALO)
        tap_rows.append(jnp.sum(conv_own * near, axis=0, keepdims=True))
    grad_gated = own_rows(mask, utterances) * total
    gate_half = gate[...]
    grad_pre = low(
        jnp.concatenate(
            [
                grad_gated * gate_half,
                grad_gated * linear[...] * gate_half * (1.0 - gate_half),
            ],
            axis=1,
        )
    )
    pack_out[:, : 2 * features] = grad_pre
    normed, inverse = normalize(own_rows(after[...], utterances))
    grad_values, gain_two, shift_two = norm_back(
        rows_dot(grad_pre, mixer_in[...]), normed, inverse, gains, 2
    )
    grad_attend = grad_mixer[...] + grad_values
    grad_attend_out[...] = grad_attend
    branch = low(grad_attend)
    pack_out[:, 2 * features :] = branch
    grad_attended = rows_dot(branch, attend_out[...])
    for head, block in enumerate(blocks_of_heads(grad_attended, utterances)):
        sent_out[head] = low(block)
    bias_sum = column_sum(grad_pre)
    put_rows(
        vector_out,
        [gain_two, shift_two, column_sum(conv_own), column_sum(branch)]
        + [bias_sum[:, :features], bias_sum[:, features:]]
        + tap_rows,
    )


def entry_back_kernel(
    core,
    returned,
    grad_attend,
    frames,
    after,
    slope,
    gains,
    feed_in,
    feed_out,
    attend_in,
    frames_out,
    pack_out,
    grad_pre_out,
    vector_out,
    weight_in,
    weight_out,
    weight_attend,
    semaphores,
):
    copies = fetch(
        [
            (attend_in.at[pl.ds(0, 3)], weight_attend),
            (feed_out.at[0], weight_out),
            (feed_in.at[0], weight_in),
        ],
        semaphores,
    )
    lanes = 2 * HEAD_DIM
    features, units = feed_in.shape[1:]

    def pack(number, rows):
        first = units // 2 + number * features
        pack_out[:, first : first + features] = rows

    grad_hidden = None
    low_rows = []
    for number in range(3):
        rows = low(
            rows_of_heads(
                [
                    wide(returned[head, :, number * lanes : (number + 1) * lanes])
                    for head in range(HEADS)
                ]
            )
        )
        pack(number, rows)
        low_rows.append(rows)
        if number == 0:
            copies[0].wait()
        term = rows_dot(rows, weight_attend[number])
        grad_hidden = term if grad_hidden is None else grad_hidden + term
    normed, inverse = normalize(after[...])
    grad_values, gain_one, shift_one = norm_back(grad_hidden, normed, inverse, gains, 1)
    grad_first = grad_attend[...] + grad_values
    grad_low = low(0.5 * grad_first)
    pack(3, grad_low)
    copies[1].wait()
    grad_pre = low(rows_dot(grad_low, weight_out[...]) * wide(slope[...]))
    for half in range(2):
        rows = grad_pre[:, half * units // 2 : (half + 1) * units // 2]

        @pl.when(core[0] == half)
        def _():
            grad_pre_out[...] = rows

        @pl.when(core[0] != half)
        def _():
            pack_out[:, : units // 2] = rows

    normed, inverse = normalize(frames[...])
    copies[2].wait()
    grad_values, gain_zero, shift_zero = norm_back(
        rows_dot(grad_pre, weight_in[...]), normed, inverse, gains, 0
    )
    frames_out[...] = grad_first + grad_values
    bias_sum = column_sum(grad_pre)
    put_rows(
        vector_out,
        [gain_zero, shift_zero, gain_one, shift_one]
        + [bias_sum[:, i : i + features] for i in range(0, bias_sum.shape[1], features)]
        + [column_sum(grad_low), column_sum(low_rows[0]), column_sum(low_rows[2])],
    )


def vectors_kernel(
    rows, gain_out, bias_out, in_bias_out, out_bias_out, attend_out, mixer_bias_out, mixer_out, taps_out
):
    middle, mixer, entry, heads = (0, 16, 32, 48)
    features = gain_out.shape[1]

    def take(out, target, start):
        out[target : target + 1, :] = rows[start : start + 1, :]

    for out, first in ((gain_out, 0), (bias_out, 1)):
        take(out, 0, entry + first)
        take(out, 1, entry + 2 + first)
        take(out, 2, mixer + first)
        take(out, 3, middle + 2 + first)
        take(out, 4, middle + first)
    for target, start in ((0, entry + 4), (1, middle + 4)):
        for column in range(4):
            in_bias_out[target : target + 1, column * features : (column + 1) * features] = rows[
                start + column : start + column + 1, :
            ]
    take(out_bias_out, 0, entry + 8)
    take(out_bias_out, 1, middle + 8)
    for target, start in enumerate((entry + 9, entry + 10, mixer + 3, heads, heads + 1)):
        take(attend_out, target, start)
    for column in range(2):
        mixer_bias_out[0:1, column * features : (column + 1) * features] = rows[
            mixer + 4 + column : mixer + 5 + column, :
        ]
    take(mixer_out, 0, mixer + 2)
    take(mixer_out, 1, middle + 9)
    taps_out[...] = rows[mixer + 6 : mixer + 6 + KERNEL, :]


def axis_bits(axis):
    return [(axis, 1 << bit) for bit in range(lax.axis_size(axis).bit_length() - 1)]


def swap(values, step):
    axis, mask = step
    return lax.ppermute(values, axis, [(i, i ^ mask) for i in range(lax.axis_size(axis))])


def side(step):
    axis, mask = step
    return (lax.axis_index(axis) // mask) % 2


def swap_all(stripes, steps):
    return [swap(rows, step) for rows, step in zip(stripes, steps)]


def add_low(first_operand, second_operand):
    total = first_operand.astype(jnp.float32) + second_operand.astype(jnp.float32)
    return total.astype(jnp.bfloat16)


def fold_kernel(stripes, arrays, parts, sides, *refs):
    for number in range(stripes):
        sources = refs[2 * arrays * number : 2 * arrays * (number + 1)]
        for keeping in range(2):
            place = sides[number] if keeping else 1 - sides[number]
            out = refs[2 * arrays * stripes + 2 * number + keeping]
            first = 0
            for array in range(arrays):
                own, other = sources[2 * array : 2 * array + 2]
                height = own.shape[0] // (2 * parts)
                for part in range(parts):
                    start = pl.multiple_of((2 * part + place) * height, 16)
                    rows = pl.ds(start, height)
                    out[first : first + height, :] = add_low(own[rows, :], other[rows, :])
                    first += height


def fold_rows(pairs, steps, parts=1):
    operands = list(zip(*(rows for pair in pairs for rows in pair)))
    heights = [sum(rows.shape[0] for rows in four[::2]) // 2 for four in operands]
    if any(rows.shape[0] // parts % 32 for four in operands for rows in four):
        sent, kept = [], []
        for four, step in zip(operands, steps):
            sums = [add_low(*four[i : i + 2]) for i in range(0, len(four), 2)]
            for place, results in ((1 - side(step), sent), (side(step), kept)):
                pieces = []
                for rows in sums:
                    height = rows.shape[0] // (2 * parts)
                    pieces += [
                        lax.dynamic_slice_in_dim(rows, (2 * part + place) * height, height, 0)
                        for part in range(parts)
                    ]
                results.append(jnp.concatenate(pieces, axis=0))
        return sent, kept

    def whole(rows):
        return pl.BlockSpec((rows, 512), lambda i, sides: (0, 0))

    outs = [height for height in heights for _ in range(2)]
    results = pl.pallas_call(
        functools.partial(fold_kernel, len(steps), len(pairs), parts),
        grid_spec=pltpu.PrefetchScalarGridSpec(
            num_scalar_prefetch=1,
            grid=(1,),
            in_specs=[whole(rows.shape[0]) for four in operands for rows in four],
            out_specs=[whole(height) for height in outs],
        ),
        out_shape=[jax.ShapeDtypeStruct((height, 512), jnp.bfloat16) for height in outs],
        compiler_params=pltpu.CompilerParams(vmem_limit_bytes=FOLD_LIMIT),
        cost_estimate=pl.CostEstimate(
            flops=0, bytes_accessed=6 * 1024 * sum(outs), transcendentals=0
        ),
    )(jnp.stack([side(step) for step in steps]), *(rows for four in operands for rows in four))
    return list(results[::2]), list(results[1::2])


def add_kernel(stripes, *refs):
    for number in range(stripes):
        refs[2 * stripes + number][...] = add_low(refs[2 * number][...], refs[2 * number + 1][...])


def add_rows(kept, arrived):
    if any(rows.shape[0] % 16 for rows in kept):
        return [add_low(*pair) for pair in zip(kept, arrived)]
    specs = [whole_array(rows.shape) for rows in kept]
    return list(
        pl.pallas_call(
            functools.partial(add_kernel, len(kept)),
            grid=(1,),
            in_specs=[spec for spec in specs for _ in range(2)],
            out_specs=specs,
            out_shape=[jax.ShapeDtypeStruct(rows.shape, rows.dtype) for rows in kept],
            compiler_params=pltpu.CompilerParams(vmem_limit_bytes=SUM_LIMIT),
        )(*(rows for pair in zip(kept, arrived) for rows in pair))
    )


def join_kernel(stripes, sides, *refs):
    for number in range(stripes):
        own, other, out = refs[2 * number], refs[2 * number + 1], refs[2 * stripes + number]
        height = own.shape[0] // 2
        for part in range(2):
            for source, place in ((own, sides[number]), (other, 1 - sides[number])):
                start = pl.multiple_of((2 * part + place) * height, 16)
                out[pl.ds(start, height), :] = source[part * height : (part + 1) * height, :]


def join_rows(stripes, arrived, steps):
    heights = [rows.shape[0] // 2 for rows in stripes]
    if any(height % 16 for height in heights):
        joined = []
        for rows, other, step, height in zip(stripes, arrived, steps, heights):
            first = side(step) == 0
            low_rows, high_rows = jnp.where(first, rows, other), jnp.where(first, other, rows)
            joined.append(
                jnp.concatenate(
                    [
                        half[part]
                        for part in (slice(0, height), slice(height, None))
                        for half in (low_rows, high_rows)
                    ],
                    axis=0,
                )
            )
        return joined

    def whole(height):
        return pl.BlockSpec((height, 512), lambda i, sides: (0, 0))

    return list(
        pl.pallas_call(
            functools.partial(join_kernel, len(stripes)),
            grid_spec=pltpu.PrefetchScalarGridSpec(
                num_scalar_prefetch=1,
                grid=(1,),
                in_specs=[whole(2 * height) for height in heights for _ in range(2)],
                out_specs=[whole(4 * height) for height in heights],
            ),
            out_shape=[jax.ShapeDtypeStruct((4 * height, 512), jnp.bfloat16) for height in heights],
            compiler_params=pltpu.CompilerParams(vmem_limit_bytes=SUM_LIMIT),
            cost_estimate=pl.CostEstimate(
                flops=0, bytes_accessed=8 * 1024 * sum(heights), transcendentals=0
            ),
        )(
            jnp.stack([side(step) for step in steps]),
            *(rows for pair in zip(stripes, arrived) for rows in pair),
        )
    )


def tie(*groups):
    return lax.optimization_barrier(groups)


def step_orders():
    utt, seq = axis_bits("utt"), axis_bits("seq")
    across, line, rest = utt[1:], seq[:1], seq[1:]
    return (
        line + across + rest,
        across + rest + line,
        rest[:1] + line + across + rest[1:],
    )


def all_shared(copies):
    return lax.all_to_all(copies, ("utt", "seq"), 0, 0, tiled=True)


def from_neighbours(head, tail):
    count = lax.axis_size("seq")
    before = lax.ppermute(tail, "seq", [(i, i + 1) for i in range(count - 1)])
    behind = lax.ppermute(head, "seq", [(i + 1, i) for i in range(count - 1)])
    return before, behind


def pair_rows(mine, theirs, start=0, width=None):
    columns = slice(start, start + (width or mine.shape[1]))
    return jnp.concatenate([mine[:, columns], theirs[:, columns]], axis=0)


def outer(left, right):
    return low(matmul(left.T, right))


def put_half(outs, side_number, half, value):
    @pl.when(side_number == half)
    def _():
        outs[1][...] = value

    @pl.when(side_number != half)
    def _():
        outs[0][...] = value


def feed_blocks(refs, outs, sides):
    hidden, grad_pre, active, grad_low = (refs[2 * i : 2 * i + 2] for i in range(4))
    hidden_cols = pair_rows(*hidden).T
    grad_rows = pair_rows(*grad_low)
    for half in range(2):
        block = low(matmul(hidden_cols, pair_rows(*grad_pre, 512 * half, 512)))
        put_half(outs[:2], sides[1], half, block)
        block = outer(pair_rows(*active, 512 * half, 512), grad_rows)
        put_half(outs[2:4], sides[2], half, block)


def second_kernel(places, *refs):
    feed_blocks(refs[:8], refs[8:], places)


def mixer_blocks_kernel(places, *refs):
    refs, outs = refs[:12], refs[12:]
    mixer = outer(pair_rows(*refs[:2]), pair_rows(*refs[2:4]))
    branch = outer(pair_rows(*refs[4:6]), pair_rows(*refs[6:8]))
    attend = outer(pair_rows(*refs[8:10]), pair_rows(*refs[10:12]))
    for half in range(2):
        pieces = (
            mixer[256 * half : 256 * half + 256],
            branch[128 * half : 128 * half + 128],
            attend[128 * half : 128 * half + 128],
        )
        put_half(outs, places[3], half, jnp.concatenate(pieces, axis=0))


def turn_kernel(places, *refs):
    for number in range(3):
        mine, theirs, out = refs[2 * number], refs[2 * number + 1], refs[8 + number]
        rows = mine.shape[0]
        out[:, :rows] = mine[...].T
        out[:, rows:] = theirs[...].T
    refs[11][...] = add_low(refs[6][...], refs[7][...])


def late_kernel(
    keeping,
    places,
    hidden_cols,
    grad_pre,
    grad_pre_other,
    active_cols,
    grad_low,
    grad_low_other,
    attend_cols,
    attend_rows,
    attend_rows_other,
    position,
    *outs,
):
    step = pl.program_id(0)
    half = places[3] if keeping else 1 - places[3]

    def blocks(left, mine, theirs):
        return low(matmul(left[...], jnp.concatenate([mine[...], theirs[...]], axis=0)))

    @pl.when(step == 0)
    def _():
        outs[0][...] = blocks(hidden_cols, grad_pre, grad_pre_other)

    @pl.when(step == 1)
    def _():
        outs[1][...] = blocks(active_cols, grad_low, grad_low_other)

    @pl.when((step == 2) & (places[0] + half < 2))
    def _():
        outs[2][...] = blocks(attend_cols, attend_rows, attend_rows_other)

    @pl.when((step == 2) & (places[0] + half == 2))
    def _():
        outs[2][...] = position[...]


def late_blocks(keeping, places, cols, grad_pre, pair):
    hidden_cols, active_cols, attend_cols, position = cols
    rows = pair[0].shape[0]

    def half(p, stripe):
        return p[stripe] if keeping else 1 - p[stripe]

    def whole(shape):
        return pl.BlockSpec(shape, lambda i, p: (0, 0))

    def attend_column(i, p):
        return (0, jnp.where(p[0] == 0, 2 + half(p, 3), 4))

    block = (rows, 512)
    return list(
        pl.pallas_call(
            functools.partial(late_kernel, keeping),
            grid_spec=pltpu.PrefetchScalarGridSpec(
                num_scalar_prefetch=1,
                grid=(3,),
                in_specs=[
                    whole(hidden_cols.shape),
                    pl.BlockSpec(block, lambda i, p: (0, half(p, 1))),
                    pl.BlockSpec(block, lambda i, p: (0, half(p, 1))),
                    pl.BlockSpec((512, 2 * rows), lambda i, p: (half(p, 2), 0)),
                    pl.BlockSpec(block, lambda i, p: (0, 5)),
                    pl.BlockSpec(block, lambda i, p: (0, 5)),
                    whole(attend_cols.shape),
                    pl.BlockSpec(block, attend_column),
                    pl.BlockSpec(block, attend_column),
                    whole(position.shape),
                ],
                out_specs=[whole((512, 512))] * 3,
            ),
            out_shape=[jax.ShapeDtypeStruct((512, 512), jnp.bfloat16)] * 3,
            compiler_params=pltpu.CompilerParams(vmem_limit_bytes=SUM_LIMIT if keeping else VMEM_LIMIT),
            cost_estimate=pl.CostEstimate(
                flops=6 * 512 * 512 * 2 * rows, bytes_accessed=6 * 10**6, transcendentals=0
            ),
        )(
            places,
            hidden_cols,
            grad_pre,
            pair[1],
            active_cols,
            *pair,
            attend_cols,
            *pair,
            position,
        )
    )


def columns(pair, width, number, by_core=False):
    index = (lambda numbers: number + numbers[0]) if by_core else number
    return [Part(array, (array.shape[0], width), (0, index)) for array in pair]


def block_sums(kernel, places, stripes, operands):
    blocks = vmem_call(
        kernel,
        [((512, 512), jnp.bfloat16)] * (2 * stripes),
        (),
        [part for pair in operands for part in pair],
        cost=7 * 10**8 * stripes,
        numbers=(places,),
    )
    return blocks[::2], blocks[1::2]


def spread_kernel(count, places, *refs):
    for source, out in zip(refs[:count], refs[-count:]):
        out[...] = wide(source[...]).reshape(out.shape)


def spread_blocks(core, halves, stripes, shapes, bases):
    def source(height, start):
        return pl.BlockSpec((height, 512), lambda i, places: (start // height + i, 0))

    def quarter(p, stripe):
        return 2 * p[0] + p[stripe]

    in_specs = [
        source(512, 0),
        source(512, 0),
        source(128, 0),
        source(64, 256),
        source(64, 384),
        source(256, 512),
    ]
    out_specs = [
        pl.BlockSpec((1, 512, 512), lambda i, p: (1 - i, 0, quarter(p, 1))),
        pl.BlockSpec((1, 512, 512), lambda i, p: (1 - i, quarter(p, 2), 0)),
        pl.BlockSpec((128, 512), lambda i, p: (2 * p[3] + i, p[0])),
        pl.BlockSpec((64, 512), lambda i, p: (2 * quarter(p, 3) + i, 0)),
        pl.BlockSpec((64, 512), lambda i, p: (2 * quarter(p, 3) + i, 0)),
        pl.BlockSpec((1, 256, 512), lambda i, p: (quarter(p, 3), i, 0)),
    ]
    pieces = [stripes[0], stripes[1]] + [stripes[2]] * 4
    return list(
        pl.pallas_call(
            functools.partial(spread_kernel, len(pieces)),
            grid_spec=pltpu.PrefetchScalarGridSpec(
                num_scalar_prefetch=1,
                grid=(2,),
                in_specs=in_specs + [pl.BlockSpec(memory_space=pl.ANY)] * len(bases),
                out_specs=out_specs,
            ),
            out_shape=[jax.ShapeDtypeStruct(shape, jnp.float32) for shape in shapes],
            input_output_aliases={1 + len(pieces) + n: n for n in range(len(bases))},
            compiler_params=pltpu.CompilerParams(vmem_limit_bytes=VMEM_LIMIT),
            cost_estimate=pl.CostEstimate(
                flops=0, bytes_accessed=6 * 512 * 3072, transcendentals=0
            ),
        )(jnp.concatenate([core, halves]), *pieces, *bases)
    )


def angle_tables(frame_count, features):
    halves = jnp.arange(features // 2, dtype=jnp.int32).astype(jnp.float32)
    frequencies = jnp.exp(halves * (-2.0 * math.log(10000.0) / features))
    fine = 32
    low_angles = jnp.arange(fine, dtype=jnp.int32).astype(jnp.float32)[:, None] * frequencies
    high_angles = (fine * jnp.arange(frame_count // fine, dtype=jnp.int32)).astype(jnp.float32)[
        :, None
    ] * frequencies
    low_sin, low_cos = jnp.sin(low_angles)[None], jnp.cos(low_angles)[None]
    high_sin, high_cos = jnp.sin(high_angles)[:, None], jnp.cos(high_angles)[:, None]
    sines = high_sin * low_cos + high_cos * low_sin
    cosines = high_cos * low_cos - high_sin * low_sin
    shape = (frame_count, features // 2)
    return sines.reshape(shape), cosines.reshape(shape)


def heads_out(blocks, groups):
    return lax.all_to_all(jnp.tile(blocks, (groups, 1, 1)), "seq", 0, 0, tiled=True)


def rows_dot(first_operand, second_operand):
    return lax.dot_general(
        first_operand, second_operand, (((1,), (1,)), ((), ())), preferred_element_type=jnp.float32
    )


def lane_side(shape, utterance):
    return (lax.broadcasted_iota(jnp.int32, shape, 1) // HEAD_DIM) == utterance


def turned_queries(content, shift, weight, sines, cosines):
    offset = (content.astype(jnp.float32) + shift).astype(jnp.bfloat16)
    half = sines.shape[1]
    spread = jnp.dot(offset, weight, preferred_element_type=jnp.float32)
    sin_part, cos_part = spread[:, :half], spread[:, half:]
    return (
        offset,
        (sin_part * sines + cos_part * cosines).astype(jnp.bfloat16),
        (cos_part * sines - sin_part * cosines).astype(jnp.bfloat16),
    )


def attend_kernel(
    limits,
    content,
    keys,
    values,
    shift,
    weight,
    sines,
    cosines,
    table,
    weights_out,
    attended_out,
    held,
):
    scale = HEAD_DIM ** (-0.5)
    content_rows = content[...]
    key_side = jnp.concatenate([table[...], keys[...]], axis=1)
    places = lax.broadcasted_iota(jnp.int32, (1, table.shape[0]), 1)
    attended = None
    for utterance in range(limits.shape[0]):
        ours = lane_side(content_rows.shape, utterance)
        mine = jnp.where(ours, content_rows, jnp.zeros_like(content_rows))
        moved = jnp.where(ours, shift[...], 0.0)
        _, turned_cos, turned_sin = turned_queries(
            mine, moved, weight[...], sines[...], cosines[...]
        )
        query_side = jnp.concatenate([turned_cos, turned_sin, mine], axis=1) * scale
        scores = rows_dot(query_side.astype(jnp.bfloat16), key_side)
        scores = jnp.where(places < limits[utterance], scores, -1000000000.0)
        raised = jnp.exp(scores - jnp.max(scores, axis=1, keepdims=True))
        totals = jnp.sum(raised, axis=1, keepdims=True)
        weights = (raised * (1.0 / totals)).astype(jnp.bfloat16)
        weights_out[utterance] = weights
        part = jnp.dot(weights, values[...], preferred_element_type=jnp.float32)
        attended = part if attended is None else jnp.where(ours, part, attended)
    if held is None:
        attended_out[...] = attended.astype(jnp.bfloat16)
        return
    step = pl.program_id(0)
    height = attended.shape[0]
    block = attended_out.shape[1] - 2 * HALO
    held[pl.ds(pl.multiple_of(HALO + step * height, 8), height), :] = attended
    for number in range(height // block):
        attended_out[step * (height // block) + number, 0:block, :] = attended[
            number * block : (number + 1) * block
        ].astype(jnp.bfloat16)

    @pl.when(step == pl.num_programs(0) - 1)
    def _():
        edge = jnp.zeros((HALO, held.shape[1]), jnp.float32)
        held[0:HALO, :] = edge
        held[held.shape[0] - HALO :, :] = edge
        for number in range(attended_out.shape[0]):
            start = number * block
            sides = jnp.concatenate(
                [
                    held[start : start + HALO, :],
                    held[start + HALO + block : start + 2 * HALO + block, :],
                ],
                axis=0,
            )
            attended_out[number, block:, :] = sides.astype(jnp.bfloat16)


def attend_back_kernel(
    weights,
    content,
    grads,
    keys,
    values,
    shift,
    weight,
    sines,
    cosines,
    table,
    *outs,
):
    step = pl.program_id(0)
    query_out, pairs_out, weight_out, sums_out, key_sums, value_sums = (None,) * (
        6 - len(outs)
    ) + outs
    scale = HEAD_DIM ** (-0.5)

    @pl.when(step == 0)
    def _():
        key_sums[...] = jnp.zeros_like(key_sums)
        value_sums[...] = jnp.zeros_like(value_sums)
        weight_out[...] = jnp.zeros_like(weight_out)
        sums_out[...] = jnp.zeros_like(sums_out)

    content_rows, grad_rows = content[...], grads[...]
    content_cols = content_rows.T
    grad_cols = grad_rows.T
    key_side = jnp.concatenate([table[...], keys[...]], axis=1)
    half = sines.shape[1]
    grad_content = grad_position = None
    for utterance in range(weights.shape[0]):
        low, high = utterance * HEAD_DIM, (utterance + 1) * HEAD_DIM
        ours = lane_side(content_rows.shape, utterance)
        probs = weights[utterance]
        wide = probs.astype(jnp.float32)
        grad_mine = jnp.where(ours, grad_rows, jnp.zeros_like(grad_rows)) * scale
        grad_probs = rows_dot(grad_mine.astype(jnp.bfloat16), values[...])
        product = wide * grad_probs
        inner = jnp.sum(product, axis=1, keepdims=True)
        grad_scores = (product - wide * inner).astype(jnp.bfloat16)
        value_sums[low:high, :] += jnp.dot(
            grad_cols[low:high, :], probs, preferred_element_type=jnp.float32
        )
        key_sums[low:high, :] += jnp.dot(
            content_cols[low:high, :], grad_scores, preferred_element_type=jnp.float32
        )
        grad_side = jnp.dot(grad_scores, key_side, preferred_element_type=jnp.float32)
        grad_cos_table = grad_side[:, :half]
        grad_sin_table = grad_side[:, half : 2 * half]
        from_table = jnp.concatenate(
            [
                grad_cos_table * sines[...] - grad_sin_table * cosines[...],
                grad_cos_table * cosines[...] + grad_sin_table * sines[...],
            ],
            axis=1,
        ).astype(jnp.bfloat16)
        offset = (content_rows.astype(jnp.float32) + shift[...]).astype(jnp.bfloat16)
        weight_out[...] += jnp.dot(
            offset.T[low:high, :], from_table, preferred_element_type=jnp.float32
        )
        content_part = grad_side[:, 2 * half :]
        position_part = rows_dot(from_table, weight[...])
        if grad_content is None:
            grad_content, grad_position = content_part, position_part
        else:
            grad_content = jnp.where(ours, content_part, grad_content)
            grad_position = jnp.where(ours, position_part, grad_position)
    grad_query = (grad_content + grad_position).astype(jnp.bfloat16)
    height, lanes = grad_query.shape
    if query_out is None:
        pairs_out[pl.ds(pl.multiple_of(step * height, 16), height), 0:lanes] = grad_query
    else:
        query_out[...] = grad_query
    sums_out[0:1, :] += jnp.sum(grad_content, axis=0, keepdims=True)
    sums_out[1:2, :] += jnp.sum(grad_position, axis=0, keepdims=True)

    @pl.when(step == pl.num_programs(0) - 1)
    def _():
        first = pairs_out.shape[1] - 2 * lanes
        pairs_out[:, first : first + lanes] = key_sums[...].T.astype(jnp.bfloat16)
        pairs_out[:, first + lanes :] = value_sums[...].T.astype(jnp.bfloat16)


def query_block(frames_all):
    return 256 if frames_all <= 1024 else 128


def whole_block(shape):
    return pl.BlockSpec(shape, lambda i: (0,) * len(shape))


def row_block(height, width):
    return pl.BlockSpec((height, width), lambda i: (i, 0))


def attend_heads(limits, content, arrived, shift, weight, sines, cosines, table, block):
    utterances = limits.shape[0]
    query_frames, lanes = content.shape[0], arrived.shape[1] // 3
    frames_all, table_width = table.shape
    height = query_block(frames_all)
    chunked = query_frames == frames_all and height % block == 0
    chunks = (frames_all // block, block + 2 * HALO, lanes)
    kernel = attend_kernel
    if not chunked:
        kernel = functools.partial(attend_kernel, held=None)
    return pl.pallas_call(
        kernel,
        grid=(query_frames // height,),
        in_specs=[
            pl.BlockSpec(memory_space=pltpu.SMEM),
            row_block(height, lanes),
            pl.BlockSpec((frames_all, lanes), lambda i: (0, 1)),
            pl.BlockSpec((frames_all, lanes), lambda i: (0, 2)),
            whole_block(shift.shape),
            whole_block(weight.shape),
            row_block(height, sines.shape[1]),
            row_block(height, sines.shape[1]),
            whole_block(table.shape),
        ],
        out_specs=[
            pl.BlockSpec((utterances, height, frames_all), lambda i: (0, i, 0)),
            whole_block(chunks) if chunked else row_block(height, lanes),
        ],
        out_shape=[
            jax.ShapeDtypeStruct((utterances, query_frames, frames_all), jnp.bfloat16),
            jax.ShapeDtypeStruct(chunks if chunked else (query_frames, lanes), jnp.bfloat16),
        ],
        scratch_shapes=[pltpu.VMEM((frames_all + 2 * HALO, lanes), jnp.float32)] * chunked,
        compiler_params=pltpu.CompilerParams(vmem_limit_bytes=VMEM_LIMIT),
        cost_estimate=pl.CostEstimate(
            flops=2 * utterances * query_frames * frames_all * (table_width + 256),
            bytes_accessed=2 * utterances * query_frames * frames_all,
            transcendentals=utterances * query_frames * frames_all,
        ),
    )(limits, content, arrived, arrived, shift, weight, sines, cosines, table)


def attend_heads_back(
    weights, content, grads, arrived, shift, weight, sines, cosines, table
):
    utterances, query_frames, frames_all = weights.shape
    lanes = arrived.shape[1] // 3
    height = query_block(frames_all)
    joined = query_frames == frames_all
    width = (3 if joined else 2) * lanes
    return pl.pallas_call(
        attend_back_kernel,
        grid=(query_frames // height,),
        in_specs=[
            pl.BlockSpec((utterances, height, frames_all), lambda i: (0, i, 0)),
            row_block(height, lanes),
            row_block(height, lanes),
            pl.BlockSpec((frames_all, lanes), lambda i: (0, 1)),
            pl.BlockSpec((frames_all, lanes), lambda i: (0, 2)),
            whole_block(shift.shape),
            whole_block(weight.shape),
            row_block(height, sines.shape[1]),
            row_block(height, sines.shape[1]),
            whole_block(table.shape),
        ],
        out_specs=([] if joined else [row_block(height, lanes)])
        + [
            whole_block((frames_all, width)),
            whole_block((HEAD_DIM, table.shape[1])),
            whole_block((8, lanes)),
        ],
        out_shape=(
            [] if joined else [jax.ShapeDtypeStruct((query_frames, lanes), jnp.bfloat16)]
        )
        + [
            jax.ShapeDtypeStruct((frames_all, width), jnp.bfloat16),
            jax.ShapeDtypeStruct((HEAD_DIM, table.shape[1]), jnp.float32),
            jax.ShapeDtypeStruct((8, lanes), jnp.float32),
        ],
        scratch_shapes=[
            pltpu.VMEM((lanes, frames_all), jnp.float32),
            pltpu.VMEM((lanes, frames_all), jnp.float32),
        ],
        compiler_params=pltpu.CompilerParams(vmem_limit_bytes=VMEM_LIMIT),
        cost_estimate=pl.CostEstimate(
            flops=2 * utterances * query_frames * frames_all * (table.shape[1] + 512),
            bytes_accessed=2 * utterances * query_frames * frames_all,
            transcendentals=0,
        ),
    )(weights, content, grads, arrived, arrived, shift, weight, sines, cosines, table)


def shards(
    frames,
    lengths,
    out_grad,
    norm_gain,
    norm_bias,
    feed_in,
    feed_in_bias,
    feed_out,
    feed_out_bias,
    attend_in,
    attend_vectors,
    attend_out,
    mixer_in,
    mixer_in_bias,
    depthwise,
    mixer_vectors,
    mixer_out,
    batch_gain,
    batch_shift,
    running_mean,
    running_variance,
):
    utt_rows, block_frames, features = frames.shape
    rows = utt_rows * block_frames
    seq_count = lax.axis_size("seq")
    seq_index = lax.axis_index("seq")
    count = lax.axis_size("utt") * seq_count
    frames_all = block_frames * seq_count
    groups = seq_count // HEADS
    head, group = seq_index % HEADS, seq_index // HEADS
    query_frames = frames_all // groups
    lanes = utt_rows * HEAD_DIM
    info = jnp.concatenate(
        [(seq_index * block_frames).reshape(1), lengths, jnp.full((1,), frames_all, jnp.int32)]
    )
    hidden_units = feed_in.shape[2]
    f32, bf16 = jnp.float32, jnp.bfloat16
    flat_frames = frames.reshape(rows, features)
    square, broad = (rows, features), (rows, hidden_units)
    extended = (utt_rows * (block_frames + 2 * HALO), features)
    row_flops = 2 * rows * features
    bind = functools.partial
    edge = ((utt_rows, 2 * HALO, features), f32)
    feed_scratch = [
        pltpu.VMEM((features, hidden_units), bf16),
        pltpu.VMEM((hidden_units, features), bf16),
    ]
    attend_scratch = pltpu.VMEM((3, features, features), bf16)
    (
        edge_head,
        edge_tail,
        after_first,
        slope_first,
        entry_pack,
        sent,
    ) = vmem_call(
        bind(entry_kernel, utt_rows),
        [
            edge,
            edge,
            (square, f32),
            (broad, bf16),
            ((rows, hidden_units + 2 * features), bf16),
            ((HEADS, block_frames, 3 * lanes), bf16),
        ],
        (),
        (
            flat_frames,
            norm_gain,
            norm_bias,
            feed_in_bias,
            feed_out_bias,
            attend_vectors,
            Part(out_grad, (utt_rows, HALO, features), (0, 0, 0)),
            Part(out_grad, (utt_rows, HALO, features), (0, block_frames // HALO - 1, 0)),
        ),
        scratch=feed_scratch + [attend_scratch, pltpu.SemaphoreType.DMA((3,))],
        cost=row_flops * (2 * hidden_units + 3 * features),
        held=(feed_in, feed_out, attend_in),
    )
    sent, edge_head, edge_tail = tie(sent, edge_head, edge_tail)
    before, behind = from_neighbours(edge_head, edge_tail)
    after_sides, grad_sides = vmem_call(
        sides_kernel,
        [((2 * utt_rows * HALO, features), f32)] * 2,
        (),
        (before, behind, norm_gain, norm_bias, feed_in_bias, feed_out_bias),
        scratch=feed_scratch + [pltpu.SemaphoreType.DMA((2,))],
        cost=row_flops * 2 * hidden_units // 4,
        held=(feed_in, feed_out),
    )
    arrived, after_sides, grad_sides = tie(heads_out(sent, groups), after_sides, grad_sides)
    arrived = arrived.reshape(frames_all, 3 * lanes)
    start_query = group * query_frames
    head_content = arrived
    if groups > 1:
        head_content = lax.dynamic_slice_in_dim(arrived, start_query, query_frames, 0)
    head_vectors = lax.dynamic_slice_in_dim(
        attend_vectors.astype(f32), head * HEAD_DIM, HEAD_DIM, 1
    )
    head_shift = jnp.tile((head_vectors[4] - head_vectors[3])[None], (1, utt_rows))
    head_weight = lax.dynamic_slice_in_dim(attend_in[3], head * HEAD_DIM, HEAD_DIM, 1).reshape(
        features // 2, 2, HEAD_DIM
    )
    head_weight = jnp.tile(
        jnp.transpose(head_weight, (2, 1, 0)).reshape(HEAD_DIM, features), (utt_rows, 1)
    )
    sines, cosines = angle_tables(frames_all, features)
    key_table = jnp.concatenate([cosines, sines], axis=1).astype(bf16)
    query_sin = lax.dynamic_slice_in_dim(sines, start_query, query_frames, 0)
    query_cos = lax.dynamic_slice_in_dim(cosines, start_query, query_frames, 0)
    weights, head_attended = attend_heads(
        lengths,
        head_content,
        arrived,
        head_shift,
        head_weight,
        query_sin,
        query_cos,
        key_table,
        block_frames,
    )

    def frames_back(blocks):
        width = blocks.shape[-1]
        blocks = blocks.reshape(1, HEADS, block_frames, width)
        if groups > 1:
            blocks = lax.dynamic_update_slice_in_dim(
                jnp.zeros((groups,) + blocks.shape[1:], blocks.dtype), blocks, group, 0
            )
        blocks = lax.all_to_all(
            blocks.reshape(seq_count, block_frames, width), "seq", 0, 0, tiled=True
        ).reshape(groups, HEADS, block_frames, width)
        return lax.dynamic_slice_in_dim(blocks, group, 1, 0)[0]

    head_attended, own_limits = tie(head_attended, lengths)
    all_limits = lax.all_gather(own_limits, "utt", tiled=True)
    if head_attended.ndim == 2:
        placed = lax.dynamic_update_slice_in_dim(
            jnp.zeros((frames_all + 2 * HALO, lanes), bf16), head_attended, HALO + start_query, 0
        )
        main, before, behind = (
            placed[start : start + frames_all].reshape(seq_count, block_frames, lanes)
            for start in (HALO, 0, 2 * HALO)
        )
        head_attended = jnp.concatenate([main, before[:, :HALO], behind[:, -HALO:]], axis=1)
    attended_blocks = lax.all_to_all(head_attended, "seq", 0, 0, tiled=True)
    attended_blocks, all_limits = tie(attended_blocks, all_limits)
    if groups > 1:
        attended_blocks = jnp.sum(
            attended_blocks.reshape((groups, HEADS) + attended_blocks.shape[1:]), axis=0
        )
    taps = depthwise.T
    padded = pltpu.VMEM((utt_rows, block_frames + 2 * HALO + 16, features), f32)
    (
        after_attend,
        mixer_pack,
        linear_half,
        gate_half,
        gated,
        convolved,
        shared,
    ) = vmem_call(
        bind(mixer_kernel, utt_rows),
        [
            (extended, f32),
            ((rows, 2 * features), bf16),
            (square, f32),
            (square, f32),
            (extended, bf16),
            (extended, f32),
            ((8 * count, 128), f32),
        ],
        (info,),
        (
            attended_blocks,
            after_first,
            after_sides,
            norm_gain,
            norm_bias,
            attend_out,
            attend_vectors,
            mixer_in,
            mixer_in_bias.reshape(1, -1),
            taps,
            mixer_vectors,
        ),
        scratch=(padded,),
        cost=row_flops * 3 * features,
    )
    (
        layer_output,
        grad_mixer,
        grad_batch,
        normed_batch,
        second_pack,
        shared,
        batch_rows,
        middle_rows,
    ) = vmem_call(
        bind(middle_kernel, utt_rows, seq_count),
        [
            (square, f32),
            (square, f32),
            (extended, f32),
            (extended, f32),
            ((rows, 2 * hidden_units + 4 * features), bf16),
            ((8 * count, 128), f32),
            ((8, features), f32),
            ((16, features), f32),
        ],
        (all_limits,),
        (
            convolved,
            all_shared(shared),
            after_attend,
            out_grad.reshape(rows, features),
            grad_sides,
            norm_gain,
            norm_bias,
            batch_gain.reshape(1, -1),
            batch_shift.reshape(1, -1),
            running_mean.reshape(1, -1),
            running_variance.reshape(1, -1),
            mixer_out,
            mixer_vectors,
            feed_in_bias,
            feed_out_bias,
        ),
        scratch=feed_scratch + [pltpu.SemaphoreType.DMA((2,))],
        cost=row_flops * (4 * hidden_units + 2 * features),
        held=(feed_in, feed_out),
    )
    phases = list(zip(*step_orders()))
    near = axis_bits("utt")[0]
    core = side(near).reshape(1)
    halves = jnp.stack([side(step) for step in phases[0]])
    places = jnp.concatenate([core, halves])
    half_units, half_features = hidden_units // 2, features // 2

    def with_pair(array):
        return [array, swap(array, near)]

    second_pair = with_pair(second_pack)
    second_sent, second_kept = block_sums(
        second_kernel,
        places,
        2,
        [
            columns(second_pair, features, 8),
            columns(second_pair, half_units, 0, True),
            columns(second_pair, half_units, 2, True),
            columns(second_pair, features, 9),
        ],
    )
    second_pair, second_sent, second_kept, shared = tie(
        second_pair, second_sent, second_kept, all_shared(shared)
    )
    (
        batch_grads,
        grad_attend,
        mixer_back_pack,
        grad_blocks,
        mixer_rows,
    ) = vmem_call(
        bind(mixer_back_kernel, utt_rows),
        [
            ((8, features), f32),
            (square, f32),
            ((rows, 3 * features), bf16),
            ((HEADS, block_frames, lanes), bf16),
            ((16, features), f32),
        ],
        (info,),
        (
            grad_batch,
            normed_batch,
            shared,
            batch_rows,
            batch_gain.reshape(1, -1),
            gated,
            linear_half,
            gate_half,
            grad_mixer,
            after_attend,
            norm_gain,
            taps,
            mixer_in,
            attend_out,
        ),
        scratch=(padded, padded),
        cost=row_flops * 4 * features,
    )
    mixer_pair, mixer_back_pair = with_pair(mixer_pack), with_pair(mixer_back_pack)
    third_sent, third_kept = block_sums(
        mixer_blocks_kernel,
        places,
        1,
        [
            columns(mixer_pair, features, 1),
            columns(mixer_back_pair, features, 0, True),
            columns(second_pair, half_features, 20, True),
            columns(second_pair, features, 11),
            columns(mixer_pair, half_features, 0, True),
            columns(mixer_back_pair, features, 2),
        ],
    )
    early_sent, early_kept = second_sent + third_sent, second_kept + third_kept
    early_arrived = swap_all(early_sent, phases[0])
    head_grad = heads_out(grad_blocks, groups).reshape(frames_all, lanes)
    if groups > 1:
        head_grad = lax.dynamic_slice_in_dim(head_grad, start_query, query_frames, 0)
    head_grad, early_kept = tie(head_grad, early_kept)
    *head_grads, head_weight_grad, head_sums = attend_heads_back(
        weights,
        head_content,
        head_grad,
        arrived,
        head_shift,
        head_weight,
        query_sin,
        query_cos,
        key_table,
    )
    head_grads, head_weight_grad, head_sums, early_arrived = tie(
        head_grads, head_weight_grad, head_sums, early_arrived
    )
    grad_blocks = head_grads[-1].reshape(seq_count, block_frames, -1)
    returned = lax.all_to_all(grad_blocks, "seq", 0, 0, tiled=True)
    if groups > 1:
        returned = jnp.sum(
            returned.astype(f32).reshape(groups, HEADS, block_frames, 2 * lanes), axis=0
        ).astype(bf16)
        returned = jnp.concatenate([frames_back(head_grads[0]), returned], axis=2)
    head_weight_grad = jnp.transpose(
        head_weight_grad.reshape(HEAD_DIM, 2, features // 2), (2, 1, 0)
    ).reshape(features, HEAD_DIM)
    position_weight_grad = lax.dynamic_update_slice_in_dim(
        jnp.zeros((features, features), f32), head_weight_grad, head * HEAD_DIM, 1
    )
    head_vector_grads = lax.dynamic_update_slice_in_dim(
        jnp.zeros((8, features), f32),
        jnp.sum(head_sums.reshape(8, utt_rows, HEAD_DIM), axis=1),
        head * HEAD_DIM,
        1,
    )
    def next_phase(kept, arrived_rows, steps):
        sent_rows, kept = fold_rows([(kept, arrived_rows)], steps)
        return kept, swap_all(tie(sent_rows)[0], steps)

    early_kept, early_arrived = next_phase(early_kept, early_arrived, phases[1])
    entry_pair = with_pair(entry_pack)
    position_pair = with_pair(position_weight_grad.astype(bf16))
    entry_cols = vmem_call(
        turn_kernel,
        [
            ((features, 2 * rows), bf16),
            ((half_units, 2 * rows), bf16),
            ((features, 2 * rows), bf16),
            ((features, features), bf16),
        ],
        (),
        columns(entry_pair, features, 4)
        + columns(entry_pair, half_units, 0, True)
        + columns(entry_pair, features, 5)
        + position_pair,
        numbers=(places,),
    )
    returned, early_arrived, entry_cols = tie(returned, early_arrived, entry_cols)
    (
        frames_grad,
        entry_back_pack,
        grad_pre_first,
        entry_rows,
    ) = vmem_call(
        entry_back_kernel,
        [
            (square, f32),
            ((rows, half_units + 4 * features), bf16),
            ((rows, half_units), bf16),
            ((16, features), f32),
        ],
        (core,),
        (
            returned,
            grad_attend,
            flat_frames,
            after_first,
            slope_first,
            norm_gain,
        ),
        scratch=feed_scratch + [attend_scratch, pltpu.SemaphoreType.DMA((3,))],
        cost=row_flops * (2 * hidden_units + 3 * features),
        held=(feed_in, feed_out, attend_in),
    )
    late_factors = (entry_cols, grad_pre_first, with_pair(entry_back_pack))
    late_sent = late_blocks(False, places, *late_factors)
    late_sent, late_factors, middle_rows = tie(late_sent, late_factors, middle_rows)
    late_arrived = swap_all(late_sent, phases[0])
    late_kept = late_blocks(True, places, *late_factors)
    flat = jnp.concatenate([middle_rows, mixer_rows, entry_rows, head_vector_grads], axis=0)
    flat_steps = [near] + [steps[0] for steps in phases]
    late_arrived, flat = tie(late_arrived, flat)
    for steps in phases[1:]:
        pairs = [(late_kept, late_arrived)]
        if steps is phases[2]:
            pairs = [(early_kept, early_arrived)] + pairs
        parts = 1 if steps in phases[1:3] else 2
        sent_rows, late_kept = fold_rows(pairs, steps, parts)
        (sent_rows,) = tie(sent_rows)
        late_arrived, flat_arrived = tie(swap_all(sent_rows, steps), swap(flat, flat_steps.pop()))
        flat = flat + flat_arrived
    sums = add_rows(late_kept, late_arrived)
    for steps in phases[:0:-1]:
        (sums,) = tie(sums)
        flat_arrived = swap(flat, flat_steps.pop()) if flat_steps else jnp.zeros_like(flat)
        arrived_rows, flat_arrived = tie(swap_all(sums, steps), flat_arrived)
        flat = flat + flat_arrived
        sums = join_rows(sums, arrived_rows, steps)
    (sums,) = tie(sums)
    vector_grads = vmem_call(
        vectors_kernel,
        [
            (norm_gain.shape, f32),
            (norm_bias.shape, f32),
            (feed_in_bias.shape, f32),
            (feed_out_bias.shape, f32),
            (attend_vectors.shape, f32),
            ((1, 2 * features), f32),
            (mixer_vectors.shape, f32),
            ((KERNEL, features), f32),
        ],
        (),
        (flat,),
    )
    vector_grads = list(vector_grads)
    vector_grads[5] = vector_grads[5].reshape(-1)
    vector_grads[7] = vector_grads[7].T
    vector_grads = [*vector_grads, batch_grads[1], batch_grads[0], batch_rows[2], batch_rows[3]]
    arrived_rows = swap_all(sums, phases[0])
    across_rows = swap_all(sums, [near] * 3)
    shapes = [feed_in.shape, feed_out.shape, mixer_in.shape, mixer_out.shape]
    shapes += [attend_out.shape, attend_in.shape]
    spread = spread_blocks(core, halves, sums, shapes, [])
    spread = spread_blocks(1 - core, halves, across_rows, shapes, spread)
    spread, arrived_rows, vector_grads = tie(spread, arrived_rows, vector_grads)
    across_rows = swap_all(arrived_rows, [near] * 3)
    spread = spread_blocks(core, 1 - halves, arrived_rows, shapes, spread)
    (
        feed_in_grad,
        feed_out_grad,
        mixer_in_grad,
        mixer_out_grad,
        attend_out_grad,
        attend_in_grad,
    ) = spread_blocks(1 - core, 1 - halves, across_rows, shapes, spread)
    (
        norm_gain_grad,
        norm_bias_grad,
        feed_in_bias_grad,
        feed_out_bias_grad,
        attend_vectors_grad,
        mixer_in_bias_grad,
        mixer_vectors_grad,
        taps_grad,
        batch_gain_grad,
        batch_shift_grad,
        new_mean,
        new_variance,
    ) = vector_grads
    return (
        layer_output.reshape(frames.shape),
        frames_grad.reshape(frames.shape),
        norm_gain_grad,
        norm_bias_grad,
        feed_in_grad,
        feed_in_bias_grad,
        feed_out_grad,
        feed_out_bias_grad,
        attend_in_grad,
        attend_vectors_grad,
        attend_out_grad,
        mixer_in_grad,
        mixer_in_bias_grad,
        taps_grad,
        mixer_vectors_grad,
        mixer_out_grad,
        batch_gain_grad,
        batch_shift_grad,
        new_mean,
        new_variance,
    )


def solution(mesh):
    return jax.shard_map(
        shards,
        mesh=mesh,
        in_specs=(
            P("utt", "seq", None),
            P("utt"),
            P("utt", "seq", None),
            P(),
            P(),
            P(),
            P(),
            P(),
            P(),
            P(),
            P(),
            P(),
            P(),
            P(),
            P(),
            P(),
            P(),
            P(),
            P(),
            P(),
            P(),
        ),
        out_specs=(
            P("utt", "seq", None),
            P("utt", "seq", None),
            P(),
            P(),
            P(),
            P(),
            P(),
            P(),
            P(),
            P(),
            P(),
            P(),
            P(),
            P(),
            P(),
            P(),
            P(),
            P(),
            P(),
            P(),
        ),
        check_vma=False,
    )
```

```python
import functools
import math

import jax
import jax.numpy as jnp
import numpy as np
from jax import lax
from jax.experimental import pallas as pl
from jax.experimental.pallas import tpu as pltpu
from jax.sharding import PartitionSpec as P

HEADS = 8
KERNEL = 9
HEAD_DIM = 64


TOP_PRECISION = lax.Precision.HIGHEST
EPSILON = 1e-05
VMEM_LIMIT = 63 * 1024 * 1024
SUM_LIMIT = 20 * 1024 * 1024
HALO = 8


def wide(values):
    return values.astype(jnp.float32)


def low(values):
    return values.astype(jnp.bfloat16)


def matmul(first_operand, second_operand):
    return jnp.dot(first_operand, second_operand, preferred_element_type=jnp.float32)


def column_sum(values):
    return jnp.sum(wide(values), axis=0, keepdims=True)


def normalize(values):
    average = jnp.mean(values, axis=-1, keepdims=True)
    centered = values - average
    spread = jnp.mean(centered * centered, axis=-1, keepdims=True)
    inverse = lax.rsqrt(spread + EPSILON)
    return centered * inverse, inverse


def scaled_norm(normed, gains, biases, number):
    return normed * wide(gains[number : number + 1, :]) + wide(biases[number : number + 1, :])


def norm_back(grad_rows, normed, inverse, gains, number, own=lambda values: values):
    scaled = grad_rows * wide(gains[number : number + 1, :])
    inner = (
        scaled
        - jnp.mean(scaled, axis=-1, keepdims=True)
        - normed * jnp.mean(scaled * normed, axis=-1, keepdims=True)
    )
    return inner * inverse, column_sum(own(grad_rows * normed)), column_sum(own(grad_rows))


def logistic(values):
    return 1.0 / (1.0 + jnp.exp(-values))


def silu_slope(preact, sigmoid):
    return sigmoid * (1.0 + preact * (1.0 - sigmoid))


def frame_places(info, rows, utterances, halo):
    per = rows // utterances
    row = lax.broadcasted_iota(jnp.int32, (rows, 1), 0)
    limit = jnp.full((rows, 1), info[utterances], jnp.int32)
    for utterance in range(utterances - 1):
        limit = jnp.where(row // per == utterance, info[1 + utterance], limit)
    return info[0] - halo + row % per, limit


def flags(condition):
    return jnp.where(condition, 1.0, 0.0)


def own_rows(values, utterances):
    per = values.shape[0] // utterances
    return jnp.concatenate(
        [values[u * per + HALO : (u + 1) * per - HALO] for u in range(utterances)], axis=0
    )


def with_sides(values, sides, utterances):
    per = values.shape[0] // utterances
    pieces = []
    for u in range(utterances):
        pieces.append(sides[2 * u * HALO : (2 * u + 1) * HALO])
        pieces.append(values[u * per : (u + 1) * per])
        pieces.append(sides[(2 * u + 1) * HALO : (2 * u + 2) * HALO])
    return jnp.concatenate(pieces, axis=0)


def blocks_of_heads(rows, utterances):
    per = rows.shape[0] // utterances
    first = lax.broadcasted_iota(jnp.int32, (per, 2 * HEAD_DIM), 1) < HEAD_DIM
    blocks = []
    for pair in range(HEADS // 2):
        columns = rows[:, pair * 2 * HEAD_DIM : (pair + 1) * 2 * HEAD_DIM]
        top, bottom = columns[:per], columns[per:]
        blocks.append(jnp.where(first, top, pltpu.roll(bottom, HEAD_DIM, 1)))
        blocks.append(jnp.where(first, pltpu.roll(top, HEAD_DIM, 1), bottom))
    return blocks


def rows_of_heads(blocks):
    per = blocks[0].shape[0]
    first = lax.broadcasted_iota(jnp.int32, (per, 2 * HEAD_DIM), 1) < HEAD_DIM
    columns = []
    for pair in range(HEADS // 2):
        left, right = blocks[2 * pair], blocks[2 * pair + 1]
        top = jnp.where(first, left, pltpu.roll(right, HEAD_DIM, 1))
        bottom = jnp.where(first, pltpu.roll(left, HEAD_DIM, 1), right)
        columns.append(jnp.concatenate([top, bottom], axis=0))
    return jnp.concatenate(columns, axis=1)


def whole_array(shape):
    return pl.BlockSpec(shape, lambda i: (0,) * len(shape))


class Part:
    def __init__(self, array, block, index):
        self.array, self.block, self.index = array, block, index

    def spec(self):
        def index(i, *numbers):
            return tuple(at(*numbers) if callable(at) else at for at in self.index)

        return pl.BlockSpec(self.block, index)


def vmem_call(kernel, shapes, smem, operands, scratch=(), cost=0, held=(), numbers=()):
    def whole(shape):
        return pl.BlockSpec(shape, lambda i, *numbers: (0,) * len(shape))

    return pl.pallas_call(
        kernel,
        grid_spec=pltpu.PrefetchScalarGridSpec(
            num_scalar_prefetch=len(numbers),
            grid=(1,),
            in_specs=[pl.BlockSpec(memory_space=pltpu.SMEM)] * len(smem)
            + [
                operand.spec() if isinstance(operand, Part) else whole(operand.shape)
                for operand in operands
            ]
            + [pl.BlockSpec(memory_space=pl.ANY)] * len(held),
            out_specs=[whole(shape) for shape, _ in shapes],
            scratch_shapes=list(scratch),
        ),
        out_shape=[jax.ShapeDtypeStruct(shape, dtype) for shape, dtype in shapes],
        compiler_params=pltpu.CompilerParams(vmem_limit_bytes=VMEM_LIMIT),
        cost_estimate=pl.CostEstimate(flops=cost, bytes_accessed=cost // 300, transcendentals=0),
    )(
        *numbers,
        *smem,
        *(operand.array if isinstance(operand, Part) else operand for operand in operands),
        *held,
    )


def fetch(pairs, semaphores):
    copies = [
        pltpu.make_async_copy(source, target, semaphores.at[number])
        for number, (source, target) in enumerate(pairs)
    ]
    for copy in copies:
        copy.start()
    return copies


def feed_rows(values, gains, biases, copies, weight_in, bias_in, weight_out, bias_out):
    normed, _ = normalize(values)
    hidden = low(scaled_norm(normed, gains, biases, 0))
    copies[0].wait()
    preact = matmul(hidden, weight_in[...]) + wide(bias_in[0:1, :])
    sigmoid = logistic(preact)
    active = low(preact * sigmoid)
    copies[1].wait()
    branch = matmul(active, weight_out[...]) + wide(bias_out[0:1, :])
    return values + 0.5 * branch, preact, sigmoid, active


def entry_kernel(
    utterances,
    frames,
    gains,
    biases,
    bias_in,
    bias_out,
    vectors,
    grads_head,
    grads_tail,
    feed_in,
    feed_out,
    attend_in,
    head_out,
    tail_out,
    after_out,
    slope_out,
    pack_out,
    sent_out,
    weight_in,
    weight_out,
    weight_attend,
    semaphores,
):
    copies = fetch(
        [
            (feed_in.at[0], weight_in),
            (feed_out.at[0], weight_out),
            (attend_in.at[pl.ds(0, 3)], weight_attend),
        ],
        semaphores,
    )
    per = frames.shape[0] // utterances
    for u in range(utterances):
        head_out[u, 0:HALO, :] = frames[u * per : u * per + HALO, :]
        head_out[u, HALO:, :] = grads_head[u]
        tail_out[u, 0:HALO, :] = frames[(u + 1) * per - HALO : (u + 1) * per, :]
        tail_out[u, HALO:, :] = grads_tail[u]
    units, features = slope_out.shape[1], frames.shape[1]
    pack_out[:, units : units + features] = low(scaled_norm(normalize(frames[...])[0], gains, biases, 0))
    after, preact, sigmoid, active = feed_rows(
        frames[...], gains, biases, copies, weight_in, bias_in, weight_out, bias_out
    )
    slope_out[...] = low(silu_slope(preact, sigmoid))
    pack_out[:, :units] = active
    after_out[...] = after
    normed, _ = normalize(after)
    hidden = low(scaled_norm(normed, gains, biases, 1))
    pack_out[:, units + features :] = hidden
    copies[2].wait()
    queries = matmul(hidden, weight_attend[0]) + wide(vectors[0:1, :])
    parts = (
        queries + wide(vectors[3:4, :]),
        matmul(hidden, weight_attend[1]),
        matmul(hidden, weight_attend[2]) + wide(vectors[1:2, :]),
    )
    lanes = 2 * HEAD_DIM
    for number, part in enumerate(parts):
        for head, block in enumerate(blocks_of_heads(part, utterances)):
            sent_out[head, :, number * lanes : (number + 1) * lanes] = low(block)


def sides_kernel(
    before,
    behind,
    gains,
    biases,
    bias_in,
    bias_out,
    feed_in,
    feed_out,
    after_out,
    grads_out,
    weight_in,
    weight_out,
    semaphores,
):
    copies = fetch([(feed_in.at[0], weight_in), (feed_out.at[0], weight_out)], semaphores)
    frames, grads = (
        jnp.concatenate(
            [
                source[u, first : first + HALO, :]
                for u in range(before.shape[0])
                for source in (before, behind)
            ],
            axis=0,
        )
        for first in (0, HALO)
    )
    grads_out[...] = grads
    after_out[...] = feed_rows(
        frames, gains, biases, copies, weight_in, bias_in, weight_out, bias_out
    )[0]


def mixer_kernel(
    utterances,
    info,
    blocks,
    after,
    after_sides,
    gains,
    biases,
    attend_out,
    vectors,
    mixer_in,
    mixer_bias,
    taps,
    mixer_vectors,
    after_out,
    pack_out,
    linear_out,
    gate_out,
    gated_out,
    convolved_out,
    sums_out,
    padded,
):
    per = after.shape[0] // utterances
    main, before, behind = [], [], []
    for head in range(HEADS):
        block = wide(blocks[head])
        main.append(block[:per])
        before.append(block[per : per + HALO])
        behind.append(block[per + HALO :])
    attended = rows_of_heads(main)
    features = after.shape[1]
    pack_out[:, :features] = low(attended)
    before, behind = rows_of_heads(before), rows_of_heads(behind)
    sides = []
    for u in range(utterances):
        sides += [before[u * HALO : (u + 1) * HALO], behind[u * HALO : (u + 1) * HALO]]
    attended = low(with_sides(attended, jnp.concatenate(sides, axis=0), utterances))
    values = with_sides(after[...], after_sides[...], utterances)
    values = values + matmul(attended, attend_out[...]) + wide(vectors[2:3, :])
    after_out[...] = values
    normed, _ = normalize(values)
    scaled = scaled_norm(normed, gains, biases, 2)
    pack_out[:, features:] = low(own_rows(scaled, utterances))
    preact = matmul(low(scaled), mixer_in[...])
    preact = preact + wide(mixer_bias[...])
    rows = values.shape[0]
    linear = preact[:, :features]
    gate = logistic(preact[:, features:])
    linear_out[...] = own_rows(linear, utterances)
    gate_out[...] = own_rows(gate, utterances)
    place, limit = frame_places(info, rows, utterances, HALO)
    mask = flags((place >= 0) & (place < limit))
    gated = low(linear * gate * mask)
    gated_out[...] = gated
    fill_padded(padded, wide(gated), utterances)
    total = None
    for offset in range(KERNEL):
        term = wide(taps[offset : offset + 1, :]) * moved(
            padded, utterances, offset - KERNEL // 2, rows // utterances
        )
        total = term if total is None else total + term
    convolved = total + wide(mixer_vectors[0:1, :])
    convolved_out[...] = convolved
    mask = own_rows(mask, utterances)
    convolved = own_rows(convolved, utterances)
    count = jnp.sum(mask, axis=0, keepdims=True)
    local_sum = jnp.sum(convolved * mask, axis=0, keepdims=True)
    centered = (convolved - local_sum / jnp.maximum(count, 1.0)) * mask
    share(sums_out, local_sum, jnp.sum(centered * centered, axis=0, keepdims=True))


def fill_padded(padded, values, utterances):
    per = values.shape[0] // utterances
    zeros = jnp.zeros((8, values.shape[1]), jnp.float32)
    for u in range(utterances):
        padded[u, 0:8, :] = zeros
        padded[u, 8 : 8 + per, :] = values[u * per : (u + 1) * per, :]
        padded[u, 8 + per : 16 + per, :] = zeros


def moved(padded, utterances, start, per, first=0):
    return jnp.concatenate(
        [
            padded[u, 8 + first + start : 8 + first + start + per, :]
            for u in range(utterances)
        ],
        axis=0,
    )


def share(sums_out, *rows):
    tile = jnp.concatenate(
        [row[:, i : i + 128] for row in rows for i in range(0, row.shape[1], 128)], axis=0
    )
    for copy in range(sums_out.shape[0] // 8):
        sums_out[copy * 8 : copy * 8 + 8, :] = tile


def as_row(tile):
    return jnp.concatenate([tile[i : i + 1] for i in range(tile.shape[0])], axis=1)


def frame_counts(limits, utt_index, shape, utterances, seq_count, per):
    place = lax.broadcasted_iota(jnp.int32, shape, 0)
    owner, first = (place // seq_count) ^ utt_index, place % seq_count * per
    total = jnp.zeros(shape, jnp.int32)
    for number in range(limits.shape[0]):
        inside = jnp.clip(limits[number] - first, 0, per)
        total = total + jnp.where(owner == number // utterances, inside, 0)
    return total.astype(jnp.float32)


def middle_kernel(
    utterances,
    seq_count,
    limits,
    utt_index,
    convolved,
    shared,
    after,
    grads,
    grad_sides,
    gains,
    biases,
    batch_gain,
    batch_shift,
    running_mean,
    running_variance,
    mixer_out,
    vectors,
    bias_in,
    bias_out,
    feed_in,
    feed_out,
    layer_out,
    grad_mixer_out,
    grad_batch_out,
    normed_out,
    pack_out,
    sums_out,
    batch_out_rows,
    vector_out,
    weight_in,
    weight_out,
    semaphores,
):
    def own(values):
        return own_rows(values, utterances)

    features, units = feed_in.shape[1:]

    def pack(number, rows):
        first = 2 * units + number * features
        pack_out[:, first : first + features] = rows

    copies = fetch([(feed_in.at[1], weight_in), (feed_out.at[1], weight_out)], semaphores)
    parts = shared[...].reshape(-1, 8, 128)
    per = grads.shape[0] // utterances
    counts = frame_counts(limits, utt_index[0], parts.shape, utterances, seq_count, per)
    totals = jnp.sum(parts, axis=0)
    valid_tile = jnp.sum(counts, axis=0)
    valid = as_row(valid_tile[:4])
    average_tile = totals / valid_tile
    drift = parts / jnp.maximum(counts, 1.0) - average_tile
    spreads = jnp.sum(counts * drift * drift, axis=0)
    average = as_row(average_tile[:4])
    variance = as_row((totals[4:] + spreads[:4]) / valid_tile[:4])
    inverse_batch = lax.rsqrt(variance + EPSILON)
    batch_out_rows[0:1, :] = inverse_batch
    batch_out_rows[1:2, :] = valid
    batch_out_rows[2:3, :] = 0.9 * running_mean[...] + 0.1 * average
    batch_out_rows[3:4, :] = 0.9 * running_variance[...] + 0.1 * variance * valid / (valid - 1.0)
    normed_batch = (convolved[...] - average) * inverse_batch
    normed_out[...] = normed_batch
    batch = normed_batch * wide(batch_gain[...]) + wide(batch_shift[...])
    batch_sigmoid = logistic(batch)
    swished = low(batch * batch_sigmoid)
    pack(2, low(own(batch * batch_sigmoid)))
    values = after[...] + matmul(swished, mixer_out[...]) + wide(vectors[1:2, :])
    normed, inverse = normalize(values)
    scaled = scaled_norm(normed, gains, biases, 3)
    pack(0, low(own(scaled)))
    copies[0].wait()
    preact = matmul(low(scaled), weight_in[...]) + wide(bias_in[1:2, :])
    sigmoid = logistic(preact)
    activated = preact * sigmoid
    active = low(activated)
    pack_out[:, units : 2 * units] = low(own(activated))
    copies[1].wait()
    branch = matmul(active, weight_out[...]) + wide(bias_out[1:2, :])
    normed_last, inverse_last = normalize(values + 0.5 * branch)
    layer_out[...] = own(scaled_norm(normed_last, gains, biases, 4))
    grad_second, gain_last, shift_last = norm_back(
        with_sides(grads[...], grad_sides[...], utterances),
        normed_last,
        inverse_last,
        gains,
        4,
        own,
    )
    grad_low = low(0.5 * grad_second)
    grad_low_own = low(own(0.5 * grad_second))
    pack(1, grad_low_own)
    grad_pre = rows_dot(grad_low, weight_out[...]) * silu_slope(preact, sigmoid)
    grad_pre_own = low(own(grad_pre))
    pack_out[:, :units] = grad_pre_own
    grad_values, gain_three, shift_three = norm_back(
        rows_dot(low(grad_pre), weight_in[...]), normed, inverse, gains, 3, own
    )
    grad_mixer = grad_second + grad_values
    grad_mixer_own = own(grad_mixer)
    grad_mixer_out[...] = grad_mixer_own
    branch_own = low(grad_mixer_own)
    pack(3, branch_own)
    grad_batch = rows_dot(low(grad_mixer), mixer_out[...]) * silu_slope(batch, batch_sigmoid)
    grad_batch_out[...] = grad_batch
    share(sums_out, column_sum(own(grad_batch)), column_sum(own(grad_batch * normed_batch)))
    bias_sum = column_sum(grad_pre_own)
    put_rows(
        vector_out,
        [gain_last, shift_last, gain_three, shift_three]
        + [bias_sum[:, i : i + features] for i in range(0, bias_sum.shape[1], features)]
        + [column_sum(grad_low_own), column_sum(branch_own)],
    )


def put_rows(out, rows):
    for number, row in enumerate(rows):
        out[number : number + 1, :] = row
    out[len(rows) :, :] = jnp.zeros((out.shape[0] - len(rows), out.shape[1]), jnp.float32)


def mixer_back_kernel(
    utterances,
    info,
    grad_batch,
    normed_batch,
    shared,
    batch_rows,
    batch_gain,
    gated,
    linear,
    gate,
    grad_mixer,
    after,
    gains,
    taps,
    mixer_in,
    attend_out,
    batch_grads_out,
    grad_attend_out,
    pack_out,
    sent_out,
    vector_out,
    padded,
    gated_padded,
):
    totals = jnp.sum(shared[...].reshape(-1, 8, 128), axis=0)
    shift_grad, gain_grad = as_row(totals[:4]), as_row(totals[4:])
    batch_grads_out[0:1, :] = shift_grad
    batch_grads_out[1:2, :] = gain_grad
    rows, features = grad_batch.shape
    place, limit = frame_places(info, rows, utterances, HALO)
    mask = flags((place >= 0) & (place < limit))
    inside = flags((place >= 0) & (place < info[utterances + 1]))
    inverse_batch, valid = batch_rows[0:1, :], batch_rows[1:2, :]
    grad_conv = low(
        inside
        * wide(batch_gain[...])
        * inverse_batch
        * (grad_batch[...] - mask / valid * (shift_grad + normed_batch[...] * gain_grad))
    )
    conv_wide = wide(grad_conv)
    fill_padded(padded, conv_wide, utterances)
    fill_padded(gated_padded, wide(gated[...]), utterances)
    conv_own = own_rows(conv_wide, utterances)
    per = rows // utterances - 2 * HALO
    margin = KERNEL // 2
    total = None
    tap_rows = []
    for offset in range(KERNEL):
        term = wide(taps[offset : offset + 1, :]) * moved(
            padded, utterances, margin - offset, per, HALO
        )
        total = term if total is None else total + term
        near = moved(gated_padded, utterances, offset - margin, per, HALO)
        tap_rows.append(jnp.sum(conv_own * near, axis=0, keepdims=True))
    grad_gated = own_rows(mask, utterances) * total
    gate_half = gate[...]
    grad_pre = low(
        jnp.concatenate(
            [
                grad_gated * gate_half,
                grad_gated * linear[...] * gate_half * (1.0 - gate_half),
            ],
            axis=1,
        )
    )
    pack_out[:, : 2 * features] = grad_pre
    normed, inverse = normalize(own_rows(after[...], utterances))
    grad_values, gain_two, shift_two = norm_back(
        rows_dot(grad_pre, mixer_in[...]), normed, inverse, gains, 2
    )
    grad_attend = grad_mixer[...] + grad_values
    grad_attend_out[...] = grad_attend
    branch = low(grad_attend)
    pack_out[:, 2 * features :] = branch
    grad_attended = rows_dot(branch, attend_out[...])
    for head, block in enumerate(blocks_of_heads(grad_attended, utterances)):
        sent_out[head] = low(block)
    bias_sum = column_sum(grad_pre)
    put_rows(
        vector_out,
        [gain_two, shift_two, column_sum(conv_own), column_sum(branch)]
        + [bias_sum[:, :features], bias_sum[:, features:]]
        + tap_rows,
    )


def entry_back_kernel(
    core,
    returned,
    grad_attend,
    frames,
    after,
    slope,
    gains,
    feed_in,
    feed_out,
    attend_in,
    frames_out,
    pack_out,
    grad_pre_out,
    vector_out,
    weight_in,
    weight_out,
    weight_attend,
    semaphores,
):
    copies = fetch(
        [
            (attend_in.at[pl.ds(0, 3)], weight_attend),
            (feed_out.at[0], weight_out),
            (feed_in.at[0], weight_in),
        ],
        semaphores,
    )
    lanes = 2 * HEAD_DIM
    features, units = feed_in.shape[1:]

    def pack(number, rows):
        first = units // 2 + number * features
        pack_out[:, first : first + features] = rows

    grad_hidden = None
    low_rows = []
    for number in range(3):
        rows = low(
            rows_of_heads(
                [
                    wide(returned[head, :, number * lanes : (number + 1) * lanes])
                    for head in range(HEADS)
                ]
            )
        )
        pack(number, rows)
        low_rows.append(rows)
        if number == 0:
            copies[0].wait()
        term = rows_dot(rows, weight_attend[number])
        grad_hidden = term if grad_hidden is None else grad_hidden + term
    normed, inverse = normalize(after[...])
    grad_values, gain_one, shift_one = norm_back(grad_hidden, normed, inverse, gains, 1)
    grad_first = grad_attend[...] + grad_values
    grad_low = low(0.5 * grad_first)
    pack(3, grad_low)
    copies[1].wait()
    grad_pre = low(rows_dot(grad_low, weight_out[...]) * wide(slope[...]))
    for half in range(2):
        rows = grad_pre[:, half * units // 2 : (half + 1) * units // 2]

        @pl.when(core[0] == half)
        def _():
            grad_pre_out[...] = rows

        @pl.when(core[0] != half)
        def _():
            pack_out[:, : units // 2] = rows

    normed, inverse = normalize(frames[...])
    copies[2].wait()
    grad_values, gain_zero, shift_zero = norm_back(
        rows_dot(grad_pre, weight_in[...]), normed, inverse, gains, 0
    )
    frames_out[...] = grad_first + grad_values
    bias_sum = column_sum(grad_pre)
    put_rows(
        vector_out,
        [gain_zero, shift_zero, gain_one, shift_one]
        + [bias_sum[:, i : i + features] for i in range(0, bias_sum.shape[1], features)]
        + [column_sum(grad_low), column_sum(low_rows[0]), column_sum(low_rows[2])],
    )


def vectors_kernel(
    rows, gain_out, bias_out, in_bias_out, out_bias_out, attend_out, mixer_bias_out, mixer_out, taps_out
):
    middle, mixer, entry, heads = (0, 16, 32, 48)
    features = gain_out.shape[1]

    def take(out, target, start):
        out[target : target + 1, :] = rows[start : start + 1, :]

    for out, first in ((gain_out, 0), (bias_out, 1)):
        take(out, 0, entry + first)
        take(out, 1, entry + 2 + first)
        take(out, 2, mixer + first)
        take(out, 3, middle + 2 + first)
        take(out, 4, middle + first)
    for target, start in ((0, entry + 4), (1, middle + 4)):
        for column in range(4):
            in_bias_out[target : target + 1, column * features : (column + 1) * features] = rows[
                start + column : start + column + 1, :
            ]
    take(out_bias_out, 0, entry + 8)
    take(out_bias_out, 1, middle + 8)
    for target, start in enumerate((entry + 9, entry + 10, mixer + 3, heads, heads + 1)):
        take(attend_out, target, start)
    for column in range(2):
        mixer_bias_out[0:1, column * features : (column + 1) * features] = rows[
            mixer + 4 + column : mixer + 5 + column, :
        ]
    take(mixer_out, 0, mixer + 2)
    take(mixer_out, 1, middle + 9)
    taps_out[...] = rows[mixer + 6 : mixer + 6 + KERNEL, :]


def axis_bits(axis):
    return [(axis, 1 << bit) for bit in range(lax.axis_size(axis).bit_length() - 1)]


def swap(values, step):
    axis, mask = step
    return lax.ppermute(values, axis, [(i, i ^ mask) for i in range(lax.axis_size(axis))])


def side(step):
    axis, mask = step
    return (lax.axis_index(axis) // mask) % 2


def swap_all(stripes, steps):
    return [swap(rows, step) for rows, step in zip(stripes, steps)]


def add_low(first_operand, second_operand):
    total = first_operand.astype(jnp.float32) + second_operand.astype(jnp.float32)
    return total.astype(jnp.bfloat16)


def fold_kernel(stripes, arrays, parts, sides, *refs):
    for number in range(stripes):
        sources = refs[2 * arrays * number : 2 * arrays * (number + 1)]
        for keeping in range(2):
            place = sides[number] if keeping else 1 - sides[number]
            out = refs[2 * arrays * stripes + 2 * number + keeping]
            first = 0
            for array in range(arrays):
                own, other = sources[2 * array : 2 * array + 2]
                height = own.shape[0] // (2 * parts)
                for part in range(parts):
                    start = pl.multiple_of((2 * part + place) * height, 16)
                    rows = pl.ds(start, height)
                    out[first : first + height, :] = add_low(own[rows, :], other[rows, :])
                    first += height


def fold_rows(pairs, steps, parts=1, limit=SUM_LIMIT):
    operands = list(zip(*(rows for pair in pairs for rows in pair)))
    heights = [sum(rows.shape[0] for rows in four[::2]) // 2 for four in operands]
    if any(rows.shape[0] // parts % 32 for four in operands for rows in four):
        sent, kept = [], []
        for four, step in zip(operands, steps):
            sums = [add_low(*four[i : i + 2]) for i in range(0, len(four), 2)]
            for place, results in ((1 - side(step), sent), (side(step), kept)):
                pieces = []
                for rows in sums:
                    height = rows.shape[0] // (2 * parts)
                    pieces += [
                        lax.dynamic_slice_in_dim(rows, (2 * part + place) * height, height, 0)
                        for part in range(parts)
                    ]
                results.append(jnp.concatenate(pieces, axis=0))
        return sent, kept

    def whole(rows):
        return pl.BlockSpec((rows, 512), lambda i, sides: (0, 0))

    outs = [height for height in heights for _ in range(2)]
    results = pl.pallas_call(
        functools.partial(fold_kernel, len(steps), len(pairs), parts),
        grid_spec=pltpu.PrefetchScalarGridSpec(
            num_scalar_prefetch=1,
            grid=(1,),
            in_specs=[whole(rows.shape[0]) for four in operands for rows in four],
            out_specs=[whole(height) for height in outs],
        ),
        out_shape=[jax.ShapeDtypeStruct((height, 512), jnp.bfloat16) for height in outs],
        compiler_params=pltpu.CompilerParams(vmem_limit_bytes=limit),
        cost_estimate=pl.CostEstimate(
            flops=0, bytes_accessed=6 * 1024 * sum(outs), transcendentals=0
        ),
    )(jnp.stack([side(step) for step in steps]), *(rows for four in operands for rows in four))
    return list(results[::2]), list(results[1::2])


def add_kernel(stripes, *refs):
    for number in range(stripes):
        refs[2 * stripes + number][...] = add_low(refs[2 * number][...], refs[2 * number + 1][...])


def add_rows(kept, arrived):
    if any(rows.shape[0] % 16 for rows in kept):
        return [add_low(*pair) for pair in zip(kept, arrived)]
    specs = [whole_array(rows.shape) for rows in kept]
    return list(
        pl.pallas_call(
            functools.partial(add_kernel, len(kept)),
            grid=(1,),
            in_specs=[spec for spec in specs for _ in range(2)],
            out_specs=specs,
            out_shape=[jax.ShapeDtypeStruct(rows.shape, rows.dtype) for rows in kept],
            compiler_params=pltpu.CompilerParams(vmem_limit_bytes=SUM_LIMIT),
        )(*(rows for pair in zip(kept, arrived) for rows in pair))
    )


def join_kernel(stripes, sides, *refs):
    for number in range(stripes):
        own, other, out = refs[2 * number], refs[2 * number + 1], refs[2 * stripes + number]
        height = own.shape[0] // 2
        for part in range(2):
            for source, place in ((own, sides[number]), (other, 1 - sides[number])):
                start = pl.multiple_of((2 * part + place) * height, 16)
                out[pl.ds(start, height), :] = source[part * height : (part + 1) * height, :]


def join_rows(stripes, arrived, steps):
    heights = [rows.shape[0] // 2 for rows in stripes]
    if any(height % 16 for height in heights):
        joined = []
        for rows, other, step, height in zip(stripes, arrived, steps, heights):
            first = side(step) == 0
            low_rows, high_rows = jnp.where(first, rows, other), jnp.where(first, other, rows)
            joined.append(
                jnp.concatenate(
                    [
                        half[part]
                        for part in (slice(0, height), slice(height, None))
                        for half in (low_rows, high_rows)
                    ],
                    axis=0,
                )
            )
        return joined

    def whole(height):
        return pl.BlockSpec((height, 512), lambda i, sides: (0, 0))

    return list(
        pl.pallas_call(
            functools.partial(join_kernel, len(stripes)),
            grid_spec=pltpu.PrefetchScalarGridSpec(
                num_scalar_prefetch=1,
                grid=(1,),
                in_specs=[whole(2 * height) for height in heights for _ in range(2)],
                out_specs=[whole(4 * height) for height in heights],
            ),
            out_shape=[jax.ShapeDtypeStruct((4 * height, 512), jnp.bfloat16) for height in heights],
            compiler_params=pltpu.CompilerParams(vmem_limit_bytes=SUM_LIMIT),
            cost_estimate=pl.CostEstimate(
                flops=0, bytes_accessed=8 * 1024 * sum(heights), transcendentals=0
            ),
        )(
            jnp.stack([side(step) for step in steps]),
            *(rows for pair in zip(stripes, arrived) for rows in pair),
        )
    )


def tie(*groups):
    return lax.optimization_barrier(groups)


def step_orders():
    utt, seq = axis_bits("utt"), axis_bits("seq")
    across, line, rest = utt[1:], seq[:1], seq[1:]
    return (
        line + across + rest,
        across + rest + line,
        rest[:1] + line + across + rest[1:],
    )


def all_shared(copies):
    return lax.all_to_all(copies, ("utt", "seq"), 0, 0, tiled=True)


def from_neighbours(head, tail):
    count = lax.axis_size("seq")
    before = lax.ppermute(tail, "seq", [(i, i + 1) for i in range(count - 1)])
    behind = lax.ppermute(head, "seq", [(i + 1, i) for i in range(count - 1)])
    return before, behind


def pair_rows(mine, theirs, start=0, width=None):
    columns = slice(start, start + (width or mine.shape[1]))
    return jnp.concatenate([mine[:, columns], theirs[:, columns]], axis=0)


def outer(left, right):
    return low(matmul(left.T, right))


def put_half(outs, side_number, half, value):
    @pl.when(side_number == half)
    def _():
        outs[1][...] = value

    @pl.when(side_number != half)
    def _():
        outs[0][...] = value


def feed_blocks(refs, outs, sides):
    hidden, grad_pre, active, grad_low = (refs[2 * i : 2 * i + 2] for i in range(4))
    hidden_cols = pair_rows(*hidden).T
    grad_rows = pair_rows(*grad_low)
    for half in range(2):
        block = low(matmul(hidden_cols, pair_rows(*grad_pre, 512 * half, 512)))
        put_half(outs[:2], sides[1], half, block)
        block = outer(pair_rows(*active, 512 * half, 512), grad_rows)
        put_half(outs[2:4], sides[2], half, block)


def second_kernel(places, *refs):
    feed_blocks(refs[:8], refs[8:], places)


def mixer_blocks_kernel(places, *refs):
    refs, outs = refs[:12], refs[12:]
    mixer = outer(pair_rows(*refs[:2]), pair_rows(*refs[2:4]))
    branch = outer(pair_rows(*refs[4:6]), pair_rows(*refs[6:8]))
    attend = outer(pair_rows(*refs[8:10]), pair_rows(*refs[10:12]))
    for half in range(2):
        pieces = (
            mixer[256 * half : 256 * half + 256],
            branch[128 * half : 128 * half + 128],
            attend[128 * half : 128 * half + 128],
        )
        put_half(outs, places[3], half, jnp.concatenate(pieces, axis=0))


def turn_kernel(places, *refs):
    for number in range(3):
        mine, theirs, out = refs[2 * number], refs[2 * number + 1], refs[8 + number]
        rows = mine.shape[0]
        out[:, :rows] = mine[...].T
        out[:, rows:] = theirs[...].T
    refs[11][...] = add_low(refs[6][...], refs[7][...])


def late_kernel(
    keeping,
    places,
    hidden_cols,
    grad_pre,
    grad_pre_other,
    active_cols,
    grad_low,
    grad_low_other,
    attend_cols,
    attend_rows,
    attend_rows_other,
    position,
    *outs,
):
    step = pl.program_id(0)
    half = places[3] if keeping else 1 - places[3]

    def blocks(left, mine, theirs):
        return low(matmul(left[...], jnp.concatenate([mine[...], theirs[...]], axis=0)))

    @pl.when(step == 0)
    def _():
        outs[0][...] = blocks(hidden_cols, grad_pre, grad_pre_other)

    @pl.when(step == 1)
    def _():
        outs[1][...] = blocks(active_cols, grad_low, grad_low_other)

    @pl.when((step == 2) & (places[0] + half < 2))
    def _():
        outs[2][...] = blocks(attend_cols, attend_rows, attend_rows_other)

    @pl.when((step == 2) & (places[0] + half == 2))
    def _():
        outs[2][...] = position[...]


def late_blocks(keeping, places, cols, grad_pre, pair):
    hidden_cols, active_cols, attend_cols, position = cols
    rows = pair[0].shape[0]

    def half(p, stripe):
        return p[stripe] if keeping else 1 - p[stripe]

    def whole(shape):
        return pl.BlockSpec(shape, lambda i, p: (0, 0))

    def attend_column(i, p):
        return (0, jnp.where(p[0] == 0, 2 + half(p, 3), 4))

    block = (rows, 512)
    return list(
        pl.pallas_call(
            functools.partial(late_kernel, keeping),
            grid_spec=pltpu.PrefetchScalarGridSpec(
                num_scalar_prefetch=1,
                grid=(3,),
                in_specs=[
                    whole(hidden_cols.shape),
                    pl.BlockSpec(block, lambda i, p: (0, half(p, 1))),
                    pl.BlockSpec(block, lambda i, p: (0, half(p, 1))),
                    pl.BlockSpec((512, 2 * rows), lambda i, p: (half(p, 2), 0)),
                    pl.BlockSpec(block, lambda i, p: (0, 5)),
                    pl.BlockSpec(block, lambda i, p: (0, 5)),
                    whole(attend_cols.shape),
                    pl.BlockSpec(block, attend_column),
                    pl.BlockSpec(block, attend_column),
                    whole(position.shape),
                ],
                out_specs=[whole((512, 512))] * 3,
            ),
            out_shape=[jax.ShapeDtypeStruct((512, 512), jnp.bfloat16)] * 3,
            compiler_params=pltpu.CompilerParams(vmem_limit_bytes=SUM_LIMIT if keeping else VMEM_LIMIT),
            cost_estimate=pl.CostEstimate(
                flops=6 * 512 * 512 * 2 * rows, bytes_accessed=6 * 10**6, transcendentals=0
            ),
        )(
            places,
            hidden_cols,
            grad_pre,
            pair[1],
            active_cols,
            *pair,
            attend_cols,
            *pair,
            position,
        )
    )


def columns(pair, width, number, by_core=False):
    index = (lambda numbers: number + numbers[0]) if by_core else number
    return [Part(array, (array.shape[0], width), (0, index)) for array in pair]


def block_sums(kernel, places, stripes, operands):
    blocks = vmem_call(
        kernel,
        [((512, 512), jnp.bfloat16)] * (2 * stripes),
        (),
        [part for pair in operands for part in pair],
        cost=7 * 10**8 * stripes,
        numbers=(places,),
    )
    return blocks[::2], blocks[1::2]


def spread_kernel(count, places, *refs):
    for source, out in zip(refs[:count], refs[-count:]):
        out[...] = wide(source[...]).reshape(out.shape)


def spread_blocks(core, halves, stripes, shapes, bases):
    def source(height, start):
        return pl.BlockSpec((height, 512), lambda i, places: (start // height + i, 0))

    def quarter(p, stripe):
        return 2 * p[0] + p[stripe]

    in_specs = [
        source(512, 0),
        source(512, 0),
        source(128, 0),
        source(64, 256),
        source(64, 384),
        source(256, 512),
    ]
    out_specs = [
        pl.BlockSpec((1, 512, 512), lambda i, p: (1 - i, 0, quarter(p, 1))),
        pl.BlockSpec((1, 512, 512), lambda i, p: (1 - i, quarter(p, 2), 0)),
        pl.BlockSpec((128, 512), lambda i, p: (2 * p[3] + i, p[0])),
        pl.BlockSpec((64, 512), lambda i, p: (2 * quarter(p, 3) + i, 0)),
        pl.BlockSpec((64, 512), lambda i, p: (2 * quarter(p, 3) + i, 0)),
        pl.BlockSpec((1, 256, 512), lambda i, p: (quarter(p, 3), i, 0)),
    ]
    pieces = [stripes[0], stripes[1]] + [stripes[2]] * 4
    return list(
        pl.pallas_call(
            functools.partial(spread_kernel, len(pieces)),
            grid_spec=pltpu.PrefetchScalarGridSpec(
                num_scalar_prefetch=1,
                grid=(2,),
                in_specs=in_specs + [pl.BlockSpec(memory_space=pl.ANY)] * len(bases),
                out_specs=out_specs,
            ),
            out_shape=[jax.ShapeDtypeStruct(shape, jnp.float32) for shape in shapes],
            input_output_aliases={1 + len(pieces) + n: n for n in range(len(bases))},
            compiler_params=pltpu.CompilerParams(vmem_limit_bytes=VMEM_LIMIT),
            cost_estimate=pl.CostEstimate(
                flops=0, bytes_accessed=6 * 512 * 3072, transcendentals=0
            ),
        )(jnp.concatenate([core, halves]), *pieces, *bases)
    )


def angle_tables(frame_count, features):
    halves = jnp.arange(features // 2, dtype=jnp.int32).astype(jnp.float32)
    frequencies = jnp.exp(halves * (-2.0 * math.log(10000.0) / features))
    fine = 32
    low_angles = jnp.arange(fine, dtype=jnp.int32).astype(jnp.float32)[:, None] * frequencies
    high_angles = (fine * jnp.arange(frame_count // fine, dtype=jnp.int32)).astype(jnp.float32)[
        :, None
    ] * frequencies
    low_sin, low_cos = jnp.sin(low_angles)[None], jnp.cos(low_angles)[None]
    high_sin, high_cos = jnp.sin(high_angles)[:, None], jnp.cos(high_angles)[:, None]
    sines = high_sin * low_cos + high_cos * low_sin
    cosines = high_cos * low_cos - high_sin * low_sin
    shape = (frame_count, features // 2)
    return sines.reshape(shape), cosines.reshape(shape)


def heads_out(blocks, groups):
    return lax.all_to_all(jnp.tile(blocks, (groups, 1, 1)), "seq", 0, 0, tiled=True)


def rows_dot(first_operand, second_operand):
    return lax.dot_general(
        first_operand, second_operand, (((1,), (1,)), ((), ())), preferred_element_type=jnp.float32
    )


def lane_side(shape, utterance):
    return (lax.broadcasted_iota(jnp.int32, shape, 1) // HEAD_DIM) == utterance


def turned_queries(content, shift, weight, sines, cosines):
    offset = (content.astype(jnp.float32) + shift).astype(jnp.bfloat16)
    half = sines.shape[1]
    spread = jnp.dot(offset, weight, preferred_element_type=jnp.float32)
    sin_part, cos_part = spread[:, :half], spread[:, half:]
    return (
        offset,
        (sin_part * sines + cos_part * cosines).astype(jnp.bfloat16),
        (cos_part * sines - sin_part * cosines).astype(jnp.bfloat16),
    )


def attend_kernel(
    limits,
    content,
    keys,
    values,
    shift,
    weight,
    sines,
    cosines,
    table,
    weights_out,
    attended_out,
    held,
):
    scale = HEAD_DIM ** (-0.5)
    weight_rows = jnp.concatenate([weight[...]] * limits.shape[0], axis=0)
    content_rows = content[...]
    key_side = jnp.concatenate([table[...], keys[...]], axis=1)
    places = lax.broadcasted_iota(jnp.int32, (1, table.shape[0]), 1)
    attended = None
    for utterance in range(limits.shape[0]):
        ours = lane_side(content_rows.shape, utterance)
        mine = jnp.where(ours, content_rows, jnp.zeros_like(content_rows))
        moved = jnp.where(ours, shift[...], 0.0)
        _, turned_cos, turned_sin = turned_queries(
            mine, moved, weight_rows, sines[...], cosines[...]
        )
        query_side = jnp.concatenate([turned_cos, turned_sin, mine], axis=1) * scale
        scores = rows_dot(query_side.astype(jnp.bfloat16), key_side)
        scores = jnp.where(places < limits[utterance], scores, -1000000000.0)
        raised = jnp.exp(scores - jnp.max(scores, axis=1, keepdims=True))
        totals = jnp.sum(raised, axis=1, keepdims=True)
        weights = (raised * (1.0 / totals)).astype(jnp.bfloat16)
        weights_out[utterance] = weights
        part = jnp.dot(weights, values[...], preferred_element_type=jnp.float32)
        attended = part if attended is None else jnp.where(ours, part, attended)
    if held is None:
        attended_out[...] = attended.astype(jnp.bfloat16)
        return
    step = pl.program_id(0)
    height = attended.shape[0]
    block = attended_out.shape[1] - 2 * HALO
    held[pl.ds(pl.multiple_of(HALO + step * height, 8), height), :] = attended
    for number in range(height // block):
        attended_out[step * (height // block) + number, 0:block, :] = attended[
            number * block : (number + 1) * block
        ].astype(jnp.bfloat16)

    @pl.when(step == pl.num_programs(0) - 1)
    def _():
        edge = jnp.zeros((HALO, held.shape[1]), jnp.float32)
        held[0:HALO, :] = edge
        held[held.shape[0] - HALO :, :] = edge
        for number in range(attended_out.shape[0]):
            start = number * block
            sides = jnp.concatenate(
                [
                    held[start : start + HALO, :],
                    held[start + HALO + block : start + 2 * HALO + block, :],
                ],
                axis=0,
            )
            attended_out[number, block:, :] = sides.astype(jnp.bfloat16)


def attend_back_kernel(
    weights,
    content,
    grads,
    keys,
    values,
    shift,
    weight,
    sines,
    cosines,
    table,
    *outs,
):
    step = pl.program_id(0)
    query_out, pairs_out, weight_out, sums_out, key_sums, value_sums = (None,) * (
        6 - len(outs)
    ) + outs
    scale = HEAD_DIM ** (-0.5)

    @pl.when(step == 0)
    def _():
        key_sums[...] = jnp.zeros_like(key_sums)
        value_sums[...] = jnp.zeros_like(value_sums)
        weight_out[...] = jnp.zeros_like(weight_out)
        sums_out[...] = jnp.zeros_like(sums_out)

    weight_rows = jnp.concatenate([weight[...]] * weights.shape[0], axis=0)
    content_rows, grad_rows = content[...], grads[...]
    content_cols = content_rows.T
    grad_cols = grad_rows.T
    key_side = jnp.concatenate([table[...], keys[...]], axis=1)
    half = sines.shape[1]
    grad_content = grad_position = None
    for utterance in range(weights.shape[0]):
        low, high = utterance * HEAD_DIM, (utterance + 1) * HEAD_DIM
        ours = lane_side(content_rows.shape, utterance)
        probs = weights[utterance]
        wide = probs.astype(jnp.float32)
        grad_mine = jnp.where(ours, grad_rows, jnp.zeros_like(grad_rows)) * scale
        grad_probs = rows_dot(grad_mine.astype(jnp.bfloat16), values[...])
        product = wide * grad_probs
        inner = jnp.sum(product, axis=1, keepdims=True)
        grad_scores = (product - wide * inner).astype(jnp.bfloat16)
        value_sums[low:high, :] += jnp.dot(
            grad_cols[low:high, :], probs, preferred_element_type=jnp.float32
        )
        key_sums[low:high, :] += jnp.dot(
            content_cols[low:high, :], grad_scores, preferred_element_type=jnp.float32
        )
        grad_side = jnp.dot(grad_scores, key_side, preferred_element_type=jnp.float32)
        grad_cos_table = grad_side[:, :half]
        grad_sin_table = grad_side[:, half : 2 * half]
        from_table = jnp.concatenate(
            [
                grad_cos_table * sines[...] - grad_sin_table * cosines[...],
                grad_cos_table * cosines[...] + grad_sin_table * sines[...],
            ],
            axis=1,
        ).astype(jnp.bfloat16)
        offset = (content_rows.astype(jnp.float32) + shift[...]).astype(jnp.bfloat16)
        weight_out[...] += jnp.dot(
            offset.T[low:high, :], from_table, preferred_element_type=jnp.float32
        )
        content_part = grad_side[:, 2 * half :]
        position_part = rows_dot(from_table, weight_rows)
        if grad_content is None:
            grad_content, grad_position = content_part, position_part
        else:
            grad_content = jnp.where(ours, content_part, grad_content)
            grad_position = jnp.where(ours, position_part, grad_position)
    grad_query = (grad_content + grad_position).astype(jnp.bfloat16)
    height, lanes = grad_query.shape
    if query_out is None:
        pairs_out[pl.ds(pl.multiple_of(step * height, 16), height), 0:lanes] = grad_query
    else:
        query_out[...] = grad_query
    sums_out[0:1, :] += jnp.sum(grad_content, axis=0, keepdims=True)
    sums_out[1:2, :] += jnp.sum(grad_position, axis=0, keepdims=True)

    @pl.when(step == pl.num_programs(0) - 1)
    def _():
        first = pairs_out.shape[1] - 2 * lanes
        pairs_out[:, first : first + lanes] = key_sums[...].T.astype(jnp.bfloat16)
        pairs_out[:, first + lanes :] = value_sums[...].T.astype(jnp.bfloat16)


def query_block(frames_all):
    return 256 if frames_all <= 1024 else 128


def whole_block(shape):
    return pl.BlockSpec(shape, lambda i: (0,) * len(shape))


def row_block(height, width):
    return pl.BlockSpec((height, width), lambda i: (i, 0))


def attend_heads(limits, content, arrived, shift, weight, sines, cosines, table, block):
    utterances = limits.shape[0]
    query_frames, lanes = content.shape[0], arrived.shape[1] // 3
    frames_all, table_width = table.shape
    height = query_block(frames_all)
    chunked = query_frames == frames_all and height % block == 0
    chunks = (frames_all // block, block + 2 * HALO, lanes)
    kernel = attend_kernel
    if not chunked:
        kernel = functools.partial(attend_kernel, held=None)
    return pl.pallas_call(
        kernel,
        grid=(query_frames // height,),
        in_specs=[
            pl.BlockSpec(memory_space=pltpu.SMEM),
            row_block(height, lanes),
            pl.BlockSpec((frames_all, lanes), lambda i: (0, 1)),
            pl.BlockSpec((frames_all, lanes), lambda i: (0, 2)),
            whole_block(shift.shape),
            whole_block(weight.shape),
            row_block(height, sines.shape[1]),
            row_block(height, sines.shape[1]),
            whole_block(table.shape),
        ],
        out_specs=[
            pl.BlockSpec((utterances, height, frames_all), lambda i: (0, i, 0)),
            whole_block(chunks) if chunked else row_block(height, lanes),
        ],
        out_shape=[
            jax.ShapeDtypeStruct((utterances, query_frames, frames_all), jnp.bfloat16),
            jax.ShapeDtypeStruct(chunks if chunked else (query_frames, lanes), jnp.bfloat16),
        ],
        scratch_shapes=[pltpu.VMEM((frames_all + 2 * HALO, lanes), jnp.float32)] * chunked,
        compiler_params=pltpu.CompilerParams(vmem_limit_bytes=VMEM_LIMIT),
        cost_estimate=pl.CostEstimate(
            flops=2 * utterances * query_frames * frames_all * (table_width + 256),
            bytes_accessed=2 * utterances * query_frames * frames_all,
            transcendentals=utterances * query_frames * frames_all,
        ),
    )(limits, content, arrived, arrived, shift, weight, sines, cosines, table)


def attend_heads_back(
    weights, content, grads, arrived, shift, weight, sines, cosines, table
):
    utterances, query_frames, frames_all = weights.shape
    lanes = arrived.shape[1] // 3
    height = query_block(frames_all)
    joined = query_frames == frames_all
    width = (3 if joined else 2) * lanes
    return pl.pallas_call(
        attend_back_kernel,
        grid=(query_frames // height,),
        in_specs=[
            pl.BlockSpec((utterances, height, frames_all), lambda i: (0, i, 0)),
            row_block(height, lanes),
            row_block(height, lanes),
            pl.BlockSpec((frames_all, lanes), lambda i: (0, 1)),
            pl.BlockSpec((frames_all, lanes), lambda i: (0, 2)),
            whole_block(shift.shape),
            whole_block(weight.shape),
            row_block(height, sines.shape[1]),
            row_block(height, sines.shape[1]),
            whole_block(table.shape),
        ],
        out_specs=([] if joined else [row_block(height, lanes)])
        + [
            whole_block((frames_all, width)),
            whole_block((HEAD_DIM, table.shape[1])),
            whole_block((8, lanes)),
        ],
        out_shape=(
            [] if joined else [jax.ShapeDtypeStruct((query_frames, lanes), jnp.bfloat16)]
        )
        + [
            jax.ShapeDtypeStruct((frames_all, width), jnp.bfloat16),
            jax.ShapeDtypeStruct((HEAD_DIM, table.shape[1]), jnp.float32),
            jax.ShapeDtypeStruct((8, lanes), jnp.float32),
        ],
        scratch_shapes=[
            pltpu.VMEM((lanes, frames_all), jnp.float32),
            pltpu.VMEM((lanes, frames_all), jnp.float32),
        ],
        compiler_params=pltpu.CompilerParams(vmem_limit_bytes=VMEM_LIMIT),
        cost_estimate=pl.CostEstimate(
            flops=2 * utterances * query_frames * frames_all * (table.shape[1] + 512),
            bytes_accessed=2 * utterances * query_frames * frames_all,
            transcendentals=0,
        ),
    )(weights, content, grads, arrived, arrived, shift, weight, sines, cosines, table)


def shards(
    frames,
    lengths,
    out_grad,
    norm_gain,
    norm_bias,
    feed_in,
    feed_in_bias,
    feed_out,
    feed_out_bias,
    attend_in,
    attend_vectors,
    attend_out,
    mixer_in,
    mixer_in_bias,
    depthwise,
    mixer_vectors,
    mixer_out,
    batch_gain,
    batch_shift,
    running_mean,
    running_variance,
):
    utt_rows, block_frames, features = frames.shape
    rows = utt_rows * block_frames
    seq_count = lax.axis_size("seq")
    seq_index = lax.axis_index("seq")
    count = lax.axis_size("utt") * seq_count
    frames_all = block_frames * seq_count
    groups = seq_count // HEADS
    head, group = seq_index % HEADS, seq_index // HEADS
    query_frames = frames_all // groups
    lanes = utt_rows * HEAD_DIM
    info = jnp.concatenate(
        [(seq_index * block_frames).reshape(1), lengths, jnp.full((1,), frames_all, jnp.int32)]
    )
    hidden_units = feed_in.shape[2]
    f32, bf16 = jnp.float32, jnp.bfloat16
    flat_frames = frames.reshape(rows, features)
    square, broad = (rows, features), (rows, hidden_units)
    extended = (utt_rows * (block_frames + 2 * HALO), features)
    row_flops = 2 * rows * features
    bind = functools.partial
    edge = ((utt_rows, 2 * HALO, features), f32)
    feed_scratch = [
        pltpu.VMEM((features, hidden_units), bf16),
        pltpu.VMEM((hidden_units, features), bf16),
    ]
    attend_scratch = pltpu.VMEM((3, features, features), bf16)
    (
        edge_head,
        edge_tail,
        after_first,
        slope_first,
        entry_pack,
        sent,
    ) = vmem_call(
        bind(entry_kernel, utt_rows),
        [
            edge,
            edge,
            (square, f32),
            (broad, bf16),
            ((rows, hidden_units + 2 * features), bf16),
            ((HEADS, block_frames, 3 * lanes), bf16),
        ],
        (),
        (
            flat_frames,
            norm_gain,
            norm_bias,
            feed_in_bias,
            feed_out_bias,
            attend_vectors,
            Part(out_grad, (utt_rows, HALO, features), (0, 0, 0)),
            Part(out_grad, (utt_rows, HALO, features), (0, block_frames // HALO - 1, 0)),
        ),
        scratch=feed_scratch + [attend_scratch, pltpu.SemaphoreType.DMA((3,))],
        cost=row_flops * (2 * hidden_units + 3 * features),
        held=(feed_in, feed_out, attend_in),
    )
    sent, all_limits, edge_head, edge_tail = tie(sent, lengths, edge_head, edge_tail)
    before, behind = from_neighbours(edge_head, edge_tail)
    arrived = heads_out(sent, groups)
    for step in axis_bits("utt"):
        all_limits = jnp.concatenate([all_limits, swap(all_limits, step)])
    arrived, all_limits = tie(arrived, all_limits)
    arrived = arrived.reshape(frames_all, 3 * lanes)
    start_query = group * query_frames
    head_content = arrived
    if groups > 1:
        head_content = lax.dynamic_slice_in_dim(arrived, start_query, query_frames, 0)
    head_vectors = lax.dynamic_slice_in_dim(
        attend_vectors.astype(f32), head * HEAD_DIM, HEAD_DIM, 1
    )
    head_shift = jnp.tile((head_vectors[4] - head_vectors[3])[None], (1, utt_rows))
    head_weight = lax.dynamic_slice_in_dim(attend_in[3], head * HEAD_DIM, HEAD_DIM, 1).reshape(
        features // 2, 2, HEAD_DIM
    )
    head_weight = jnp.transpose(head_weight, (2, 1, 0)).reshape(HEAD_DIM, features)
    sines, cosines = angle_tables(frames_all, features)
    key_table = jnp.concatenate([cosines, sines], axis=1).astype(bf16)
    query_sin = lax.dynamic_slice_in_dim(sines, start_query, query_frames, 0)
    query_cos = lax.dynamic_slice_in_dim(cosines, start_query, query_frames, 0)
    weights, head_attended = attend_heads(
        lengths,
        head_content,
        arrived,
        head_shift,
        head_weight,
        query_sin,
        query_cos,
        key_table,
        block_frames,
    )

    def frames_back(blocks):
        width = blocks.shape[-1]
        blocks = blocks.reshape(1, HEADS, block_frames, width)
        if groups > 1:
            blocks = lax.dynamic_update_slice_in_dim(
                jnp.zeros((groups,) + blocks.shape[1:], blocks.dtype), blocks, group, 0
            )
        blocks = lax.all_to_all(
            blocks.reshape(seq_count, block_frames, width), "seq", 0, 0, tiled=True
        ).reshape(groups, HEADS, block_frames, width)
        return lax.dynamic_slice_in_dim(blocks, group, 1, 0)[0]

    head_attended, before, behind = tie(head_attended, before, behind)
    after_sides, grad_sides = vmem_call(
        sides_kernel,
        [((2 * utt_rows * HALO, features), f32)] * 2,
        (),
        (before, behind, norm_gain, norm_bias, feed_in_bias, feed_out_bias),
        scratch=feed_scratch + [pltpu.SemaphoreType.DMA((2,))],
        cost=row_flops * 2 * hidden_units // 4,
        held=(feed_in, feed_out),
    )
    if head_attended.ndim == 2:
        placed = lax.dynamic_update_slice_in_dim(
            jnp.zeros((frames_all + 2 * HALO, lanes), bf16), head_attended, HALO + start_query, 0
        )
        main, before, behind = (
            placed[start : start + frames_all].reshape(seq_count, block_frames, lanes)
            for start in (HALO, 0, 2 * HALO)
        )
        head_attended = jnp.concatenate([main, before[:, :HALO], behind[:, -HALO:]], axis=1)
    attended_blocks = lax.all_to_all(head_attended, "seq", 0, 0, tiled=True)
    attended_blocks, after_sides, grad_sides = tie(attended_blocks, after_sides, grad_sides)
    if groups > 1:
        attended_blocks = jnp.sum(
            attended_blocks.reshape((groups, HEADS) + attended_blocks.shape[1:]), axis=0
        )
    taps = depthwise.T
    padded = pltpu.VMEM((utt_rows, block_frames + 2 * HALO + 16, features), f32)
    (
        after_attend,
        mixer_pack,
        linear_half,
        gate_half,
        gated,
        convolved,
        shared,
    ) = vmem_call(
        bind(mixer_kernel, utt_rows),
        [
            (extended, f32),
            ((rows, 2 * features), bf16),
            (square, f32),
            (square, f32),
            (extended, bf16),
            (extended, f32),
            ((8 * count, 128), f32),
        ],
        (info,),
        (
            attended_blocks,
            after_first,
            after_sides,
            norm_gain,
            norm_bias,
            attend_out,
            attend_vectors,
            mixer_in,
            mixer_in_bias.reshape(1, -1),
            taps,
            mixer_vectors,
        ),
        scratch=(padded,),
        cost=row_flops * 3 * features,
    )
    (
        layer_output,
        grad_mixer,
        grad_batch,
        normed_batch,
        second_pack,
        shared,
        batch_rows,
        middle_rows,
    ) = vmem_call(
        bind(middle_kernel, utt_rows, seq_count),
        [
            (square, f32),
            (square, f32),
            (extended, f32),
            (extended, f32),
            ((rows, 2 * hidden_units + 4 * features), bf16),
            ((8 * count, 128), f32),
            ((8, features), f32),
            ((16, features), f32),
        ],
        (all_limits, lax.axis_index("utt").reshape(1)),
        (
            convolved,
            all_shared(shared),
            after_attend,
            out_grad.reshape(rows, features),
            grad_sides,
            norm_gain,
            norm_bias,
            batch_gain.reshape(1, -1),
            batch_shift.reshape(1, -1),
            running_mean.reshape(1, -1),
            running_variance.reshape(1, -1),
            mixer_out,
            mixer_vectors,
            feed_in_bias,
            feed_out_bias,
        ),
        scratch=feed_scratch + [pltpu.SemaphoreType.DMA((2,))],
        cost=row_flops * (4 * hidden_units + 2 * features),
        held=(feed_in, feed_out),
    )
    phases = list(zip(*step_orders()))
    near = axis_bits("utt")[0]
    core = side(near).reshape(1)
    halves = jnp.stack([side(step) for step in phases[0]])
    places = jnp.concatenate([core, halves])
    half_units, half_features = hidden_units // 2, features // 2

    def with_pair(array):
        return [array, swap(array, near)]

    second_pair = with_pair(second_pack)
    second_sent, second_kept = block_sums(
        second_kernel,
        places,
        2,
        [
            columns(second_pair, features, 8),
            columns(second_pair, half_units, 0, True),
            columns(second_pair, half_units, 2, True),
            columns(second_pair, features, 9),
        ],
    )
    second_pair, second_sent, second_kept, shared = tie(
        second_pair, second_sent, second_kept, all_shared(shared)
    )
    (
        batch_grads,
        grad_attend,
        mixer_back_pack,
        grad_blocks,
        mixer_rows,
    ) = vmem_call(
        bind(mixer_back_kernel, utt_rows),
        [
            ((8, features), f32),
            (square, f32),
            ((rows, 3 * features), bf16),
            ((HEADS, block_frames, lanes), bf16),
            ((16, features), f32),
        ],
        (info,),
        (
            grad_batch,
            normed_batch,
            shared,
            batch_rows,
            batch_gain.reshape(1, -1),
            gated,
            linear_half,
            gate_half,
            grad_mixer,
            after_attend,
            norm_gain,
            taps,
            mixer_in,
            attend_out,
        ),
        scratch=(padded, padded),
        cost=row_flops * 4 * features,
    )
    mixer_pair, mixer_back_pair = with_pair(mixer_pack), with_pair(mixer_back_pack)
    third_sent, third_kept = block_sums(
        mixer_blocks_kernel,
        places,
        1,
        [
            columns(mixer_pair, features, 1),
            columns(mixer_back_pair, features, 0, True),
            columns(second_pair, half_features, 20, True),
            columns(second_pair, features, 11),
            columns(mixer_pair, half_features, 0, True),
            columns(mixer_back_pair, features, 2),
        ],
    )
    early_sent, early_kept = second_sent + third_sent, second_kept + third_kept
    early_arrived = swap_all(early_sent, phases[0])
    head_grad = heads_out(grad_blocks, groups).reshape(frames_all, lanes)
    if groups > 1:
        head_grad = lax.dynamic_slice_in_dim(head_grad, start_query, query_frames, 0)
    head_grad, early_kept = tie(head_grad, early_kept)
    *head_grads, head_weight_grad, head_sums = attend_heads_back(
        weights,
        head_content,
        head_grad,
        arrived,
        head_shift,
        head_weight,
        query_sin,
        query_cos,
        key_table,
    )
    head_grads, head_weight_grad, head_sums, early_arrived = tie(
        head_grads, head_weight_grad, head_sums, early_arrived
    )
    grad_blocks = head_grads[-1].reshape(seq_count, block_frames, -1)
    returned = lax.all_to_all(grad_blocks, "seq", 0, 0, tiled=True)
    if groups > 1:
        returned = jnp.sum(
            returned.astype(f32).reshape(groups, HEADS, block_frames, 2 * lanes), axis=0
        ).astype(bf16)
        returned = jnp.concatenate([frames_back(head_grads[0]), returned], axis=2)
    head_weight_grad = jnp.transpose(
        head_weight_grad.reshape(HEAD_DIM, 2, features // 2), (2, 1, 0)
    ).reshape(features, HEAD_DIM)
    position_weight_grad = lax.dynamic_update_slice_in_dim(
        jnp.zeros((features, features), f32), head_weight_grad, head * HEAD_DIM, 1
    )
    head_vector_grads = lax.dynamic_update_slice_in_dim(
        jnp.zeros((8, features), f32),
        jnp.sum(head_sums.reshape(8, utt_rows, HEAD_DIM), axis=1),
        head * HEAD_DIM,
        1,
    )
    def next_phase(kept, arrived_rows, steps):
        sent_rows, kept = fold_rows([(kept, arrived_rows)], steps, 1, VMEM_LIMIT)
        return kept, swap_all(tie(sent_rows)[0], steps)

    early_kept, early_arrived = next_phase(early_kept, early_arrived, phases[1])
    entry_pair = with_pair(entry_pack)
    position_pair = with_pair(position_weight_grad.astype(bf16))
    entry_cols = vmem_call(
        turn_kernel,
        [
            ((features, 2 * rows), bf16),
            ((half_units, 2 * rows), bf16),
            ((features, 2 * rows), bf16),
            ((features, features), bf16),
        ],
        (),
        columns(entry_pair, features, 4)
        + columns(entry_pair, half_units, 0, True)
        + columns(entry_pair, features, 5)
        + position_pair,
        numbers=(places,),
    )
    returned, early_arrived, entry_cols = tie(returned, early_arrived, entry_cols)
    (
        frames_grad,
        entry_back_pack,
        grad_pre_first,
        entry_rows,
    ) = vmem_call(
        entry_back_kernel,
        [
            (square, f32),
            ((rows, half_units + 4 * features), bf16),
            ((rows, half_units), bf16),
            ((16, features), f32),
        ],
        (core,),
        (
            returned,
            grad_attend,
            flat_frames,
            after_first,
            slope_first,
            norm_gain,
        ),
        scratch=feed_scratch + [attend_scratch, pltpu.SemaphoreType.DMA((3,))],
        cost=row_flops * (2 * hidden_units + 3 * features),
        held=(feed_in, feed_out, attend_in),
    )
    late_factors = (entry_cols, grad_pre_first, with_pair(entry_back_pack))
    late_sent = late_blocks(False, places, *late_factors)
    late_sent, late_factors, middle_rows = tie(late_sent, late_factors, middle_rows)
    late_arrived = swap_all(late_sent, phases[0])
    late_kept = late_blocks(True, places, *late_factors)
    flat = jnp.concatenate([middle_rows, mixer_rows, entry_rows, head_vector_grads], axis=0)
    flat_steps = [near] + [steps[0] for steps in phases]
    def in_turn(arrived_rows, steps, work):
        nonlocal flat
        flat_arrived = swap(flat, flat_steps.pop()) if flat_steps else jnp.zeros_like(flat)
        after, next_arrived = None, []
        for i, rows in enumerate(arrived_rows):
            if after is not None:
                rows, _ = tie(rows, after)
            if i == len(arrived_rows) - 1:
                rows, flat_arrived = tie(rows, flat_arrived)
            after = work(i, rows)
            next_arrived.append(swap(after, steps[i]) if steps else after)
        flat = flat + flat_arrived
        return next_arrived

    late_kept = list(late_kept)
    for steps in phases[1:]:

        def fold(i, rows):
            pairs = [([late_kept[i]], [rows])]
            if steps is phases[2]:
                pairs = [([early_kept[i]], [early_arrived[i]])] + pairs
            parts = 1 if steps in phases[1:3] else 2
            (sent_rows,), (late_kept[i],) = fold_rows(pairs, [steps[i]], parts)
            return sent_rows

        late_arrived = in_turn(late_arrived, steps, fold)
    sums = [None] * len(late_arrived)

    def add(i, rows):
        (sums[i],) = add_rows([late_kept[i]], [rows])
        return sums[i]

    arrived_rows = in_turn(late_arrived, phases[-1], add)
    for number in range(len(phases) - 1, 0, -1):

        def join(i, rows):
            (sums[i],) = join_rows([sums[i]], [rows], [phases[number][i]])
            return sums[i]

        arrived_rows = in_turn(arrived_rows, phases[number - 1], join)
    for step in flat_steps:
        flat = flat + swap(flat, step)
    vector_grads = vmem_call(
        vectors_kernel,
        [
            (norm_gain.shape, f32),
            (norm_bias.shape, f32),
            (feed_in_bias.shape, f32),
            (feed_out_bias.shape, f32),
            (attend_vectors.shape, f32),
            ((1, 2 * features), f32),
            (mixer_vectors.shape, f32),
            ((KERNEL, features), f32),
        ],
        (),
        (flat,),
    )
    vector_grads = list(vector_grads)
    vector_grads[5] = vector_grads[5].reshape(-1)
    vector_grads[7] = vector_grads[7].T
    vector_grads = [*vector_grads, batch_grads[1], batch_grads[0], batch_rows[2], batch_rows[3]]
    across_rows = swap_all(sums, [near] * 3)
    shapes = [feed_in.shape, feed_out.shape, mixer_in.shape, mixer_out.shape]
    shapes += [attend_out.shape, attend_in.shape]
    spread = spread_blocks(core, halves, sums, shapes, [])
    spread = spread_blocks(1 - core, halves, across_rows, shapes, spread)
    spread, arrived_rows, vector_grads = tie(spread, arrived_rows, vector_grads)
    across_rows = swap_all(arrived_rows, [near] * 3)
    spread = spread_blocks(core, 1 - halves, arrived_rows, shapes, spread)
    (
        feed_in_grad,
        feed_out_grad,
        mixer_in_grad,
        mixer_out_grad,
        attend_out_grad,
        attend_in_grad,
    ) = spread_blocks(1 - core, 1 - halves, across_rows, shapes, spread)
    (
        norm_gain_grad,
        norm_bias_grad,
        feed_in_bias_grad,
        feed_out_bias_grad,
        attend_vectors_grad,
        mixer_in_bias_grad,
        mixer_vectors_grad,
        taps_grad,
        batch_gain_grad,
        batch_shift_grad,
        new_mean,
        new_variance,
    ) = vector_grads
    return (
        layer_output.reshape(frames.shape),
        frames_grad.reshape(frames.shape),
        norm_gain_grad,
        norm_bias_grad,
        feed_in_grad,
        feed_in_bias_grad,
        feed_out_grad,
        feed_out_bias_grad,
        attend_in_grad,
        attend_vectors_grad,
        attend_out_grad,
        mixer_in_grad,
        mixer_in_bias_grad,
        taps_grad,
        mixer_vectors_grad,
        mixer_out_grad,
        batch_gain_grad,
        batch_shift_grad,
        new_mean,
        new_variance,
    )


def solution(mesh):
    return jax.shard_map(
        shards,
        mesh=mesh,
        in_specs=(
            P("utt", "seq", None),
            P("utt"),
            P("utt", "seq", None),
            P(),
            P(),
            P(),
            P(),
            P(),
            P(),
            P(),
            P(),
            P(),
            P(),
            P(),
            P(),
            P(),
            P(),
            P(),
            P(),
            P(),
            P(),
        ),
        out_specs=(
            P("utt", "seq", None),
            P("utt", "seq", None),
            P(),
            P(),
            P(),
            P(),
            P(),
            P(),
            P(),
            P(),
            P(),
            P(),
            P(),
            P(),
            P(),
            P(),
            P(),
            P(),
            P(),
            P(),
        ),
        check_vma=False,
    )
```

```python
import functools
import math

import jax
import jax.numpy as jnp
import numpy as np
from jax import lax
from jax.experimental import pallas as pl
from jax.experimental.pallas import tpu as pltpu
from jax.sharding import PartitionSpec as P

HEADS = 8
KERNEL = 9
HEAD_DIM = 64


TOP_PRECISION = lax.Precision.HIGHEST
EPSILON = 1e-05
VMEM_LIMIT = 63 * 1024 * 1024
SUM_LIMIT = 20 * 1024 * 1024
HALO = 8
ROW_TILE = 32


def wide(values):
    return values.astype(jnp.float32)


def low(values):
    return values.astype(jnp.bfloat16)


def matmul(first_operand, second_operand):
    return jnp.dot(first_operand, second_operand, preferred_element_type=jnp.float32)


def column_sum(values):
    return jnp.sum(wide(values), axis=0, keepdims=True)


def normalize(values):
    average = jnp.mean(values, axis=-1, keepdims=True)
    centered = values - average
    spread = jnp.mean(centered * centered, axis=-1, keepdims=True)
    inverse = lax.rsqrt(spread + EPSILON)
    return centered * inverse, inverse


def scaled_norm(normed, gains, biases, number):
    return normed * wide(gains[number : number + 1, :]) + wide(biases[number : number + 1, :])


def norm_back(grad_rows, normed, inverse, gains, number, own=lambda values: values):
    scaled = grad_rows * wide(gains[number : number + 1, :])
    inner = (
        scaled
        - jnp.mean(scaled, axis=-1, keepdims=True)
        - normed * jnp.mean(scaled * normed, axis=-1, keepdims=True)
    )
    return inner * inverse, column_sum(own(grad_rows * normed)), column_sum(own(grad_rows))


def logistic(values):
    return 1.0 / (1.0 + jnp.exp(-values))


def silu_slope(preact, sigmoid):
    return sigmoid * (1.0 + preact * (1.0 - sigmoid))


def frame_places(info, rows, utterances, halo):
    own = rows - 2 * utterances * halo
    per = own // utterances
    row = lax.broadcasted_iota(jnp.int32, (rows, 1), 0)
    aside = row - own
    owner = jnp.where(aside < 0, row // per, aside // (2 * halo))
    near = aside % (2 * halo)
    place = jnp.where(aside < 0, row % per, near - halo + jnp.where(near < halo, 0, per))
    limit = jnp.full((rows, 1), info[utterances], jnp.int32)
    for utterance in range(utterances - 1):
        limit = jnp.where(owner == utterance, info[1 + utterance], limit)
    return info[0] + place, limit


def flags(condition):
    return jnp.where(condition, 1.0, 0.0)


def own_rows(values, utterances):
    return values[: values.shape[0] - 2 * utterances * HALO]


def with_sides(values, sides):
    return jnp.concatenate([values, sides], axis=0)


def blocks_of_heads(rows, utterances):
    per = rows.shape[0] // utterances
    first = lax.broadcasted_iota(jnp.int32, (per, 2 * HEAD_DIM), 1) < HEAD_DIM
    blocks = []
    for pair in range(HEADS // 2):
        columns = rows[:, pair * 2 * HEAD_DIM : (pair + 1) * 2 * HEAD_DIM]
        top, bottom = columns[:per], columns[per:]
        blocks.append(jnp.where(first, top, pltpu.roll(bottom, HEAD_DIM, 1)))
        blocks.append(jnp.where(first, pltpu.roll(top, HEAD_DIM, 1), bottom))
    return blocks


def rows_of_heads(blocks):
    per = blocks[0].shape[0]
    first = lax.broadcasted_iota(jnp.int32, (per, 2 * HEAD_DIM), 1) < HEAD_DIM
    columns = []
    for pair in range(HEADS // 2):
        left, right = blocks[2 * pair], blocks[2 * pair + 1]
        top = jnp.where(first, left, pltpu.roll(right, HEAD_DIM, 1))
        bottom = jnp.where(first, pltpu.roll(left, HEAD_DIM, 1), right)
        columns.append(jnp.concatenate([top, bottom], axis=0))
    return jnp.concatenate(columns, axis=1)


def whole_array(shape):
    return pl.BlockSpec(shape, lambda i: (0,) * len(shape))


class Part:
    def __init__(self, array, block, index):
        self.array, self.block, self.index = array, block, index

    def spec(self):
        def index(i, *numbers):
            return tuple(at(*numbers) if callable(at) else at for at in self.index)

        return pl.BlockSpec(self.block, index)


def vmem_call(kernel, shapes, smem, operands, scratch=(), cost=0, held=(), numbers=()):
    def whole(shape):
        return pl.BlockSpec(shape, lambda i, *numbers: (0,) * len(shape))

    return pl.pallas_call(
        kernel,
        grid_spec=pltpu.PrefetchScalarGridSpec(
            num_scalar_prefetch=len(numbers),
            grid=(1,),
            in_specs=[pl.BlockSpec(memory_space=pltpu.SMEM)] * len(smem)
            + [
                operand.spec() if isinstance(operand, Part) else whole(operand.shape)
                for operand in operands
            ]
            + [pl.BlockSpec(memory_space=pl.ANY)] * len(held),
            out_specs=[whole(shape) for shape, _ in shapes],
            scratch_shapes=list(scratch),
        ),
        out_shape=[jax.ShapeDtypeStruct(shape, dtype) for shape, dtype in shapes],
        compiler_params=pltpu.CompilerParams(vmem_limit_bytes=VMEM_LIMIT),
        cost_estimate=pl.CostEstimate(flops=cost, bytes_accessed=cost // 300, transcendentals=0),
    )(
        *numbers,
        *smem,
        *(operand.array if isinstance(operand, Part) else operand for operand in operands),
        *held,
    )


def fetch(pairs, semaphores):
    copies = [
        pltpu.make_async_copy(source, target, semaphores.at[number])
        for number, (source, target) in enumerate(pairs)
    ]
    for copy in copies:
        copy.start()
    return copies


def feed_rows(values, gains, biases, copies, weight_in, bias_in, weight_out, bias_out):
    normed, _ = normalize(values)
    hidden = low(scaled_norm(normed, gains, biases, 0))
    copies[0].wait()
    preact = matmul(hidden, weight_in[...]) + wide(bias_in[0:1, :])
    sigmoid = logistic(preact)
    active = low(preact * sigmoid)
    copies[1].wait()
    branch = matmul(active, weight_out[...]) + wide(bias_out[0:1, :])
    return values + 0.5 * branch, preact, sigmoid, active


def entry_kernel(
    utterances,
    frames,
    gains,
    biases,
    bias_in,
    bias_out,
    vectors,
    grads_head,
    grads_tail,
    feed_in,
    feed_out,
    attend_in,
    head_out,
    tail_out,
    after_out,
    slope_out,
    pack_out,
    sent_out,
    weight_in,
    weight_out,
    weight_attend,
    semaphores,
):
    copies = fetch(
        [
            (feed_in.at[0], weight_in),
            (feed_out.at[0], weight_out),
            (attend_in.at[pl.ds(0, 3)], weight_attend),
        ],
        semaphores,
    )
    per = frames.shape[0] // utterances
    for u in range(utterances):
        head_out[u, 0:HALO, :] = frames[u * per : u * per + HALO, :]
        head_out[u, HALO:, :] = grads_head[u]
        tail_out[u, 0:HALO, :] = frames[(u + 1) * per - HALO : (u + 1) * per, :]
        tail_out[u, HALO:, :] = grads_tail[u]
    units, features = slope_out.shape[1], frames.shape[1]
    pack_out[:, units : units + features] = low(scaled_norm(normalize(frames[...])[0], gains, biases, 0))
    after, preact, sigmoid, active = feed_rows(
        frames[...], gains, biases, copies, weight_in, bias_in, weight_out, bias_out
    )
    slope_out[...] = low(silu_slope(preact, sigmoid))
    pack_out[:, :units] = active
    after_out[...] = after
    normed, _ = normalize(after)
    hidden = low(scaled_norm(normed, gains, biases, 1))
    pack_out[:, units + features :] = hidden
    copies[2].wait()
    queries = matmul(hidden, weight_attend[0]) + wide(vectors[0:1, :])
    parts = (
        queries + wide(vectors[3:4, :]),
        matmul(hidden, weight_attend[1]),
        matmul(hidden, weight_attend[2]) + wide(vectors[1:2, :]),
    )
    lanes = 2 * HEAD_DIM
    for number, part in enumerate(parts):
        for head, block in enumerate(blocks_of_heads(part, utterances)):
            sent_out[head, :, number * lanes : (number + 1) * lanes] = low(block)


def sides_kernel(
    before,
    behind,
    gains,
    biases,
    bias_in,
    bias_out,
    feed_in,
    feed_out,
    after_out,
    grads_out,
    weight_in,
    weight_out,
    semaphores,
):
    copies = fetch([(feed_in.at[0], weight_in), (feed_out.at[0], weight_out)], semaphores)
    frames, grads = (
        jnp.concatenate(
            [
                source[u, first : first + HALO, :]
                for u in range(before.shape[0])
                for source in (before, behind)
            ],
            axis=0,
        )
        for first in (0, HALO)
    )
    grads_out[...] = grads
    after_out[...] = feed_rows(
        frames, gains, biases, copies, weight_in, bias_in, weight_out, bias_out
    )[0]


def mixer_kernel(
    utterances,
    info,
    blocks,
    after,
    after_sides,
    gains,
    biases,
    attend_out,
    vectors,
    mixer_in,
    mixer_bias,
    taps,
    mixer_vectors,
    after_out,
    pack_out,
    linear_out,
    gate_out,
    gated_out,
    convolved_out,
    sums_out,
    padded,
):
    per = after.shape[0] // utterances
    main, before, behind = [], [], []
    for head in range(HEADS):
        block = wide(blocks[head])
        main.append(block[:per])
        before.append(block[per : per + HALO])
        behind.append(block[per + HALO :])
    attended = rows_of_heads(main)
    features = after.shape[1]
    pack_out[:, :features] = low(attended)
    before, behind = rows_of_heads(before), rows_of_heads(behind)
    sides = []
    for u in range(utterances):
        sides += [before[u * HALO : (u + 1) * HALO], behind[u * HALO : (u + 1) * HALO]]
    attended = low(with_sides(attended, jnp.concatenate(sides, axis=0)))
    values = with_sides(after[...], after_sides[...])
    values = values + matmul(attended, attend_out[...]) + wide(vectors[2:3, :])
    after_out[...] = values
    normed, _ = normalize(values)
    scaled = scaled_norm(normed, gains, biases, 2)
    pack_out[:, features:] = low(own_rows(scaled, utterances))
    preact = matmul(low(scaled), mixer_in[...])
    preact = preact + wide(mixer_bias[...])
    rows = values.shape[0]
    linear = preact[:, :features]
    gate = logistic(preact[:, features:])
    linear_out[...] = own_rows(linear, utterances)
    gate_out[...] = own_rows(gate, utterances)
    place, limit = frame_places(info, rows, utterances, HALO)
    mask = flags((place >= 0) & (place < limit))
    gated = low(linear * gate * mask)
    gated_out[...] = gated
    fill_padded(padded, wide(gated), utterances)
    total = None
    for offset in range(KERNEL):
        term = wide(taps[offset : offset + 1, :]) * moved(
            padded, utterances, offset - KERNEL // 2, True
        )
        total = term if total is None else total + term
    convolved = total + wide(mixer_vectors[0:1, :])
    convolved_out[...] = convolved
    mask = own_rows(mask, utterances)
    convolved = own_rows(convolved, utterances)
    count = jnp.sum(mask, axis=0, keepdims=True)
    local_sum = jnp.sum(convolved * mask, axis=0, keepdims=True)
    centered = (convolved - local_sum / jnp.maximum(count, 1.0)) * mask
    share(sums_out, local_sum, jnp.sum(centered * centered, axis=0, keepdims=True))


def fill_padded(padded, values, utterances):
    own = values.shape[0] - 2 * utterances * HALO
    per = own // utterances
    zeros = jnp.zeros((HALO, values.shape[1]), jnp.float32)
    for u in range(utterances):
        aside = own + 2 * u * HALO
        padded[u, 0:HALO, :] = zeros
        padded[u, HALO : 2 * HALO, :] = values[aside : aside + HALO, :]
        padded[u, 2 * HALO : 2 * HALO + per, :] = values[u * per : (u + 1) * per, :]
        padded[u, 2 * HALO + per : 3 * HALO + per, :] = values[aside + HALO : aside + 2 * HALO, :]
        padded[u, 3 * HALO + per :, :] = zeros


def moved(padded, utterances, start, sides=False):
    per = padded.shape[1] - 4 * HALO
    pieces = [(u, 2 * HALO, per) for u in range(utterances)]
    if sides:
        for u in range(utterances):
            pieces += [(u, HALO, HALO), (u, 2 * HALO + per, HALO)]
    return jnp.concatenate(
        [padded[u, first + start : first + start + height, :] for u, first, height in pieces],
        axis=0,
    )


def share(sums_out, *rows):
    tile = jnp.concatenate(
        [row[:, i : i + 128] for row in rows for i in range(0, row.shape[1], 128)], axis=0
    )
    for copy in range(sums_out.shape[0] // 8):
        sums_out[copy * 8 : copy * 8 + 8, :] = tile


def as_row(tile):
    return jnp.concatenate([tile[i : i + 1] for i in range(tile.shape[0])], axis=1)


def frame_counts(limits, utt_index, shape, utterances, seq_count, per):
    place = lax.broadcasted_iota(jnp.int32, shape, 0)
    owner, first = (place // seq_count) ^ utt_index, place % seq_count * per
    total = jnp.zeros(shape, jnp.int32)
    for number in range(limits.shape[0]):
        inside = jnp.clip(limits[number] - first, 0, per)
        total = total + jnp.where(owner == number // utterances, inside, 0)
    return total.astype(jnp.float32)


def middle_kernel(
    utterances,
    seq_count,
    limits,
    utt_index,
    convolved,
    shared,
    after,
    grads,
    grad_sides,
    gains,
    biases,
    batch_gain,
    batch_shift,
    running_mean,
    running_variance,
    mixer_out,
    vectors,
    bias_in,
    bias_out,
    feed_in,
    feed_out,
    layer_out,
    grad_mixer_out,
    grad_batch_out,
    normed_out,
    pack_out,
    sums_out,
    batch_out_rows,
    vector_out,
    weight_in,
    weight_out,
    semaphores,
):
    def own(values):
        return own_rows(values, utterances)

    features, units = feed_in.shape[1:]

    def pack(number, rows):
        first = 2 * units + number * features
        pack_out[:, first : first + features] = rows

    copies = fetch([(feed_in.at[1], weight_in), (feed_out.at[1], weight_out)], semaphores)
    parts = shared[...].reshape(-1, 8, 128)
    per = grads.shape[0] // utterances
    counts = frame_counts(limits, utt_index[0], parts.shape, utterances, seq_count, per)
    totals = jnp.sum(parts, axis=0)
    valid_tile = jnp.sum(counts, axis=0)
    valid = as_row(valid_tile[:4])
    average_tile = totals / valid_tile
    drift = parts / jnp.maximum(counts, 1.0) - average_tile
    spreads = jnp.sum(counts * drift * drift, axis=0)
    average = as_row(average_tile[:4])
    variance = as_row((totals[4:] + spreads[:4]) / valid_tile[:4])
    inverse_batch = lax.rsqrt(variance + EPSILON)
    batch_out_rows[0:1, :] = inverse_batch
    batch_out_rows[1:2, :] = valid
    batch_out_rows[2:3, :] = 0.9 * running_mean[...] + 0.1 * average
    batch_out_rows[3:4, :] = 0.9 * running_variance[...] + 0.1 * variance * valid / (valid - 1.0)
    normed_batch = (convolved[...] - average) * inverse_batch
    normed_out[...] = normed_batch
    batch = normed_batch * wide(batch_gain[...]) + wide(batch_shift[...])
    batch_sigmoid = logistic(batch)
    swished = low(batch * batch_sigmoid)
    pack(2, own(swished))
    values = after[...] + matmul(swished, mixer_out[...]) + wide(vectors[1:2, :])
    normed, inverse = normalize(values)
    scaled = scaled_norm(normed, gains, biases, 3)
    hidden = low(scaled)
    pack(0, own(hidden))
    copies[0].wait()
    preact = matmul(hidden, weight_in[...]) + wide(bias_in[1:2, :])
    sigmoid = logistic(preact)
    active = low(preact * sigmoid)
    pack_out[:, units : 2 * units] = own(active)
    copies[1].wait()
    branch = matmul(active, weight_out[...]) + wide(bias_out[1:2, :])
    normed_last, inverse_last = normalize(values + 0.5 * branch)
    layer_out[...] = own(scaled_norm(normed_last, gains, biases, 4))
    grad_second, gain_last, shift_last = norm_back(
        with_sides(grads[...], grad_sides[...]),
        normed_last,
        inverse_last,
        gains,
        4,
        own,
    )
    grad_low = low(0.5 * grad_second)
    grad_low_own = own(grad_low)
    pack(1, grad_low_own)
    grad_pre = low(rows_dot(grad_low, weight_out[...]) * silu_slope(preact, sigmoid))
    grad_pre_own = own(grad_pre)
    pack_out[:, :units] = grad_pre_own
    grad_values, gain_three, shift_three = norm_back(
        rows_dot(grad_pre, weight_in[...]), normed, inverse, gains, 3, own
    )
    grad_mixer = grad_second + grad_values
    grad_mixer_own = own(grad_mixer)
    grad_mixer_out[...] = grad_mixer_own
    branch_own = low(grad_mixer_own)
    pack(3, branch_own)
    grad_batch = rows_dot(low(grad_mixer), mixer_out[...]) * silu_slope(batch, batch_sigmoid)
    grad_batch_out[...] = grad_batch
    share(sums_out, column_sum(own(grad_batch)), column_sum(own(grad_batch * normed_batch)))
    bias_sum = column_sum(grad_pre_own)
    put_rows(
        vector_out,
        [gain_last, shift_last, gain_three, shift_three]
        + [bias_sum[:, i : i + features] for i in range(0, bias_sum.shape[1], features)]
        + [column_sum(grad_low_own), column_sum(branch_own)],
    )


def put_rows(out, rows):
    for number, row in enumerate(rows):
        out[number : number + 1, :] = row
    out[len(rows) :, :] = jnp.zeros((out.shape[0] - len(rows), out.shape[1]), jnp.float32)


def mixer_back_kernel(
    utterances,
    info,
    grad_batch,
    normed_batch,
    shared,
    batch_rows,
    batch_gain,
    gated,
    linear,
    gate,
    grad_mixer,
    after,
    gains,
    taps,
    mixer_in,
    attend_out,
    batch_grads_out,
    grad_attend_out,
    pack_out,
    sent_out,
    vector_out,
    padded,
    gated_padded,
):
    totals = jnp.sum(shared[...].reshape(-1, 8, 128), axis=0)
    shift_grad, gain_grad = as_row(totals[:4]), as_row(totals[4:])
    batch_grads_out[0:1, :] = shift_grad
    batch_grads_out[1:2, :] = gain_grad
    rows, features = grad_batch.shape
    place, limit = frame_places(info, rows, utterances, HALO)
    mask = flags((place >= 0) & (place < limit))
    inside = flags((place >= 0) & (place < info[utterances + 1]))
    inverse_batch, valid = batch_rows[0:1, :], batch_rows[1:2, :]
    grad_conv = low(
        inside
        * wide(batch_gain[...])
        * inverse_batch
        * (grad_batch[...] - mask / valid * (shift_grad + normed_batch[...] * gain_grad))
    )
    conv_wide = wide(grad_conv)
    fill_padded(padded, conv_wide, utterances)
    fill_padded(gated_padded, wide(gated[...]), utterances)
    conv_own = own_rows(conv_wide, utterances)
    margin = KERNEL // 2
    total = None
    tap_rows = []
    for offset in range(KERNEL):
        term = wide(taps[offset : offset + 1, :]) * moved(padded, utterances, margin - offset)
        total = term if total is None else total + term
        near = moved(gated_padded, utterances, offset - margin)
        tap_rows.append(jnp.sum(conv_own * near, axis=0, keepdims=True))
    grad_gated = own_rows(mask, utterances) * total
    gate_half = gate[...]
    grad_pre = low(
        jnp.concatenate(
            [
                grad_gated * gate_half,
                grad_gated * linear[...] * gate_half * (1.0 - gate_half),
            ],
            axis=1,
        )
    )
    pack_out[:, : 2 * features] = grad_pre
    normed, inverse = normalize(own_rows(after[...], utterances))
    grad_values, gain_two, shift_two = norm_back(
        rows_dot(grad_pre, mixer_in[...]), normed, inverse, gains, 2
    )
    grad_attend = grad_mixer[...] + grad_values
    grad_attend_out[...] = grad_attend
    branch = low(grad_attend)
    pack_out[:, 2 * features :] = branch
    grad_attended = rows_dot(branch, attend_out[...])
    for head, block in enumerate(blocks_of_heads(grad_attended, utterances)):
        sent_out[head] = low(block)
    bias_sum = column_sum(grad_pre)
    put_rows(
        vector_out,
        [gain_two, shift_two, column_sum(conv_own), column_sum(branch)]
        + [bias_sum[:, :features], bias_sum[:, features:]]
        + tap_rows,
    )


def entry_back_kernel(
    core,
    returned,
    grad_attend,
    frames,
    after,
    slope,
    gains,
    feed_in,
    feed_out,
    attend_in,
    frames_out,
    pack_out,
    grad_pre_out,
    vector_out,
    weight_in,
    weight_out,
    weight_attend,
    semaphores,
):
    copies = fetch(
        [
            (attend_in.at[pl.ds(0, 3)], weight_attend),
            (feed_out.at[0], weight_out),
            (feed_in.at[0], weight_in),
        ],
        semaphores,
    )
    lanes = 2 * HEAD_DIM
    features, units = feed_in.shape[1:]

    def pack(number, rows):
        first = units // 2 + number * features
        pack_out[:, first : first + features] = rows

    grad_hidden = None
    low_rows = []
    for number in range(3):
        rows = low(
            rows_of_heads(
                [
                    wide(returned[head, :, number * lanes : (number + 1) * lanes])
                    for head in range(HEADS)
                ]
            )
        )
        pack(number, rows)
        low_rows.append(rows)
        if number == 0:
            copies[0].wait()
        term = rows_dot(rows, weight_attend[number])
        grad_hidden = term if grad_hidden is None else grad_hidden + term
    normed, inverse = normalize(after[...])
    grad_values, gain_one, shift_one = norm_back(grad_hidden, normed, inverse, gains, 1)
    grad_first = grad_attend[...] + grad_values
    grad_low = low(0.5 * grad_first)
    pack(3, grad_low)
    copies[1].wait()
    grad_pre = low(rows_dot(grad_low, weight_out[...]) * wide(slope[...]))
    for half in range(2):
        rows = grad_pre[:, half * units // 2 : (half + 1) * units // 2]

        @pl.when(core[0] == half)
        def _():
            grad_pre_out[...] = rows

        @pl.when(core[0] != half)
        def _():
            pack_out[:, : units // 2] = rows

    normed, inverse = normalize(frames[...])
    copies[2].wait()
    grad_values, gain_zero, shift_zero = norm_back(
        rows_dot(grad_pre, weight_in[...]), normed, inverse, gains, 0
    )
    frames_out[...] = grad_first + grad_values
    bias_sum = column_sum(grad_pre)
    put_rows(
        vector_out,
        [gain_zero, shift_zero, gain_one, shift_one]
        + [bias_sum[:, i : i + features] for i in range(0, bias_sum.shape[1], features)]
        + [column_sum(grad_low), column_sum(low_rows[0]), column_sum(low_rows[2])],
    )


def vectors_kernel(
    rows, gain_out, bias_out, in_bias_out, out_bias_out, attend_out, mixer_bias_out, mixer_out, taps_out
):
    middle, mixer, entry, heads = (0, 16, 32, 48)
    features = gain_out.shape[1]

    def take(out, target, start):
        out[target : target + 1, :] = rows[start : start + 1, :]

    for out, first in ((gain_out, 0), (bias_out, 1)):
        take(out, 0, entry + first)
        take(out, 1, entry + 2 + first)
        take(out, 2, mixer + first)
        take(out, 3, middle + 2 + first)
        take(out, 4, middle + first)
    for target, start in ((0, entry + 4), (1, middle + 4)):
        for column in range(4):
            in_bias_out[target : target + 1, column * features : (column + 1) * features] = rows[
                start + column : start + column + 1, :
            ]
    take(out_bias_out, 0, entry + 8)
    take(out_bias_out, 1, middle + 8)
    for target, start in enumerate((entry + 9, entry + 10, mixer + 3, heads, heads + 1)):
        take(attend_out, target, start)
    for column in range(2):
        mixer_bias_out[0:1, column * features : (column + 1) * features] = rows[
            mixer + 4 + column : mixer + 5 + column, :
        ]
    take(mixer_out, 0, mixer + 2)
    take(mixer_out, 1, middle + 9)
    taps_out[...] = rows[mixer + 6 : mixer + 6 + KERNEL, :]


def axis_bits(axis):
    return [(axis, 1 << bit) for bit in range(lax.axis_size(axis).bit_length() - 1)]


def swap(values, step):
    axis, mask = step
    return lax.ppermute(values, axis, [(i, i ^ mask) for i in range(lax.axis_size(axis))])


def side(step):
    axis, mask = step
    return (lax.axis_index(axis) // mask) % 2


def swap_all(stripes, steps):
    return [swap(rows, step) for rows, step in zip(stripes, steps)]


def add_low(first_operand, second_operand):
    total = first_operand.astype(jnp.float32) + second_operand.astype(jnp.float32)
    return total.astype(jnp.bfloat16)


def fold_kernel(stripes, arrays, parts, sides, *refs):
    for number in range(stripes):
        sources = refs[2 * arrays * number : 2 * arrays * (number + 1)]
        for keeping in range(2):
            place = sides[number] if keeping else 1 - sides[number]
            out = refs[2 * arrays * stripes + 2 * number + keeping]
            first = 0
            for array in range(arrays):
                own, other = sources[2 * array : 2 * array + 2]
                height = own.shape[0] // (2 * parts)
                for part in range(parts):
                    start = pl.multiple_of((2 * part + place) * height, 16)
                    rows = pl.ds(start, height)
                    out[first : first + height, :] = add_low(own[rows, :], other[rows, :])
                    first += height


def fold_rows(pairs, steps, parts=1, limit=SUM_LIMIT):
    operands = list(zip(*(rows for pair in pairs for rows in pair)))
    heights = [sum(rows.shape[0] for rows in four[::2]) // 2 for four in operands]
    if any(rows.shape[0] // parts % 32 for four in operands for rows in four):
        sent, kept = [], []
        for four, step in zip(operands, steps):
            sums = [add_low(*four[i : i + 2]) for i in range(0, len(four), 2)]
            for place, results in ((1 - side(step), sent), (side(step), kept)):
                pieces = []
                for rows in sums:
                    height = rows.shape[0] // (2 * parts)
                    pieces += [
                        lax.dynamic_slice_in_dim(rows, (2 * part + place) * height, height, 0)
                        for part in range(parts)
                    ]
                results.append(jnp.concatenate(pieces, axis=0))
        return sent, kept

    def whole(rows):
        return pl.BlockSpec((rows, 512), lambda i, sides: (0, 0))

    outs = [height for height in heights for _ in range(2)]
    results = pl.pallas_call(
        functools.partial(fold_kernel, len(steps), len(pairs), parts),
        grid_spec=pltpu.PrefetchScalarGridSpec(
            num_scalar_prefetch=1,
            grid=(1,),
            in_specs=[whole(rows.shape[0]) for four in operands for rows in four],
            out_specs=[whole(height) for height in outs],
        ),
        out_shape=[jax.ShapeDtypeStruct((height, 512), jnp.bfloat16) for height in outs],
        compiler_params=pltpu.CompilerParams(vmem_limit_bytes=limit),
        cost_estimate=pl.CostEstimate(
            flops=0, bytes_accessed=6 * 1024 * sum(outs), transcendentals=0
        ),
    )(jnp.stack([side(step) for step in steps]), *(rows for four in operands for rows in four))
    return list(results[::2]), list(results[1::2])


def add_kernel(stripes, *refs):
    for number in range(stripes):
        refs[2 * stripes + number][...] = add_low(refs[2 * number][...], refs[2 * number + 1][...])


def add_rows(kept, arrived):
    if any(rows.shape[0] % 16 for rows in kept):
        return [add_low(*pair) for pair in zip(kept, arrived)]
    specs = [whole_array(rows.shape) for rows in kept]
    return list(
        pl.pallas_call(
            functools.partial(add_kernel, len(kept)),
            grid=(1,),
            in_specs=[spec for spec in specs for _ in range(2)],
            out_specs=specs,
            out_shape=[jax.ShapeDtypeStruct(rows.shape, rows.dtype) for rows in kept],
            compiler_params=pltpu.CompilerParams(vmem_limit_bytes=SUM_LIMIT),
        )(*(rows for pair in zip(kept, arrived) for rows in pair))
    )


def join_kernel(stripes, sides, *refs):
    for number in range(stripes):
        own, other, out = refs[2 * number], refs[2 * number + 1], refs[2 * stripes + number]
        height = own.shape[0] // 2
        for part in range(2):
            for source, place in ((own, sides[number]), (other, 1 - sides[number])):
                start = pl.multiple_of((2 * part + place) * height, 16)
                out[pl.ds(start, height), :] = source[part * height : (part + 1) * height, :]


def join_rows(stripes, arrived, steps):
    heights = [rows.shape[0] // 2 for rows in stripes]
    if any(height % 16 for height in heights):
        joined = []
        for rows, other, step, height in zip(stripes, arrived, steps, heights):
            first = side(step) == 0
            low_rows, high_rows = jnp.where(first, rows, other), jnp.where(first, other, rows)
            joined.append(
                jnp.concatenate(
                    [
                        half[part]
                        for part in (slice(0, height), slice(height, None))
                        for half in (low_rows, high_rows)
                    ],
                    axis=0,
                )
            )
        return joined

    def whole(height):
        return pl.BlockSpec((height, 512), lambda i, sides: (0, 0))

    return list(
        pl.pallas_call(
            functools.partial(join_kernel, len(stripes)),
            grid_spec=pltpu.PrefetchScalarGridSpec(
                num_scalar_prefetch=1,
                grid=(1,),
                in_specs=[whole(2 * height) for height in heights for _ in range(2)],
                out_specs=[whole(4 * height) for height in heights],
            ),
            out_shape=[jax.ShapeDtypeStruct((4 * height, 512), jnp.bfloat16) for height in heights],
            compiler_params=pltpu.CompilerParams(vmem_limit_bytes=SUM_LIMIT),
            cost_estimate=pl.CostEstimate(
                flops=0, bytes_accessed=8 * 1024 * sum(heights), transcendentals=0
            ),
        )(
            jnp.stack([side(step) for step in steps]),
            *(rows for pair in zip(stripes, arrived) for rows in pair),
        )
    )


def tie(*groups):
    return lax.optimization_barrier(groups)


def step_orders():
    utt, seq = axis_bits("utt"), axis_bits("seq")
    across, line, rest = utt[1:], seq[:1], seq[1:]
    return (
        line + across + rest,
        across + rest + line,
        rest[:1] + line + across + rest[1:],
    )


def all_shared(copies):
    return lax.all_to_all(copies, ("utt", "seq"), 0, 0, tiled=True)


def from_neighbours(head, tail):
    count = lax.axis_size("seq")
    before = lax.ppermute(tail, "seq", [(i, i + 1) for i in range(count - 1)])
    behind = lax.ppermute(head, "seq", [(i + 1, i) for i in range(count - 1)])
    return before, behind


def pair_rows(mine, theirs, start=0, width=None):
    columns = slice(start, start + (width or mine.shape[1]))
    return jnp.concatenate([mine[:, columns], theirs[:, columns]], axis=0)


def outer(left, right):
    return low(matmul(left.T, right))


def put_half(outs, side_number, half, value):
    @pl.when(side_number == half)
    def _():
        outs[1][...] = value

    @pl.when(side_number != half)
    def _():
        outs[0][...] = value


def feed_blocks(refs, outs, sides):
    hidden, grad_pre, active, grad_low = (refs[2 * i : 2 * i + 2] for i in range(4))
    hidden_cols = pair_rows(*hidden).T
    grad_rows = pair_rows(*grad_low)
    for half in range(2):
        block = low(matmul(hidden_cols, pair_rows(*grad_pre, 512 * half, 512)))
        put_half(outs[:2], sides[1], half, block)
        block = outer(pair_rows(*active, 512 * half, 512), grad_rows)
        put_half(outs[2:4], sides[2], half, block)


def second_kernel(places, *refs):
    feed_blocks(refs[:8], refs[8:], places)


def mixer_blocks_kernel(places, *refs):
    refs, outs = refs[:12], refs[12:]
    mixer = outer(pair_rows(*refs[:2]), pair_rows(*refs[2:4]))
    branch = outer(pair_rows(*refs[4:6]), pair_rows(*refs[6:8]))
    attend = outer(pair_rows(*refs[8:10]), pair_rows(*refs[10:12]))
    for half in range(2):
        pieces = (
            mixer[256 * half : 256 * half + 256],
            branch[128 * half : 128 * half + 128],
            attend[128 * half : 128 * half + 128],
        )
        put_half(outs, places[3], half, jnp.concatenate(pieces, axis=0))


def turn_kernel(places, *refs):
    for number in range(3):
        mine, theirs, out = refs[2 * number], refs[2 * number + 1], refs[8 + number]
        rows = mine.shape[0]
        out[:, :rows] = mine[...].T
        out[:, rows:] = theirs[...].T
    refs[11][...] = add_low(refs[6][...], refs[7][...])


def late_kernel(
    keeping,
    places,
    hidden_cols,
    grad_pre,
    grad_pre_other,
    active_cols,
    grad_low,
    grad_low_other,
    attend_cols,
    attend_rows,
    attend_rows_other,
    position,
    *outs,
):
    step = pl.program_id(0)
    half = places[3] if keeping else 1 - places[3]

    def blocks(left, mine, theirs):
        return low(matmul(left[...], jnp.concatenate([mine[...], theirs[...]], axis=0)))

    @pl.when(step == 0)
    def _():
        outs[0][...] = blocks(hidden_cols, grad_pre, grad_pre_other)

    @pl.when(step == 1)
    def _():
        outs[1][...] = blocks(active_cols, grad_low, grad_low_other)

    @pl.when((step == 2) & (places[0] + half < 2))
    def _():
        outs[2][...] = blocks(attend_cols, attend_rows, attend_rows_other)

    @pl.when((step == 2) & (places[0] + half == 2))
    def _():
        outs[2][...] = position[...]


def late_blocks(keeping, places, cols, grad_pre, pair):
    hidden_cols, active_cols, attend_cols, position = cols
    rows = pair[0].shape[0]

    def half(p, stripe):
        return p[stripe] if keeping else 1 - p[stripe]

    def whole(shape):
        return pl.BlockSpec(shape, lambda i, p: (0, 0))

    def attend_column(i, p):
        return (0, jnp.where(p[0] == 0, 2 + half(p, 3), 4))

    block = (rows, 512)
    return list(
        pl.pallas_call(
            functools.partial(late_kernel, keeping),
            grid_spec=pltpu.PrefetchScalarGridSpec(
                num_scalar_prefetch=1,
                grid=(3,),
                in_specs=[
                    whole(hidden_cols.shape),
                    pl.BlockSpec(block, lambda i, p: (0, half(p, 1))),
                    pl.BlockSpec(block, lambda i, p: (0, half(p, 1))),
                    pl.BlockSpec((512, 2 * rows), lambda i, p: (half(p, 2), 0)),
                    pl.BlockSpec(block, lambda i, p: (0, 5)),
                    pl.BlockSpec(block, lambda i, p: (0, 5)),
                    whole(attend_cols.shape),
                    pl.BlockSpec(block, attend_column),
                    pl.BlockSpec(block, attend_column),
                    whole(position.shape),
                ],
                out_specs=[whole((512, 512))] * 3,
            ),
            out_shape=[jax.ShapeDtypeStruct((512, 512), jnp.bfloat16)] * 3,
            compiler_params=pltpu.CompilerParams(vmem_limit_bytes=SUM_LIMIT if keeping else VMEM_LIMIT),
            cost_estimate=pl.CostEstimate(
                flops=6 * 512 * 512 * 2 * rows, bytes_accessed=6 * 10**6, transcendentals=0
            ),
        )(
            places,
            hidden_cols,
            grad_pre,
            pair[1],
            active_cols,
            *pair,
            attend_cols,
            *pair,
            position,
        )
    )


def columns(pair, width, number, by_core=False):
    index = (lambda numbers: number + numbers[0]) if by_core else number
    return [Part(array, (array.shape[0], width), (0, index)) for array in pair]


def block_sums(kernel, places, stripes, operands):
    blocks = vmem_call(
        kernel,
        [((512, 512), jnp.bfloat16)] * (2 * stripes),
        (),
        [part for pair in operands for part in pair],
        cost=7 * 10**8 * stripes,
        numbers=(places,),
    )
    return blocks[::2], blocks[1::2]


def spread_kernel(places, first, second, third, *refs):
    feed_in, feed_out, mixer_in, mixer_out, attend_out, attend_in = refs[-14:-8]
    held, wide_rows = refs[-8:-5], refs[-5:-2]
    arrive, leave = refs[-2:]
    core, half = places[0], places[3]
    quarters = [pl.multiple_of(512 * (2 * core + places[1 + i]), 512) for i in range(3)]
    coming = []
    for part in range(2):
        for number, source in enumerate((first, second, third)):
            rows = pl.ds(512 * part, 512)
            coming.append(
                pltpu.make_async_copy(
                    source.at[rows], held[number].at[rows], arrive.at[3 * part + number]
                )
            )
    for copy in coming:
        copy.start()
    going = []
    for part in range(2):
        for number in range(3):
            coming[3 * part + number].wait()
            rows = pl.ds(512 * part, 512)
            wide_rows[number][rows, :] = wide(held[number][rows, :])
            layer = 1 - part
            if number == 0:
                targets = [(512, feed_in.at[layer, :, pl.ds(quarters[0], 512)])]
            elif number == 1:
                targets = [(512, feed_out.at[layer, pl.ds(quarters[1], 512)])]
            elif part == 1:
                targets = [(512, attend_in.at[2 * core + half])]
            else:
                tall = pl.ds(pl.multiple_of(256 * half, 256), 256)
                flat = pl.ds(pl.multiple_of(128 * (2 * core + half), 128), 128)
                side_columns = pl.ds(pl.multiple_of(512 * core, 512), 512)
                targets = [
                    (256, mixer_in.at[tall, side_columns]),
                    (128, mixer_out.at[flat]),
                    (128, attend_out.at[flat]),
                ]
            start = 512 * part
            for height, target in targets:
                copy = pltpu.make_async_copy(
                    wide_rows[number].at[pl.ds(start, height)], target, leave.at[len(going)]
                )
                copy.start()
                going.append(copy)
                start += height
    for copy in going:
        copy.wait()


def spread_blocks(places, stripes, shapes, bases):
    anywhere = pl.BlockSpec(memory_space=pl.ANY)
    return list(
        pl.pallas_call(
            spread_kernel,
            in_specs=[pl.BlockSpec(memory_space=pltpu.SMEM)] + [anywhere] * (3 + len(bases)),
            out_specs=[anywhere] * len(shapes),
            out_shape=[jax.ShapeDtypeStruct(shape, jnp.float32) for shape in shapes],
            scratch_shapes=[pltpu.VMEM((1024, 512), jnp.bfloat16)] * 3
            + [pltpu.VMEM((1024, 512), jnp.float32)] * 3
            + [pltpu.SemaphoreType.DMA((6,)), pltpu.SemaphoreType.DMA((8,))],
            input_output_aliases={4 + n: n for n in range(len(bases))},
            compiler_params=pltpu.CompilerParams(vmem_limit_bytes=VMEM_LIMIT),
            cost_estimate=pl.CostEstimate(
                flops=1024, bytes_accessed=1024, transcendentals=0
            ),
        )(places, *stripes, *bases)
    )


def angle_tables(frame_count, features):
    halves = jnp.arange(features // 2, dtype=jnp.int32).astype(jnp.float32)
    frequencies = jnp.exp(halves * (-2.0 * math.log(10000.0) / features))
    fine = 32
    low_angles = jnp.arange(fine, dtype=jnp.int32).astype(jnp.float32)[:, None] * frequencies
    high_angles = (fine * jnp.arange(frame_count // fine, dtype=jnp.int32)).astype(jnp.float32)[
        :, None
    ] * frequencies
    low_sin, low_cos = jnp.sin(low_angles)[None], jnp.cos(low_angles)[None]
    high_sin, high_cos = jnp.sin(high_angles)[:, None], jnp.cos(high_angles)[:, None]
    sines = high_sin * low_cos + high_cos * low_sin
    cosines = high_cos * low_cos - high_sin * low_sin
    shape = (frame_count, features // 2)
    return sines.reshape(shape), cosines.reshape(shape)


def heads_out(blocks, groups):
    return lax.all_to_all(jnp.tile(blocks, (groups, 1, 1)), "seq", 0, 0, tiled=True)


def rows_dot(first_operand, second_operand):
    return lax.dot_general(
        first_operand, second_operand, (((1,), (1,)), ((), ())), preferred_element_type=jnp.float32
    )


def lane_side(shape, utterance):
    return (lax.broadcasted_iota(jnp.int32, shape, 1) // HEAD_DIM) == utterance


def turned_queries(content, shift, weight, sines, cosines):
    offset = (content.astype(jnp.float32) + shift).astype(jnp.bfloat16)
    half = sines.shape[1]
    spread = jnp.dot(offset, weight, preferred_element_type=jnp.float32)
    sin_part, cos_part = spread[:, :half], spread[:, half:]
    return (
        offset,
        (sin_part * sines + cos_part * cosines).astype(jnp.bfloat16),
        (cos_part * sines - sin_part * cosines).astype(jnp.bfloat16),
    )


def attend_kernel(
    limits,
    content,
    keys,
    values,
    shift,
    weight,
    sines,
    cosines,
    table,
    weights_out,
    attended_out,
    held,
    scores,
):
    scale = HEAD_DIM ** (-0.5)
    weight_rows = jnp.concatenate([weight[...]] * limits.shape[0], axis=0)
    content_rows = content[...]
    key_side = jnp.concatenate([table[...], keys[...]], axis=1)
    places = lax.broadcasted_iota(jnp.int32, (1, table.shape[0]), 1)
    attended = None
    for utterance in range(limits.shape[0]):
        ours = lane_side(content_rows.shape, utterance)
        mine = jnp.where(ours, content_rows, jnp.zeros_like(content_rows))
        moved = jnp.where(ours, shift[...], 0.0)
        _, turned_cos, turned_sin = turned_queries(
            mine, moved, weight_rows, sines[...], cosines[...]
        )
        query_side = jnp.concatenate([turned_cos, turned_sin, mine], axis=1) * scale
        scores[utterance] = rows_dot(query_side.astype(jnp.bfloat16), key_side)
    for utterance in range(limits.shape[0]):
        allowed = places < limits[utterance]
        for start in range(0, scores.shape[1], ROW_TILE):
            rows = slice(start, start + ROW_TILE)
            tile = jnp.where(allowed, scores[utterance, rows, :], -1000000000.0)
            raised = jnp.exp(tile - jnp.max(tile, axis=1, keepdims=True))
            totals = jnp.sum(raised, axis=1, keepdims=True)
            weights_out[utterance, rows, :] = low(raised * (1.0 / totals))
    for utterance in range(limits.shape[0]):
        ours = lane_side(content_rows.shape, utterance)
        part = matmul(weights_out[utterance], values[...])
        attended = part if attended is None else jnp.where(ours, part, attended)
    if held is None:
        attended_out[...] = attended.astype(jnp.bfloat16)
        return
    step = pl.program_id(0)
    height = attended.shape[0]
    block = attended_out.shape[1] - 2 * HALO
    held[pl.ds(pl.multiple_of(HALO + step * height, 8), height), :] = attended
    for number in range(height // block):
        attended_out[step * (height // block) + number, 0:block, :] = attended[
            number * block : (number + 1) * block
        ].astype(jnp.bfloat16)

    @pl.when(step == pl.num_programs(0) - 1)
    def _():
        edge = jnp.zeros((HALO, held.shape[1]), jnp.float32)
        held[0:HALO, :] = edge
        held[held.shape[0] - HALO :, :] = edge
        for number in range(attended_out.shape[0]):
            start = number * block
            sides = jnp.concatenate(
                [
                    held[start : start + HALO, :],
                    held[start + HALO + block : start + 2 * HALO + block, :],
                ],
                axis=0,
            )
            attended_out[number, block:, :] = sides.astype(jnp.bfloat16)


def attend_back_kernel(
    weights,
    content,
    grads,
    keys,
    values,
    shift,
    weight,
    sines,
    cosines,
    table,
    *outs,
):
    step = pl.program_id(0)
    *outs, grad_probs, grad_scores = outs
    query_out, pairs_out, weight_out, sums_out, key_sums, value_sums = (
        [None] * (6 - len(outs)) + outs
    )
    scale = HEAD_DIM ** (-0.5)

    @pl.when(step == 0)
    def _():
        key_sums[...] = jnp.zeros_like(key_sums)
        value_sums[...] = jnp.zeros_like(value_sums)
        weight_out[...] = jnp.zeros_like(weight_out)
        sums_out[...] = jnp.zeros_like(sums_out)

    weight_rows = jnp.concatenate([weight[...]] * weights.shape[0], axis=0)
    content_rows, grad_rows = content[...], grads[...]
    content_cols = content_rows.T
    grad_cols = grad_rows.T
    key_side = jnp.concatenate([table[...], keys[...]], axis=1)
    half = sines.shape[1]
    grad_content = grad_position = None
    for utterance in range(weights.shape[0]):
        ours = lane_side(content_rows.shape, utterance)
        grad_mine = jnp.where(ours, grad_rows, jnp.zeros_like(grad_rows)) * scale
        grad_probs[utterance] = rows_dot(grad_mine.astype(jnp.bfloat16), values[...])
    for utterance in range(weights.shape[0]):
        first, last = utterance * HEAD_DIM, (utterance + 1) * HEAD_DIM
        ours = lane_side(content_rows.shape, utterance)
        probs = weights[utterance]
        for start in range(0, grad_probs.shape[1], ROW_TILE):
            rows = slice(start, start + ROW_TILE)
            tile = wide(weights[utterance, rows, :])
            product = tile * grad_probs[utterance, rows, :]
            inner = jnp.sum(product, axis=1, keepdims=True)
            grad_scores[utterance, rows, :] = low(product - tile * inner)
        value_sums[first:last, :] += jnp.dot(
            grad_cols[first:last, :], probs, preferred_element_type=jnp.float32
        )
        key_sums[first:last, :] += jnp.dot(
            content_cols[first:last, :], grad_scores[utterance], preferred_element_type=jnp.float32
        )
        grad_side = matmul(grad_scores[utterance], key_side)
        grad_cos_table = grad_side[:, :half]
        grad_sin_table = grad_side[:, half : 2 * half]
        from_table = jnp.concatenate(
            [
                grad_cos_table * sines[...] - grad_sin_table * cosines[...],
                grad_cos_table * cosines[...] + grad_sin_table * sines[...],
            ],
            axis=1,
        ).astype(jnp.bfloat16)
        offset = (content_rows.astype(jnp.float32) + shift[...]).astype(jnp.bfloat16)
        weight_out[...] += jnp.dot(
            offset.T[first:last, :], from_table, preferred_element_type=jnp.float32
        )
        content_part = grad_side[:, 2 * half :]
        position_part = rows_dot(from_table, weight_rows)
        if grad_content is None:
            grad_content, grad_position = content_part, position_part
        else:
            grad_content = jnp.where(ours, content_part, grad_content)
            grad_position = jnp.where(ours, position_part, grad_position)
    grad_query = (grad_content + grad_position).astype(jnp.bfloat16)
    height, lanes = grad_query.shape
    if query_out is None:
        pairs_out[pl.ds(pl.multiple_of(step * height, 16), height), 0:lanes] = grad_query
    else:
        query_out[...] = grad_query
    sums_out[0:1, :] += jnp.sum(grad_content, axis=0, keepdims=True)
    sums_out[1:2, :] += jnp.sum(grad_position, axis=0, keepdims=True)

    @pl.when(step == pl.num_programs(0) - 1)
    def _():
        first = pairs_out.shape[1] - 2 * lanes
        pairs_out[:, first : first + lanes] = key_sums[...].T.astype(jnp.bfloat16)
        pairs_out[:, first + lanes :] = value_sums[...].T.astype(jnp.bfloat16)


def query_block(frames_all, most=256):
    return most if frames_all <= 1024 else 128


def whole_block(shape):
    return pl.BlockSpec(shape, lambda i: (0,) * len(shape))


def row_block(height, width):
    return pl.BlockSpec((height, width), lambda i: (i, 0))


def attend_heads(limits, content, arrived, shift, weight, sines, cosines, table, block):
    utterances = limits.shape[0]
    query_frames, lanes = content.shape[0], arrived.shape[1] // 3
    frames_all, table_width = table.shape
    height = query_block(frames_all, 512)
    chunked = query_frames == frames_all and height % block == 0
    chunks = (frames_all // block, block + 2 * HALO, lanes)
    kernel = attend_kernel
    if not chunked:
        kernel = lambda *refs: attend_kernel(*refs[:-1], None, refs[-1])
    return pl.pallas_call(
        kernel,
        grid=(query_frames // height,),
        in_specs=[
            pl.BlockSpec(memory_space=pltpu.SMEM),
            row_block(height, lanes),
            pl.BlockSpec((frames_all, lanes), lambda i: (0, 1)),
            pl.BlockSpec((frames_all, lanes), lambda i: (0, 2)),
            whole_block(shift.shape),
            whole_block(weight.shape),
            row_block(height, sines.shape[1]),
            row_block(height, sines.shape[1]),
            whole_block(table.shape),
        ],
        out_specs=[
            pl.BlockSpec((utterances, height, frames_all), lambda i: (0, i, 0)),
            whole_block(chunks) if chunked else row_block(height, lanes),
        ],
        out_shape=[
            jax.ShapeDtypeStruct((utterances, query_frames, frames_all), jnp.bfloat16),
            jax.ShapeDtypeStruct(chunks if chunked else (query_frames, lanes), jnp.bfloat16),
        ],
        scratch_shapes=[pltpu.VMEM((frames_all + 2 * HALO, lanes), jnp.float32)] * chunked
        + [pltpu.VMEM((utterances, height, frames_all), jnp.float32)],
        compiler_params=pltpu.CompilerParams(vmem_limit_bytes=VMEM_LIMIT),
        cost_estimate=pl.CostEstimate(
            flops=2 * utterances * query_frames * frames_all * (table_width + 256),
            bytes_accessed=2 * utterances * query_frames * frames_all,
            transcendentals=utterances * query_frames * frames_all,
        ),
    )(limits, content, arrived, arrived, shift, weight, sines, cosines, table)


def attend_heads_back(
    weights, content, grads, arrived, shift, weight, sines, cosines, table
):
    utterances, query_frames, frames_all = weights.shape
    lanes = arrived.shape[1] // 3
    height = query_block(frames_all)
    joined = query_frames == frames_all
    width = (3 if joined else 2) * lanes
    return pl.pallas_call(
        attend_back_kernel,
        grid=(query_frames // height,),
        in_specs=[
            pl.BlockSpec((utterances, height, frames_all), lambda i: (0, i, 0)),
            row_block(height, lanes),
            row_block(height, lanes),
            pl.BlockSpec((frames_all, lanes), lambda i: (0, 1)),
            pl.BlockSpec((frames_all, lanes), lambda i: (0, 2)),
            whole_block(shift.shape),
            whole_block(weight.shape),
            row_block(height, sines.shape[1]),
            row_block(height, sines.shape[1]),
            whole_block(table.shape),
        ],
        out_specs=([] if joined else [row_block(height, lanes)])
        + [
            whole_block((frames_all, width)),
            whole_block((HEAD_DIM, table.shape[1])),
            whole_block((8, lanes)),
        ],
        out_shape=(
            [] if joined else [jax.ShapeDtypeStruct((query_frames, lanes), jnp.bfloat16)]
        )
        + [
            jax.ShapeDtypeStruct((frames_all, width), jnp.bfloat16),
            jax.ShapeDtypeStruct((HEAD_DIM, table.shape[1]), jnp.float32),
            jax.ShapeDtypeStruct((8, lanes), jnp.float32),
        ],
        scratch_shapes=[
            pltpu.VMEM((lanes, frames_all), jnp.float32),
            pltpu.VMEM((lanes, frames_all), jnp.float32),
            pltpu.VMEM((utterances, height, frames_all), jnp.float32),
            pltpu.VMEM((utterances, height, frames_all), jnp.bfloat16),
        ],
        compiler_params=pltpu.CompilerParams(vmem_limit_bytes=VMEM_LIMIT),
        cost_estimate=pl.CostEstimate(
            flops=2 * utterances * query_frames * frames_all * (table.shape[1] + 512),
            bytes_accessed=2 * utterances * query_frames * frames_all,
            transcendentals=0,
        ),
    )(weights, content, grads, arrived, arrived, shift, weight, sines, cosines, table)


def shards(
    frames,
    lengths,
    out_grad,
    norm_gain,
    norm_bias,
    feed_in,
    feed_in_bias,
    feed_out,
    feed_out_bias,
    attend_in,
    attend_vectors,
    attend_out,
    mixer_in,
    mixer_in_bias,
    depthwise,
    mixer_vectors,
    mixer_out,
    batch_gain,
    batch_shift,
    running_mean,
    running_variance,
):
    utt_rows, block_frames, features = frames.shape
    rows = utt_rows * block_frames
    seq_count = lax.axis_size("seq")
    seq_index = lax.axis_index("seq")
    count = lax.axis_size("utt") * seq_count
    frames_all = block_frames * seq_count
    groups = seq_count // HEADS
    head, group = seq_index % HEADS, seq_index // HEADS
    query_frames = frames_all // groups
    lanes = utt_rows * HEAD_DIM
    info = jnp.concatenate(
        [(seq_index * block_frames).reshape(1), lengths, jnp.full((1,), frames_all, jnp.int32)]
    )
    hidden_units = feed_in.shape[2]
    f32, bf16 = jnp.float32, jnp.bfloat16
    flat_frames = frames.reshape(rows, features)
    square, broad = (rows, features), (rows, hidden_units)
    extended = (utt_rows * (block_frames + 2 * HALO), features)
    row_flops = 2 * rows * features
    bind = functools.partial
    edge = ((utt_rows, 2 * HALO, features), f32)
    feed_scratch = [
        pltpu.VMEM((features, hidden_units), bf16),
        pltpu.VMEM((hidden_units, features), bf16),
    ]
    attend_scratch = pltpu.VMEM((3, features, features), bf16)
    (
        edge_head,
        edge_tail,
        after_first,
        slope_first,
        entry_pack,
        sent,
    ) = vmem_call(
        bind(entry_kernel, utt_rows),
        [
            edge,
            edge,
            (square, f32),
            (broad, bf16),
            ((rows, hidden_units + 2 * features), bf16),
            ((HEADS, block_frames, 3 * lanes), bf16),
        ],
        (),
        (
            flat_frames,
            norm_gain,
            norm_bias,
            feed_in_bias,
            feed_out_bias,
            attend_vectors,
            Part(out_grad, (utt_rows, HALO, features), (0, 0, 0)),
            Part(out_grad, (utt_rows, HALO, features), (0, block_frames // HALO - 1, 0)),
        ),
        scratch=feed_scratch + [attend_scratch, pltpu.SemaphoreType.DMA((3,))],
        cost=row_flops * (2 * hidden_units + 3 * features),
        held=(feed_in, feed_out, attend_in),
    )
    sent, all_limits, edge_head, edge_tail = tie(sent, lengths, edge_head, edge_tail)
    before, behind = from_neighbours(edge_head, edge_tail)
    arrived = heads_out(sent, groups)
    for step in axis_bits("utt"):
        all_limits = jnp.concatenate([all_limits, swap(all_limits, step)])
    arrived, all_limits = tie(arrived, all_limits)
    arrived = arrived.reshape(frames_all, 3 * lanes)
    start_query = group * query_frames
    head_content = arrived
    if groups > 1:
        head_content = lax.dynamic_slice_in_dim(arrived, start_query, query_frames, 0)
    head_vectors = lax.dynamic_slice_in_dim(
        attend_vectors.astype(f32), head * HEAD_DIM, HEAD_DIM, 1
    )
    head_shift = jnp.tile((head_vectors[4] - head_vectors[3])[None], (1, utt_rows))
    head_weight = lax.dynamic_slice_in_dim(attend_in[3], head * HEAD_DIM, HEAD_DIM, 1).reshape(
        features // 2, 2, HEAD_DIM
    )
    head_weight = jnp.transpose(head_weight, (2, 1, 0)).reshape(HEAD_DIM, features)
    sines, cosines = angle_tables(frames_all, features)
    key_table = jnp.concatenate([cosines, sines], axis=1).astype(bf16)
    query_sin = lax.dynamic_slice_in_dim(sines, start_query, query_frames, 0)
    query_cos = lax.dynamic_slice_in_dim(cosines, start_query, query_frames, 0)
    weights, head_attended = attend_heads(
        lengths,
        head_content,
        arrived,
        head_shift,
        head_weight,
        query_sin,
        query_cos,
        key_table,
        block_frames,
    )

    def frames_back(blocks):
        width = blocks.shape[-1]
        blocks = blocks.reshape(1, HEADS, block_frames, width)
        if groups > 1:
            blocks = lax.dynamic_update_slice_in_dim(
                jnp.zeros((groups,) + blocks.shape[1:], blocks.dtype), blocks, group, 0
            )
        blocks = lax.all_to_all(
            blocks.reshape(seq_count, block_frames, width), "seq", 0, 0, tiled=True
        ).reshape(groups, HEADS, block_frames, width)
        return lax.dynamic_slice_in_dim(blocks, group, 1, 0)[0]

    head_attended, before, behind = tie(head_attended, before, behind)
    after_sides, grad_sides = vmem_call(
        sides_kernel,
        [((2 * utt_rows * HALO, features), f32)] * 2,
        (),
        (before, behind, norm_gain, norm_bias, feed_in_bias, feed_out_bias),
        scratch=feed_scratch + [pltpu.SemaphoreType.DMA((2,))],
        cost=row_flops * 2 * hidden_units // 4,
        held=(feed_in, feed_out),
    )
    if head_attended.ndim == 2:
        placed = lax.dynamic_update_slice_in_dim(
            jnp.zeros((frames_all + 2 * HALO, lanes), bf16), head_attended, HALO + start_query, 0
        )
        main, before, behind = (
            placed[start : start + frames_all].reshape(seq_count, block_frames, lanes)
            for start in (HALO, 0, 2 * HALO)
        )
        head_attended = jnp.concatenate([main, before[:, :HALO], behind[:, -HALO:]], axis=1)
    attended_blocks = lax.all_to_all(head_attended, "seq", 0, 0, tiled=True)
    attended_blocks, after_sides, grad_sides = tie(attended_blocks, after_sides, grad_sides)
    if groups > 1:
        attended_blocks = jnp.sum(
            attended_blocks.reshape((groups, HEADS) + attended_blocks.shape[1:]), axis=0
        )
    taps = depthwise.T
    padded = pltpu.VMEM((utt_rows, block_frames + 2 * HALO + 16, features), f32)
    (
        after_attend,
        mixer_pack,
        linear_half,
        gate_half,
        gated,
        convolved,
        shared,
    ) = vmem_call(
        bind(mixer_kernel, utt_rows),
        [
            (extended, f32),
            ((rows, 2 * features), bf16),
            (square, f32),
            (square, f32),
            (extended, bf16),
            (extended, f32),
            ((8 * count, 128), f32),
        ],
        (info,),
        (
            attended_blocks,
            after_first,
            after_sides,
            norm_gain,
            norm_bias,
            attend_out,
            attend_vectors,
            mixer_in,
            mixer_in_bias.reshape(1, -1),
            taps,
            mixer_vectors,
        ),
        scratch=(padded,),
        cost=row_flops * 3 * features,
    )
    (
        layer_output,
        grad_mixer,
        grad_batch,
        normed_batch,
        second_pack,
        shared,
        batch_rows,
        middle_rows,
    ) = vmem_call(
        bind(middle_kernel, utt_rows, seq_count),
        [
            (square, f32),
            (square, f32),
            (extended, f32),
            (extended, f32),
            ((rows, 2 * hidden_units + 4 * features), bf16),
            ((8 * count, 128), f32),
            ((8, features), f32),
            ((16, features), f32),
        ],
        (all_limits, lax.axis_index("utt").reshape(1)),
        (
            convolved,
            all_shared(shared),
            after_attend,
            out_grad.reshape(rows, features),
            grad_sides,
            norm_gain,
            norm_bias,
            batch_gain.reshape(1, -1),
            batch_shift.reshape(1, -1),
            running_mean.reshape(1, -1),
            running_variance.reshape(1, -1),
            mixer_out,
            mixer_vectors,
            feed_in_bias,
            feed_out_bias,
        ),
        scratch=feed_scratch + [pltpu.SemaphoreType.DMA((2,))],
        cost=row_flops * (4 * hidden_units + 2 * features),
        held=(feed_in, feed_out),
    )
    phases = list(zip(*step_orders()))
    near = axis_bits("utt")[0]
    core = side(near).reshape(1)
    halves = jnp.stack([side(step) for step in phases[0]])
    places = jnp.concatenate([core, halves])
    half_units, half_features = hidden_units // 2, features // 2

    def with_pair(array):
        return [array, swap(array, near)]

    second_pair = with_pair(second_pack)
    second_sent, second_kept = block_sums(
        second_kernel,
        places,
        2,
        [
            columns(second_pair, features, 8),
            columns(second_pair, half_units, 0, True),
            columns(second_pair, half_units, 2, True),
            columns(second_pair, features, 9),
        ],
    )
    other_places = [
        jnp.concatenate([near_core, near_halves])
        for near_halves in (halves, 1 - halves)
        for near_core in (core, 1 - core)
    ][1:]
    second_pair, second_sent, second_kept, shared, other_places = tie(
        second_pair, second_sent, second_kept, all_shared(shared), other_places
    )
    (
        batch_grads,
        grad_attend,
        mixer_back_pack,
        grad_blocks,
        mixer_rows,
    ) = vmem_call(
        bind(mixer_back_kernel, utt_rows),
        [
            ((8, features), f32),
            (square, f32),
            ((rows, 3 * features), bf16),
            ((HEADS, block_frames, lanes), bf16),
            ((16, features), f32),
        ],
        (info,),
        (
            grad_batch,
            normed_batch,
            shared,
            batch_rows,
            batch_gain.reshape(1, -1),
            gated,
            linear_half,
            gate_half,
            grad_mixer,
            after_attend,
            norm_gain,
            taps,
            mixer_in,
            attend_out,
        ),
        scratch=(padded, padded),
        cost=row_flops * 4 * features,
    )
    mixer_pair, mixer_back_pair = with_pair(mixer_pack), with_pair(mixer_back_pack)
    third_sent, third_kept = block_sums(
        mixer_blocks_kernel,
        places,
        1,
        [
            columns(mixer_pair, features, 1),
            columns(mixer_back_pair, features, 0, True),
            columns(second_pair, half_features, 20, True),
            columns(second_pair, features, 11),
            columns(mixer_pair, half_features, 0, True),
            columns(mixer_back_pair, features, 2),
        ],
    )
    early_sent, early_kept = second_sent + third_sent, second_kept + third_kept
    early_arrived = swap_all(early_sent, phases[0])
    head_grad = heads_out(grad_blocks, groups).reshape(frames_all, lanes)
    if groups > 1:
        head_grad = lax.dynamic_slice_in_dim(head_grad, start_query, query_frames, 0)
    head_grad, early_kept = tie(head_grad, early_kept)
    *head_grads, head_weight_grad, head_sums = attend_heads_back(
        weights,
        head_content,
        head_grad,
        arrived,
        head_shift,
        head_weight,
        query_sin,
        query_cos,
        key_table,
    )
    head_grads, head_weight_grad, head_sums, early_arrived = tie(
        head_grads, head_weight_grad, head_sums, early_arrived
    )
    grad_blocks = head_grads[-1].reshape(seq_count, block_frames, -1)
    returned = lax.all_to_all(grad_blocks, "seq", 0, 0, tiled=True)
    if groups > 1:
        returned = jnp.sum(
            returned.astype(f32).reshape(groups, HEADS, block_frames, 2 * lanes), axis=0
        ).astype(bf16)
        returned = jnp.concatenate([frames_back(head_grads[0]), returned], axis=2)
    head_vector_grads = lax.dynamic_update_slice_in_dim(
        jnp.zeros((8, features), f32),
        jnp.sum(head_sums.reshape(8, utt_rows, HEAD_DIM), axis=1),
        head * HEAD_DIM,
        1,
    )
    early_sent, early_kept = fold_rows([(early_kept, early_arrived)], phases[1], 1, VMEM_LIMIT)
    early_sent, head_weight_grad = tie(early_sent, head_weight_grad)
    early_arrived = swap_all(early_sent, phases[1])
    head_weight_grad = jnp.transpose(
        head_weight_grad.reshape(HEAD_DIM, 2, features // 2), (2, 1, 0)
    ).reshape(features, HEAD_DIM)
    position_weight_grad = lax.dynamic_update_slice_in_dim(
        jnp.zeros((features, features), f32), head_weight_grad, head * HEAD_DIM, 1
    )
    entry_pair = with_pair(entry_pack)
    position_pair = with_pair(position_weight_grad.astype(bf16))
    entry_cols = vmem_call(
        turn_kernel,
        [
            ((features, 2 * rows), bf16),
            ((half_units, 2 * rows), bf16),
            ((features, 2 * rows), bf16),
            ((features, features), bf16),
        ],
        (),
        columns(entry_pair, features, 4)
        + columns(entry_pair, half_units, 0, True)
        + columns(entry_pair, features, 5)
        + position_pair,
        numbers=(places,),
    )
    returned, early_arrived, entry_cols = tie(returned, early_arrived, entry_cols)
    (
        frames_grad,
        entry_back_pack,
        grad_pre_first,
        entry_rows,
    ) = vmem_call(
        entry_back_kernel,
        [
            (square, f32),
            ((rows, half_units + 4 * features), bf16),
            ((rows, half_units), bf16),
            ((16, features), f32),
        ],
        (core,),
        (
            returned,
            grad_attend,
            flat_frames,
            after_first,
            slope_first,
            norm_gain,
        ),
        scratch=feed_scratch + [attend_scratch, pltpu.SemaphoreType.DMA((3,))],
        cost=row_flops * (2 * hidden_units + 3 * features),
        held=(feed_in, feed_out, attend_in),
    )
    late_factors = (entry_cols, grad_pre_first, with_pair(entry_back_pack))
    late_sent = late_blocks(False, places, *late_factors)
    late_sent, late_factors, middle_rows = tie(late_sent, late_factors, middle_rows)
    late_arrived = swap_all(late_sent, phases[0])
    late_kept = late_blocks(True, places, *late_factors)
    flat = jnp.concatenate([middle_rows, mixer_rows, entry_rows, head_vector_grads], axis=0)
    flat_steps = [near] + [steps[0] for steps in phases]
    def in_turn(arrived_rows, steps, work):
        nonlocal flat
        flat_arrived = swap(flat, flat_steps.pop()) if flat_steps else jnp.zeros_like(flat)
        after, next_arrived = None, []
        for i, rows in enumerate(arrived_rows):
            if after is not None:
                rows, _ = tie(rows, after)
            if i == len(arrived_rows) - 1:
                rows, flat_arrived = tie(rows, flat_arrived)
            after = work(i, rows)
            next_arrived.append(swap(after, steps[i]) if steps else after)
        flat = flat + flat_arrived
        return next_arrived

    late_kept = list(late_kept)
    for steps in phases[1:]:

        def fold(i, rows):
            pairs = [([late_kept[i]], [rows])]
            if steps is phases[2]:
                pairs = [([early_kept[i]], [early_arrived[i]])] + pairs
            parts = 1 if steps in phases[1:3] else 2
            (sent_rows,), (late_kept[i],) = fold_rows(pairs, [steps[i]], parts)
            return sent_rows

        late_arrived = in_turn(late_arrived, steps, fold)
    sums = [None] * len(late_arrived)

    def add(i, rows):
        (sums[i],) = add_rows([late_kept[i]], [rows])
        return sums[i]

    arrived_rows = in_turn(late_arrived, phases[-1], add)
    for number in range(len(phases) - 1, 0, -1):

        def join(i, rows):
            (sums[i],) = join_rows([sums[i]], [rows], [phases[number][i]])
            return sums[i]

        arrived_rows = in_turn(arrived_rows, phases[number - 1], join)
    for step in flat_steps:
        flat = flat + swap(flat, step)
    vector_grads = vmem_call(
        vectors_kernel,
        [
            (norm_gain.shape, f32),
            (norm_bias.shape, f32),
            (feed_in_bias.shape, f32),
            (feed_out_bias.shape, f32),
            (attend_vectors.shape, f32),
            ((1, 2 * features), f32),
            (mixer_vectors.shape, f32),
            ((KERNEL, features), f32),
        ],
        (),
        (flat,),
    )
    vector_grads = list(vector_grads)
    vector_grads[5] = vector_grads[5].reshape(-1)
    vector_grads[7] = vector_grads[7].T
    vector_grads = [*vector_grads, batch_grads[1], batch_grads[0], batch_rows[2], batch_rows[3]]
    across_rows = swap_all(sums, [near] * 3)
    shapes = [feed_in.shape, feed_out.shape, mixer_in.shape, mixer_out.shape]
    shapes += [attend_out.shape, attend_in.shape]
    spread = spread_blocks(places, sums, shapes, [])
    spread = spread_blocks(other_places[0], across_rows, shapes, spread)
    spread, arrived_rows, vector_grads = tie(spread, arrived_rows, vector_grads)
    across_rows = swap_all(arrived_rows, [near] * 3)
    spread = spread_blocks(other_places[1], arrived_rows, shapes, spread)
    (
        feed_in_grad,
        feed_out_grad,
        mixer_in_grad,
        mixer_out_grad,
        attend_out_grad,
        attend_in_grad,
    ) = spread_blocks(other_places[2], across_rows, shapes, spread)
    (
        norm_gain_grad,
        norm_bias_grad,
        feed_in_bias_grad,
        feed_out_bias_grad,
        attend_vectors_grad,
        mixer_in_bias_grad,
        mixer_vectors_grad,
        taps_grad,
        batch_gain_grad,
        batch_shift_grad,
        new_mean,
        new_variance,
    ) = vector_grads
    return (
        layer_output.reshape(frames.shape),
        frames_grad.reshape(frames.shape),
        norm_gain_grad,
        norm_bias_grad,
        feed_in_grad,
        feed_in_bias_grad,
        feed_out_grad,
        feed_out_bias_grad,
        attend_in_grad,
        attend_vectors_grad,
        attend_out_grad,
        mixer_in_grad,
        mixer_in_bias_grad,
        taps_grad,
        mixer_vectors_grad,
        mixer_out_grad,
        batch_gain_grad,
        batch_shift_grad,
        new_mean,
        new_variance,
    )


def solution(mesh):
    return jax.shard_map(
        shards,
        mesh=mesh,
        in_specs=(
            P("utt", "seq", None),
            P("utt"),
            P("utt", "seq", None),
            P(),
            P(),
            P(),
            P(),
            P(),
            P(),
            P(),
            P(),
            P(),
            P(),
            P(),
            P(),
            P(),
            P(),
            P(),
            P(),
            P(),
            P(),
        ),
        out_specs=(
            P("utt", "seq", None),
            P("utt", "seq", None),
            P(),
            P(),
            P(),
            P(),
            P(),
            P(),
            P(),
            P(),
            P(),
            P(),
            P(),
            P(),
            P(),
            P(),
            P(),
            P(),
            P(),
            P(),
        ),
        check_vma=False,
    )
```

```python
import functools
import math

import jax
import jax.numpy as jnp
import numpy as np
from jax import lax
from jax.experimental import pallas as pl
from jax.experimental.pallas import tpu as pltpu
from jax.sharding import PartitionSpec as P

HEADS = 8
KERNEL = 9
HEAD_DIM = 64


TOP_PRECISION = lax.Precision.HIGHEST
EPSILON = 1e-05
VMEM_LIMIT = 63 * 1024 * 1024
SUM_LIMIT = 20 * 1024 * 1024
HALO = 8
ROW_TILE = 32


def wide(values):
    return values.astype(jnp.float32)


def low(values):
    return values.astype(jnp.bfloat16)


def matmul(first_operand, second_operand):
    return jnp.dot(first_operand, second_operand, preferred_element_type=jnp.float32)


def column_sum(values):
    return jnp.sum(wide(values), axis=0, keepdims=True)


def normalize(values):
    average = jnp.mean(values, axis=-1, keepdims=True)
    centered = values - average
    spread = jnp.mean(centered * centered, axis=-1, keepdims=True)
    inverse = lax.rsqrt(spread + EPSILON)
    return centered * inverse, inverse


def scaled_norm(normed, gains, biases, number):
    return normed * wide(gains[number : number + 1, :]) + wide(biases[number : number + 1, :])


def norm_back(grad_rows, normed, inverse, gains, number, own=lambda values: values):
    scaled = grad_rows * wide(gains[number : number + 1, :])
    inner = (
        scaled
        - jnp.mean(scaled, axis=-1, keepdims=True)
        - normed * jnp.mean(scaled * normed, axis=-1, keepdims=True)
    )
    return inner * inverse, column_sum(own(grad_rows * normed)), column_sum(own(grad_rows))


def logistic(values):
    return 1.0 / (1.0 + jnp.exp(-values))


def silu_slope(preact, sigmoid):
    return sigmoid * (1.0 + preact * (1.0 - sigmoid))


def frame_places(info, rows, utterances, halo):
    own = rows - 2 * utterances * halo
    per = own // utterances
    row = lax.broadcasted_iota(jnp.int32, (rows, 1), 0)
    aside = row - own
    owner = jnp.where(aside < 0, row // per, aside // (2 * halo))
    near = aside % (2 * halo)
    place = jnp.where(aside < 0, row % per, near - halo + jnp.where(near < halo, 0, per))
    limit = jnp.full((rows, 1), info[utterances], jnp.int32)
    for utterance in range(utterances - 1):
        limit = jnp.where(owner == utterance, info[1 + utterance], limit)
    return info[0] + place, limit


def flags(condition):
    return jnp.where(condition, 1.0, 0.0)


def own_rows(values, utterances):
    return values[: values.shape[0] - 2 * utterances * HALO]


def with_sides(values, sides):
    return jnp.concatenate([values, sides], axis=0)


def blocks_of_heads(rows, utterances):
    per = rows.shape[0] // utterances
    first = lax.broadcasted_iota(jnp.int32, (per, 2 * HEAD_DIM), 1) < HEAD_DIM
    blocks = []
    for pair in range(HEADS // 2):
        columns = rows[:, pair * 2 * HEAD_DIM : (pair + 1) * 2 * HEAD_DIM]
        top, bottom = columns[:per], columns[per:]
        blocks.append(jnp.where(first, top, pltpu.roll(bottom, HEAD_DIM, 1)))
        blocks.append(jnp.where(first, pltpu.roll(top, HEAD_DIM, 1), bottom))
    return blocks


def rows_of_heads(blocks):
    per = blocks[0].shape[0]
    first = lax.broadcasted_iota(jnp.int32, (per, 2 * HEAD_DIM), 1) < HEAD_DIM
    columns = []
    for pair in range(HEADS // 2):
        left, right = blocks[2 * pair], blocks[2 * pair + 1]
        top = jnp.where(first, left, pltpu.roll(right, HEAD_DIM, 1))
        bottom = jnp.where(first, pltpu.roll(left, HEAD_DIM, 1), right)
        columns.append(jnp.concatenate([top, bottom], axis=0))
    return jnp.concatenate(columns, axis=1)


def whole_array(shape):
    return pl.BlockSpec(shape, lambda i: (0,) * len(shape))


class Part:
    def __init__(self, array, block, index):
        self.array, self.block, self.index = array, block, index

    def spec(self):
        def index(i, *numbers):
            return tuple(at(*numbers) if callable(at) else at for at in self.index)

        return pl.BlockSpec(self.block, index)


def vmem_call(kernel, shapes, smem, operands, scratch=(), cost=0, held=(), numbers=()):
    def whole(shape):
        return pl.BlockSpec(shape, lambda i, *numbers: (0,) * len(shape))

    return pl.pallas_call(
        kernel,
        grid_spec=pltpu.PrefetchScalarGridSpec(
            num_scalar_prefetch=len(numbers),
            grid=(1,),
            in_specs=[pl.BlockSpec(memory_space=pltpu.SMEM)] * len(smem)
            + [
                operand.spec() if isinstance(operand, Part) else whole(operand.shape)
                for operand in operands
            ]
            + [pl.BlockSpec(memory_space=pl.ANY)] * len(held),
            out_specs=[whole(shape) for shape, _ in shapes],
            scratch_shapes=list(scratch),
        ),
        out_shape=[jax.ShapeDtypeStruct(shape, dtype) for shape, dtype in shapes],
        compiler_params=pltpu.CompilerParams(vmem_limit_bytes=VMEM_LIMIT),
        cost_estimate=pl.CostEstimate(flops=cost, bytes_accessed=cost // 300, transcendentals=0),
    )(
        *numbers,
        *smem,
        *(operand.array if isinstance(operand, Part) else operand for operand in operands),
        *held,
    )


def fetch(pairs, semaphores):
    copies = [
        pltpu.make_async_copy(source, target, semaphores.at[number])
        for number, (source, target) in enumerate(pairs)
    ]
    for copy in copies:
        copy.start()
    return copies


def feed_rows(values, gains, biases, copies, weight_in, bias_in, weight_out, bias_out):
    normed, _ = normalize(values)
    hidden = low(scaled_norm(normed, gains, biases, 0))
    copies[0].wait()
    preact = matmul(hidden, weight_in[...]) + wide(bias_in[0:1, :])
    sigmoid = logistic(preact)
    active = low(preact * sigmoid)
    copies[1].wait()
    branch = matmul(active, weight_out[...]) + wide(bias_out[0:1, :])
    return values + 0.5 * branch, preact, sigmoid, active


def entry_kernel(
    utterances,
    frames,
    gains,
    biases,
    bias_in,
    bias_out,
    vectors,
    grads_head,
    grads_tail,
    feed_in,
    feed_out,
    attend_in,
    head_out,
    tail_out,
    after_out,
    slope_out,
    pack_out,
    sent_out,
    weight_in,
    weight_out,
    weight_attend,
    semaphores,
):
    copies = fetch(
        [
            (feed_in.at[0], weight_in),
            (feed_out.at[0], weight_out),
            (attend_in.at[pl.ds(0, 3)], weight_attend),
        ],
        semaphores,
    )
    per = frames.shape[0] // utterances
    for u in range(utterances):
        head_out[u, 0:HALO, :] = frames[u * per : u * per + HALO, :]
        head_out[u, HALO:, :] = grads_head[u]
        tail_out[u, 0:HALO, :] = frames[(u + 1) * per - HALO : (u + 1) * per, :]
        tail_out[u, HALO:, :] = grads_tail[u]
    units, features = slope_out.shape[1], frames.shape[1]
    pack_out[:, units : units + features] = low(scaled_norm(normalize(frames[...])[0], gains, biases, 0))
    after, preact, sigmoid, active = feed_rows(
        frames[...], gains, biases, copies, weight_in, bias_in, weight_out, bias_out
    )
    slope_out[...] = low(silu_slope(preact, sigmoid))
    pack_out[:, :units] = active
    after_out[...] = after
    normed, _ = normalize(after)
    hidden = low(scaled_norm(normed, gains, biases, 1))
    pack_out[:, units + features :] = hidden
    copies[2].wait()
    queries = matmul(hidden, weight_attend[0]) + wide(vectors[0:1, :])
    parts = (
        queries + wide(vectors[3:4, :]),
        matmul(hidden, weight_attend[1]),
        matmul(hidden, weight_attend[2]) + wide(vectors[1:2, :]),
    )
    lanes = 2 * HEAD_DIM
    for number, part in enumerate(parts):
        for head, block in enumerate(blocks_of_heads(part, utterances)):
            sent_out[head, :, number * lanes : (number + 1) * lanes] = low(block)


def sides_kernel(
    before,
    behind,
    gains,
    biases,
    bias_in,
    bias_out,
    feed_in,
    feed_out,
    after_out,
    grads_out,
    weight_in,
    weight_out,
    semaphores,
):
    copies = fetch([(feed_in.at[0], weight_in), (feed_out.at[0], weight_out)], semaphores)
    frames, grads = (
        jnp.concatenate(
            [
                source[u, first : first + HALO, :]
                for u in range(before.shape[0])
                for source in (before, behind)
            ],
            axis=0,
        )
        for first in (0, HALO)
    )
    grads_out[...] = grads
    after_out[...] = feed_rows(
        frames, gains, biases, copies, weight_in, bias_in, weight_out, bias_out
    )[0]


def mixer_kernel(
    utterances,
    info,
    blocks,
    after,
    after_sides,
    gains,
    biases,
    attend_out,
    vectors,
    mixer_in,
    mixer_bias,
    taps,
    mixer_vectors,
    after_out,
    pack_out,
    linear_out,
    gate_out,
    gated_out,
    convolved_out,
    sums_out,
    padded,
):
    per = after.shape[0] // utterances
    main, before, behind = [], [], []
    for head in range(HEADS):
        block = wide(blocks[head])
        main.append(block[:per])
        before.append(block[per : per + HALO])
        behind.append(block[per + HALO :])
    attended = rows_of_heads(main)
    features = after.shape[1]
    pack_out[:, :features] = low(attended)
    before, behind = rows_of_heads(before), rows_of_heads(behind)
    sides = []
    for u in range(utterances):
        sides += [before[u * HALO : (u + 1) * HALO], behind[u * HALO : (u + 1) * HALO]]
    attended = low(with_sides(attended, jnp.concatenate(sides, axis=0)))
    values = with_sides(after[...], after_sides[...])
    values = values + matmul(attended, attend_out[...]) + wide(vectors[2:3, :])
    after_out[...] = values
    normed, _ = normalize(values)
    scaled = scaled_norm(normed, gains, biases, 2)
    pack_out[:, features:] = low(own_rows(scaled, utterances))
    preact = matmul(low(scaled), mixer_in[...])
    preact = preact + wide(mixer_bias[...])
    rows = values.shape[0]
    linear = preact[:, :features]
    gate = logistic(preact[:, features:])
    linear_out[...] = own_rows(linear, utterances)
    gate_out[...] = own_rows(gate, utterances)
    place, limit = frame_places(info, rows, utterances, HALO)
    mask = flags((place >= 0) & (place < limit))
    gated = low(linear * gate * mask)
    gated_out[...] = gated
    fill_padded(padded, wide(gated), utterances)
    total = None
    for offset in range(KERNEL):
        term = wide(taps[offset : offset + 1, :]) * moved(
            padded, utterances, offset - KERNEL // 2, True
        )
        total = term if total is None else total + term
    convolved = total + wide(mixer_vectors[0:1, :])
    convolved_out[...] = convolved
    mask = own_rows(mask, utterances)
    convolved = own_rows(convolved, utterances)
    count = jnp.sum(mask, axis=0, keepdims=True)
    local_sum = jnp.sum(convolved * mask, axis=0, keepdims=True)
    centered = (convolved - local_sum / jnp.maximum(count, 1.0)) * mask
    share(sums_out, local_sum, jnp.sum(centered * centered, axis=0, keepdims=True))


def fill_padded(padded, values, utterances):
    own = values.shape[0] - 2 * utterances * HALO
    per = own // utterances
    zeros = jnp.zeros((HALO, values.shape[1]), jnp.float32)
    for u in range(utterances):
        aside = own + 2 * u * HALO
        padded[u, 0:HALO, :] = zeros
        padded[u, HALO : 2 * HALO, :] = values[aside : aside + HALO, :]
        padded[u, 2 * HALO : 2 * HALO + per, :] = values[u * per : (u + 1) * per, :]
        padded[u, 2 * HALO + per : 3 * HALO + per, :] = values[aside + HALO : aside + 2 * HALO, :]
        padded[u, 3 * HALO + per :, :] = zeros


def moved(padded, utterances, start, sides=False):
    per = padded.shape[1] - 4 * HALO
    pieces = [(u, 2 * HALO, per) for u in range(utterances)]
    if sides:
        for u in range(utterances):
            pieces += [(u, HALO, HALO), (u, 2 * HALO + per, HALO)]
    return jnp.concatenate(
        [padded[u, first + start : first + start + height, :] for u, first, height in pieces],
        axis=0,
    )


def share(sums_out, *rows):
    tile = jnp.concatenate(
        [row[:, i : i + 128] for row in rows for i in range(0, row.shape[1], 128)], axis=0
    )
    for copy in range(sums_out.shape[0] // 8):
        sums_out[copy * 8 : copy * 8 + 8, :] = tile


def as_row(tile):
    return jnp.concatenate([tile[i : i + 1] for i in range(tile.shape[0])], axis=1)


def frame_counts(limits, utt_index, shape, utterances, seq_count, per):
    place = lax.broadcasted_iota(jnp.int32, shape, 0)
    owner, first = (place // seq_count) ^ utt_index, place % seq_count * per
    total = jnp.zeros(shape, jnp.int32)
    for number in range(limits.shape[0]):
        inside = jnp.clip(limits[number] - first, 0, per)
        total = total + jnp.where(owner == number // utterances, inside, 0)
    return total.astype(jnp.float32)


def middle_kernel(
    utterances,
    seq_count,
    limits,
    utt_index,
    convolved,
    shared,
    after,
    grads,
    grad_sides,
    gains,
    biases,
    batch_gain,
    batch_shift,
    running_mean,
    running_variance,
    mixer_out,
    vectors,
    bias_in,
    bias_out,
    feed_in,
    feed_out,
    layer_out,
    grad_mixer_out,
    grad_batch_out,
    normed_out,
    pack_out,
    sums_out,
    batch_out_rows,
    vector_out,
    weight_in,
    weight_out,
    semaphores,
):
    def own(values):
        return own_rows(values, utterances)

    features, units = feed_in.shape[1:]

    def pack(number, rows):
        first = 2 * units + number * features
        pack_out[:, first : first + features] = rows

    copies = fetch([(feed_in.at[1], weight_in), (feed_out.at[1], weight_out)], semaphores)
    parts = shared[...].reshape(-1, 8, 128)
    per = grads.shape[0] // utterances
    counts = frame_counts(limits, utt_index[0], parts.shape, utterances, seq_count, per)
    totals = jnp.sum(parts, axis=0)
    valid_tile = jnp.sum(counts, axis=0)
    valid = as_row(valid_tile[:4])
    average_tile = totals / valid_tile
    drift = parts / jnp.maximum(counts, 1.0) - average_tile
    spreads = jnp.sum(counts * drift * drift, axis=0)
    average = as_row(average_tile[:4])
    variance = as_row((totals[4:] + spreads[:4]) / valid_tile[:4])
    inverse_batch = lax.rsqrt(variance + EPSILON)
    batch_out_rows[0:1, :] = inverse_batch
    batch_out_rows[1:2, :] = valid
    batch_out_rows[2:3, :] = 0.9 * running_mean[...] + 0.1 * average
    batch_out_rows[3:4, :] = 0.9 * running_variance[...] + 0.1 * variance * valid / (valid - 1.0)
    normed_batch = (convolved[...] - average) * inverse_batch
    normed_out[...] = normed_batch
    batch = normed_batch * wide(batch_gain[...]) + wide(batch_shift[...])
    batch_sigmoid = logistic(batch)
    swished = low(batch * batch_sigmoid)
    pack(2, own(swished))
    values = after[...] + matmul(swished, mixer_out[...]) + wide(vectors[1:2, :])
    normed, inverse = normalize(values)
    scaled = scaled_norm(normed, gains, biases, 3)
    hidden = low(scaled)
    pack(0, own(hidden))
    copies[0].wait()
    preact = matmul(hidden, weight_in[...]) + wide(bias_in[1:2, :])
    sigmoid = logistic(preact)
    active = low(preact * sigmoid)
    pack_out[:, units : 2 * units] = own(active)
    copies[1].wait()
    branch = matmul(active, weight_out[...]) + wide(bias_out[1:2, :])
    normed_last, inverse_last = normalize(values + 0.5 * branch)
    layer_out[...] = own(scaled_norm(normed_last, gains, biases, 4))
    grad_second, gain_last, shift_last = norm_back(
        with_sides(grads[...], grad_sides[...]),
        normed_last,
        inverse_last,
        gains,
        4,
        own,
    )
    grad_low = low(0.5 * grad_second)
    grad_low_own = own(grad_low)
    pack(1, grad_low_own)
    grad_pre = low(rows_dot(grad_low, weight_out[...]) * silu_slope(preact, sigmoid))
    grad_pre_own = own(grad_pre)
    pack_out[:, :units] = grad_pre_own
    grad_values, gain_three, shift_three = norm_back(
        rows_dot(grad_pre, weight_in[...]), normed, inverse, gains, 3, own
    )
    grad_mixer = grad_second + grad_values
    grad_mixer_own = own(grad_mixer)
    grad_mixer_out[...] = grad_mixer_own
    branch_own = low(grad_mixer_own)
    pack(3, branch_own)
    grad_batch = rows_dot(low(grad_mixer), mixer_out[...]) * silu_slope(batch, batch_sigmoid)
    grad_batch_out[...] = grad_batch
    share(sums_out, column_sum(own(grad_batch)), column_sum(own(grad_batch * normed_batch)))
    bias_sum = column_sum(grad_pre_own)
    put_rows(
        vector_out,
        [gain_last, shift_last, gain_three, shift_three]
        + [bias_sum[:, i : i + features] for i in range(0, bias_sum.shape[1], features)]
        + [column_sum(grad_low_own), column_sum(branch_own)],
    )


def put_rows(out, rows):
    for number, row in enumerate(rows):
        out[number : number + 1, :] = row
    out[len(rows) :, :] = jnp.zeros((out.shape[0] - len(rows), out.shape[1]), jnp.float32)


def mixer_back_kernel(
    utterances,
    info,
    grad_batch,
    normed_batch,
    shared,
    batch_rows,
    batch_gain,
    gated,
    linear,
    gate,
    grad_mixer,
    after,
    gains,
    taps,
    mixer_in,
    attend_out,
    batch_grads_out,
    grad_attend_out,
    pack_out,
    sent_out,
    vector_out,
    padded,
    gated_padded,
):
    totals = jnp.sum(shared[...].reshape(-1, 8, 128), axis=0)
    shift_grad, gain_grad = as_row(totals[:4]), as_row(totals[4:])
    batch_grads_out[0:1, :] = shift_grad
    batch_grads_out[1:2, :] = gain_grad
    rows, features = grad_batch.shape
    place, limit = frame_places(info, rows, utterances, HALO)
    mask = flags((place >= 0) & (place < limit))
    inside = flags((place >= 0) & (place < info[utterances + 1]))
    inverse_batch, valid = batch_rows[0:1, :], batch_rows[1:2, :]
    grad_conv = low(
        inside
        * wide(batch_gain[...])
        * inverse_batch
        * (grad_batch[...] - mask / valid * (shift_grad + normed_batch[...] * gain_grad))
    )
    conv_wide = wide(grad_conv)
    fill_padded(padded, conv_wide, utterances)
    fill_padded(gated_padded, wide(gated[...]), utterances)
    conv_own = own_rows(conv_wide, utterances)
    margin = KERNEL // 2
    total = None
    tap_rows = []
    for offset in range(KERNEL):
        term = wide(taps[offset : offset + 1, :]) * moved(padded, utterances, margin - offset)
        total = term if total is None else total + term
        near = moved(gated_padded, utterances, offset - margin)
        tap_rows.append(jnp.sum(conv_own * near, axis=0, keepdims=True))
    grad_gated = own_rows(mask, utterances) * total
    gate_half = gate[...]
    grad_pre = low(
        jnp.concatenate(
            [
                grad_gated * gate_half,
                grad_gated * linear[...] * gate_half * (1.0 - gate_half),
            ],
            axis=1,
        )
    )
    pack_out[:, : 2 * features] = grad_pre
    normed, inverse = normalize(own_rows(after[...], utterances))
    grad_values, gain_two, shift_two = norm_back(
        rows_dot(grad_pre, mixer_in[...]), normed, inverse, gains, 2
    )
    grad_attend = grad_mixer[...] + grad_values
    grad_attend_out[...] = grad_attend
    branch = low(grad_attend)
    pack_out[:, 2 * features :] = branch
    grad_attended = rows_dot(branch, attend_out[...])
    for head, block in enumerate(blocks_of_heads(grad_attended, utterances)):
        sent_out[head] = low(block)
    bias_sum = column_sum(grad_pre)
    put_rows(
        vector_out,
        [gain_two, shift_two, column_sum(conv_own), column_sum(branch)]
        + [bias_sum[:, :features], bias_sum[:, features:]]
        + tap_rows,
    )


def entry_back_kernel(
    core,
    returned,
    grad_attend,
    frames,
    after,
    slope,
    gains,
    feed_in,
    feed_out,
    attend_in,
    frames_out,
    pack_out,
    grad_pre_out,
    vector_out,
    weight_in,
    weight_out,
    weight_attend,
    semaphores,
):
    copies = fetch(
        [
            (attend_in.at[pl.ds(0, 3)], weight_attend),
            (feed_out.at[0], weight_out),
            (feed_in.at[0], weight_in),
        ],
        semaphores,
    )
    lanes = 2 * HEAD_DIM
    features, units = feed_in.shape[1:]

    def pack(number, rows):
        first = units // 2 + number * features
        pack_out[:, first : first + features] = rows

    grad_hidden = None
    low_rows = []
    for number in range(3):
        rows = low(
            rows_of_heads(
                [
                    wide(returned[head, :, number * lanes : (number + 1) * lanes])
                    for head in range(HEADS)
                ]
            )
        )
        pack(number, rows)
        low_rows.append(rows)
        if number == 0:
            copies[0].wait()
        term = rows_dot(rows, weight_attend[number])
        grad_hidden = term if grad_hidden is None else grad_hidden + term
    normed, inverse = normalize(after[...])
    grad_values, gain_one, shift_one = norm_back(grad_hidden, normed, inverse, gains, 1)
    grad_first = grad_attend[...] + grad_values
    grad_low = low(0.5 * grad_first)
    pack(3, grad_low)
    copies[1].wait()
    grad_pre = low(rows_dot(grad_low, weight_out[...]) * wide(slope[...]))
    for half in range(2):
        rows = grad_pre[:, half * units // 2 : (half + 1) * units // 2]

        @pl.when(core[0] == half)
        def _():
            grad_pre_out[...] = rows

        @pl.when(core[0] != half)
        def _():
            pack_out[:, : units // 2] = rows

    normed, inverse = normalize(frames[...])
    copies[2].wait()
    grad_values, gain_zero, shift_zero = norm_back(
        rows_dot(grad_pre, weight_in[...]), normed, inverse, gains, 0
    )
    frames_out[...] = grad_first + grad_values
    bias_sum = column_sum(grad_pre)
    put_rows(
        vector_out,
        [gain_zero, shift_zero, gain_one, shift_one]
        + [bias_sum[:, i : i + features] for i in range(0, bias_sum.shape[1], features)]
        + [column_sum(grad_low), column_sum(low_rows[0]), column_sum(low_rows[2])],
    )


def vectors_kernel(
    rows, gain_out, bias_out, in_bias_out, out_bias_out, attend_out, mixer_bias_out, mixer_out, taps_out
):
    middle, mixer, entry, heads = (0, 16, 32, 48)
    features = gain_out.shape[1]

    def take(out, target, start):
        out[target : target + 1, :] = rows[start : start + 1, :]

    for out, first in ((gain_out, 0), (bias_out, 1)):
        take(out, 0, entry + first)
        take(out, 1, entry + 2 + first)
        take(out, 2, mixer + first)
        take(out, 3, middle + 2 + first)
        take(out, 4, middle + first)
    for target, start in ((0, entry + 4), (1, middle + 4)):
        for column in range(4):
            in_bias_out[target : target + 1, column * features : (column + 1) * features] = rows[
                start + column : start + column + 1, :
            ]
    take(out_bias_out, 0, entry + 8)
    take(out_bias_out, 1, middle + 8)
    for target, start in enumerate((entry + 9, entry + 10, mixer + 3, heads, heads + 1)):
        take(attend_out, target, start)
    for column in range(2):
        mixer_bias_out[0:1, column * features : (column + 1) * features] = rows[
            mixer + 4 + column : mixer + 5 + column, :
        ]
    take(mixer_out, 0, mixer + 2)
    take(mixer_out, 1, middle + 9)
    taps_out[...] = rows[mixer + 6 : mixer + 6 + KERNEL, :]


def axis_bits(axis):
    return [(axis, 1 << bit) for bit in range(lax.axis_size(axis).bit_length() - 1)]


def swap(values, step):
    axis, mask = step
    return lax.ppermute(values, axis, [(i, i ^ mask) for i in range(lax.axis_size(axis))])


def side(step):
    axis, mask = step
    return (lax.axis_index(axis) // mask) % 2


def swap_all(stripes, steps):
    return [swap(rows, step) for rows, step in zip(stripes, steps)]


def add_low(first_operand, second_operand):
    total = first_operand.astype(jnp.float32) + second_operand.astype(jnp.float32)
    return total.astype(jnp.bfloat16)


def fold_kernel(stripes, arrays, parts, sides, *refs):
    for number in range(stripes):
        sources = refs[2 * arrays * number : 2 * arrays * (number + 1)]
        for keeping in range(2):
            place = sides[number] if keeping else 1 - sides[number]
            out = refs[2 * arrays * stripes + 2 * number + keeping]
            first = 0
            for array in range(arrays):
                own, other = sources[2 * array : 2 * array + 2]
                height = own.shape[0] // (2 * parts)
                for part in range(parts):
                    start = pl.multiple_of((2 * part + place) * height, 16)
                    rows = pl.ds(start, height)
                    out[first : first + height, :] = add_low(own[rows, :], other[rows, :])
                    first += height


def fold_rows(pairs, steps, parts=1, limit=SUM_LIMIT):
    operands = list(zip(*(rows for pair in pairs for rows in pair)))
    heights = [sum(rows.shape[0] for rows in four[::2]) // 2 for four in operands]
    if any(rows.shape[0] // parts % 32 for four in operands for rows in four):
        sent, kept = [], []
        for four, step in zip(operands, steps):
            sums = [add_low(*four[i : i + 2]) for i in range(0, len(four), 2)]
            for place, results in ((1 - side(step), sent), (side(step), kept)):
                pieces = []
                for rows in sums:
                    height = rows.shape[0] // (2 * parts)
                    pieces += [
                        lax.dynamic_slice_in_dim(rows, (2 * part + place) * height, height, 0)
                        for part in range(parts)
                    ]
                results.append(jnp.concatenate(pieces, axis=0))
        return sent, kept

    def whole(rows):
        return pl.BlockSpec((rows, 512), lambda i, sides: (0, 0))

    outs = [height for height in heights for _ in range(2)]
    results = pl.pallas_call(
        functools.partial(fold_kernel, len(steps), len(pairs), parts),
        grid_spec=pltpu.PrefetchScalarGridSpec(
            num_scalar_prefetch=1,
            grid=(1,),
            in_specs=[whole(rows.shape[0]) for four in operands for rows in four],
            out_specs=[whole(height) for height in outs],
        ),
        out_shape=[jax.ShapeDtypeStruct((height, 512), jnp.bfloat16) for height in outs],
        compiler_params=pltpu.CompilerParams(vmem_limit_bytes=limit),
        cost_estimate=pl.CostEstimate(
            flops=0, bytes_accessed=6 * 1024 * sum(outs), transcendentals=0
        ),
    )(jnp.stack([side(step) for step in steps]), *(rows for four in operands for rows in four))
    return list(results[::2]), list(results[1::2])


def add_kernel(stripes, *refs):
    for number in range(stripes):
        refs[2 * stripes + number][...] = add_low(refs[2 * number][...], refs[2 * number + 1][...])


def add_rows(kept, arrived):
    if any(rows.shape[0] % 16 for rows in kept):
        return [add_low(*pair) for pair in zip(kept, arrived)]
    specs = [whole_array(rows.shape) for rows in kept]
    return list(
        pl.pallas_call(
            functools.partial(add_kernel, len(kept)),
            grid=(1,),
            in_specs=[spec for spec in specs for _ in range(2)],
            out_specs=specs,
            out_shape=[jax.ShapeDtypeStruct(rows.shape, rows.dtype) for rows in kept],
            compiler_params=pltpu.CompilerParams(vmem_limit_bytes=SUM_LIMIT),
        )(*(rows for pair in zip(kept, arrived) for rows in pair))
    )


def join_kernel(stripes, sides, *refs):
    for number in range(stripes):
        own, other, out = refs[2 * number], refs[2 * number + 1], refs[2 * stripes + number]
        height = own.shape[0] // 2
        for part in range(2):
            for source, place in ((own, sides[number]), (other, 1 - sides[number])):
                start = pl.multiple_of((2 * part + place) * height, 16)
                out[pl.ds(start, height), :] = source[part * height : (part + 1) * height, :]


def join_rows(stripes, arrived, steps):
    heights = [rows.shape[0] // 2 for rows in stripes]
    if any(height % 16 for height in heights):
        joined = []
        for rows, other, step, height in zip(stripes, arrived, steps, heights):
            first = side(step) == 0
            low_rows, high_rows = jnp.where(first, rows, other), jnp.where(first, other, rows)
            joined.append(
                jnp.concatenate(
                    [
                        half[part]
                        for part in (slice(0, height), slice(height, None))
                        for half in (low_rows, high_rows)
                    ],
                    axis=0,
                )
            )
        return joined

    def whole(height):
        return pl.BlockSpec((height, 512), lambda i, sides: (0, 0))

    return list(
        pl.pallas_call(
            functools.partial(join_kernel, len(stripes)),
            grid_spec=pltpu.PrefetchScalarGridSpec(
                num_scalar_prefetch=1,
                grid=(1,),
                in_specs=[whole(2 * height) for height in heights for _ in range(2)],
                out_specs=[whole(4 * height) for height in heights],
            ),
            out_shape=[jax.ShapeDtypeStruct((4 * height, 512), jnp.bfloat16) for height in heights],
            compiler_params=pltpu.CompilerParams(vmem_limit_bytes=SUM_LIMIT),
            cost_estimate=pl.CostEstimate(
                flops=0, bytes_accessed=8 * 1024 * sum(heights), transcendentals=0
            ),
        )(
            jnp.stack([side(step) for step in steps]),
            *(rows for pair in zip(stripes, arrived) for rows in pair),
        )
    )


def tie(*groups):
    return lax.optimization_barrier(groups)


def step_orders():
    utt, seq = axis_bits("utt"), axis_bits("seq")
    across, line, rest = utt[1:], seq[:1], seq[1:]
    return (
        line + across + rest,
        across + rest + line,
        rest[:1] + line + across + rest[1:],
    )


def all_shared(copies):
    return lax.all_to_all(copies, ("utt", "seq"), 0, 0, tiled=True)


def from_neighbours(head, tail):
    count = lax.axis_size("seq")
    before = lax.ppermute(tail, "seq", [(i, i + 1) for i in range(count - 1)])
    behind = lax.ppermute(head, "seq", [(i + 1, i) for i in range(count - 1)])
    return before, behind


def pair_rows(mine, theirs, start=0, width=None):
    columns = slice(start, start + (width or mine.shape[1]))
    return jnp.concatenate([mine[:, columns], theirs[:, columns]], axis=0)


def outer(left, right):
    return low(matmul(left.T, right))


def put_half(outs, side_number, half, value):
    @pl.when(side_number == half)
    def _():
        outs[1][...] = value

    @pl.when(side_number != half)
    def _():
        outs[0][...] = value


def feed_blocks(refs, outs, sides):
    hidden, grad_pre, active, grad_low = (refs[2 * i : 2 * i + 2] for i in range(4))
    hidden_cols = pair_rows(*hidden).T
    grad_rows = pair_rows(*grad_low)
    for half in range(2):
        block = low(matmul(hidden_cols, pair_rows(*grad_pre, 512 * half, 512)))
        put_half(outs[:2], sides[1], half, block)
        block = outer(pair_rows(*active, 512 * half, 512), grad_rows)
        put_half(outs[2:4], sides[2], half, block)


def second_kernel(places, *refs):
    feed_blocks(refs[:8], refs[8:], places)


def mixer_blocks_kernel(places, *refs):
    refs, outs = refs[:12], refs[12:]
    mixer = outer(pair_rows(*refs[:2]), pair_rows(*refs[2:4]))
    branch = outer(pair_rows(*refs[4:6]), pair_rows(*refs[6:8]))
    attend = outer(pair_rows(*refs[8:10]), pair_rows(*refs[10:12]))
    for half in range(2):
        pieces = (
            mixer[256 * half : 256 * half + 256],
            branch[128 * half : 128 * half + 128],
            attend[128 * half : 128 * half + 128],
        )
        put_half(outs, places[3], half, jnp.concatenate(pieces, axis=0))


def turn_kernel(places, *refs):
    for number in range(3):
        mine, theirs, out = refs[2 * number], refs[2 * number + 1], refs[8 + number]
        rows = mine.shape[0]
        out[:, :rows] = mine[...].T
        out[:, rows:] = theirs[...].T
    refs[11][...] = add_low(refs[6][...], refs[7][...])


def late_kernel(
    keeping,
    places,
    hidden_cols,
    grad_pre,
    grad_pre_other,
    active_cols,
    grad_low,
    grad_low_other,
    attend_cols,
    attend_rows,
    attend_rows_other,
    position,
    *outs,
):
    step = pl.program_id(0)
    half = places[3] if keeping else 1 - places[3]

    def blocks(left, mine, theirs):
        return low(matmul(left[...], jnp.concatenate([mine[...], theirs[...]], axis=0)))

    @pl.when(step == 0)
    def _():
        outs[0][...] = blocks(hidden_cols, grad_pre, grad_pre_other)

    @pl.when(step == 1)
    def _():
        outs[1][...] = blocks(active_cols, grad_low, grad_low_other)

    @pl.when((step == 2) & (places[0] + half < 2))
    def _():
        outs[2][...] = blocks(attend_cols, attend_rows, attend_rows_other)

    @pl.when((step == 2) & (places[0] + half == 2))
    def _():
        outs[2][...] = position[...]


def late_blocks(keeping, places, cols, grad_pre, pair):
    hidden_cols, active_cols, attend_cols, position = cols
    rows = pair[0].shape[0]

    def half(p, stripe):
        return p[stripe] if keeping else 1 - p[stripe]

    def whole(shape):
        return pl.BlockSpec(shape, lambda i, p: (0, 0))

    def attend_column(i, p):
        return (0, jnp.where(p[0] == 0, 2 + half(p, 3), 4))

    block = (rows, 512)
    return list(
        pl.pallas_call(
            functools.partial(late_kernel, keeping),
            grid_spec=pltpu.PrefetchScalarGridSpec(
                num_scalar_prefetch=1,
                grid=(3,),
                in_specs=[
                    whole(hidden_cols.shape),
                    pl.BlockSpec(block, lambda i, p: (0, half(p, 1))),
                    pl.BlockSpec(block, lambda i, p: (0, half(p, 1))),
                    pl.BlockSpec((512, 2 * rows), lambda i, p: (half(p, 2), 0)),
                    pl.BlockSpec(block, lambda i, p: (0, 5)),
                    pl.BlockSpec(block, lambda i, p: (0, 5)),
                    whole(attend_cols.shape),
                    pl.BlockSpec(block, attend_column),
                    pl.BlockSpec(block, attend_column),
                    whole(position.shape),
                ],
                out_specs=[whole((512, 512))] * 3,
            ),
            out_shape=[jax.ShapeDtypeStruct((512, 512), jnp.bfloat16)] * 3,
            compiler_params=pltpu.CompilerParams(vmem_limit_bytes=SUM_LIMIT if keeping else VMEM_LIMIT),
            cost_estimate=pl.CostEstimate(
                flops=6 * 512 * 512 * 2 * rows, bytes_accessed=6 * 10**6, transcendentals=0
            ),
        )(
            places,
            hidden_cols,
            grad_pre,
            pair[1],
            active_cols,
            *pair,
            attend_cols,
            *pair,
            position,
        )
    )


def columns(pair, width, number, by_core=False):
    index = (lambda numbers: number + numbers[0]) if by_core else number
    return [Part(array, (array.shape[0], width), (0, index)) for array in pair]


def block_sums(kernel, places, stripes, operands):
    blocks = vmem_call(
        kernel,
        [((512, 512), jnp.bfloat16)] * (2 * stripes),
        (),
        [part for pair in operands for part in pair],
        cost=7 * 10**8 * stripes,
        numbers=(places,),
    )
    return blocks[::2], blocks[1::2]


def spread_kernel(places, first, second, third, *refs):
    feed_in, feed_out, mixer_in, mixer_out, attend_out, attend_in = refs[-14:-8]
    held, wide_rows = refs[-8:-5], refs[-5:-2]
    arrive, leave = refs[-2:]
    core, half = places[0], places[3]
    quarters = [pl.multiple_of(512 * (2 * core + places[1 + i]), 512) for i in range(3)]
    coming = []
    for part in range(2):
        for number, source in enumerate((first, second, third)):
            rows = pl.ds(512 * part, 512)
            coming.append(
                pltpu.make_async_copy(
                    source.at[rows], held[number].at[rows], arrive.at[3 * part + number]
                )
            )
    for copy in coming:
        copy.start()
    going = []
    for part in range(2):
        for number in range(3):
            coming[3 * part + number].wait()
            rows = pl.ds(512 * part, 512)
            wide_rows[number][rows, :] = wide(held[number][rows, :])
            layer = 1 - part
            if number == 0:
                targets = [(512, feed_in.at[layer, :, pl.ds(quarters[0], 512)])]
            elif number == 1:
                targets = [(512, feed_out.at[layer, pl.ds(quarters[1], 512)])]
            elif part == 1:
                targets = [(512, attend_in.at[2 * core + half])]
            else:
                tall = pl.ds(pl.multiple_of(256 * half, 256), 256)
                flat = pl.ds(pl.multiple_of(128 * (2 * core + half), 128), 128)
                side_columns = pl.ds(pl.multiple_of(512 * core, 512), 512)
                targets = [
                    (256, mixer_in.at[tall, side_columns]),
                    (128, mixer_out.at[flat]),
                    (128, attend_out.at[flat]),
                ]
            start = 512 * part
            for height, target in targets:
                copy = pltpu.make_async_copy(
                    wide_rows[number].at[pl.ds(start, height)], target, leave.at[len(going)]
                )
                copy.start()
                going.append(copy)
                start += height
    for copy in going:
        copy.wait()


def spread_blocks(places, stripes, shapes, bases):
    anywhere = pl.BlockSpec(memory_space=pl.ANY)
    return list(
        pl.pallas_call(
            spread_kernel,
            in_specs=[pl.BlockSpec(memory_space=pltpu.SMEM)] + [anywhere] * (3 + len(bases)),
            out_specs=[anywhere] * len(shapes),
            out_shape=[jax.ShapeDtypeStruct(shape, jnp.float32) for shape in shapes],
            scratch_shapes=[pltpu.VMEM((1024, 512), jnp.bfloat16)] * 3
            + [pltpu.VMEM((1024, 512), jnp.float32)] * 3
            + [pltpu.SemaphoreType.DMA((6,)), pltpu.SemaphoreType.DMA((8,))],
            input_output_aliases={4 + n: n for n in range(len(bases))},
            compiler_params=pltpu.CompilerParams(vmem_limit_bytes=VMEM_LIMIT),
            cost_estimate=pl.CostEstimate(
                flops=1024, bytes_accessed=1024, transcendentals=0
            ),
        )(places, *stripes, *bases)
    )


def angle_tables(frame_count, features):
    halves = jnp.arange(features // 2, dtype=jnp.int32).astype(jnp.float32)
    frequencies = jnp.exp(halves * (-2.0 * math.log(10000.0) / features))
    fine = 32
    low_angles = jnp.arange(fine, dtype=jnp.int32).astype(jnp.float32)[:, None] * frequencies
    high_angles = (fine * jnp.arange(frame_count // fine, dtype=jnp.int32)).astype(jnp.float32)[
        :, None
    ] * frequencies
    low_sin, low_cos = jnp.sin(low_angles)[None], jnp.cos(low_angles)[None]
    high_sin, high_cos = jnp.sin(high_angles)[:, None], jnp.cos(high_angles)[:, None]
    sines = high_sin * low_cos + high_cos * low_sin
    cosines = high_cos * low_cos - high_sin * low_sin
    shape = (frame_count, features // 2)
    return sines.reshape(shape), cosines.reshape(shape)


def heads_out(blocks, groups):
    return lax.all_to_all(jnp.tile(blocks, (groups, 1, 1)), "seq", 0, 0, tiled=True)


def rows_dot(first_operand, second_operand):
    return lax.dot_general(
        first_operand, second_operand, (((1,), (1,)), ((), ())), preferred_element_type=jnp.float32
    )


def lane_side(shape, utterance):
    return (lax.broadcasted_iota(jnp.int32, shape, 1) // HEAD_DIM) == utterance


def turned_queries(content, shift, weight, sines, cosines):
    offset = (content.astype(jnp.float32) + shift).astype(jnp.bfloat16)
    half = sines.shape[1]
    spread = jnp.dot(offset, weight, preferred_element_type=jnp.float32)
    sin_part, cos_part = spread[:, :half], spread[:, half:]
    return (
        offset,
        (sin_part * sines + cos_part * cosines).astype(jnp.bfloat16),
        (cos_part * sines - sin_part * cosines).astype(jnp.bfloat16),
    )


def attend_kernel(
    limits,
    content,
    keys,
    values,
    shift,
    weight,
    sines,
    cosines,
    table,
    weights_out,
    attended_out,
    held,
    scores,
):
    scale = HEAD_DIM ** (-0.5)
    weight_rows = jnp.concatenate([weight[...]] * limits.shape[0], axis=0)
    content_rows = content[...]
    key_side = jnp.concatenate([table[...], keys[...]], axis=1)
    places = lax.broadcasted_iota(jnp.int32, (1, table.shape[0]), 1)
    attended = None
    for utterance in range(limits.shape[0]):
        ours = lane_side(content_rows.shape, utterance)
        mine = jnp.where(ours, content_rows, jnp.zeros_like(content_rows))
        moved = jnp.where(ours, shift[...], 0.0)
        _, turned_cos, turned_sin = turned_queries(
            mine, moved, weight_rows, sines[...], cosines[...]
        )
        query_side = jnp.concatenate([turned_cos, turned_sin, mine], axis=1) * scale
        scores[utterance] = rows_dot(query_side.astype(jnp.bfloat16), key_side)
    for utterance in range(limits.shape[0]):
        allowed = places < limits[utterance]
        for start in range(0, scores.shape[1], ROW_TILE):
            rows = slice(start, start + ROW_TILE)
            tile = jnp.where(allowed, scores[utterance, rows, :], -1000000000.0)
            raised = jnp.exp(tile - jnp.max(tile, axis=1, keepdims=True))
            totals = jnp.sum(raised, axis=1, keepdims=True)
            weights_out[utterance, rows, :] = low(raised * (1.0 / totals))
    for utterance in range(limits.shape[0]):
        ours = lane_side(content_rows.shape, utterance)
        part = matmul(weights_out[utterance], values[...])
        attended = part if attended is None else jnp.where(ours, part, attended)
    if held is None:
        attended_out[...] = attended.astype(jnp.bfloat16)
        return
    step = pl.program_id(0)
    height = attended.shape[0]
    block = attended_out.shape[1] - 2 * HALO
    held[pl.ds(pl.multiple_of(HALO + step * height, 8), height), :] = attended
    for number in range(height // block):
        attended_out[step * (height // block) + number, 0:block, :] = attended[
            number * block : (number + 1) * block
        ].astype(jnp.bfloat16)

    @pl.when(step == pl.num_programs(0) - 1)
    def _():
        edge = jnp.zeros((HALO, held.shape[1]), jnp.float32)
        held[0:HALO, :] = edge
        held[held.shape[0] - HALO :, :] = edge
        for number in range(attended_out.shape[0]):
            start = number * block
            sides = jnp.concatenate(
                [
                    held[start : start + HALO, :],
                    held[start + HALO + block : start + 2 * HALO + block, :],
                ],
                axis=0,
            )
            attended_out[number, block:, :] = sides.astype(jnp.bfloat16)


def attend_back_kernel(
    weights,
    content,
    grads,
    keys,
    values,
    shift,
    weight,
    sines,
    cosines,
    table,
    *outs,
):
    step = pl.program_id(0)
    *outs, grad_probs, grad_scores = outs
    query_out, pairs_out, weight_out, sums_out, key_sums, value_sums = (
        [None] * (6 - len(outs)) + outs
    )
    scale = HEAD_DIM ** (-0.5)

    @pl.when(step == 0)
    def _():
        key_sums[...] = jnp.zeros_like(key_sums)
        value_sums[...] = jnp.zeros_like(value_sums)
        weight_out[...] = jnp.zeros_like(weight_out)
        sums_out[...] = jnp.zeros_like(sums_out)

    weight_rows = jnp.concatenate([weight[...]] * weights.shape[0], axis=0)
    content_rows, grad_rows = content[...], grads[...]
    content_cols = content_rows.T
    grad_cols = grad_rows.T
    key_side = jnp.concatenate([table[...], keys[...]], axis=1)
    half = sines.shape[1]
    grad_content = grad_position = None
    for utterance in range(weights.shape[0]):
        ours = lane_side(content_rows.shape, utterance)
        grad_mine = jnp.where(ours, grad_rows, jnp.zeros_like(grad_rows)) * scale
        grad_probs[utterance] = rows_dot(grad_mine.astype(jnp.bfloat16), values[...])
    for utterance in range(weights.shape[0]):
        first, last = utterance * HEAD_DIM, (utterance + 1) * HEAD_DIM
        ours = lane_side(content_rows.shape, utterance)
        probs = weights[utterance]
        for start in range(0, grad_probs.shape[1], ROW_TILE):
            rows = slice(start, start + ROW_TILE)
            tile = wide(weights[utterance, rows, :])
            product = tile * grad_probs[utterance, rows, :]
            inner = jnp.sum(product, axis=1, keepdims=True)
            grad_scores[utterance, rows, :] = low(product - tile * inner)
        value_sums[first:last, :] += jnp.dot(
            grad_cols[first:last, :], probs, preferred_element_type=jnp.float32
        )
        key_sums[first:last, :] += jnp.dot(
            content_cols[first:last, :], grad_scores[utterance], preferred_element_type=jnp.float32
        )
        grad_side = matmul(grad_scores[utterance], key_side)
        grad_cos_table = grad_side[:, :half]
        grad_sin_table = grad_side[:, half : 2 * half]
        from_table = jnp.concatenate(
            [
                grad_cos_table * sines[...] - grad_sin_table * cosines[...],
                grad_cos_table * cosines[...] + grad_sin_table * sines[...],
            ],
            axis=1,
        ).astype(jnp.bfloat16)
        offset = (content_rows.astype(jnp.float32) + shift[...]).astype(jnp.bfloat16)
        weight_out[...] += jnp.dot(
            offset.T[first:last, :], from_table, preferred_element_type=jnp.float32
        )
        content_part = grad_side[:, 2 * half :]
        position_part = rows_dot(from_table, weight_rows)
        if grad_content is None:
            grad_content, grad_position = content_part, position_part
        else:
            grad_content = jnp.where(ours, content_part, grad_content)
            grad_position = jnp.where(ours, position_part, grad_position)
    grad_query = (grad_content + grad_position).astype(jnp.bfloat16)
    height, lanes = grad_query.shape
    if query_out is None:
        pairs_out[pl.ds(pl.multiple_of(step * height, 16), height), 0:lanes] = grad_query
    else:
        query_out[...] = grad_query
    sums_out[0:1, :] += jnp.sum(grad_content, axis=0, keepdims=True)
    sums_out[1:2, :] += jnp.sum(grad_position, axis=0, keepdims=True)

    @pl.when(step == pl.num_programs(0) - 1)
    def _():
        first = pairs_out.shape[1] - 2 * lanes
        pairs_out[:, first : first + lanes] = key_sums[...].T.astype(jnp.bfloat16)
        pairs_out[:, first + lanes :] = value_sums[...].T.astype(jnp.bfloat16)


def query_block(frames_all, most=256):
    return most if frames_all <= 1024 else 128


def whole_block(shape):
    return pl.BlockSpec(shape, lambda i: (0,) * len(shape))


def row_block(height, width):
    return pl.BlockSpec((height, width), lambda i: (i, 0))


def attend_heads(limits, content, arrived, shift, weight, sines, cosines, table, block):
    utterances = limits.shape[0]
    query_frames, lanes = content.shape[0], arrived.shape[1] // 3
    frames_all, table_width = table.shape
    height = query_block(frames_all)
    chunked = query_frames == frames_all and height % block == 0
    chunks = (frames_all // block, block + 2 * HALO, lanes)
    kernel = attend_kernel
    if not chunked:
        kernel = lambda *refs: attend_kernel(*refs[:-1], None, refs[-1])
    return pl.pallas_call(
        kernel,
        grid=(query_frames // height,),
        in_specs=[
            pl.BlockSpec(memory_space=pltpu.SMEM),
            row_block(height, lanes),
            pl.BlockSpec((frames_all, lanes), lambda i: (0, 1)),
            pl.BlockSpec((frames_all, lanes), lambda i: (0, 2)),
            whole_block(shift.shape),
            whole_block(weight.shape),
            row_block(height, sines.shape[1]),
            row_block(height, sines.shape[1]),
            whole_block(table.shape),
        ],
        out_specs=[
            pl.BlockSpec((utterances, height, frames_all), lambda i: (0, i, 0)),
            whole_block(chunks) if chunked else row_block(height, lanes),
        ],
        out_shape=[
            jax.ShapeDtypeStruct((utterances, query_frames, frames_all), jnp.bfloat16),
            jax.ShapeDtypeStruct(chunks if chunked else (query_frames, lanes), jnp.bfloat16),
        ],
        scratch_shapes=[pltpu.VMEM((frames_all + 2 * HALO, lanes), jnp.float32)] * chunked
        + [pltpu.VMEM((utterances, height, frames_all), jnp.float32)],
        compiler_params=pltpu.CompilerParams(vmem_limit_bytes=VMEM_LIMIT),
        cost_estimate=pl.CostEstimate(
            flops=2 * utterances * query_frames * frames_all * (table_width + 256),
            bytes_accessed=2 * utterances * query_frames * frames_all,
            transcendentals=utterances * query_frames * frames_all,
        ),
    )(limits, content, arrived, arrived, shift, weight, sines, cosines, table)


def attend_heads_back(
    weights, content, grads, arrived, shift, weight, sines, cosines, table
):
    utterances, query_frames, frames_all = weights.shape
    lanes = arrived.shape[1] // 3
    height = query_block(frames_all)
    joined = query_frames == frames_all
    width = (3 if joined else 2) * lanes
    return pl.pallas_call(
        attend_back_kernel,
        grid=(query_frames // height,),
        in_specs=[
            pl.BlockSpec((utterances, height, frames_all), lambda i: (0, i, 0)),
            row_block(height, lanes),
            row_block(height, lanes),
            pl.BlockSpec((frames_all, lanes), lambda i: (0, 1)),
            pl.BlockSpec((frames_all, lanes), lambda i: (0, 2)),
            whole_block(shift.shape),
            whole_block(weight.shape),
            row_block(height, sines.shape[1]),
            row_block(height, sines.shape[1]),
            whole_block(table.shape),
        ],
        out_specs=([] if joined else [row_block(height, lanes)])
        + [
            whole_block((frames_all, width)),
            whole_block((HEAD_DIM, table.shape[1])),
            whole_block((8, lanes)),
        ],
        out_shape=(
            [] if joined else [jax.ShapeDtypeStruct((query_frames, lanes), jnp.bfloat16)]
        )
        + [
            jax.ShapeDtypeStruct((frames_all, width), jnp.bfloat16),
            jax.ShapeDtypeStruct((HEAD_DIM, table.shape[1]), jnp.float32),
            jax.ShapeDtypeStruct((8, lanes), jnp.float32),
        ],
        scratch_shapes=[
            pltpu.VMEM((lanes, frames_all), jnp.float32),
            pltpu.VMEM((lanes, frames_all), jnp.float32),
            pltpu.VMEM((utterances, height, frames_all), jnp.float32),
            pltpu.VMEM((utterances, height, frames_all), jnp.bfloat16),
        ],
        compiler_params=pltpu.CompilerParams(vmem_limit_bytes=VMEM_LIMIT),
        cost_estimate=pl.CostEstimate(
            flops=2 * utterances * query_frames * frames_all * (table.shape[1] + 512),
            bytes_accessed=2 * utterances * query_frames * frames_all,
            transcendentals=0,
        ),
    )(weights, content, grads, arrived, arrived, shift, weight, sines, cosines, table)


def shards(
    frames,
    lengths,
    out_grad,
    norm_gain,
    norm_bias,
    feed_in,
    feed_in_bias,
    feed_out,
    feed_out_bias,
    attend_in,
    attend_vectors,
    attend_out,
    mixer_in,
    mixer_in_bias,
    depthwise,
    mixer_vectors,
    mixer_out,
    batch_gain,
    batch_shift,
    running_mean,
    running_variance,
):
    utt_rows, block_frames, features = frames.shape
    rows = utt_rows * block_frames
    seq_count = lax.axis_size("seq")
    seq_index = lax.axis_index("seq")
    count = lax.axis_size("utt") * seq_count
    frames_all = block_frames * seq_count
    groups = seq_count // HEADS
    head, group = seq_index % HEADS, seq_index // HEADS
    query_frames = frames_all // groups
    lanes = utt_rows * HEAD_DIM
    info = jnp.concatenate(
        [(seq_index * block_frames).reshape(1), lengths, jnp.full((1,), frames_all, jnp.int32)]
    )
    hidden_units = feed_in.shape[2]
    f32, bf16 = jnp.float32, jnp.bfloat16
    flat_frames = frames.reshape(rows, features)
    square, broad = (rows, features), (rows, hidden_units)
    extended = (utt_rows * (block_frames + 2 * HALO), features)
    row_flops = 2 * rows * features
    bind = functools.partial
    edge = ((utt_rows, 2 * HALO, features), f32)
    feed_scratch = [
        pltpu.VMEM((features, hidden_units), bf16),
        pltpu.VMEM((hidden_units, features), bf16),
    ]
    attend_scratch = pltpu.VMEM((3, features, features), bf16)
    (
        edge_head,
        edge_tail,
        after_first,
        slope_first,
        entry_pack,
        sent,
    ) = vmem_call(
        bind(entry_kernel, utt_rows),
        [
            edge,
            edge,
            (square, f32),
            (broad, bf16),
            ((rows, hidden_units + 2 * features), bf16),
            ((HEADS, block_frames, 3 * lanes), bf16),
        ],
        (),
        (
            flat_frames,
            norm_gain,
            norm_bias,
            feed_in_bias,
            feed_out_bias,
            attend_vectors,
            Part(out_grad, (utt_rows, HALO, features), (0, 0, 0)),
            Part(out_grad, (utt_rows, HALO, features), (0, block_frames // HALO - 1, 0)),
        ),
        scratch=feed_scratch + [attend_scratch, pltpu.SemaphoreType.DMA((3,))],
        cost=row_flops * (2 * hidden_units + 3 * features),
        held=(feed_in, feed_out, attend_in),
    )
    sent, all_limits, edge_head, edge_tail = tie(sent, lengths, edge_head, edge_tail)
    before, behind = from_neighbours(edge_head, edge_tail)
    arrived = heads_out(sent, groups)
    for step in axis_bits("utt"):
        all_limits = jnp.concatenate([all_limits, swap(all_limits, step)])
    arrived, all_limits = tie(arrived, all_limits)
    arrived = arrived.reshape(frames_all, 3 * lanes)
    start_query = group * query_frames
    head_content = arrived
    if groups > 1:
        head_content = lax.dynamic_slice_in_dim(arrived, start_query, query_frames, 0)
    head_vectors = lax.dynamic_slice_in_dim(
        attend_vectors.astype(f32), head * HEAD_DIM, HEAD_DIM, 1
    )
    head_shift = jnp.tile((head_vectors[4] - head_vectors[3])[None], (1, utt_rows))
    head_weight = lax.dynamic_slice_in_dim(attend_in[3], head * HEAD_DIM, HEAD_DIM, 1).reshape(
        features // 2, 2, HEAD_DIM
    )
    head_weight = jnp.transpose(head_weight, (2, 1, 0)).reshape(HEAD_DIM, features)
    sines, cosines = angle_tables(frames_all, features)
    key_table = jnp.concatenate([cosines, sines], axis=1).astype(bf16)
    query_sin = lax.dynamic_slice_in_dim(sines, start_query, query_frames, 0)
    query_cos = lax.dynamic_slice_in_dim(cosines, start_query, query_frames, 0)
    weights, head_attended = attend_heads(
        lengths,
        head_content,
        arrived,
        head_shift,
        head_weight,
        query_sin,
        query_cos,
        key_table,
        block_frames,
    )

    def frames_back(blocks):
        width = blocks.shape[-1]
        blocks = blocks.reshape(1, HEADS, block_frames, width)
        if groups > 1:
            blocks = lax.dynamic_update_slice_in_dim(
                jnp.zeros((groups,) + blocks.shape[1:], blocks.dtype), blocks, group, 0
            )
        blocks = lax.all_to_all(
            blocks.reshape(seq_count, block_frames, width), "seq", 0, 0, tiled=True
        ).reshape(groups, HEADS, block_frames, width)
        return lax.dynamic_slice_in_dim(blocks, group, 1, 0)[0]

    head_attended, before, behind = tie(head_attended, before, behind)
    after_sides, grad_sides = vmem_call(
        sides_kernel,
        [((2 * utt_rows * HALO, features), f32)] * 2,
        (),
        (before, behind, norm_gain, norm_bias, feed_in_bias, feed_out_bias),
        scratch=feed_scratch + [pltpu.SemaphoreType.DMA((2,))],
        cost=row_flops * 2 * hidden_units // 4,
        held=(feed_in, feed_out),
    )
    if head_attended.ndim == 2:
        placed = lax.dynamic_update_slice_in_dim(
            jnp.zeros((frames_all + 2 * HALO, lanes), bf16), head_attended, HALO + start_query, 0
        )
        main, before, behind = (
            placed[start : start + frames_all].reshape(seq_count, block_frames, lanes)
            for start in (HALO, 0, 2 * HALO)
        )
        head_attended = jnp.concatenate([main, before[:, :HALO], behind[:, -HALO:]], axis=1)
    attended_blocks = lax.all_to_all(head_attended, "seq", 0, 0, tiled=True)
    attended_blocks, after_sides, grad_sides = tie(attended_blocks, after_sides, grad_sides)
    if groups > 1:
        attended_blocks = jnp.sum(
            attended_blocks.reshape((groups, HEADS) + attended_blocks.shape[1:]), axis=0
        )
    taps = depthwise.T
    padded = pltpu.VMEM((utt_rows, block_frames + 2 * HALO + 16, features), f32)
    (
        after_attend,
        mixer_pack,
        linear_half,
        gate_half,
        gated,
        convolved,
        shared,
    ) = vmem_call(
        bind(mixer_kernel, utt_rows),
        [
            (extended, f32),
            ((rows, 2 * features), bf16),
            (square, f32),
            (square, f32),
            (extended, bf16),
            (extended, f32),
            ((8 * count, 128), f32),
        ],
        (info,),
        (
            attended_blocks,
            after_first,
            after_sides,
            norm_gain,
            norm_bias,
            attend_out,
            attend_vectors,
            mixer_in,
            mixer_in_bias.reshape(1, -1),
            taps,
            mixer_vectors,
        ),
        scratch=(padded,),
        cost=row_flops * 3 * features,
    )
    (
        layer_output,
        grad_mixer,
        grad_batch,
        normed_batch,
        second_pack,
        shared,
        batch_rows,
        middle_rows,
    ) = vmem_call(
        bind(middle_kernel, utt_rows, seq_count),
        [
            (square, f32),
            (square, f32),
            (extended, f32),
            (extended, f32),
            ((rows, 2 * hidden_units + 4 * features), bf16),
            ((8 * count, 128), f32),
            ((8, features), f32),
            ((16, features), f32),
        ],
        (all_limits, lax.axis_index("utt").reshape(1)),
        (
            convolved,
            all_shared(shared),
            after_attend,
            out_grad.reshape(rows, features),
            grad_sides,
            norm_gain,
            norm_bias,
            batch_gain.reshape(1, -1),
            batch_shift.reshape(1, -1),
            running_mean.reshape(1, -1),
            running_variance.reshape(1, -1),
            mixer_out,
            mixer_vectors,
            feed_in_bias,
            feed_out_bias,
        ),
        scratch=feed_scratch + [pltpu.SemaphoreType.DMA((2,))],
        cost=row_flops * (4 * hidden_units + 2 * features),
        held=(feed_in, feed_out),
    )
    phases = list(zip(*step_orders()))
    near = axis_bits("utt")[0]
    core = side(near).reshape(1)
    halves = jnp.stack([side(step) for step in phases[0]])
    places = jnp.concatenate([core, halves])
    half_units, half_features = hidden_units // 2, features // 2

    def with_pair(array):
        return [array, swap(array, near)]

    second_pair = with_pair(second_pack)
    second_sent, second_kept = block_sums(
        second_kernel,
        places,
        2,
        [
            columns(second_pair, features, 8),
            columns(second_pair, half_units, 0, True),
            columns(second_pair, half_units, 2, True),
            columns(second_pair, features, 9),
        ],
    )
    other_places = [
        jnp.concatenate([near_core, near_halves])
        for near_halves in (halves, 1 - halves)
        for near_core in (core, 1 - core)
    ][1:]
    second_pair, second_sent, second_kept, shared, other_places = tie(
        second_pair, second_sent, second_kept, all_shared(shared), other_places
    )
    (
        batch_grads,
        grad_attend,
        mixer_back_pack,
        grad_blocks,
        mixer_rows,
    ) = vmem_call(
        bind(mixer_back_kernel, utt_rows),
        [
            ((8, features), f32),
            (square, f32),
            ((rows, 3 * features), bf16),
            ((HEADS, block_frames, lanes), bf16),
            ((16, features), f32),
        ],
        (info,),
        (
            grad_batch,
            normed_batch,
            shared,
            batch_rows,
            batch_gain.reshape(1, -1),
            gated,
            linear_half,
            gate_half,
            grad_mixer,
            after_attend,
            norm_gain,
            taps,
            mixer_in,
            attend_out,
        ),
        scratch=(padded, padded),
        cost=row_flops * 4 * features,
    )
    mixer_pair, mixer_back_pair = with_pair(mixer_pack), with_pair(mixer_back_pack)
    third_sent, third_kept = block_sums(
        mixer_blocks_kernel,
        places,
        1,
        [
            columns(mixer_pair, features, 1),
            columns(mixer_back_pair, features, 0, True),
            columns(second_pair, half_features, 20, True),
            columns(second_pair, features, 11),
            columns(mixer_pair, half_features, 0, True),
            columns(mixer_back_pair, features, 2),
        ],
    )
    early_sent, early_kept = second_sent + third_sent, second_kept + third_kept
    early_arrived = swap_all(early_sent, phases[0])
    head_grad = heads_out(grad_blocks, groups).reshape(frames_all, lanes)
    if groups > 1:
        head_grad = lax.dynamic_slice_in_dim(head_grad, start_query, query_frames, 0)
    head_grad, early_kept = tie(head_grad, early_kept)
    *head_grads, head_weight_grad, head_sums = attend_heads_back(
        weights,
        head_content,
        head_grad,
        arrived,
        head_shift,
        head_weight,
        query_sin,
        query_cos,
        key_table,
    )
    head_grads, head_weight_grad, head_sums, early_arrived = tie(
        head_grads, head_weight_grad, head_sums, early_arrived
    )
    grad_blocks = head_grads[-1].reshape(seq_count, block_frames, -1)
    returned = lax.all_to_all(grad_blocks, "seq", 0, 0, tiled=True)
    if groups > 1:
        returned = jnp.sum(
            returned.astype(f32).reshape(groups, HEADS, block_frames, 2 * lanes), axis=0
        ).astype(bf16)
        returned = jnp.concatenate([frames_back(head_grads[0]), returned], axis=2)
    head_vector_grads = lax.dynamic_update_slice_in_dim(
        jnp.zeros((8, features), f32),
        jnp.sum(head_sums.reshape(8, utt_rows, HEAD_DIM), axis=1),
        head * HEAD_DIM,
        1,
    )
    early_sent, early_kept = fold_rows([(early_kept, early_arrived)], phases[1], 1, VMEM_LIMIT)
    early_sent, head_weight_grad = tie(early_sent, head_weight_grad)
    early_arrived = swap_all(early_sent, phases[1])
    head_weight_grad = jnp.transpose(
        head_weight_grad.reshape(HEAD_DIM, 2, features // 2), (2, 1, 0)
    ).reshape(features, HEAD_DIM)
    position_weight_grad = lax.dynamic_update_slice_in_dim(
        jnp.zeros((features, features), f32), head_weight_grad, head * HEAD_DIM, 1
    )
    entry_pair = with_pair(entry_pack)
    position_pair = with_pair(position_weight_grad.astype(bf16))
    entry_cols = vmem_call(
        turn_kernel,
        [
            ((features, 2 * rows), bf16),
            ((half_units, 2 * rows), bf16),
            ((features, 2 * rows), bf16),
            ((features, features), bf16),
        ],
        (),
        columns(entry_pair, features, 4)
        + columns(entry_pair, half_units, 0, True)
        + columns(entry_pair, features, 5)
        + position_pair,
        numbers=(places,),
    )
    returned, early_arrived, entry_cols = tie(returned, early_arrived, entry_cols)
    (
        frames_grad,
        entry_back_pack,
        grad_pre_first,
        entry_rows,
    ) = vmem_call(
        entry_back_kernel,
        [
            (square, f32),
            ((rows, half_units + 4 * features), bf16),
            ((rows, half_units), bf16),
            ((16, features), f32),
        ],
        (core,),
        (
            returned,
            grad_attend,
            flat_frames,
            after_first,
            slope_first,
            norm_gain,
        ),
        scratch=feed_scratch + [attend_scratch, pltpu.SemaphoreType.DMA((3,))],
        cost=row_flops * (2 * hidden_units + 3 * features),
        held=(feed_in, feed_out, attend_in),
    )
    late_factors = (entry_cols, grad_pre_first, with_pair(entry_back_pack))
    late_sent = late_blocks(False, places, *late_factors)
    late_sent, late_factors, middle_rows = tie(late_sent, late_factors, middle_rows)
    late_arrived = swap_all(late_sent, phases[0])
    late_kept = late_blocks(True, places, *late_factors)
    flat = jnp.concatenate([middle_rows, mixer_rows, entry_rows, head_vector_grads], axis=0)
    flat_steps = [near] + [steps[0] for steps in phases]
    def in_turn(arrived_rows, steps, work):
        nonlocal flat
        flat_arrived = swap(flat, flat_steps.pop()) if flat_steps else jnp.zeros_like(flat)
        after, next_arrived = None, []
        for i, rows in enumerate(arrived_rows):
            if after is not None:
                rows, _ = tie(rows, after)
            if i == len(arrived_rows) - 1:
                rows, flat_arrived = tie(rows, flat_arrived)
            after = work(i, rows)
            next_arrived.append(swap(after, steps[i]) if steps else after)
        flat = flat + flat_arrived
        return next_arrived

    late_kept = list(late_kept)
    for steps in phases[1:]:

        def fold(i, rows):
            pairs = [([late_kept[i]], [rows])]
            if steps is phases[2]:
                pairs = [([early_kept[i]], [early_arrived[i]])] + pairs
            parts = 1 if steps in phases[1:3] else 2
            (sent_rows,), (late_kept[i],) = fold_rows(pairs, [steps[i]], parts)
            return sent_rows

        late_arrived = in_turn(late_arrived, steps, fold)
    sums = [None] * len(late_arrived)

    def add(i, rows):
        (sums[i],) = add_rows([late_kept[i]], [rows])
        return sums[i]

    arrived_rows = in_turn(late_arrived, phases[-1], add)
    for number in range(len(phases) - 1, 0, -1):

        def join(i, rows):
            (sums[i],) = join_rows([sums[i]], [rows], [phases[number][i]])
            return sums[i]

        arrived_rows = in_turn(arrived_rows, phases[number - 1], join)
    for step in flat_steps:
        flat = flat + swap(flat, step)
    vector_grads = vmem_call(
        vectors_kernel,
        [
            (norm_gain.shape, f32),
            (norm_bias.shape, f32),
            (feed_in_bias.shape, f32),
            (feed_out_bias.shape, f32),
            (attend_vectors.shape, f32),
            ((1, 2 * features), f32),
            (mixer_vectors.shape, f32),
            ((KERNEL, features), f32),
        ],
        (),
        (flat,),
    )
    vector_grads = list(vector_grads)
    vector_grads[5] = vector_grads[5].reshape(-1)
    vector_grads[7] = vector_grads[7].T
    vector_grads = [*vector_grads, batch_grads[1], batch_grads[0], batch_rows[2], batch_rows[3]]
    across_rows = swap_all(sums, [near] * 3)
    shapes = [feed_in.shape, feed_out.shape, mixer_in.shape, mixer_out.shape]
    shapes += [attend_out.shape, attend_in.shape]
    spread = spread_blocks(places, sums, shapes, [])
    spread = spread_blocks(other_places[0], across_rows, shapes, spread)
    spread, arrived_rows, vector_grads = tie(spread, arrived_rows, vector_grads)
    across_rows = swap_all(arrived_rows, [near] * 3)
    spread = spread_blocks(other_places[1], arrived_rows, shapes, spread)
    (
        feed_in_grad,
        feed_out_grad,
        mixer_in_grad,
        mixer_out_grad,
        attend_out_grad,
        attend_in_grad,
    ) = spread_blocks(other_places[2], across_rows, shapes, spread)
    (
        norm_gain_grad,
        norm_bias_grad,
        feed_in_bias_grad,
        feed_out_bias_grad,
        attend_vectors_grad,
        mixer_in_bias_grad,
        mixer_vectors_grad,
        taps_grad,
        batch_gain_grad,
        batch_shift_grad,
        new_mean,
        new_variance,
    ) = vector_grads
    return (
        layer_output.reshape(frames.shape),
        frames_grad.reshape(frames.shape),
        norm_gain_grad,
        norm_bias_grad,
        feed_in_grad,
        feed_in_bias_grad,
        feed_out_grad,
        feed_out_bias_grad,
        attend_in_grad,
        attend_vectors_grad,
        attend_out_grad,
        mixer_in_grad,
        mixer_in_bias_grad,
        taps_grad,
        mixer_vectors_grad,
        mixer_out_grad,
        batch_gain_grad,
        batch_shift_grad,
        new_mean,
        new_variance,
    )


def solution(mesh):
    return jax.shard_map(
        shards,
        mesh=mesh,
        in_specs=(
            P("utt", "seq", None),
            P("utt"),
            P("utt", "seq", None),
            P(),
            P(),
            P(),
            P(),
            P(),
            P(),
            P(),
            P(),
            P(),
            P(),
            P(),
            P(),
            P(),
            P(),
            P(),
            P(),
            P(),
            P(),
        ),
        out_specs=(
            P("utt", "seq", None),
            P("utt", "seq", None),
            P(),
            P(),
            P(),
            P(),
            P(),
            P(),
            P(),
            P(),
            P(),
            P(),
            P(),
            P(),
            P(),
            P(),
            P(),
            P(),
            P(),
            P(),
        ),
        check_vma=False,
    )
```

```python
import functools
import math

import jax
import jax.numpy as jnp
import numpy as np
from jax import lax
from jax.experimental import pallas as pl
from jax.experimental.pallas import tpu as pltpu
from jax.sharding import PartitionSpec as P

HEADS = 8
KERNEL = 9
HEAD_DIM = 64


TOP_PRECISION = lax.Precision.HIGHEST
EPSILON = 1e-05
VMEM_LIMIT = 64 * 1024 * 1024
SUM_LIMIT = 20 * 1024 * 1024
HALO = 8
ROW_TILE = 32


def wide(values):
    return values.astype(jnp.float32)


def low(values):
    return values.astype(jnp.bfloat16)


def matmul(first_operand, second_operand):
    return jnp.dot(first_operand, second_operand, preferred_element_type=jnp.float32)


def column_sum(values):
    return jnp.sum(wide(values), axis=0, keepdims=True)


def normalize(values):
    average = jnp.mean(values, axis=-1, keepdims=True)
    centered = values - average
    spread = jnp.mean(centered * centered, axis=-1, keepdims=True)
    inverse = lax.rsqrt(spread + EPSILON)
    return centered * inverse, inverse


def scaled_norm(normed, gains, biases, number):
    return normed * wide(gains[number : number + 1, :]) + wide(biases[number : number + 1, :])


def norm_back(grad_rows, normed, inverse, gains, number, own=lambda values: values):
    scaled = grad_rows * wide(gains[number : number + 1, :])
    inner = (
        scaled
        - jnp.mean(scaled, axis=-1, keepdims=True)
        - normed * jnp.mean(scaled * normed, axis=-1, keepdims=True)
    )
    return inner * inverse, column_sum(own(grad_rows * normed)), column_sum(own(grad_rows))


def logistic(values):
    return 1.0 / (1.0 + jnp.exp(-values))


def silu_slope(preact, sigmoid):
    return sigmoid * (1.0 + preact * (1.0 - sigmoid))


def frame_places(info, rows, utterances, halo):
    own = rows - 2 * utterances * halo
    per = own // utterances
    row = lax.broadcasted_iota(jnp.int32, (rows, 1), 0)
    aside = row - own
    owner = jnp.where(aside < 0, row // per, aside // (2 * halo))
    near = aside % (2 * halo)
    place = jnp.where(aside < 0, row % per, near - halo + jnp.where(near < halo, 0, per))
    limit = jnp.full((rows, 1), info[utterances], jnp.int32)
    for utterance in range(utterances - 1):
        limit = jnp.where(owner == utterance, info[1 + utterance], limit)
    return info[0] + place, limit


def flags(condition):
    return jnp.where(condition, 1.0, 0.0)


def own_rows(values, utterances):
    return values[: values.shape[0] - 2 * utterances * HALO]


def with_sides(values, sides):
    return jnp.concatenate([values, sides], axis=0)


def blocks_of_heads(rows, utterances):
    per = rows.shape[0] // utterances
    first = lax.broadcasted_iota(jnp.int32, (per, 2 * HEAD_DIM), 1) < HEAD_DIM
    blocks = []
    for pair in range(HEADS // 2):
        columns = rows[:, pair * 2 * HEAD_DIM : (pair + 1) * 2 * HEAD_DIM]
        top, bottom = columns[:per], columns[per:]
        blocks.append(jnp.where(first, top, pltpu.roll(bottom, HEAD_DIM, 1)))
        blocks.append(jnp.where(first, pltpu.roll(top, HEAD_DIM, 1), bottom))
    return blocks


def rows_of_heads(blocks):
    per = blocks[0].shape[0]
    first = lax.broadcasted_iota(jnp.int32, (per, 2 * HEAD_DIM), 1) < HEAD_DIM
    columns = []
    for pair in range(HEADS // 2):
        left, right = blocks[2 * pair], blocks[2 * pair + 1]
        top = jnp.where(first, left, pltpu.roll(right, HEAD_DIM, 1))
        bottom = jnp.where(first, pltpu.roll(left, HEAD_DIM, 1), right)
        columns.append(jnp.concatenate([top, bottom], axis=0))
    return jnp.concatenate(columns, axis=1)


def whole_array(shape):
    return pl.BlockSpec(shape, lambda i: (0,) * len(shape))


class Part:
    def __init__(self, array, block, index):
        self.array, self.block, self.index = array, block, index

    def spec(self):
        def index(i, *numbers):
            return tuple(at(*numbers) if callable(at) else at for at in self.index)

        return pl.BlockSpec(self.block, index)


def vmem_call(kernel, shapes, smem, operands, scratch=(), cost=0, held=(), numbers=()):
    def whole(shape):
        return pl.BlockSpec(shape, lambda i, *numbers: (0,) * len(shape))

    return pl.pallas_call(
        kernel,
        grid_spec=pltpu.PrefetchScalarGridSpec(
            num_scalar_prefetch=len(numbers),
            grid=(1,),
            in_specs=[pl.BlockSpec(memory_space=pltpu.SMEM)] * len(smem)
            + [
                operand.spec() if isinstance(operand, Part) else whole(operand.shape)
                for operand in operands
            ]
            + [pl.BlockSpec(memory_space=pl.ANY)] * len(held),
            out_specs=[whole(shape) for shape, _ in shapes],
            scratch_shapes=list(scratch),
        ),
        out_shape=[jax.ShapeDtypeStruct(shape, dtype) for shape, dtype in shapes],
        compiler_params=pltpu.CompilerParams(vmem_limit_bytes=VMEM_LIMIT),
        cost_estimate=pl.CostEstimate(flops=cost, bytes_accessed=cost // 300, transcendentals=0),
    )(
        *numbers,
        *smem,
        *(operand.array if isinstance(operand, Part) else operand for operand in operands),
        *held,
    )


def fetch(pairs, semaphores):
    copies = [
        pltpu.make_async_copy(source, target, semaphores.at[number])
        for number, (source, target) in enumerate(pairs)
    ]
    for copy in copies:
        copy.start()
    return copies


def feed_rows(values, gains, biases, copies, weight_in, bias_in, weight_out, bias_out):
    normed, _ = normalize(values)
    hidden = low(scaled_norm(normed, gains, biases, 0))
    copies[0].wait()
    preact = matmul(hidden, weight_in[...]) + wide(bias_in[0:1, :])
    sigmoid = logistic(preact)
    active = low(preact * sigmoid)
    copies[1].wait()
    branch = matmul(active, weight_out[...]) + wide(bias_out[0:1, :])
    return values + 0.5 * branch, preact, sigmoid, active


def entry_kernel(
    utterances,
    frames,
    gains,
    biases,
    bias_in,
    bias_out,
    vectors,
    grads_head,
    grads_tail,
    feed_in,
    feed_out,
    attend_in,
    head_out,
    tail_out,
    after_out,
    slope_out,
    pack_out,
    sent_out,
    weight_in,
    weight_out,
    weight_attend,
    semaphores,
):
    copies = fetch(
        [
            (feed_in.at[0], weight_in),
            (feed_out.at[0], weight_out),
            (attend_in.at[pl.ds(0, 3)], weight_attend),
        ],
        semaphores,
    )
    per = frames.shape[0] // utterances
    for u in range(utterances):
        head_out[u, 0:HALO, :] = frames[u * per : u * per + HALO, :]
        head_out[u, HALO:, :] = grads_head[u]
        tail_out[u, 0:HALO, :] = frames[(u + 1) * per - HALO : (u + 1) * per, :]
        tail_out[u, HALO:, :] = grads_tail[u]
    units, features = slope_out.shape[1], frames.shape[1]
    pack_out[:, units : units + features] = low(scaled_norm(normalize(frames[...])[0], gains, biases, 0))
    after, preact, sigmoid, active = feed_rows(
        frames[...], gains, biases, copies, weight_in, bias_in, weight_out, bias_out
    )
    slope_out[...] = low(silu_slope(preact, sigmoid))
    pack_out[:, :units] = active
    after_out[...] = after
    normed, _ = normalize(after)
    hidden = low(scaled_norm(normed, gains, biases, 1))
    pack_out[:, units + features :] = hidden
    copies[2].wait()
    queries = matmul(hidden, weight_attend[0]) + wide(vectors[0:1, :])
    parts = (
        queries + wide(vectors[3:4, :]),
        matmul(hidden, weight_attend[1]),
        matmul(hidden, weight_attend[2]) + wide(vectors[1:2, :]),
    )
    lanes = 2 * HEAD_DIM
    for number, part in enumerate(parts):
        for head, block in enumerate(blocks_of_heads(part, utterances)):
            sent_out[head, :, number * lanes : (number + 1) * lanes] = low(block)


def sides_kernel(
    before,
    behind,
    gains,
    biases,
    bias_in,
    bias_out,
    feed_in,
    feed_out,
    after_out,
    grads_out,
    weight_in,
    weight_out,
    semaphores,
):
    copies = fetch([(feed_in.at[0], weight_in), (feed_out.at[0], weight_out)], semaphores)
    frames, grads = (
        jnp.concatenate(
            [
                source[u, first : first + HALO, :]
                for u in range(before.shape[0])
                for source in (before, behind)
            ],
            axis=0,
        )
        for first in (0, HALO)
    )
    grads_out[...] = grads
    after_out[...] = feed_rows(
        frames, gains, biases, copies, weight_in, bias_in, weight_out, bias_out
    )[0]


def mixer_kernel(
    utterances,
    info,
    blocks,
    after,
    after_sides,
    gains,
    biases,
    attend_out,
    vectors,
    mixer_in,
    mixer_bias,
    taps,
    mixer_vectors,
    after_out,
    pack_out,
    linear_out,
    gate_out,
    gated_out,
    convolved_out,
    sums_out,
    padded,
):
    per = after.shape[0] // utterances
    main, before, behind = [], [], []
    for head in range(HEADS):
        block = wide(blocks[head])
        main.append(block[:per])
        before.append(block[per : per + HALO])
        behind.append(block[per + HALO :])
    attended = rows_of_heads(main)
    features = after.shape[1]
    pack_out[:, :features] = low(attended)
    before, behind = rows_of_heads(before), rows_of_heads(behind)
    sides = []
    for u in range(utterances):
        sides += [before[u * HALO : (u + 1) * HALO], behind[u * HALO : (u + 1) * HALO]]
    attended = low(with_sides(attended, jnp.concatenate(sides, axis=0)))
    values = with_sides(after[...], after_sides[...])
    values = values + matmul(attended, attend_out[...]) + wide(vectors[2:3, :])
    after_out[...] = values
    normed, _ = normalize(values)
    scaled = scaled_norm(normed, gains, biases, 2)
    pack_out[:, features:] = low(own_rows(scaled, utterances))
    preact = matmul(low(scaled), mixer_in[...])
    preact = preact + wide(mixer_bias[...])
    rows = values.shape[0]
    linear = preact[:, :features]
    gate = logistic(preact[:, features:])
    linear_out[...] = own_rows(linear, utterances)
    gate_out[...] = own_rows(gate, utterances)
    place, limit = frame_places(info, rows, utterances, HALO)
    mask = flags((place >= 0) & (place < limit))
    gated = low(linear * gate * mask)
    gated_out[...] = gated
    fill_padded(padded, wide(gated), utterances)
    total = None
    for offset in range(KERNEL):
        term = wide(taps[offset : offset + 1, :]) * moved(
            padded, utterances, offset - KERNEL // 2, True
        )
        total = term if total is None else total + term
    convolved = total + wide(mixer_vectors[0:1, :])
    convolved_out[...] = convolved
    mask = own_rows(mask, utterances)
    convolved = own_rows(convolved, utterances)
    count = jnp.sum(mask, axis=0, keepdims=True)
    local_sum = jnp.sum(convolved * mask, axis=0, keepdims=True)
    centered = (convolved - local_sum / jnp.maximum(count, 1.0)) * mask
    share(sums_out, local_sum, jnp.sum(centered * centered, axis=0, keepdims=True))


def fill_padded(padded, values, utterances):
    own = values.shape[0] - 2 * utterances * HALO
    per = own // utterances
    zeros = jnp.zeros((HALO, values.shape[1]), jnp.float32)
    for u in range(utterances):
        aside = own + 2 * u * HALO
        padded[u, 0:HALO, :] = zeros
        padded[u, HALO : 2 * HALO, :] = values[aside : aside + HALO, :]
        padded[u, 2 * HALO : 2 * HALO + per, :] = values[u * per : (u + 1) * per, :]
        padded[u, 2 * HALO + per : 3 * HALO + per, :] = values[aside + HALO : aside + 2 * HALO, :]
        padded[u, 3 * HALO + per :, :] = zeros


def moved(padded, utterances, start, sides=False):
    per = padded.shape[1] - 4 * HALO
    pieces = [(u, 2 * HALO, per) for u in range(utterances)]
    if sides:
        for u in range(utterances):
            pieces += [(u, HALO, HALO), (u, 2 * HALO + per, HALO)]
    return jnp.concatenate(
        [padded[u, first + start : first + start + height, :] for u, first, height in pieces],
        axis=0,
    )


def share(sums_out, *rows):
    tile = jnp.concatenate(
        [row[:, i : i + 128] for row in rows for i in range(0, row.shape[1], 128)], axis=0
    )
    for copy in range(sums_out.shape[0] // 8):
        sums_out[copy * 8 : copy * 8 + 8, :] = tile


def as_row(tile):
    return jnp.concatenate([tile[i : i + 1] for i in range(tile.shape[0])], axis=1)


def frame_counts(limits, utt_index, shape, utterances, seq_count, per):
    place = lax.broadcasted_iota(jnp.int32, shape, 0)
    owner, first = (place // seq_count) ^ utt_index, place % seq_count * per
    total = jnp.zeros(shape, jnp.int32)
    for number in range(limits.shape[0]):
        inside = jnp.clip(limits[number] - first, 0, per)
        total = total + jnp.where(owner == number // utterances, inside, 0)
    return total.astype(jnp.float32)


def middle_kernel(
    utterances,
    seq_count,
    limits,
    utt_index,
    convolved,
    shared,
    after,
    grads,
    grad_sides,
    gains,
    biases,
    batch_gain,
    batch_shift,
    running_mean,
    running_variance,
    mixer_out,
    vectors,
    bias_in,
    bias_out,
    feed_in,
    feed_out,
    layer_out,
    grad_mixer_out,
    grad_batch_out,
    normed_out,
    pack_out,
    sums_out,
    batch_out_rows,
    vector_out,
    weight_in,
    weight_out,
    semaphores,
):
    def own(values):
        return own_rows(values, utterances)

    features, units = feed_in.shape[1:]

    def pack(number, rows):
        first = 2 * units + number * features
        pack_out[:, first : first + features] = rows

    copies = fetch([(feed_in.at[1], weight_in), (feed_out.at[1], weight_out)], semaphores)
    parts = shared[...].reshape(-1, 8, 128)
    per = grads.shape[0] // utterances
    counts = frame_counts(limits, utt_index[0], parts.shape, utterances, seq_count, per)
    totals = jnp.sum(parts, axis=0)
    valid_tile = jnp.sum(counts, axis=0)
    valid = as_row(valid_tile[:4])
    average_tile = totals / valid_tile
    drift = parts / jnp.maximum(counts, 1.0) - average_tile
    spreads = jnp.sum(counts * drift * drift, axis=0)
    average = as_row(average_tile[:4])
    variance = as_row((totals[4:] + spreads[:4]) / valid_tile[:4])
    inverse_batch = lax.rsqrt(variance + EPSILON)
    batch_out_rows[0:1, :] = inverse_batch
    batch_out_rows[1:2, :] = valid
    batch_out_rows[2:3, :] = 0.9 * running_mean[...] + 0.1 * average
    batch_out_rows[3:4, :] = 0.9 * running_variance[...] + 0.1 * variance * valid / (valid - 1.0)
    normed_batch = (convolved[...] - average) * inverse_batch
    normed_out[...] = normed_batch
    batch = normed_batch * wide(batch_gain[...]) + wide(batch_shift[...])
    batch_sigmoid = logistic(batch)
    swished = low(batch * batch_sigmoid)
    pack(2, own(swished))
    values = after[...] + matmul(swished, mixer_out[...]) + wide(vectors[1:2, :])
    normed, inverse = normalize(values)
    scaled = scaled_norm(normed, gains, biases, 3)
    hidden = low(scaled)
    pack(0, own(hidden))
    copies[0].wait()
    preact = matmul(hidden, weight_in[...]) + wide(bias_in[1:2, :])
    sigmoid = logistic(preact)
    active = low(preact * sigmoid)
    pack_out[:, units : 2 * units] = own(active)
    copies[1].wait()
    branch = matmul(active, weight_out[...]) + wide(bias_out[1:2, :])
    normed_last, inverse_last = normalize(values + 0.5 * branch)
    layer_out[...] = own(scaled_norm(normed_last, gains, biases, 4))
    grad_second, gain_last, shift_last = norm_back(
        with_sides(grads[...], grad_sides[...]),
        normed_last,
        inverse_last,
        gains,
        4,
        own,
    )
    grad_low = low(0.5 * grad_second)
    grad_low_own = own(grad_low)
    pack(1, grad_low_own)
    grad_pre = low(rows_dot(grad_low, weight_out[...]) * silu_slope(preact, sigmoid))
    grad_pre_own = own(grad_pre)
    pack_out[:, :units] = grad_pre_own
    grad_values, gain_three, shift_three = norm_back(
        rows_dot(grad_pre, weight_in[...]), normed, inverse, gains, 3, own
    )
    grad_mixer = grad_second + grad_values
    grad_mixer_own = own(grad_mixer)
    grad_mixer_out[...] = grad_mixer_own
    branch_own = low(grad_mixer_own)
    pack(3, branch_own)
    grad_batch = rows_dot(low(grad_mixer), mixer_out[...]) * silu_slope(batch, batch_sigmoid)
    grad_batch_out[...] = grad_batch
    share(sums_out, column_sum(own(grad_batch)), column_sum(own(grad_batch * normed_batch)))
    bias_sum = column_sum(grad_pre_own)
    put_rows(
        vector_out,
        [gain_last, shift_last, gain_three, shift_three]
        + [bias_sum[:, i : i + features] for i in range(0, bias_sum.shape[1], features)]
        + [column_sum(grad_low_own), column_sum(branch_own)],
    )


def put_rows(out, rows):
    for number, row in enumerate(rows):
        out[number : number + 1, :] = row
    out[len(rows) :, :] = jnp.zeros((out.shape[0] - len(rows), out.shape[1]), jnp.float32)


def mixer_back_kernel(
    utterances,
    info,
    grad_batch,
    normed_batch,
    shared,
    batch_rows,
    batch_gain,
    gated,
    linear,
    gate,
    grad_mixer,
    after,
    gains,
    taps,
    mixer_in,
    attend_out,
    batch_grads_out,
    grad_attend_out,
    pack_out,
    sent_out,
    vector_out,
    padded,
    gated_padded,
):
    totals = jnp.sum(shared[...].reshape(-1, 8, 128), axis=0)
    shift_grad, gain_grad = as_row(totals[:4]), as_row(totals[4:])
    batch_grads_out[0:1, :] = shift_grad
    batch_grads_out[1:2, :] = gain_grad
    rows, features = grad_batch.shape
    place, limit = frame_places(info, rows, utterances, HALO)
    mask = flags((place >= 0) & (place < limit))
    inside = flags((place >= 0) & (place < info[utterances + 1]))
    inverse_batch, valid = batch_rows[0:1, :], batch_rows[1:2, :]
    grad_conv = low(
        inside
        * wide(batch_gain[...])
        * inverse_batch
        * (grad_batch[...] - mask / valid * (shift_grad + normed_batch[...] * gain_grad))
    )
    conv_wide = wide(grad_conv)
    fill_padded(padded, conv_wide, utterances)
    fill_padded(gated_padded, wide(gated[...]), utterances)
    conv_own = own_rows(conv_wide, utterances)
    margin = KERNEL // 2
    total = None
    tap_rows = []
    for offset in range(KERNEL):
        term = wide(taps[offset : offset + 1, :]) * moved(padded, utterances, margin - offset)
        total = term if total is None else total + term
        near = moved(gated_padded, utterances, offset - margin)
        tap_rows.append(jnp.sum(conv_own * near, axis=0, keepdims=True))
    grad_gated = own_rows(mask, utterances) * total
    gate_half = gate[...]
    grad_pre = low(
        jnp.concatenate(
            [
                grad_gated * gate_half,
                grad_gated * linear[...] * gate_half * (1.0 - gate_half),
            ],
            axis=1,
        )
    )
    pack_out[:, : 2 * features] = grad_pre
    normed, inverse = normalize(own_rows(after[...], utterances))
    grad_values, gain_two, shift_two = norm_back(
        rows_dot(grad_pre, mixer_in[...]), normed, inverse, gains, 2
    )
    grad_attend = grad_mixer[...] + grad_values
    grad_attend_out[...] = grad_attend
    branch = low(grad_attend)
    pack_out[:, 2 * features :] = branch
    grad_attended = rows_dot(branch, attend_out[...])
    for head, block in enumerate(blocks_of_heads(grad_attended, utterances)):
        sent_out[head] = low(block)
    bias_sum = column_sum(grad_pre)
    put_rows(
        vector_out,
        [gain_two, shift_two, column_sum(conv_own), column_sum(branch)]
        + [bias_sum[:, :features], bias_sum[:, features:]]
        + tap_rows,
    )


def entry_back_kernel(
    core,
    returned,
    grad_attend,
    frames,
    after,
    slope,
    gains,
    feed_in,
    feed_out,
    attend_in,
    frames_out,
    pack_out,
    grad_pre_out,
    vector_out,
    weight_in,
    weight_out,
    weight_attend,
    semaphores,
):
    copies = fetch(
        [
            (attend_in.at[pl.ds(0, 3)], weight_attend),
            (feed_out.at[0], weight_out),
            (feed_in.at[0], weight_in),
        ],
        semaphores,
    )
    lanes = 2 * HEAD_DIM
    features, units = feed_in.shape[1:]

    def pack(number, rows):
        first = units // 2 + number * features
        pack_out[:, first : first + features] = rows

    grad_hidden = None
    low_rows = []
    for number in range(3):
        rows = low(
            rows_of_heads(
                [
                    wide(returned[head, :, number * lanes : (number + 1) * lanes])
                    for head in range(HEADS)
                ]
            )
        )
        pack(number, rows)
        low_rows.append(rows)
        if number == 0:
            copies[0].wait()
        term = rows_dot(rows, weight_attend[number])
        grad_hidden = term if grad_hidden is None else grad_hidden + term
    normed, inverse = normalize(after[...])
    grad_values, gain_one, shift_one = norm_back(grad_hidden, normed, inverse, gains, 1)
    grad_first = grad_attend[...] + grad_values
    grad_low = low(0.5 * grad_first)
    pack(3, grad_low)
    copies[1].wait()
    grad_pre = low(rows_dot(grad_low, weight_out[...]) * wide(slope[...]))
    for half in range(2):
        rows = grad_pre[:, half * units // 2 : (half + 1) * units // 2]

        @pl.when(core[0] == half)
        def _():
            grad_pre_out[...] = rows

        @pl.when(core[0] != half)
        def _():
            pack_out[:, : units // 2] = rows

    normed, inverse = normalize(frames[...])
    copies[2].wait()
    grad_values, gain_zero, shift_zero = norm_back(
        rows_dot(grad_pre, weight_in[...]), normed, inverse, gains, 0
    )
    frames_out[...] = grad_first + grad_values
    bias_sum = column_sum(grad_pre)
    put_rows(
        vector_out,
        [gain_zero, shift_zero, gain_one, shift_one]
        + [bias_sum[:, i : i + features] for i in range(0, bias_sum.shape[1], features)]
        + [column_sum(grad_low), column_sum(low_rows[0]), column_sum(low_rows[2])],
    )


def vectors_kernel(
    rows, gain_out, bias_out, in_bias_out, out_bias_out, attend_out, mixer_bias_out, mixer_out, taps_out
):
    middle, mixer, entry, heads = (0, 16, 32, 48)
    features = gain_out.shape[1]

    def take(out, target, start):
        out[target : target + 1, :] = rows[start : start + 1, :]

    for out, first in ((gain_out, 0), (bias_out, 1)):
        take(out, 0, entry + first)
        take(out, 1, entry + 2 + first)
        take(out, 2, mixer + first)
        take(out, 3, middle + 2 + first)
        take(out, 4, middle + first)
    for target, start in ((0, entry + 4), (1, middle + 4)):
        for column in range(4):
            in_bias_out[target : target + 1, column * features : (column + 1) * features] = rows[
                start + column : start + column + 1, :
            ]
    take(out_bias_out, 0, entry + 8)
    take(out_bias_out, 1, middle + 8)
    for target, start in enumerate((entry + 9, entry + 10, mixer + 3, heads, heads + 1)):
        take(attend_out, target, start)
    for column in range(2):
        mixer_bias_out[0:1, column * features : (column + 1) * features] = rows[
            mixer + 4 + column : mixer + 5 + column, :
        ]
    take(mixer_out, 0, mixer + 2)
    take(mixer_out, 1, middle + 9)
    taps_out[...] = rows[mixer + 6 : mixer + 6 + KERNEL, :]


def axis_bits(axis):
    return [(axis, 1 << bit) for bit in range(lax.axis_size(axis).bit_length() - 1)]


def swap(values, step):
    axis, mask = step
    return lax.ppermute(values, axis, [(i, i ^ mask) for i in range(lax.axis_size(axis))])


def side(step):
    axis, mask = step
    return (lax.axis_index(axis) // mask) % 2


def swap_all(stripes, steps):
    return [swap(rows, step) for rows, step in zip(stripes, steps)]


def add_low(first_operand, second_operand):
    total = first_operand.astype(jnp.float32) + second_operand.astype(jnp.float32)
    return total.astype(jnp.bfloat16)


def fold_kernel(stripes, arrays, parts, sides, *refs):
    for number in range(stripes):
        sources = refs[2 * arrays * number : 2 * arrays * (number + 1)]
        for keeping in range(2):
            place = sides[number] if keeping else 1 - sides[number]
            out = refs[2 * arrays * stripes + 2 * number + keeping]
            first = 0
            for array in range(arrays):
                own, other = sources[2 * array : 2 * array + 2]
                height = own.shape[0] // (2 * parts)
                for part in range(parts):
                    start = pl.multiple_of((2 * part + place) * height, 16)
                    rows = pl.ds(start, height)
                    out[first : first + height, :] = add_low(own[rows, :], other[rows, :])
                    first += height


def fold_rows(pairs, steps, parts=1, limit=SUM_LIMIT):
    operands = list(zip(*(rows for pair in pairs for rows in pair)))
    heights = [sum(rows.shape[0] for rows in four[::2]) // 2 for four in operands]
    if any(rows.shape[0] // parts % 32 for four in operands for rows in four):
        sent, kept = [], []
        for four, step in zip(operands, steps):
            sums = [add_low(*four[i : i + 2]) for i in range(0, len(four), 2)]
            for place, results in ((1 - side(step), sent), (side(step), kept)):
                pieces = []
                for rows in sums:
                    height = rows.shape[0] // (2 * parts)
                    pieces += [
                        lax.dynamic_slice_in_dim(rows, (2 * part + place) * height, height, 0)
                        for part in range(parts)
                    ]
                results.append(jnp.concatenate(pieces, axis=0))
        return sent, kept

    def whole(rows):
        return pl.BlockSpec((rows, 512), lambda i, sides: (0, 0))

    outs = [height for height in heights for _ in range(2)]
    results = pl.pallas_call(
        functools.partial(fold_kernel, len(steps), len(pairs), parts),
        grid_spec=pltpu.PrefetchScalarGridSpec(
            num_scalar_prefetch=1,
            grid=(1,),
            in_specs=[whole(rows.shape[0]) for four in operands for rows in four],
            out_specs=[whole(height) for height in outs],
        ),
        out_shape=[jax.ShapeDtypeStruct((height, 512), jnp.bfloat16) for height in outs],
        compiler_params=pltpu.CompilerParams(vmem_limit_bytes=limit),
        cost_estimate=pl.CostEstimate(
            flops=0, bytes_accessed=6 * 1024 * sum(outs), transcendentals=0
        ),
    )(jnp.stack([side(step) for step in steps]), *(rows for four in operands for rows in four))
    return list(results[::2]), list(results[1::2])


def add_kernel(stripes, *refs):
    for number in range(stripes):
        refs[2 * stripes + number][...] = add_low(refs[2 * number][...], refs[2 * number + 1][...])


def add_rows(kept, arrived):
    if any(rows.shape[0] % 16 for rows in kept):
        return [add_low(*pair) for pair in zip(kept, arrived)]
    specs = [whole_array(rows.shape) for rows in kept]
    return list(
        pl.pallas_call(
            functools.partial(add_kernel, len(kept)),
            grid=(1,),
            in_specs=[spec for spec in specs for _ in range(2)],
            out_specs=specs,
            out_shape=[jax.ShapeDtypeStruct(rows.shape, rows.dtype) for rows in kept],
            compiler_params=pltpu.CompilerParams(vmem_limit_bytes=SUM_LIMIT),
        )(*(rows for pair in zip(kept, arrived) for rows in pair))
    )


def join_kernel(stripes, sides, *refs):
    for number in range(stripes):
        own, other, out = refs[2 * number], refs[2 * number + 1], refs[2 * stripes + number]
        height = own.shape[0] // 2
        for part in range(2):
            for source, place in ((own, sides[number]), (other, 1 - sides[number])):
                start = pl.multiple_of((2 * part + place) * height, 16)
                out[pl.ds(start, height), :] = source[part * height : (part + 1) * height, :]


def join_rows(stripes, arrived, steps):
    heights = [rows.shape[0] // 2 for rows in stripes]
    if any(height % 16 for height in heights):
        joined = []
        for rows, other, step, height in zip(stripes, arrived, steps, heights):
            first = side(step) == 0
            low_rows, high_rows = jnp.where(first, rows, other), jnp.where(first, other, rows)
            joined.append(
                jnp.concatenate(
                    [
                        half[part]
                        for part in (slice(0, height), slice(height, None))
                        for half in (low_rows, high_rows)
                    ],
                    axis=0,
                )
            )
        return joined

    def whole(height):
        return pl.BlockSpec((height, 512), lambda i, sides: (0, 0))

    return list(
        pl.pallas_call(
            functools.partial(join_kernel, len(stripes)),
            grid_spec=pltpu.PrefetchScalarGridSpec(
                num_scalar_prefetch=1,
                grid=(1,),
                in_specs=[whole(2 * height) for height in heights for _ in range(2)],
                out_specs=[whole(4 * height) for height in heights],
            ),
            out_shape=[jax.ShapeDtypeStruct((4 * height, 512), jnp.bfloat16) for height in heights],
            compiler_params=pltpu.CompilerParams(vmem_limit_bytes=SUM_LIMIT),
            cost_estimate=pl.CostEstimate(
                flops=0, bytes_accessed=8 * 1024 * sum(heights), transcendentals=0
            ),
        )(
            jnp.stack([side(step) for step in steps]),
            *(rows for pair in zip(stripes, arrived) for rows in pair),
        )
    )


def tie(*groups):
    return lax.optimization_barrier(groups)


def step_orders():
    utt, seq = axis_bits("utt"), axis_bits("seq")
    across, line, rest = utt[1:], seq[:1], seq[1:]
    return (
        line + across + rest,
        across + rest + line,
        rest[:1] + line + across + rest[1:],
    )


def all_shared(copies):
    return lax.all_to_all(copies, ("utt", "seq"), 0, 0, tiled=True)


def from_neighbours(head, tail):
    count = lax.axis_size("seq")
    before = lax.ppermute(tail, "seq", [(i, i + 1) for i in range(count - 1)])
    behind = lax.ppermute(head, "seq", [(i + 1, i) for i in range(count - 1)])
    return before, behind


def pair_rows(mine, theirs, start=0, width=None):
    columns = slice(start, start + (width or mine.shape[1]))
    return jnp.concatenate([mine[:, columns], theirs[:, columns]], axis=0)


def outer(left, right):
    return low(matmul(left.T, right))


def put_half(outs, side_number, half, value):
    @pl.when(side_number == half)
    def _():
        outs[1][...] = value

    @pl.when(side_number != half)
    def _():
        outs[0][...] = value


def feed_blocks(refs, outs, sides):
    hidden, grad_pre, active, grad_low = (refs[2 * i : 2 * i + 2] for i in range(4))
    hidden_cols = pair_rows(*hidden).T
    grad_rows = pair_rows(*grad_low)
    for half in range(2):
        block = low(matmul(hidden_cols, pair_rows(*grad_pre, 512 * half, 512)))
        put_half(outs[:2], sides[1], half, block)
        block = outer(pair_rows(*active, 512 * half, 512), grad_rows)
        put_half(outs[2:4], sides[2], half, block)


def second_kernel(places, *refs):
    feed_blocks(refs[:8], refs[8:], places)


def mixer_blocks_kernel(places, *refs):
    refs, outs = refs[:12], refs[12:]
    mixer = outer(pair_rows(*refs[:2]), pair_rows(*refs[2:4]))
    branch = outer(pair_rows(*refs[4:6]), pair_rows(*refs[6:8]))
    attend = outer(pair_rows(*refs[8:10]), pair_rows(*refs[10:12]))
    for half in range(2):
        pieces = (
            mixer[256 * half : 256 * half + 256],
            branch[128 * half : 128 * half + 128],
            attend[128 * half : 128 * half + 128],
        )
        put_half(outs, places[3], half, jnp.concatenate(pieces, axis=0))


def turn_kernel(places, *refs):
    for number in range(3):
        mine, theirs, out = refs[2 * number], refs[2 * number + 1], refs[8 + number]
        rows = mine.shape[0]
        out[:, :rows] = mine[...].T
        out[:, rows:] = theirs[...].T
    refs[11][...] = add_low(refs[6][...], refs[7][...])


def late_kernel(
    keeping,
    places,
    hidden_cols,
    grad_pre,
    grad_pre_other,
    active_cols,
    grad_low,
    grad_low_other,
    attend_cols,
    attend_rows,
    attend_rows_other,
    position,
    *outs,
):
    step = pl.program_id(0)
    half = places[3] if keeping else 1 - places[3]

    def blocks(left, mine, theirs):
        return low(matmul(left[...], jnp.concatenate([mine[...], theirs[...]], axis=0)))

    @pl.when(step == 0)
    def _():
        outs[0][...] = blocks(hidden_cols, grad_pre, grad_pre_other)

    @pl.when(step == 1)
    def _():
        outs[1][...] = blocks(active_cols, grad_low, grad_low_other)

    @pl.when((step == 2) & (places[0] + half < 2))
    def _():
        outs[2][...] = blocks(attend_cols, attend_rows, attend_rows_other)

    @pl.when((step == 2) & (places[0] + half == 2))
    def _():
        outs[2][...] = position[...]


def late_blocks(keeping, places, cols, grad_pre, pair):
    hidden_cols, active_cols, attend_cols, position = cols
    rows = pair[0].shape[0]

    def half(p, stripe):
        return p[stripe] if keeping else 1 - p[stripe]

    def whole(shape):
        return pl.BlockSpec(shape, lambda i, p: (0, 0))

    def attend_column(i, p):
        return (0, jnp.where(p[0] == 0, 2 + half(p, 3), 4))

    block = (rows, 512)
    return list(
        pl.pallas_call(
            functools.partial(late_kernel, keeping),
            grid_spec=pltpu.PrefetchScalarGridSpec(
                num_scalar_prefetch=1,
                grid=(3,),
                in_specs=[
                    whole(hidden_cols.shape),
                    pl.BlockSpec(block, lambda i, p: (0, half(p, 1))),
                    pl.BlockSpec(block, lambda i, p: (0, half(p, 1))),
                    pl.BlockSpec((512, 2 * rows), lambda i, p: (half(p, 2), 0)),
                    pl.BlockSpec(block, lambda i, p: (0, 5)),
                    pl.BlockSpec(block, lambda i, p: (0, 5)),
                    whole(attend_cols.shape),
                    pl.BlockSpec(block, attend_column),
                    pl.BlockSpec(block, attend_column),
                    whole(position.shape),
                ],
                out_specs=[whole((512, 512))] * 3,
            ),
            out_shape=[jax.ShapeDtypeStruct((512, 512), jnp.bfloat16)] * 3,
            compiler_params=pltpu.CompilerParams(vmem_limit_bytes=SUM_LIMIT if keeping else VMEM_LIMIT),
            cost_estimate=pl.CostEstimate(
                flops=6 * 512 * 512 * 2 * rows, bytes_accessed=6 * 10**6, transcendentals=0
            ),
        )(
            places,
            hidden_cols,
            grad_pre,
            pair[1],
            active_cols,
            *pair,
            attend_cols,
            *pair,
            position,
        )
    )


def columns(pair, width, number, by_core=False):
    index = (lambda numbers: number + numbers[0]) if by_core else number
    return [Part(array, (array.shape[0], width), (0, index)) for array in pair]


def block_sums(kernel, places, stripes, operands):
    blocks = vmem_call(
        kernel,
        [((512, 512), jnp.bfloat16)] * (2 * stripes),
        (),
        [part for pair in operands for part in pair],
        cost=7 * 10**8 * stripes,
        numbers=(places,),
    )
    return blocks[::2], blocks[1::2]


def spread_kernel(places, first, second, third, *refs):
    feed_in, feed_out, mixer_in, mixer_out, attend_out, attend_in = refs[-14:-8]
    held, wide_rows = refs[-8:-5], refs[-5:-2]
    arrive, leave = refs[-2:]
    core, half = places[0], places[3]
    quarters = [pl.multiple_of(512 * (2 * core + places[1 + i]), 512) for i in range(3)]
    coming = []
    for part in range(2):
        for number, source in enumerate((first, second, third)):
            rows = pl.ds(512 * part, 512)
            coming.append(
                pltpu.make_async_copy(
                    source.at[rows], held[number].at[rows], arrive.at[3 * part + number]
                )
            )
    for copy in coming:
        copy.start()
    going = []
    for part in range(2):
        for number in range(3):
            coming[3 * part + number].wait()
            rows = pl.ds(512 * part, 512)
            wide_rows[number][rows, :] = wide(held[number][rows, :])
            layer = 1 - part
            if number == 0:
                targets = [(512, feed_in.at[layer, :, pl.ds(quarters[0], 512)])]
            elif number == 1:
                targets = [(512, feed_out.at[layer, pl.ds(quarters[1], 512)])]
            elif part == 1:
                targets = [(512, attend_in.at[2 * core + half])]
            else:
                tall = pl.ds(pl.multiple_of(256 * half, 256), 256)
                flat = pl.ds(pl.multiple_of(128 * (2 * core + half), 128), 128)
                side_columns = pl.ds(pl.multiple_of(512 * core, 512), 512)
                targets = [
                    (256, mixer_in.at[tall, side_columns]),
                    (128, mixer_out.at[flat]),
                    (128, attend_out.at[flat]),
                ]
            start = 512 * part
            for height, target in targets:
                copy = pltpu.make_async_copy(
                    wide_rows[number].at[pl.ds(start, height)], target, leave.at[len(going)]
                )
                copy.start()
                going.append(copy)
                start += height
    for copy in going:
        copy.wait()


def spread_blocks(places, stripes, shapes, bases):
    anywhere = pl.BlockSpec(memory_space=pl.ANY)
    return list(
        pl.pallas_call(
            spread_kernel,
            in_specs=[pl.BlockSpec(memory_space=pltpu.SMEM)] + [anywhere] * (3 + len(bases)),
            out_specs=[anywhere] * len(shapes),
            out_shape=[jax.ShapeDtypeStruct(shape, jnp.float32) for shape in shapes],
            scratch_shapes=[pltpu.VMEM((1024, 512), jnp.bfloat16)] * 3
            + [pltpu.VMEM((1024, 512), jnp.float32)] * 3
            + [pltpu.SemaphoreType.DMA((6,)), pltpu.SemaphoreType.DMA((8,))],
            input_output_aliases={4 + n: n for n in range(len(bases))},
            compiler_params=pltpu.CompilerParams(vmem_limit_bytes=VMEM_LIMIT),
            cost_estimate=pl.CostEstimate(
                flops=1024, bytes_accessed=1024, transcendentals=0
            ),
        )(places, *stripes, *bases)
    )


def angle_tables(frame_count, features):
    halves = jnp.arange(features // 2, dtype=jnp.int32).astype(jnp.float32)
    frequencies = jnp.exp(halves * (-2.0 * math.log(10000.0) / features))
    fine = 32
    low_angles = jnp.arange(fine, dtype=jnp.int32).astype(jnp.float32)[:, None] * frequencies
    high_angles = (fine * jnp.arange(frame_count // fine, dtype=jnp.int32)).astype(jnp.float32)[
        :, None
    ] * frequencies
    low_sin, low_cos = jnp.sin(low_angles)[None], jnp.cos(low_angles)[None]
    high_sin, high_cos = jnp.sin(high_angles)[:, None], jnp.cos(high_angles)[:, None]
    sines = high_sin * low_cos + high_cos * low_sin
    cosines = high_cos * low_cos - high_sin * low_sin
    shape = (frame_count, features // 2)
    return sines.reshape(shape), cosines.reshape(shape)


def heads_out(blocks, groups):
    return lax.all_to_all(jnp.tile(blocks, (groups, 1, 1)), "seq", 0, 0, tiled=True)


def rows_dot(first_operand, second_operand):
    return lax.dot_general(
        first_operand, second_operand, (((1,), (1,)), ((), ())), preferred_element_type=jnp.float32
    )


def lane_side(shape, utterance):
    return (lax.broadcasted_iota(jnp.int32, shape, 1) // HEAD_DIM) == utterance


def turned_queries(content, shift, weight, sines, cosines):
    offset = (content.astype(jnp.float32) + shift).astype(jnp.bfloat16)
    half = sines.shape[1]
    spread = jnp.dot(offset, weight, preferred_element_type=jnp.float32)
    sin_part, cos_part = spread[:, :half], spread[:, half:]
    return (
        offset,
        (sin_part * sines + cos_part * cosines).astype(jnp.bfloat16),
        (cos_part * sines - sin_part * cosines).astype(jnp.bfloat16),
    )


def attend_kernel(
    limits,
    content,
    keys,
    values,
    shift,
    weight,
    sines,
    cosines,
    table,
    weights_out,
    attended_out,
    held,
    scores,
):
    scale = HEAD_DIM ** (-0.5)
    weight_rows = jnp.concatenate([weight[...]] * limits.shape[0], axis=0)
    content_rows = content[...]
    key_side = jnp.concatenate([table[...], keys[...]], axis=1)
    places = lax.broadcasted_iota(jnp.int32, (1, table.shape[0]), 1)
    attended = None
    for utterance in range(limits.shape[0]):
        ours = lane_side(content_rows.shape, utterance)
        mine = jnp.where(ours, content_rows, jnp.zeros_like(content_rows))
        moved = jnp.where(ours, shift[...], 0.0)
        _, turned_cos, turned_sin = turned_queries(
            mine, moved, weight_rows, sines[...], cosines[...]
        )
        query_side = jnp.concatenate([turned_cos, turned_sin, mine], axis=1) * scale
        scores[utterance] = rows_dot(query_side.astype(jnp.bfloat16), key_side)
    for utterance in range(limits.shape[0]):
        allowed = places < limits[utterance]
        for start in range(0, scores.shape[1], ROW_TILE):
            rows = slice(start, start + ROW_TILE)
            tile = jnp.where(allowed, scores[utterance, rows, :], -1000000000.0)
            raised = jnp.exp(tile - jnp.max(tile, axis=1, keepdims=True))
            totals = jnp.sum(raised, axis=1, keepdims=True)
            weights_out[utterance, rows, :] = low(raised * (1.0 / totals))
    for utterance in range(limits.shape[0]):
        ours = lane_side(content_rows.shape, utterance)
        part = matmul(weights_out[utterance], values[...])
        attended = part if attended is None else jnp.where(ours, part, attended)
    if held is None:
        attended_out[...] = attended.astype(jnp.bfloat16)
        return
    step = pl.program_id(0)
    height = attended.shape[0]
    block = attended_out.shape[1] - 2 * HALO
    held[pl.ds(pl.multiple_of(HALO + step * height, 8), height), :] = attended
    for number in range(height // block):
        attended_out[step * (height // block) + number, 0:block, :] = attended[
            number * block : (number + 1) * block
        ].astype(jnp.bfloat16)

    @pl.when(step == pl.num_programs(0) - 1)
    def _():
        edge = jnp.zeros((HALO, held.shape[1]), jnp.float32)
        held[0:HALO, :] = edge
        held[held.shape[0] - HALO :, :] = edge
        for number in range(attended_out.shape[0]):
            start = number * block
            sides = jnp.concatenate(
                [
                    held[start : start + HALO, :],
                    held[start + HALO + block : start + 2 * HALO + block, :],
                ],
                axis=0,
            )
            attended_out[number, block:, :] = sides.astype(jnp.bfloat16)


def attend_back_kernel(
    weights,
    content,
    grads,
    keys,
    values,
    shift,
    weight,
    sines,
    cosines,
    table,
    *outs,
):
    step = pl.program_id(0)
    *outs, grad_probs, grad_scores = outs
    query_out, pairs_out, weight_out, sums_out, key_sums, value_sums = (
        [None] * (6 - len(outs)) + outs
    )
    scale = HEAD_DIM ** (-0.5)

    @pl.when(step == 0)
    def _():
        key_sums[...] = jnp.zeros_like(key_sums)
        value_sums[...] = jnp.zeros_like(value_sums)
        weight_out[...] = jnp.zeros_like(weight_out)
        sums_out[...] = jnp.zeros_like(sums_out)

    weight_rows = jnp.concatenate([weight[...]] * weights.shape[0], axis=0)
    content_rows, grad_rows = content[...], grads[...]
    content_cols = content_rows.T
    grad_cols = grad_rows.T
    key_side = jnp.concatenate([table[...], keys[...]], axis=1)
    half = sines.shape[1]
    grad_content = grad_position = None
    for utterance in range(weights.shape[0]):
        ours = lane_side(content_rows.shape, utterance)
        grad_mine = jnp.where(ours, grad_rows, jnp.zeros_like(grad_rows)) * scale
        grad_probs[utterance] = rows_dot(grad_mine.astype(jnp.bfloat16), values[...])
    for utterance in range(weights.shape[0]):
        first, last = utterance * HEAD_DIM, (utterance + 1) * HEAD_DIM
        ours = lane_side(content_rows.shape, utterance)
        probs = weights[utterance]
        for start in range(0, grad_probs.shape[1], ROW_TILE):
            rows = slice(start, start + ROW_TILE)
            tile = wide(weights[utterance, rows, :])
            product = tile * grad_probs[utterance, rows, :]
            inner = jnp.sum(product, axis=1, keepdims=True)
            grad_scores[utterance, rows, :] = low(product - tile * inner)
        value_sums[first:last, :] += jnp.dot(
            grad_cols[first:last, :], probs, preferred_element_type=jnp.float32
        )
        key_sums[first:last, :] += jnp.dot(
            content_cols[first:last, :], grad_scores[utterance], preferred_element_type=jnp.float32
        )
        grad_side = matmul(grad_scores[utterance], key_side)
        grad_cos_table = grad_side[:, :half]
        grad_sin_table = grad_side[:, half : 2 * half]
        from_table = jnp.concatenate(
            [
                grad_cos_table * sines[...] - grad_sin_table * cosines[...],
                grad_cos_table * cosines[...] + grad_sin_table * sines[...],
            ],
            axis=1,
        ).astype(jnp.bfloat16)
        offset = (content_rows.astype(jnp.float32) + shift[...]).astype(jnp.bfloat16)
        weight_out[...] += jnp.dot(
            offset.T[first:last, :], from_table, preferred_element_type=jnp.float32
        )
        content_part = grad_side[:, 2 * half :]
        position_part = rows_dot(from_table, weight_rows)
        if grad_content is None:
            grad_content, grad_position = content_part, position_part
        else:
            grad_content = jnp.where(ours, content_part, grad_content)
            grad_position = jnp.where(ours, position_part, grad_position)
    grad_query = (grad_content + grad_position).astype(jnp.bfloat16)
    height, lanes = grad_query.shape
    if query_out is None:
        pairs_out[pl.ds(pl.multiple_of(step * height, 16), height), 0:lanes] = grad_query
    else:
        query_out[...] = grad_query
    sums_out[0:1, :] += jnp.sum(grad_content, axis=0, keepdims=True)
    sums_out[1:2, :] += jnp.sum(grad_position, axis=0, keepdims=True)

    @pl.when(step == pl.num_programs(0) - 1)
    def _():
        first = pairs_out.shape[1] - 2 * lanes
        pairs_out[:, first : first + lanes] = key_sums[...].T.astype(jnp.bfloat16)
        pairs_out[:, first + lanes :] = value_sums[...].T.astype(jnp.bfloat16)


def query_block(frames_all, most=256):
    return most if frames_all <= 1024 else 128


def whole_block(shape):
    return pl.BlockSpec(shape, lambda i: (0,) * len(shape))


def row_block(height, width):
    return pl.BlockSpec((height, width), lambda i: (i, 0))


def attend_heads(limits, content, arrived, shift, weight, sines, cosines, table, block):
    utterances = limits.shape[0]
    query_frames, lanes = content.shape[0], arrived.shape[1] // 3
    frames_all, table_width = table.shape
    height = query_block(frames_all)
    chunked = query_frames == frames_all and height % block == 0
    chunks = (frames_all // block, block + 2 * HALO, lanes)
    kernel = attend_kernel
    if not chunked:
        kernel = lambda *refs: attend_kernel(*refs[:-1], None, refs[-1])
    return pl.pallas_call(
        kernel,
        grid=(query_frames // height,),
        in_specs=[
            pl.BlockSpec(memory_space=pltpu.SMEM),
            row_block(height, lanes),
            pl.BlockSpec((frames_all, lanes), lambda i: (0, 1)),
            pl.BlockSpec((frames_all, lanes), lambda i: (0, 2)),
            whole_block(shift.shape),
            whole_block(weight.shape),
            row_block(height, sines.shape[1]),
            row_block(height, sines.shape[1]),
            whole_block(table.shape),
        ],
        out_specs=[
            pl.BlockSpec((utterances, height, frames_all), lambda i: (0, i, 0)),
            whole_block(chunks) if chunked else row_block(height, lanes),
        ],
        out_shape=[
            jax.ShapeDtypeStruct((utterances, query_frames, frames_all), jnp.bfloat16),
            jax.ShapeDtypeStruct(chunks if chunked else (query_frames, lanes), jnp.bfloat16),
        ],
        scratch_shapes=[pltpu.VMEM((frames_all + 2 * HALO, lanes), jnp.float32)] * chunked
        + [pltpu.VMEM((utterances, height, frames_all), jnp.float32)],
        compiler_params=pltpu.CompilerParams(vmem_limit_bytes=VMEM_LIMIT),
        cost_estimate=pl.CostEstimate(
            flops=2 * utterances * query_frames * frames_all * (table_width + 256),
            bytes_accessed=2 * utterances * query_frames * frames_all,
            transcendentals=utterances * query_frames * frames_all,
        ),
    )(limits, content, arrived, arrived, shift, weight, sines, cosines, table)


def attend_heads_back(
    weights, content, grads, arrived, shift, weight, sines, cosines, table
):
    utterances, query_frames, frames_all = weights.shape
    lanes = arrived.shape[1] // 3
    height = query_block(frames_all)
    joined = query_frames == frames_all
    width = (3 if joined else 2) * lanes
    return pl.pallas_call(
        attend_back_kernel,
        grid=(query_frames // height,),
        in_specs=[
            pl.BlockSpec((utterances, height, frames_all), lambda i: (0, i, 0)),
            row_block(height, lanes),
            row_block(height, lanes),
            pl.BlockSpec((frames_all, lanes), lambda i: (0, 1)),
            pl.BlockSpec((frames_all, lanes), lambda i: (0, 2)),
            whole_block(shift.shape),
            whole_block(weight.shape),
            row_block(height, sines.shape[1]),
            row_block(height, sines.shape[1]),
            whole_block(table.shape),
        ],
        out_specs=([] if joined else [row_block(height, lanes)])
        + [
            whole_block((frames_all, width)),
            whole_block((HEAD_DIM, table.shape[1])),
            whole_block((8, lanes)),
        ],
        out_shape=(
            [] if joined else [jax.ShapeDtypeStruct((query_frames, lanes), jnp.bfloat16)]
        )
        + [
            jax.ShapeDtypeStruct((frames_all, width), jnp.bfloat16),
            jax.ShapeDtypeStruct((HEAD_DIM, table.shape[1]), jnp.float32),
            jax.ShapeDtypeStruct((8, lanes), jnp.float32),
        ],
        scratch_shapes=[
            pltpu.VMEM((lanes, frames_all), jnp.float32),
            pltpu.VMEM((lanes, frames_all), jnp.float32),
            pltpu.VMEM((utterances, height, frames_all), jnp.float32),
            pltpu.VMEM((utterances, height, frames_all), jnp.bfloat16),
        ],
        compiler_params=pltpu.CompilerParams(vmem_limit_bytes=VMEM_LIMIT),
        cost_estimate=pl.CostEstimate(
            flops=2 * utterances * query_frames * frames_all * (table.shape[1] + 512),
            bytes_accessed=2 * utterances * query_frames * frames_all,
            transcendentals=0,
        ),
    )(weights, content, grads, arrived, arrived, shift, weight, sines, cosines, table)


def shards(
    frames,
    lengths,
    out_grad,
    norm_gain,
    norm_bias,
    feed_in,
    feed_in_bias,
    feed_out,
    feed_out_bias,
    attend_in,
    attend_vectors,
    attend_out,
    mixer_in,
    mixer_in_bias,
    depthwise,
    mixer_vectors,
    mixer_out,
    batch_gain,
    batch_shift,
    running_mean,
    running_variance,
):
    utt_rows, block_frames, features = frames.shape
    rows = utt_rows * block_frames
    seq_count = lax.axis_size("seq")
    seq_index = lax.axis_index("seq")
    count = lax.axis_size("utt") * seq_count
    frames_all = block_frames * seq_count
    groups = seq_count // HEADS
    head, group = seq_index % HEADS, seq_index // HEADS
    query_frames = frames_all // groups
    lanes = utt_rows * HEAD_DIM
    info = jnp.concatenate(
        [(seq_index * block_frames).reshape(1), lengths, jnp.full((1,), frames_all, jnp.int32)]
    )
    hidden_units = feed_in.shape[2]
    f32, bf16 = jnp.float32, jnp.bfloat16
    flat_frames = frames.reshape(rows, features)
    square, broad = (rows, features), (rows, hidden_units)
    extended = (utt_rows * (block_frames + 2 * HALO), features)
    row_flops = 2 * rows * features
    bind = functools.partial
    edge = ((utt_rows, 2 * HALO, features), f32)
    feed_scratch = [
        pltpu.VMEM((features, hidden_units), bf16),
        pltpu.VMEM((hidden_units, features), bf16),
    ]
    attend_scratch = pltpu.VMEM((3, features, features), bf16)
    (
        edge_head,
        edge_tail,
        after_first,
        slope_first,
        entry_pack,
        sent,
    ) = vmem_call(
        bind(entry_kernel, utt_rows),
        [
            edge,
            edge,
            (square, f32),
            (broad, bf16),
            ((rows, hidden_units + 2 * features), bf16),
            ((HEADS, block_frames, 3 * lanes), bf16),
        ],
        (),
        (
            flat_frames,
            norm_gain,
            norm_bias,
            feed_in_bias,
            feed_out_bias,
            attend_vectors,
            Part(out_grad, (utt_rows, HALO, features), (0, 0, 0)),
            Part(out_grad, (utt_rows, HALO, features), (0, block_frames // HALO - 1, 0)),
        ),
        scratch=feed_scratch + [attend_scratch, pltpu.SemaphoreType.DMA((3,))],
        cost=row_flops * (2 * hidden_units + 3 * features),
        held=(feed_in, feed_out, attend_in),
    )
    sent, all_limits, edge_head, edge_tail = tie(sent, lengths, edge_head, edge_tail)
    before, behind = from_neighbours(edge_head, edge_tail)
    arrived = heads_out(sent, groups)
    for step in axis_bits("utt"):
        all_limits = jnp.concatenate([all_limits, swap(all_limits, step)])
    arrived, all_limits = tie(arrived, all_limits)
    arrived = arrived.reshape(frames_all, 3 * lanes)
    start_query = group * query_frames
    head_content = arrived
    if groups > 1:
        head_content = lax.dynamic_slice_in_dim(arrived, start_query, query_frames, 0)
    head_vectors = lax.dynamic_slice_in_dim(
        attend_vectors.astype(f32), head * HEAD_DIM, HEAD_DIM, 1
    )
    head_shift = jnp.tile((head_vectors[4] - head_vectors[3])[None], (1, utt_rows))
    head_weight = lax.dynamic_slice_in_dim(attend_in[3], head * HEAD_DIM, HEAD_DIM, 1).reshape(
        features // 2, 2, HEAD_DIM
    )
    head_weight = jnp.transpose(head_weight, (2, 1, 0)).reshape(HEAD_DIM, features)
    sines, cosines = angle_tables(frames_all, features)
    key_table = jnp.concatenate([cosines, sines], axis=1).astype(bf16)
    query_sin = lax.dynamic_slice_in_dim(sines, start_query, query_frames, 0)
    query_cos = lax.dynamic_slice_in_dim(cosines, start_query, query_frames, 0)
    weights, head_attended = attend_heads(
        lengths,
        head_content,
        arrived,
        head_shift,
        head_weight,
        query_sin,
        query_cos,
        key_table,
        block_frames,
    )

    def frames_back(blocks):
        width = blocks.shape[-1]
        blocks = blocks.reshape(1, HEADS, block_frames, width)
        if groups > 1:
            blocks = lax.dynamic_update_slice_in_dim(
                jnp.zeros((groups,) + blocks.shape[1:], blocks.dtype), blocks, group, 0
            )
        blocks = lax.all_to_all(
            blocks.reshape(seq_count, block_frames, width), "seq", 0, 0, tiled=True
        ).reshape(groups, HEADS, block_frames, width)
        return lax.dynamic_slice_in_dim(blocks, group, 1, 0)[0]

    head_attended, before, behind = tie(head_attended, before, behind)
    after_sides, grad_sides = vmem_call(
        sides_kernel,
        [((2 * utt_rows * HALO, features), f32)] * 2,
        (),
        (before, behind, norm_gain, norm_bias, feed_in_bias, feed_out_bias),
        scratch=feed_scratch + [pltpu.SemaphoreType.DMA((2,))],
        cost=row_flops * 2 * hidden_units // 4,
        held=(feed_in, feed_out),
    )
    if head_attended.ndim == 2:
        placed = lax.dynamic_update_slice_in_dim(
            jnp.zeros((frames_all + 2 * HALO, lanes), bf16), head_attended, HALO + start_query, 0
        )
        main, before, behind = (
            placed[start : start + frames_all].reshape(seq_count, block_frames, lanes)
            for start in (HALO, 0, 2 * HALO)
        )
        head_attended = jnp.concatenate([main, before[:, :HALO], behind[:, -HALO:]], axis=1)
    attended_blocks = lax.all_to_all(head_attended, "seq", 0, 0, tiled=True)
    attended_blocks, after_sides, grad_sides = tie(attended_blocks, after_sides, grad_sides)
    if groups > 1:
        attended_blocks = jnp.sum(
            attended_blocks.reshape((groups, HEADS) + attended_blocks.shape[1:]), axis=0
        )
    taps = depthwise.T
    padded = pltpu.VMEM((utt_rows, block_frames + 2 * HALO + 16, features), f32)
    (
        after_attend,
        mixer_pack,
        linear_half,
        gate_half,
        gated,
        convolved,
        shared,
    ) = vmem_call(
        bind(mixer_kernel, utt_rows),
        [
            (extended, f32),
            ((rows, 2 * features), bf16),
            (square, f32),
            (square, f32),
            (extended, bf16),
            (extended, f32),
            ((8 * count, 128), f32),
        ],
        (info,),
        (
            attended_blocks,
            after_first,
            after_sides,
            norm_gain,
            norm_bias,
            attend_out,
            attend_vectors,
            mixer_in,
            mixer_in_bias.reshape(1, -1),
            taps,
            mixer_vectors,
        ),
        scratch=(padded,),
        cost=row_flops * 3 * features,
    )
    (
        layer_output,
        grad_mixer,
        grad_batch,
        normed_batch,
        second_pack,
        shared,
        batch_rows,
        middle_rows,
    ) = vmem_call(
        bind(middle_kernel, utt_rows, seq_count),
        [
            (square, f32),
            (square, f32),
            (extended, f32),
            (extended, f32),
            ((rows, 2 * hidden_units + 4 * features), bf16),
            ((8 * count, 128), f32),
            ((8, features), f32),
            ((16, features), f32),
        ],
        (all_limits, lax.axis_index("utt").reshape(1)),
        (
            convolved,
            all_shared(shared),
            after_attend,
            out_grad.reshape(rows, features),
            grad_sides,
            norm_gain,
            norm_bias,
            batch_gain.reshape(1, -1),
            batch_shift.reshape(1, -1),
            running_mean.reshape(1, -1),
            running_variance.reshape(1, -1),
            mixer_out,
            mixer_vectors,
            feed_in_bias,
            feed_out_bias,
        ),
        scratch=feed_scratch + [pltpu.SemaphoreType.DMA((2,))],
        cost=row_flops * (4 * hidden_units + 2 * features),
        held=(feed_in, feed_out),
    )
    phases = list(zip(*step_orders()))
    near = axis_bits("utt")[0]
    core = side(near).reshape(1)
    halves = jnp.stack([side(step) for step in phases[0]])
    places = jnp.concatenate([core, halves])
    half_units, half_features = hidden_units // 2, features // 2

    def with_pair(array):
        return [array, swap(array, near)]

    second_pair = with_pair(second_pack)
    second_sent, second_kept = block_sums(
        second_kernel,
        places,
        2,
        [
            columns(second_pair, features, 8),
            columns(second_pair, half_units, 0, True),
            columns(second_pair, half_units, 2, True),
            columns(second_pair, features, 9),
        ],
    )
    other_places = [
        jnp.concatenate([near_core, near_halves])
        for near_halves in (halves, 1 - halves)
        for near_core in (core, 1 - core)
    ][1:]
    second_pair, second_sent, second_kept, shared, other_places = tie(
        second_pair, second_sent, second_kept, all_shared(shared), other_places
    )
    (
        batch_grads,
        grad_attend,
        mixer_back_pack,
        grad_blocks,
        mixer_rows,
    ) = vmem_call(
        bind(mixer_back_kernel, utt_rows),
        [
            ((8, features), f32),
            (square, f32),
            ((rows, 3 * features), bf16),
            ((HEADS, block_frames, lanes), bf16),
            ((16, features), f32),
        ],
        (info,),
        (
            grad_batch,
            normed_batch,
            shared,
            batch_rows,
            batch_gain.reshape(1, -1),
            gated,
            linear_half,
            gate_half,
            grad_mixer,
            after_attend,
            norm_gain,
            taps,
            mixer_in,
            attend_out,
        ),
        scratch=(padded, padded),
        cost=row_flops * 4 * features,
    )
    mixer_pair, mixer_back_pair = with_pair(mixer_pack), with_pair(mixer_back_pack)
    third_sent, third_kept = block_sums(
        mixer_blocks_kernel,
        places,
        1,
        [
            columns(mixer_pair, features, 1),
            columns(mixer_back_pair, features, 0, True),
            columns(second_pair, half_features, 20, True),
            columns(second_pair, features, 11),
            columns(mixer_pair, half_features, 0, True),
            columns(mixer_back_pair, features, 2),
        ],
    )
    early_sent, early_kept = second_sent + third_sent, second_kept + third_kept
    early_arrived = swap_all(early_sent, phases[0])
    head_grad = heads_out(grad_blocks, groups).reshape(frames_all, lanes)
    if groups > 1:
        head_grad = lax.dynamic_slice_in_dim(head_grad, start_query, query_frames, 0)
    head_grad, early_kept = tie(head_grad, early_kept)
    *head_grads, head_weight_grad, head_sums = attend_heads_back(
        weights,
        head_content,
        head_grad,
        arrived,
        head_shift,
        head_weight,
        query_sin,
        query_cos,
        key_table,
    )
    head_grads, head_weight_grad, head_sums, early_arrived = tie(
        head_grads, head_weight_grad, head_sums, early_arrived
    )
    grad_blocks = head_grads[-1].reshape(seq_count, block_frames, -1)
    returned = lax.all_to_all(grad_blocks, "seq", 0, 0, tiled=True)
    if groups > 1:
        returned = jnp.sum(
            returned.astype(f32).reshape(groups, HEADS, block_frames, 2 * lanes), axis=0
        ).astype(bf16)
        returned = jnp.concatenate([frames_back(head_grads[0]), returned], axis=2)
    head_vector_grads = lax.dynamic_update_slice_in_dim(
        jnp.zeros((8, features), f32),
        jnp.sum(head_sums.reshape(8, utt_rows, HEAD_DIM), axis=1),
        head * HEAD_DIM,
        1,
    )
    early_sent, early_kept = fold_rows([(early_kept, early_arrived)], phases[1], 1, VMEM_LIMIT)
    early_sent, head_weight_grad = tie(early_sent, head_weight_grad)
    early_arrived = swap_all(early_sent, phases[1])
    head_weight_grad = jnp.transpose(
        head_weight_grad.reshape(HEAD_DIM, 2, features // 2), (2, 1, 0)
    ).reshape(features, HEAD_DIM)
    position_weight_grad = lax.dynamic_update_slice_in_dim(
        jnp.zeros((features, features), f32), head_weight_grad, head * HEAD_DIM, 1
    )
    entry_pair = with_pair(entry_pack)
    position_pair = with_pair(position_weight_grad.astype(bf16))
    entry_cols = vmem_call(
        turn_kernel,
        [
            ((features, 2 * rows), bf16),
            ((half_units, 2 * rows), bf16),
            ((features, 2 * rows), bf16),
            ((features, features), bf16),
        ],
        (),
        columns(entry_pair, features, 4)
        + columns(entry_pair, half_units, 0, True)
        + columns(entry_pair, features, 5)
        + position_pair,
        numbers=(places,),
    )
    returned, early_arrived, entry_cols = tie(returned, early_arrived, entry_cols)
    (
        frames_grad,
        entry_back_pack,
        grad_pre_first,
        entry_rows,
    ) = vmem_call(
        entry_back_kernel,
        [
            (square, f32),
            ((rows, half_units + 4 * features), bf16),
            ((rows, half_units), bf16),
            ((16, features), f32),
        ],
        (core,),
        (
            returned,
            grad_attend,
            flat_frames,
            after_first,
            slope_first,
            norm_gain,
        ),
        scratch=feed_scratch + [attend_scratch, pltpu.SemaphoreType.DMA((3,))],
        cost=row_flops * (2 * hidden_units + 3 * features),
        held=(feed_in, feed_out, attend_in),
    )
    late_factors = (entry_cols, grad_pre_first, with_pair(entry_back_pack))
    late_sent = late_blocks(False, places, *late_factors)
    late_sent, late_factors, middle_rows = tie(late_sent, late_factors, middle_rows)
    late_arrived = swap_all(late_sent, phases[0])
    late_kept = late_blocks(True, places, *late_factors)
    flat = jnp.concatenate([middle_rows, mixer_rows, entry_rows, head_vector_grads], axis=0)
    flat_steps = [near] + [steps[0] for steps in phases]
    def in_turn(arrived_rows, steps, work):
        nonlocal flat
        flat_arrived = swap(flat, flat_steps.pop()) if flat_steps else jnp.zeros_like(flat)
        after, next_arrived = None, []
        for i, rows in enumerate(arrived_rows):
            if after is not None:
                rows, _ = tie(rows, after)
            if i == len(arrived_rows) - 1:
                rows, flat_arrived = tie(rows, flat_arrived)
            after = work(i, rows)
            next_arrived.append(swap(after, steps[i]) if steps else after)
        flat = flat + flat_arrived
        return next_arrived

    late_kept = list(late_kept)
    for steps in phases[1:]:

        def fold(i, rows):
            pairs = [([late_kept[i]], [rows])]
            if steps is phases[2]:
                pairs = [([early_kept[i]], [early_arrived[i]])] + pairs
            parts = 1 if steps in phases[1:3] else 2
            (sent_rows,), (late_kept[i],) = fold_rows(pairs, [steps[i]], parts)
            return sent_rows

        late_arrived = in_turn(late_arrived, steps, fold)
    sums = [None] * len(late_arrived)

    def add(i, rows):
        (sums[i],) = add_rows([late_kept[i]], [rows])
        return sums[i]

    arrived_rows = in_turn(late_arrived, phases[-1], add)
    for number in range(len(phases) - 1, 0, -1):

        def join(i, rows):
            (sums[i],) = join_rows([sums[i]], [rows], [phases[number][i]])
            return sums[i]

        arrived_rows = in_turn(arrived_rows, phases[number - 1], join)
    for step in flat_steps:
        flat = flat + swap(flat, step)
    vector_grads = vmem_call(
        vectors_kernel,
        [
            (norm_gain.shape, f32),
            (norm_bias.shape, f32),
            (feed_in_bias.shape, f32),
            (feed_out_bias.shape, f32),
            (attend_vectors.shape, f32),
            ((1, 2 * features), f32),
            (mixer_vectors.shape, f32),
            ((KERNEL, features), f32),
        ],
        (),
        (flat,),
    )
    vector_grads = list(vector_grads)
    vector_grads[5] = vector_grads[5].reshape(-1)
    vector_grads[7] = vector_grads[7].T
    vector_grads = [*vector_grads, batch_grads[1], batch_grads[0], batch_rows[2], batch_rows[3]]
    across_rows = swap_all(sums, [near] * 3)
    shapes = [feed_in.shape, feed_out.shape, mixer_in.shape, mixer_out.shape]
    shapes += [attend_out.shape, attend_in.shape]
    spread = spread_blocks(places, sums, shapes, [])
    spread = spread_blocks(other_places[0], across_rows, shapes, spread)
    spread, arrived_rows, vector_grads = tie(spread, arrived_rows, vector_grads)
    across_rows = swap_all(arrived_rows, [near] * 3)
    spread = spread_blocks(other_places[1], arrived_rows, shapes, spread)
    (
        feed_in_grad,
        feed_out_grad,
        mixer_in_grad,
        mixer_out_grad,
        attend_out_grad,
        attend_in_grad,
    ) = spread_blocks(other_places[2], across_rows, shapes, spread)
    (
        norm_gain_grad,
        norm_bias_grad,
        feed_in_bias_grad,
        feed_out_bias_grad,
        attend_vectors_grad,
        mixer_in_bias_grad,
        mixer_vectors_grad,
        taps_grad,
        batch_gain_grad,
        batch_shift_grad,
        new_mean,
        new_variance,
    ) = vector_grads
    return (
        layer_output.reshape(frames.shape),
        frames_grad.reshape(frames.shape),
        norm_gain_grad,
        norm_bias_grad,
        feed_in_grad,
        feed_in_bias_grad,
        feed_out_grad,
        feed_out_bias_grad,
        attend_in_grad,
        attend_vectors_grad,
        attend_out_grad,
        mixer_in_grad,
        mixer_in_bias_grad,
        taps_grad,
        mixer_vectors_grad,
        mixer_out_grad,
        batch_gain_grad,
        batch_shift_grad,
        new_mean,
        new_variance,
    )


def solution(mesh):
    return jax.shard_map(
        shards,
        mesh=mesh,
        in_specs=(
            P("utt", "seq", None),
            P("utt"),
            P("utt", "seq", None),
            P(),
            P(),
            P(),
            P(),
            P(),
            P(),
            P(),
            P(),
            P(),
            P(),
            P(),
            P(),
            P(),
            P(),
            P(),
            P(),
            P(),
            P(),
        ),
        out_specs=(
            P("utt", "seq", None),
            P("utt", "seq", None),
            P(),
            P(),
            P(),
            P(),
            P(),
            P(),
            P(),
            P(),
            P(),
            P(),
            P(),
            P(),
            P(),
            P(),
            P(),
            P(),
            P(),
            P(),
        ),
        check_vma=False,
    )
```

```python
import functools
import math

import jax
import jax.numpy as jnp
import numpy as np
from jax import lax
from jax.experimental import pallas as pl
from jax.experimental.pallas import tpu as pltpu
from jax.sharding import PartitionSpec as P

HEADS = 8
KERNEL = 9
HEAD_DIM = 64


TOP_PRECISION = lax.Precision.HIGHEST
EPSILON = 1e-05
VMEM_LIMIT = 64 * 1024 * 1024
SUM_LIMIT = 20 * 1024 * 1024
HALO = 8
ROW_TILE = 32
AHEAD = 13


def wide(values):
    return values.astype(jnp.float32)


def low(values):
    return values.astype(jnp.bfloat16)


def matmul(first_operand, second_operand):
    return jnp.dot(first_operand, second_operand, preferred_element_type=jnp.float32)


def column_sum(values):
    return jnp.sum(wide(values), axis=0, keepdims=True)


def normalize(values):
    average = jnp.mean(values, axis=-1, keepdims=True)
    centered = values - average
    spread = jnp.mean(centered * centered, axis=-1, keepdims=True)
    inverse = lax.rsqrt(spread + EPSILON)
    return centered * inverse, inverse


def scaled_norm(normed, gains, biases, number):
    return normed * wide(gains[number : number + 1, :]) + wide(biases[number : number + 1, :])


def norm_back(grad_rows, normed, inverse, gains, number, own=lambda values: values):
    scaled = grad_rows * wide(gains[number : number + 1, :])
    inner = (
        scaled
        - jnp.mean(scaled, axis=-1, keepdims=True)
        - normed * jnp.mean(scaled * normed, axis=-1, keepdims=True)
    )
    return inner * inverse, column_sum(own(grad_rows * normed)), column_sum(own(grad_rows))


def logistic(values):
    return 1.0 / (1.0 + jnp.exp(-values))


def silu_slope(preact, sigmoid):
    return sigmoid * (1.0 + preact * (1.0 - sigmoid))


def frame_places(info, rows, utterances, halo):
    own = rows - 2 * utterances * halo
    per = own // utterances
    row = lax.broadcasted_iota(jnp.int32, (rows, 1), 0)
    aside = row - own
    owner = jnp.where(aside < 0, row // per, aside // (2 * halo))
    near = aside % (2 * halo)
    place = jnp.where(aside < 0, row % per, near - halo + jnp.where(near < halo, 0, per))
    limit = jnp.full((rows, 1), info[utterances], jnp.int32)
    for utterance in range(utterances - 1):
        limit = jnp.where(owner == utterance, info[1 + utterance], limit)
    return info[0] + place, limit


def flags(condition):
    return jnp.where(condition, 1.0, 0.0)


def own_rows(values, utterances):
    return values[: values.shape[0] - 2 * utterances * HALO]


def with_sides(values, sides):
    return jnp.concatenate([values, sides], axis=0)


def blocks_of_heads(rows, utterances):
    per = rows.shape[0] // utterances
    first = lax.broadcasted_iota(jnp.int32, (per, 2 * HEAD_DIM), 1) < HEAD_DIM
    blocks = []
    for pair in range(HEADS // 2):
        columns = rows[:, pair * 2 * HEAD_DIM : (pair + 1) * 2 * HEAD_DIM]
        top, bottom = columns[:per], columns[per:]
        blocks.append(jnp.where(first, top, pltpu.roll(bottom, HEAD_DIM, 1)))
        blocks.append(jnp.where(first, pltpu.roll(top, HEAD_DIM, 1), bottom))
    return blocks


def rows_of_heads(blocks):
    per = blocks[0].shape[0]
    first = lax.broadcasted_iota(jnp.int32, (per, 2 * HEAD_DIM), 1) < HEAD_DIM
    columns = []
    for pair in range(HEADS // 2):
        left, right = blocks[2 * pair], blocks[2 * pair + 1]
        top = jnp.where(first, left, pltpu.roll(right, HEAD_DIM, 1))
        bottom = jnp.where(first, pltpu.roll(left, HEAD_DIM, 1), right)
        columns.append(jnp.concatenate([top, bottom], axis=0))
    return jnp.concatenate(columns, axis=1)


def whole_array(shape):
    return pl.BlockSpec(shape, lambda i: (0,) * len(shape))


class Part:
    def __init__(self, array, block, index):
        self.array, self.block, self.index = array, block, index

    def spec(self):
        def index(i, *numbers):
            return tuple(at(*numbers) if callable(at) else at for at in self.index)

        return pl.BlockSpec(self.block, index)


def vmem_call(kernel, shapes, smem, operands, scratch=(), cost=0, held=(), numbers=()):
    def whole(shape):
        return pl.BlockSpec(shape, lambda i, *numbers: (0,) * len(shape))

    return pl.pallas_call(
        kernel,
        grid_spec=pltpu.PrefetchScalarGridSpec(
            num_scalar_prefetch=len(numbers),
            grid=(1,),
            in_specs=[pl.BlockSpec(memory_space=pltpu.SMEM)] * len(smem)
            + [
                operand.spec() if isinstance(operand, Part) else whole(operand.shape)
                for operand in operands
            ]
            + [pl.BlockSpec(memory_space=pl.ANY)] * len(held),
            out_specs=[whole(shape) for shape, _ in shapes],
            scratch_shapes=list(scratch),
        ),
        out_shape=[jax.ShapeDtypeStruct(shape, dtype) for shape, dtype in shapes],
        compiler_params=pltpu.CompilerParams(vmem_limit_bytes=VMEM_LIMIT),
        cost_estimate=pl.CostEstimate(flops=cost, bytes_accessed=cost // 300, transcendentals=0),
    )(
        *numbers,
        *smem,
        *(operand.array if isinstance(operand, Part) else operand for operand in operands),
        *held,
    )


def fetch(pairs, semaphores):
    copies = [
        pltpu.make_async_copy(source, target, semaphores.at[number])
        for number, (source, target) in enumerate(pairs)
    ]
    for copy in copies:
        copy.start()
    return copies


def feed_rows(values, gains, biases, copies, weight_in, bias_in, weight_out, bias_out):
    normed, _ = normalize(values)
    hidden = low(scaled_norm(normed, gains, biases, 0))
    copies[0].wait()
    preact = matmul(hidden, weight_in[...]) + wide(bias_in[0:1, :])
    sigmoid = logistic(preact)
    active = low(preact * sigmoid)
    copies[1].wait()
    branch = matmul(active, weight_out[...]) + wide(bias_out[0:1, :])
    return values + 0.5 * branch, preact, sigmoid, active


def entry_kernel(
    utterances,
    frames,
    gains,
    biases,
    bias_in,
    bias_out,
    vectors,
    grads_head,
    grads_tail,
    feed_in,
    feed_out,
    attend_in,
    head_out,
    tail_out,
    after_out,
    slope_out,
    pack_out,
    sent_out,
    weight_in,
    weight_out,
    weight_attend,
    semaphores,
):
    copies = fetch(
        [
            (feed_in.at[0], weight_in),
            (feed_out.at[0], weight_out),
            (attend_in.at[pl.ds(0, 3)], weight_attend),
        ],
        semaphores,
    )
    per = frames.shape[0] // utterances
    for u in range(utterances):
        head_out[u, 0:HALO, :] = frames[u * per : u * per + HALO, :]
        head_out[u, HALO:, :] = grads_head[u]
        tail_out[u, 0:HALO, :] = frames[(u + 1) * per - HALO : (u + 1) * per, :]
        tail_out[u, HALO:, :] = grads_tail[u]
    units, features = slope_out.shape[1], frames.shape[1]
    pack_out[:, units : units + features] = low(scaled_norm(normalize(frames[...])[0], gains, biases, 0))
    after, preact, sigmoid, active = feed_rows(
        frames[...], gains, biases, copies, weight_in, bias_in, weight_out, bias_out
    )
    slope_out[...] = low(silu_slope(preact, sigmoid))
    pack_out[:, :units] = active
    after_out[...] = after
    normed, _ = normalize(after)
    hidden = low(scaled_norm(normed, gains, biases, 1))
    pack_out[:, units + features :] = hidden
    copies[2].wait()
    queries = matmul(hidden, weight_attend[0]) + wide(vectors[0:1, :])
    parts = (
        queries + wide(vectors[3:4, :]),
        matmul(hidden, weight_attend[1]),
        matmul(hidden, weight_attend[2]) + wide(vectors[1:2, :]),
    )
    lanes = 2 * HEAD_DIM
    for number, part in enumerate(parts):
        for head, block in enumerate(blocks_of_heads(part, utterances)):
            sent_out[head, :, number * lanes : (number + 1) * lanes] = low(block)


def sides_kernel(
    before,
    behind,
    gains,
    biases,
    bias_in,
    bias_out,
    feed_in,
    feed_out,
    after_out,
    grads_out,
    weight_in,
    weight_out,
    semaphores,
):
    copies = fetch([(feed_in.at[0], weight_in), (feed_out.at[0], weight_out)], semaphores)
    frames, grads = (
        jnp.concatenate(
            [
                source[u, first : first + HALO, :]
                for u in range(before.shape[0])
                for source in (before, behind)
            ],
            axis=0,
        )
        for first in (0, HALO)
    )
    grads_out[...] = grads
    after_out[...] = feed_rows(
        frames, gains, biases, copies, weight_in, bias_in, weight_out, bias_out
    )[0]


def mixer_kernel(
    utterances,
    info,
    blocks,
    after,
    after_sides,
    gains,
    biases,
    attend_out,
    vectors,
    mixer_in,
    mixer_bias,
    taps,
    mixer_vectors,
    after_out,
    pack_out,
    linear_out,
    gate_out,
    gated_out,
    convolved_out,
    sums_out,
    padded,
):
    per = after.shape[0] // utterances
    main, before, behind = [], [], []
    for head in range(HEADS):
        block = wide(blocks[head])
        main.append(block[:per])
        before.append(block[per : per + HALO])
        behind.append(block[per + HALO :])
    attended = rows_of_heads(main)
    features = after.shape[1]
    pack_out[:, :features] = low(attended)
    before, behind = rows_of_heads(before), rows_of_heads(behind)
    sides = []
    for u in range(utterances):
        sides += [before[u * HALO : (u + 1) * HALO], behind[u * HALO : (u + 1) * HALO]]
    attended = low(with_sides(attended, jnp.concatenate(sides, axis=0)))
    values = with_sides(after[...], after_sides[...])
    values = values + matmul(attended, attend_out[...]) + wide(vectors[2:3, :])
    after_out[...] = values
    normed, _ = normalize(values)
    scaled = scaled_norm(normed, gains, biases, 2)
    pack_out[:, features:] = low(own_rows(scaled, utterances))
    preact = matmul(low(scaled), mixer_in[...])
    preact = preact + wide(mixer_bias[...])
    rows = values.shape[0]
    linear = preact[:, :features]
    gate = logistic(preact[:, features:])
    linear_out[...] = own_rows(linear, utterances)
    gate_out[...] = own_rows(gate, utterances)
    place, limit = frame_places(info, rows, utterances, HALO)
    mask = flags((place >= 0) & (place < limit))
    gated = low(linear * gate * mask)
    gated_out[...] = gated
    fill_padded(padded, wide(gated), utterances)
    total = None
    for offset in range(KERNEL):
        term = wide(taps[offset : offset + 1, :]) * moved(
            padded, utterances, offset - KERNEL // 2, True
        )
        total = term if total is None else total + term
    convolved = total + wide(mixer_vectors[0:1, :])
    convolved_out[...] = convolved
    mask = own_rows(mask, utterances)
    convolved = own_rows(convolved, utterances)
    count = jnp.sum(mask, axis=0, keepdims=True)
    local_sum = jnp.sum(convolved * mask, axis=0, keepdims=True)
    centered = (convolved - local_sum / jnp.maximum(count, 1.0)) * mask
    share(sums_out, local_sum, jnp.sum(centered * centered, axis=0, keepdims=True))


def fill_padded(padded, values, utterances):
    own = values.shape[0] - 2 * utterances * HALO
    per = own // utterances
    zeros = jnp.zeros((HALO, values.shape[1]), jnp.float32)
    for u in range(utterances):
        aside = own + 2 * u * HALO
        padded[u, 0:HALO, :] = zeros
        padded[u, HALO : 2 * HALO, :] = values[aside : aside + HALO, :]
        padded[u, 2 * HALO : 2 * HALO + per, :] = values[u * per : (u + 1) * per, :]
        padded[u, 2 * HALO + per : 3 * HALO + per, :] = values[aside + HALO : aside + 2 * HALO, :]
        padded[u, 3 * HALO + per :, :] = zeros


def moved(padded, utterances, start, sides=False):
    per = padded.shape[1] - 4 * HALO
    pieces = [(u, 2 * HALO, per) for u in range(utterances)]
    if sides:
        for u in range(utterances):
            pieces += [(u, HALO, HALO), (u, 2 * HALO + per, HALO)]
    return jnp.concatenate(
        [padded[u, first + start : first + start + height, :] for u, first, height in pieces],
        axis=0,
    )


def share(sums_out, *rows):
    tile = jnp.concatenate(
        [row[:, i : i + 128] for row in rows for i in range(0, row.shape[1], 128)], axis=0
    )
    for copy in range(sums_out.shape[0] // 8):
        sums_out[copy * 8 : copy * 8 + 8, :] = tile


def as_row(tile):
    return jnp.concatenate([tile[i : i + 1] for i in range(tile.shape[0])], axis=1)


def frame_counts(limits, utt_index, shape, utterances, seq_count, per):
    place = lax.broadcasted_iota(jnp.int32, shape, 0)
    owner, first = (place // seq_count) ^ utt_index, place % seq_count * per
    total = jnp.zeros(shape, jnp.int32)
    for number in range(limits.shape[0]):
        inside = jnp.clip(limits[number] - first, 0, per)
        total = total + jnp.where(owner == number // utterances, inside, 0)
    return total.astype(jnp.float32)


def middle_kernel(
    utterances,
    seq_count,
    limits,
    utt_index,
    convolved,
    shared,
    after,
    grads,
    grad_sides,
    gains,
    biases,
    batch_gain,
    batch_shift,
    running_mean,
    running_variance,
    mixer_out,
    vectors,
    bias_in,
    bias_out,
    feed_in,
    feed_out,
    layer_out,
    grad_mixer_out,
    grad_batch_out,
    normed_out,
    pack_out,
    sums_out,
    batch_out_rows,
    vector_out,
    weight_in,
    weight_out,
    semaphores,
):
    def own(values):
        return own_rows(values, utterances)

    features, units = feed_in.shape[1:]

    def pack(number, rows):
        first = 2 * units + number * features
        pack_out[:, first : first + features] = rows

    copies = fetch([(feed_in.at[1], weight_in), (feed_out.at[1], weight_out)], semaphores)
    parts = shared[...].reshape(-1, 8, 128)
    per = grads.shape[0] // utterances
    counts = frame_counts(limits, utt_index[0], parts.shape, utterances, seq_count, per)
    totals = jnp.sum(parts, axis=0)
    valid_tile = jnp.sum(counts, axis=0)
    valid = as_row(valid_tile[:4])
    average_tile = totals / valid_tile
    drift = parts / jnp.maximum(counts, 1.0) - average_tile
    spreads = jnp.sum(counts * drift * drift, axis=0)
    average = as_row(average_tile[:4])
    variance = as_row((totals[4:] + spreads[:4]) / valid_tile[:4])
    inverse_batch = lax.rsqrt(variance + EPSILON)
    batch_out_rows[0:1, :] = inverse_batch
    batch_out_rows[1:2, :] = valid
    batch_out_rows[2:3, :] = 0.9 * running_mean[...] + 0.1 * average
    batch_out_rows[3:4, :] = 0.9 * running_variance[...] + 0.1 * variance * valid / (valid - 1.0)
    normed_batch = (convolved[...] - average) * inverse_batch
    normed_out[...] = normed_batch
    batch = normed_batch * wide(batch_gain[...]) + wide(batch_shift[...])
    batch_sigmoid = logistic(batch)
    swished = low(batch * batch_sigmoid)
    pack(2, own(swished))
    values = after[...] + matmul(swished, mixer_out[...]) + wide(vectors[1:2, :])
    normed, inverse = normalize(values)
    scaled = scaled_norm(normed, gains, biases, 3)
    hidden = low(scaled)
    pack(0, own(hidden))
    copies[0].wait()
    preact = matmul(hidden, weight_in[...]) + wide(bias_in[1:2, :])
    sigmoid = logistic(preact)
    active = low(preact * sigmoid)
    pack_out[:, units : 2 * units] = own(active)
    copies[1].wait()
    branch = matmul(active, weight_out[...]) + wide(bias_out[1:2, :])
    normed_last, inverse_last = normalize(values + 0.5 * branch)
    layer_out[...] = own(scaled_norm(normed_last, gains, biases, 4))
    grad_second, gain_last, shift_last = norm_back(
        with_sides(grads[...], grad_sides[...]),
        normed_last,
        inverse_last,
        gains,
        4,
        own,
    )
    grad_low = low(0.5 * grad_second)
    grad_low_own = own(grad_low)
    pack(1, grad_low_own)
    grad_pre = low(rows_dot(grad_low, weight_out[...]) * silu_slope(preact, sigmoid))
    grad_pre_own = own(grad_pre)
    pack_out[:, :units] = grad_pre_own
    grad_values, gain_three, shift_three = norm_back(
        rows_dot(grad_pre, weight_in[...]), normed, inverse, gains, 3, own
    )
    grad_mixer = grad_second + grad_values
    grad_mixer_own = own(grad_mixer)
    grad_mixer_out[...] = grad_mixer_own
    branch_own = low(grad_mixer_own)
    pack(3, branch_own)
    grad_batch = rows_dot(low(grad_mixer), mixer_out[...]) * silu_slope(batch, batch_sigmoid)
    grad_batch_out[...] = grad_batch
    share(sums_out, column_sum(own(grad_batch)), column_sum(own(grad_batch * normed_batch)))
    bias_sum = column_sum(grad_pre_own)
    put_rows(
        vector_out,
        [gain_last, shift_last, gain_three, shift_three]
        + [bias_sum[:, i : i + features] for i in range(0, bias_sum.shape[1], features)]
        + [column_sum(grad_low_own), column_sum(branch_own)],
    )


def put_rows(out, rows):
    for number, row in enumerate(rows):
        out[number : number + 1, :] = row
    out[len(rows) :, :] = jnp.zeros((out.shape[0] - len(rows), out.shape[1]), jnp.float32)


def mixer_back_kernel(
    utterances,
    info,
    grad_batch,
    normed_batch,
    shared,
    batch_rows,
    batch_gain,
    gated,
    linear,
    gate,
    grad_mixer,
    after,
    gains,
    taps,
    mixer_in,
    attend_out,
    batch_grads_out,
    grad_attend_out,
    pack_out,
    sent_out,
    vector_out,
    padded,
    gated_padded,
):
    totals = jnp.sum(shared[...].reshape(-1, 8, 128), axis=0)
    shift_grad, gain_grad = as_row(totals[:4]), as_row(totals[4:])
    batch_grads_out[0:1, :] = shift_grad
    batch_grads_out[1:2, :] = gain_grad
    rows, features = grad_batch.shape
    place, limit = frame_places(info, rows, utterances, HALO)
    mask = flags((place >= 0) & (place < limit))
    inside = flags((place >= 0) & (place < info[utterances + 1]))
    inverse_batch, valid = batch_rows[0:1, :], batch_rows[1:2, :]
    grad_conv = low(
        inside
        * wide(batch_gain[...])
        * inverse_batch
        * (grad_batch[...] - mask / valid * (shift_grad + normed_batch[...] * gain_grad))
    )
    conv_wide = wide(grad_conv)
    fill_padded(padded, conv_wide, utterances)
    fill_padded(gated_padded, wide(gated[...]), utterances)
    conv_own = own_rows(conv_wide, utterances)
    margin = KERNEL // 2
    total = None
    tap_rows = []
    for offset in range(KERNEL):
        term = wide(taps[offset : offset + 1, :]) * moved(padded, utterances, margin - offset)
        total = term if total is None else total + term
        near = moved(gated_padded, utterances, offset - margin)
        tap_rows.append(jnp.sum(conv_own * near, axis=0, keepdims=True))
    grad_gated = own_rows(mask, utterances) * total
    gate_half = gate[...]
    grad_pre = low(
        jnp.concatenate(
            [
                grad_gated * gate_half,
                grad_gated * linear[...] * gate_half * (1.0 - gate_half),
            ],
            axis=1,
        )
    )
    pack_out[:, : 2 * features] = grad_pre
    normed, inverse = normalize(own_rows(after[...], utterances))
    grad_values, gain_two, shift_two = norm_back(
        rows_dot(grad_pre, mixer_in[...]), normed, inverse, gains, 2
    )
    grad_attend = grad_mixer[...] + grad_values
    grad_attend_out[...] = grad_attend
    branch = low(grad_attend)
    pack_out[:, 2 * features :] = branch
    grad_attended = rows_dot(branch, attend_out[...])
    for head, block in enumerate(blocks_of_heads(grad_attended, utterances)):
        sent_out[head] = low(block)
    bias_sum = column_sum(grad_pre)
    put_rows(
        vector_out,
        [gain_two, shift_two, column_sum(conv_own), column_sum(branch)]
        + [bias_sum[:, :features], bias_sum[:, features:]]
        + tap_rows,
    )


def entry_back_kernel(
    core,
    returned,
    grad_attend,
    frames,
    after,
    slope,
    gains,
    feed_in,
    feed_out,
    attend_in,
    frames_out,
    pack_out,
    grad_pre_out,
    vector_out,
    weight_in,
    weight_out,
    weight_attend,
    semaphores,
):
    copies = fetch(
        [
            (attend_in.at[pl.ds(0, 3)], weight_attend),
            (feed_out.at[0], weight_out),
            (feed_in.at[0], weight_in),
        ],
        semaphores,
    )
    lanes = 2 * HEAD_DIM
    features, units = feed_in.shape[1:]

    def pack(number, rows):
        first = units // 2 + number * features
        pack_out[:, first : first + features] = rows

    grad_hidden = None
    low_rows = []
    for number in range(3):
        rows = low(
            rows_of_heads(
                [
                    wide(returned[head, :, number * lanes : (number + 1) * lanes])
                    for head in range(HEADS)
                ]
            )
        )
        pack(number, rows)
        low_rows.append(rows)
        if number == 0:
            copies[0].wait()
        term = rows_dot(rows, weight_attend[number])
        grad_hidden = term if grad_hidden is None else grad_hidden + term
    normed, inverse = normalize(after[...])
    grad_values, gain_one, shift_one = norm_back(grad_hidden, normed, inverse, gains, 1)
    grad_first = grad_attend[...] + grad_values
    grad_low = low(0.5 * grad_first)
    pack(3, grad_low)
    copies[1].wait()
    grad_pre = low(rows_dot(grad_low, weight_out[...]) * wide(slope[...]))
    for half in range(2):
        rows = grad_pre[:, half * units // 2 : (half + 1) * units // 2]

        @pl.when(core[0] == half)
        def _():
            grad_pre_out[...] = rows

        @pl.when(core[0] != half)
        def _():
            pack_out[:, : units // 2] = rows

    normed, inverse = normalize(frames[...])
    copies[2].wait()
    grad_values, gain_zero, shift_zero = norm_back(
        rows_dot(grad_pre, weight_in[...]), normed, inverse, gains, 0
    )
    frames_out[...] = grad_first + grad_values
    bias_sum = column_sum(grad_pre)
    put_rows(
        vector_out,
        [gain_zero, shift_zero, gain_one, shift_one]
        + [bias_sum[:, i : i + features] for i in range(0, bias_sum.shape[1], features)]
        + [column_sum(grad_low), column_sum(low_rows[0]), column_sum(low_rows[2])],
    )


def vectors_kernel(
    rows, gain_out, bias_out, in_bias_out, out_bias_out, attend_out, mixer_bias_out, mixer_out, taps_out
):
    middle, mixer, entry, heads = (0, 16, 32, 48)
    features = gain_out.shape[1]

    def take(out, target, start):
        out[target : target + 1, :] = rows[start : start + 1, :]

    for out, first in ((gain_out, 0), (bias_out, 1)):
        take(out, 0, entry + first)
        take(out, 1, entry + 2 + first)
        take(out, 2, mixer + first)
        take(out, 3, middle + 2 + first)
        take(out, 4, middle + first)
    for target, start in ((0, entry + 4), (1, middle + 4)):
        for column in range(4):
            in_bias_out[target : target + 1, column * features : (column + 1) * features] = rows[
                start + column : start + column + 1, :
            ]
    take(out_bias_out, 0, entry + 8)
    take(out_bias_out, 1, middle + 8)
    for target, start in enumerate((entry + 9, entry + 10, mixer + 3, heads, heads + 1)):
        take(attend_out, target, start)
    for column in range(2):
        mixer_bias_out[0:1, column * features : (column + 1) * features] = rows[
            mixer + 4 + column : mixer + 5 + column, :
        ]
    take(mixer_out, 0, mixer + 2)
    take(mixer_out, 1, middle + 9)
    taps_out[...] = rows[mixer + 6 : mixer + 6 + KERNEL, :]


def axis_bits(axis):
    return [(axis, 1 << bit) for bit in range(lax.axis_size(axis).bit_length() - 1)]


def swap(values, step):
    axis, mask = step
    return lax.ppermute(values, axis, [(i, i ^ mask) for i in range(lax.axis_size(axis))])


def side(step):
    axis, mask = step
    return (lax.axis_index(axis) // mask) % 2


def swap_all(stripes, steps):
    return [swap(rows, step) for rows, step in zip(stripes, steps)]


def add_low(first_operand, second_operand):
    total = first_operand.astype(jnp.float32) + second_operand.astype(jnp.float32)
    return total.astype(jnp.bfloat16)


def fold_kernel(stripes, arrays, parts, sides, *refs):
    for number in range(stripes):
        sources = refs[2 * arrays * number : 2 * arrays * (number + 1)]
        for keeping in range(2):
            place = sides[number] if keeping else 1 - sides[number]
            out = refs[2 * arrays * stripes + 2 * number + keeping]
            first = 0
            for array in range(arrays):
                own, other = sources[2 * array : 2 * array + 2]
                height = own.shape[0] // (2 * parts)
                for part in range(parts):
                    start = pl.multiple_of((2 * part + place) * height, 16)
                    rows = pl.ds(start, height)
                    out[first : first + height, :] = add_low(own[rows, :], other[rows, :])
                    first += height


def fold_rows(pairs, steps, parts=1, limit=SUM_LIMIT):
    operands = list(zip(*(rows for pair in pairs for rows in pair)))
    heights = [sum(rows.shape[0] for rows in four[::2]) // 2 for four in operands]
    if any(rows.shape[0] // parts % 32 for four in operands for rows in four):
        sent, kept = [], []
        for four, step in zip(operands, steps):
            sums = [add_low(*four[i : i + 2]) for i in range(0, len(four), 2)]
            for place, results in ((1 - side(step), sent), (side(step), kept)):
                pieces = []
                for rows in sums:
                    height = rows.shape[0] // (2 * parts)
                    pieces += [
                        lax.dynamic_slice_in_dim(rows, (2 * part + place) * height, height, 0)
                        for part in range(parts)
                    ]
                results.append(jnp.concatenate(pieces, axis=0))
        return sent, kept

    def whole(rows):
        return pl.BlockSpec((rows, 512), lambda i, sides: (0, 0))

    outs = [height for height in heights for _ in range(2)]
    results = pl.pallas_call(
        functools.partial(fold_kernel, len(steps), len(pairs), parts),
        grid_spec=pltpu.PrefetchScalarGridSpec(
            num_scalar_prefetch=1,
            grid=(1,),
            in_specs=[whole(rows.shape[0]) for four in operands for rows in four],
            out_specs=[whole(height) for height in outs],
        ),
        out_shape=[jax.ShapeDtypeStruct((height, 512), jnp.bfloat16) for height in outs],
        compiler_params=pltpu.CompilerParams(vmem_limit_bytes=limit),
        cost_estimate=pl.CostEstimate(
            flops=0, bytes_accessed=6 * 1024 * sum(outs), transcendentals=0
        ),
    )(jnp.stack([side(step) for step in steps]), *(rows for four in operands for rows in four))
    return list(results[::2]), list(results[1::2])


def add_kernel(stripes, *refs):
    for number in range(stripes):
        refs[2 * stripes + number][...] = add_low(refs[2 * number][...], refs[2 * number + 1][...])


def add_rows(kept, arrived):
    if any(rows.shape[0] % 16 for rows in kept):
        return [add_low(*pair) for pair in zip(kept, arrived)]
    specs = [whole_array(rows.shape) for rows in kept]
    return list(
        pl.pallas_call(
            functools.partial(add_kernel, len(kept)),
            grid=(1,),
            in_specs=[spec for spec in specs for _ in range(2)],
            out_specs=specs,
            out_shape=[jax.ShapeDtypeStruct(rows.shape, rows.dtype) for rows in kept],
            compiler_params=pltpu.CompilerParams(vmem_limit_bytes=SUM_LIMIT),
        )(*(rows for pair in zip(kept, arrived) for rows in pair))
    )


def join_kernel(stripes, sides, *refs):
    for number in range(stripes):
        own, other, out = refs[2 * number], refs[2 * number + 1], refs[2 * stripes + number]
        height = own.shape[0] // 2
        for part in range(2):
            for source, place in ((own, sides[number]), (other, 1 - sides[number])):
                start = pl.multiple_of((2 * part + place) * height, 16)
                out[pl.ds(start, height), :] = source[part * height : (part + 1) * height, :]


def join_rows(stripes, arrived, steps):
    heights = [rows.shape[0] // 2 for rows in stripes]
    if any(height % 16 for height in heights):
        joined = []
        for rows, other, step, height in zip(stripes, arrived, steps, heights):
            first = side(step) == 0
            low_rows, high_rows = jnp.where(first, rows, other), jnp.where(first, other, rows)
            joined.append(
                jnp.concatenate(
                    [
                        half[part]
                        for part in (slice(0, height), slice(height, None))
                        for half in (low_rows, high_rows)
                    ],
                    axis=0,
                )
            )
        return joined

    def whole(height):
        return pl.BlockSpec((height, 512), lambda i, sides: (0, 0))

    return list(
        pl.pallas_call(
            functools.partial(join_kernel, len(stripes)),
            grid_spec=pltpu.PrefetchScalarGridSpec(
                num_scalar_prefetch=1,
                grid=(1,),
                in_specs=[whole(2 * height) for height in heights for _ in range(2)],
                out_specs=[whole(4 * height) for height in heights],
            ),
            out_shape=[jax.ShapeDtypeStruct((4 * height, 512), jnp.bfloat16) for height in heights],
            compiler_params=pltpu.CompilerParams(vmem_limit_bytes=SUM_LIMIT),
            cost_estimate=pl.CostEstimate(
                flops=0, bytes_accessed=8 * 1024 * sum(heights), transcendentals=0
            ),
        )(
            jnp.stack([side(step) for step in steps]),
            *(rows for pair in zip(stripes, arrived) for rows in pair),
        )
    )


def tie(*groups):
    return lax.optimization_barrier(groups)


def step_orders():
    utt, seq = axis_bits("utt"), axis_bits("seq")
    across, line, rest = utt[1:], seq[:1], seq[1:]
    return (
        line + across + rest,
        across + rest + line,
        rest[:1] + line + across + rest[1:],
    )


def all_shared(copies):
    return lax.all_to_all(copies, ("utt", "seq"), 0, 0, tiled=True)


def from_neighbours(head, tail):
    count = lax.axis_size("seq")
    before = lax.ppermute(tail, "seq", [(i, i + 1) for i in range(count - 1)])
    behind = lax.ppermute(head, "seq", [(i + 1, i) for i in range(count - 1)])
    return before, behind


def pair_rows(mine, theirs, start=0, width=None):
    columns = slice(start, start + (width or mine.shape[1]))
    return jnp.concatenate([mine[:, columns], theirs[:, columns]], axis=0)


def outer(left, right):
    return low(matmul(left.T, right))


def put_half(outs, side_number, half, value):
    @pl.when(side_number == half)
    def _():
        outs[1][...] = value

    @pl.when(side_number != half)
    def _():
        outs[0][...] = value


def feed_blocks(refs, outs, sides):
    hidden, grad_pre, active, grad_low = (refs[2 * i : 2 * i + 2] for i in range(4))
    hidden_cols = pair_rows(*hidden).T
    grad_rows = pair_rows(*grad_low)
    for half in range(2):
        block = low(matmul(hidden_cols, pair_rows(*grad_pre, 512 * half, 512)))
        put_half(outs[:2], sides[1], half, block)
        block = outer(pair_rows(*active, 512 * half, 512), grad_rows)
        put_half(outs[2:4], sides[2], half, block)


def second_kernel(places, *refs):
    feed_blocks(refs[:8], refs[8:], places)


def mixer_blocks_kernel(places, *refs):
    refs, outs = refs[:12], refs[12:]
    mixer = outer(pair_rows(*refs[:2]), pair_rows(*refs[2:4]))
    branch = outer(pair_rows(*refs[4:6]), pair_rows(*refs[6:8]))
    attend = outer(pair_rows(*refs[8:10]), pair_rows(*refs[10:12]))
    for half in range(2):
        pieces = (
            mixer[256 * half : 256 * half + 256],
            branch[128 * half : 128 * half + 128],
            attend[128 * half : 128 * half + 128],
        )
        put_half(outs, places[3], half, jnp.concatenate(pieces, axis=0))


def turn_kernel(places, *refs):
    for number in range(3):
        mine, theirs, out = refs[2 * number], refs[2 * number + 1], refs[8 + number]
        rows = mine.shape[0]
        out[:, :rows] = mine[...].T
        out[:, rows:] = theirs[...].T
    refs[11][...] = add_low(refs[6][...], refs[7][...])


def late_kernel(
    keeping,
    places,
    hidden_cols,
    grad_pre,
    grad_pre_other,
    active_cols,
    grad_low,
    grad_low_other,
    attend_cols,
    attend_rows,
    attend_rows_other,
    position,
    *outs,
):
    step = pl.program_id(0)
    half = places[3] if keeping else 1 - places[3]

    def blocks(left, mine, theirs):
        return low(matmul(left[...], jnp.concatenate([mine[...], theirs[...]], axis=0)))

    @pl.when(step == 0)
    def _():
        outs[0][...] = blocks(hidden_cols, grad_pre, grad_pre_other)

    @pl.when(step == 1)
    def _():
        outs[1][...] = blocks(active_cols, grad_low, grad_low_other)

    @pl.when((step == 2) & (places[0] + half < 2))
    def _():
        outs[2][...] = blocks(attend_cols, attend_rows, attend_rows_other)

    @pl.when((step == 2) & (places[0] + half == 2))
    def _():
        outs[2][...] = position[...]


def late_blocks(keeping, places, cols, grad_pre, pair):
    hidden_cols, active_cols, attend_cols, position = cols
    rows = pair[0].shape[0]

    def half(p, stripe):
        return p[stripe] if keeping else 1 - p[stripe]

    def whole(shape):
        return pl.BlockSpec(shape, lambda i, p: (0, 0))

    def attend_column(i, p):
        return (0, jnp.where(p[0] == 0, 2 + half(p, 3), 4))

    block = (rows, 512)
    return list(
        pl.pallas_call(
            functools.partial(late_kernel, keeping),
            grid_spec=pltpu.PrefetchScalarGridSpec(
                num_scalar_prefetch=1,
                grid=(3,),
                in_specs=[
                    whole(hidden_cols.shape),
                    pl.BlockSpec(block, lambda i, p: (0, half(p, 1))),
                    pl.BlockSpec(block, lambda i, p: (0, half(p, 1))),
                    pl.BlockSpec((512, 2 * rows), lambda i, p: (half(p, 2), 0)),
                    pl.BlockSpec(block, lambda i, p: (0, 5)),
                    pl.BlockSpec(block, lambda i, p: (0, 5)),
                    whole(attend_cols.shape),
                    pl.BlockSpec(block, attend_column),
                    pl.BlockSpec(block, attend_column),
                    whole(position.shape),
                ],
                out_specs=[whole((512, 512))] * 3,
            ),
            out_shape=[jax.ShapeDtypeStruct((512, 512), jnp.bfloat16)] * 3,
            compiler_params=pltpu.CompilerParams(vmem_limit_bytes=SUM_LIMIT if keeping else VMEM_LIMIT),
            cost_estimate=pl.CostEstimate(
                flops=6 * 512 * 512 * 2 * rows, bytes_accessed=6 * 10**6, transcendentals=0
            ),
        )(
            places,
            hidden_cols,
            grad_pre,
            pair[1],
            active_cols,
            *pair,
            attend_cols,
            *pair,
            position,
        )
    )


def columns(pair, width, number, by_core=False):
    index = (lambda numbers: number + numbers[0]) if by_core else number
    return [Part(array, (array.shape[0], width), (0, index)) for array in pair]


def block_sums(kernel, places, stripes, operands):
    blocks = vmem_call(
        kernel,
        [((512, 512), jnp.bfloat16)] * (2 * stripes),
        (),
        [part for pair in operands for part in pair],
        cost=7 * 10**8 * stripes,
        numbers=(places,),
    )
    return blocks[::2], blocks[1::2]


def spread_kernel(places, first, second, third, *refs):
    feed_in, feed_out, mixer_in, mixer_out, attend_out, attend_in = refs[-14:-8]
    held, wide_rows = refs[-8:-5], refs[-5:-2]
    arrive, leave = refs[-2:]
    core, half = places[0], places[3]
    quarters = [pl.multiple_of(512 * (2 * core + places[1 + i]), 512) for i in range(3)]
    pieces = []
    for part in range(2):
        layer = 1 - part
        for start in (0, 256):
            rows = pl.ds(start, 256)
            pieces.append((0, 512 * part + start, feed_in.at[layer, rows, pl.ds(quarters[0], 512)]))
            out_rows = pl.ds(pl.multiple_of(quarters[1] + start, 256), 256)
            pieces.append((1, 512 * part + start, feed_out.at[layer, out_rows]))
            if part == 1:
                pieces.append((2, 512 + start, attend_in.at[2 * core + half, rows]))
            elif start == 0:
                tall = pl.ds(pl.multiple_of(256 * half, 256), 256)
                side_columns = pl.ds(pl.multiple_of(512 * core, 512), 512)
                pieces.append((2, 0, mixer_in.at[tall, side_columns]))
            else:
                flat = pl.ds(pl.multiple_of(128 * (2 * core + half), 128), 128)
                pieces.append((2, 256, mixer_out.at[flat]))
                pieces.append((2, 384, attend_out.at[flat]))
    coming = []
    for number, (stripe, start, target) in enumerate(pieces):
        rows = pl.ds(start, target.shape[0])
        coming.append(
            pltpu.make_async_copy(
                (first, second, third)[stripe].at[rows], held[stripe].at[rows], arrive.at[number]
            )
        )
    for copy in coming[:AHEAD]:
        copy.start()
    going = []
    for number, (stripe, start, target) in enumerate(pieces):
        coming[number].wait()
        if number + AHEAD < len(coming):
            coming[number + AHEAD].start()
        rows = pl.ds(start, target.shape[0])
        wide_rows[stripe][rows, :] = wide(held[stripe][rows, :])
        copy = pltpu.make_async_copy(wide_rows[stripe].at[rows], target, leave.at[number])
        copy.start()
        going.append(copy)
    for copy in going:
        copy.wait()


def spread_blocks(places, stripes, shapes, bases):
    anywhere = pl.BlockSpec(memory_space=pl.ANY)
    return list(
        pl.pallas_call(
            spread_kernel,
            in_specs=[pl.BlockSpec(memory_space=pltpu.SMEM)] + [anywhere] * (3 + len(bases)),
            out_specs=[anywhere] * len(shapes),
            out_shape=[jax.ShapeDtypeStruct(shape, jnp.float32) for shape in shapes],
            scratch_shapes=[pltpu.VMEM((1024, 512), jnp.bfloat16)] * 3
            + [pltpu.VMEM((1024, 512), jnp.float32)] * 3
            + [pltpu.SemaphoreType.DMA((13,)), pltpu.SemaphoreType.DMA((13,))],
            input_output_aliases={4 + n: n for n in range(len(bases))},
            compiler_params=pltpu.CompilerParams(vmem_limit_bytes=VMEM_LIMIT),
            cost_estimate=pl.CostEstimate(
                flops=1024, bytes_accessed=1024, transcendentals=0
            ),
        )(places, *stripes, *bases)
    )


def angle_tables(frame_count, features):
    halves = jnp.arange(features // 2, dtype=jnp.int32).astype(jnp.float32)
    frequencies = jnp.exp(halves * (-2.0 * math.log(10000.0) / features))
    fine = 32
    low_angles = jnp.arange(fine, dtype=jnp.int32).astype(jnp.float32)[:, None] * frequencies
    high_angles = (fine * jnp.arange(frame_count // fine, dtype=jnp.int32)).astype(jnp.float32)[
        :, None
    ] * frequencies
    low_sin, low_cos = jnp.sin(low_angles)[None], jnp.cos(low_angles)[None]
    high_sin, high_cos = jnp.sin(high_angles)[:, None], jnp.cos(high_angles)[:, None]
    sines = high_sin * low_cos + high_cos * low_sin
    cosines = high_cos * low_cos - high_sin * low_sin
    shape = (frame_count, features // 2)
    return sines.reshape(shape), cosines.reshape(shape)


def heads_out(blocks, groups):
    return lax.all_to_all(jnp.tile(blocks, (groups, 1, 1)), "seq", 0, 0, tiled=True)


def rows_dot(first_operand, second_operand):
    return lax.dot_general(
        first_operand, second_operand, (((1,), (1,)), ((), ())), preferred_element_type=jnp.float32
    )


def lane_side(shape, utterance):
    return (lax.broadcasted_iota(jnp.int32, shape, 1) // HEAD_DIM) == utterance


def turned_queries(content, shift, weight, sines, cosines):
    offset = (content.astype(jnp.float32) + shift).astype(jnp.bfloat16)
    half = sines.shape[1]
    spread = jnp.dot(offset, weight, preferred_element_type=jnp.float32)
    sin_part, cos_part = spread[:, :half], spread[:, half:]
    return (
        offset,
        (sin_part * sines + cos_part * cosines).astype(jnp.bfloat16),
        (cos_part * sines - sin_part * cosines).astype(jnp.bfloat16),
    )


def attend_kernel(
    limits,
    content,
    keys,
    values,
    shift,
    weight,
    sines,
    cosines,
    table,
    weights_out,
    attended_out,
    held,
    scores,
):
    scale = HEAD_DIM ** (-0.5)
    weight_rows = jnp.concatenate([weight[...]] * limits.shape[0], axis=0)
    content_rows = content[...]
    key_side = jnp.concatenate([table[...], keys[...]], axis=1)
    places = lax.broadcasted_iota(jnp.int32, (1, table.shape[0]), 1)
    attended = None
    for utterance in range(limits.shape[0]):
        ours = lane_side(content_rows.shape, utterance)
        mine = jnp.where(ours, content_rows, jnp.zeros_like(content_rows))
        moved = jnp.where(ours, shift[...], 0.0)
        _, turned_cos, turned_sin = turned_queries(
            mine, moved, weight_rows, sines[...], cosines[...]
        )
        query_side = jnp.concatenate([turned_cos, turned_sin, mine], axis=1) * scale
        scores[utterance] = rows_dot(query_side.astype(jnp.bfloat16), key_side)
    for utterance in range(limits.shape[0]):
        allowed = places < limits[utterance]
        for start in range(0, scores.shape[1], ROW_TILE):
            rows = slice(start, start + ROW_TILE)
            tile = jnp.where(allowed, scores[utterance, rows, :], -1000000000.0)
            raised = jnp.exp(tile - jnp.max(tile, axis=1, keepdims=True))
            totals = jnp.sum(raised, axis=1, keepdims=True)
            weights_out[utterance, rows, :] = low(raised * (1.0 / totals))
    for utterance in range(limits.shape[0]):
        ours = lane_side(content_rows.shape, utterance)
        part = matmul(weights_out[utterance], values[...])
        attended = part if attended is None else jnp.where(ours, part, attended)
    if held is None:
        attended_out[...] = attended.astype(jnp.bfloat16)
        return
    step = pl.program_id(0)
    height = attended.shape[0]
    block = attended_out.shape[1] - 2 * HALO
    held[pl.ds(pl.multiple_of(HALO + step * height, 8), height), :] = attended
    for number in range(height // block):
        attended_out[step * (height // block) + number, 0:block, :] = attended[
            number * block : (number + 1) * block
        ].astype(jnp.bfloat16)

    @pl.when(step == pl.num_programs(0) - 1)
    def _():
        edge = jnp.zeros((HALO, held.shape[1]), jnp.float32)
        held[0:HALO, :] = edge
        held[held.shape[0] - HALO :, :] = edge
        for number in range(attended_out.shape[0]):
            start = number * block
            sides = jnp.concatenate(
                [
                    held[start : start + HALO, :],
                    held[start + HALO + block : start + 2 * HALO + block, :],
                ],
                axis=0,
            )
            attended_out[number, block:, :] = sides.astype(jnp.bfloat16)


def attend_back_kernel(
    weights,
    content,
    grads,
    keys,
    values,
    shift,
    weight,
    sines,
    cosines,
    table,
    *outs,
):
    step = pl.program_id(0)
    *outs, grad_probs, grad_scores = outs
    query_out, pairs_out, weight_out, sums_out, key_sums, value_sums = (
        [None] * (6 - len(outs)) + outs
    )
    scale = HEAD_DIM ** (-0.5)

    @pl.when(step == 0)
    def _():
        key_sums[...] = jnp.zeros_like(key_sums)
        value_sums[...] = jnp.zeros_like(value_sums)
        weight_out[...] = jnp.zeros_like(weight_out)
        sums_out[...] = jnp.zeros_like(sums_out)

    weight_rows = jnp.concatenate([weight[...]] * weights.shape[0], axis=0)
    content_rows, grad_rows = content[...], grads[...]
    content_cols = content_rows.T
    grad_cols = grad_rows.T
    key_side = jnp.concatenate([table[...], keys[...]], axis=1)
    half = sines.shape[1]
    grad_content = grad_position = None
    for utterance in range(weights.shape[0]):
        ours = lane_side(content_rows.shape, utterance)
        grad_mine = jnp.where(ours, grad_rows, jnp.zeros_like(grad_rows)) * scale
        grad_probs[utterance] = rows_dot(grad_mine.astype(jnp.bfloat16), values[...])
    for utterance in range(weights.shape[0]):
        first, last = utterance * HEAD_DIM, (utterance + 1) * HEAD_DIM
        ours = lane_side(content_rows.shape, utterance)
        probs = weights[utterance]
        for start in range(0, grad_probs.shape[1], ROW_TILE):
            rows = slice(start, start + ROW_TILE)
            tile = wide(weights[utterance, rows, :])
            product = tile * grad_probs[utterance, rows, :]
            inner = jnp.sum(product, axis=1, keepdims=True)
            grad_scores[utterance, rows, :] = low(product - tile * inner)
        value_sums[first:last, :] += jnp.dot(
            grad_cols[first:last, :], probs, preferred_element_type=jnp.float32
        )
        key_sums[first:last, :] += jnp.dot(
            content_cols[first:last, :], grad_scores[utterance], preferred_element_type=jnp.float32
        )
        grad_side = matmul(grad_scores[utterance], key_side)
        grad_cos_table = grad_side[:, :half]
        grad_sin_table = grad_side[:, half : 2 * half]
        from_table = jnp.concatenate(
            [
                grad_cos_table * sines[...] - grad_sin_table * cosines[...],
                grad_cos_table * cosines[...] + grad_sin_table * sines[...],
            ],
            axis=1,
        ).astype(jnp.bfloat16)
        offset = (content_rows.astype(jnp.float32) + shift[...]).astype(jnp.bfloat16)
        weight_out[...] += jnp.dot(
            offset.T[first:last, :], from_table, preferred_element_type=jnp.float32
        )
        content_part = grad_side[:, 2 * half :]
        position_part = rows_dot(from_table, weight_rows)
        if grad_content is None:
            grad_content, grad_position = content_part, position_part
        else:
            grad_content = jnp.where(ours, content_part, grad_content)
            grad_position = jnp.where(ours, position_part, grad_position)
    grad_query = (grad_content + grad_position).astype(jnp.bfloat16)
    height, lanes = grad_query.shape
    if query_out is None:
        pairs_out[pl.ds(pl.multiple_of(step * height, 16), height), 0:lanes] = grad_query
    else:
        query_out[...] = grad_query
    sums_out[0:1, :] += jnp.sum(grad_content, axis=0, keepdims=True)
    sums_out[1:2, :] += jnp.sum(grad_position, axis=0, keepdims=True)

    @pl.when(step == pl.num_programs(0) - 1)
    def _():
        first = pairs_out.shape[1] - 2 * lanes
        pairs_out[:, first : first + lanes] = key_sums[...].T.astype(jnp.bfloat16)
        pairs_out[:, first + lanes :] = value_sums[...].T.astype(jnp.bfloat16)


def query_block(frames_all, most=256):
    return most if frames_all <= 1024 else 128


def whole_block(shape):
    return pl.BlockSpec(shape, lambda i: (0,) * len(shape))


def row_block(height, width):
    return pl.BlockSpec((height, width), lambda i: (i, 0))


def attend_heads(limits, content, arrived, shift, weight, sines, cosines, table, block):
    utterances = limits.shape[0]
    query_frames, lanes = content.shape[0], arrived.shape[1] // 3
    frames_all, table_width = table.shape
    height = query_block(frames_all)
    chunked = query_frames == frames_all and height % block == 0
    chunks = (frames_all // block, block + 2 * HALO, lanes)
    kernel = attend_kernel
    if not chunked:
        kernel = lambda *refs: attend_kernel(*refs[:-1], None, refs[-1])
    return pl.pallas_call(
        kernel,
        grid=(query_frames // height,),
        in_specs=[
            pl.BlockSpec(memory_space=pltpu.SMEM),
            row_block(height, lanes),
            pl.BlockSpec((frames_all, lanes), lambda i: (0, 1)),
            pl.BlockSpec((frames_all, lanes), lambda i: (0, 2)),
            whole_block(shift.shape),
            whole_block(weight.shape),
            row_block(height, sines.shape[1]),
            row_block(height, sines.shape[1]),
            whole_block(table.shape),
        ],
        out_specs=[
            pl.BlockSpec((utterances, height, frames_all), lambda i: (0, i, 0)),
            whole_block(chunks) if chunked else row_block(height, lanes),
        ],
        out_shape=[
            jax.ShapeDtypeStruct((utterances, query_frames, frames_all), jnp.bfloat16),
            jax.ShapeDtypeStruct(chunks if chunked else (query_frames, lanes), jnp.bfloat16),
        ],
        scratch_shapes=[pltpu.VMEM((frames_all + 2 * HALO, lanes), jnp.float32)] * chunked
        + [pltpu.VMEM((utterances, height, frames_all), jnp.float32)],
        compiler_params=pltpu.CompilerParams(vmem_limit_bytes=VMEM_LIMIT),
        cost_estimate=pl.CostEstimate(
            flops=2 * utterances * query_frames * frames_all * (table_width + 256),
            bytes_accessed=2 * utterances * query_frames * frames_all,
            transcendentals=utterances * query_frames * frames_all,
        ),
    )(limits, content, arrived, arrived, shift, weight, sines, cosines, table)


def attend_heads_back(
    weights, content, grads, arrived, shift, weight, sines, cosines, table
):
    utterances, query_frames, frames_all = weights.shape
    lanes = arrived.shape[1] // 3
    height = query_block(frames_all)
    joined = query_frames == frames_all
    width = (3 if joined else 2) * lanes
    return pl.pallas_call(
        attend_back_kernel,
        grid=(query_frames // height,),
        in_specs=[
            pl.BlockSpec((utterances, height, frames_all), lambda i: (0, i, 0)),
            row_block(height, lanes),
            row_block(height, lanes),
            pl.BlockSpec((frames_all, lanes), lambda i: (0, 1)),
            pl.BlockSpec((frames_all, lanes), lambda i: (0, 2)),
            whole_block(shift.shape),
            whole_block(weight.shape),
            row_block(height, sines.shape[1]),
            row_block(height, sines.shape[1]),
            whole_block(table.shape),
        ],
        out_specs=([] if joined else [row_block(height, lanes)])
        + [
            whole_block((frames_all, width)),
            whole_block((HEAD_DIM, table.shape[1])),
            whole_block((8, lanes)),
        ],
        out_shape=(
            [] if joined else [jax.ShapeDtypeStruct((query_frames, lanes), jnp.bfloat16)]
        )
        + [
            jax.ShapeDtypeStruct((frames_all, width), jnp.bfloat16),
            jax.ShapeDtypeStruct((HEAD_DIM, table.shape[1]), jnp.float32),
            jax.ShapeDtypeStruct((8, lanes), jnp.float32),
        ],
        scratch_shapes=[
            pltpu.VMEM((lanes, frames_all), jnp.float32),
            pltpu.VMEM((lanes, frames_all), jnp.float32),
            pltpu.VMEM((utterances, height, frames_all), jnp.float32),
            pltpu.VMEM((utterances, height, frames_all), jnp.bfloat16),
        ],
        compiler_params=pltpu.CompilerParams(vmem_limit_bytes=VMEM_LIMIT),
        cost_estimate=pl.CostEstimate(
            flops=2 * utterances * query_frames * frames_all * (table.shape[1] + 512),
            bytes_accessed=2 * utterances * query_frames * frames_all,
            transcendentals=0,
        ),
    )(weights, content, grads, arrived, arrived, shift, weight, sines, cosines, table)


def shards(
    frames,
    lengths,
    out_grad,
    norm_gain,
    norm_bias,
    feed_in,
    feed_in_bias,
    feed_out,
    feed_out_bias,
    attend_in,
    attend_vectors,
    attend_out,
    mixer_in,
    mixer_in_bias,
    depthwise,
    mixer_vectors,
    mixer_out,
    batch_gain,
    batch_shift,
    running_mean,
    running_variance,
):
    utt_rows, block_frames, features = frames.shape
    rows = utt_rows * block_frames
    seq_count = lax.axis_size("seq")
    seq_index = lax.axis_index("seq")
    count = lax.axis_size("utt") * seq_count
    frames_all = block_frames * seq_count
    groups = seq_count // HEADS
    head, group = seq_index % HEADS, seq_index // HEADS
    query_frames = frames_all // groups
    lanes = utt_rows * HEAD_DIM
    info = jnp.concatenate(
        [(seq_index * block_frames).reshape(1), lengths, jnp.full((1,), frames_all, jnp.int32)]
    )
    hidden_units = feed_in.shape[2]
    f32, bf16 = jnp.float32, jnp.bfloat16
    flat_frames = frames.reshape(rows, features)
    square, broad = (rows, features), (rows, hidden_units)
    extended = (utt_rows * (block_frames + 2 * HALO), features)
    row_flops = 2 * rows * features
    bind = functools.partial
    edge = ((utt_rows, 2 * HALO, features), f32)
    feed_scratch = [
        pltpu.VMEM((features, hidden_units), bf16),
        pltpu.VMEM((hidden_units, features), bf16),
    ]
    attend_scratch = pltpu.VMEM((3, features, features), bf16)
    (
        edge_head,
        edge_tail,
        after_first,
        slope_first,
        entry_pack,
        sent,
    ) = vmem_call(
        bind(entry_kernel, utt_rows),
        [
            edge,
            edge,
            (square, f32),
            (broad, bf16),
            ((rows, hidden_units + 2 * features), bf16),
            ((HEADS, block_frames, 3 * lanes), bf16),
        ],
        (),
        (
            flat_frames,
            norm_gain,
            norm_bias,
            feed_in_bias,
            feed_out_bias,
            attend_vectors,
            Part(out_grad, (utt_rows, HALO, features), (0, 0, 0)),
            Part(out_grad, (utt_rows, HALO, features), (0, block_frames // HALO - 1, 0)),
        ),
        scratch=feed_scratch + [attend_scratch, pltpu.SemaphoreType.DMA((3,))],
        cost=row_flops * (2 * hidden_units + 3 * features),
        held=(feed_in, feed_out, attend_in),
    )
    sent, all_limits, edge_head, edge_tail = tie(sent, lengths, edge_head, edge_tail)
    before, behind = from_neighbours(edge_head, edge_tail)
    arrived = heads_out(sent, groups)
    for step in axis_bits("utt"):
        all_limits = jnp.concatenate([all_limits, swap(all_limits, step)])
    arrived, all_limits = tie(arrived, all_limits)
    arrived = arrived.reshape(frames_all, 3 * lanes)
    start_query = group * query_frames
    head_content = arrived
    if groups > 1:
        head_content = lax.dynamic_slice_in_dim(arrived, start_query, query_frames, 0)
    head_vectors = lax.dynamic_slice_in_dim(
        attend_vectors.astype(f32), head * HEAD_DIM, HEAD_DIM, 1
    )
    head_shift = jnp.tile((head_vectors[4] - head_vectors[3])[None], (1, utt_rows))
    head_weight = lax.dynamic_slice_in_dim(attend_in[3], head * HEAD_DIM, HEAD_DIM, 1).reshape(
        features // 2, 2, HEAD_DIM
    )
    head_weight = jnp.transpose(head_weight, (2, 1, 0)).reshape(HEAD_DIM, features)
    sines, cosines = angle_tables(frames_all, features)
    key_table = jnp.concatenate([cosines, sines], axis=1).astype(bf16)
    query_sin = lax.dynamic_slice_in_dim(sines, start_query, query_frames, 0)
    query_cos = lax.dynamic_slice_in_dim(cosines, start_query, query_frames, 0)
    weights, head_attended = attend_heads(
        lengths,
        head_content,
        arrived,
        head_shift,
        head_weight,
        query_sin,
        query_cos,
        key_table,
        block_frames,
    )

    def frames_back(blocks):
        width = blocks.shape[-1]
        blocks = blocks.reshape(1, HEADS, block_frames, width)
        if groups > 1:
            blocks = lax.dynamic_update_slice_in_dim(
                jnp.zeros((groups,) + blocks.shape[1:], blocks.dtype), blocks, group, 0
            )
        blocks = lax.all_to_all(
            blocks.reshape(seq_count, block_frames, width), "seq", 0, 0, tiled=True
        ).reshape(groups, HEADS, block_frames, width)
        return lax.dynamic_slice_in_dim(blocks, group, 1, 0)[0]

    head_attended, before, behind = tie(head_attended, before, behind)
    after_sides, grad_sides = vmem_call(
        sides_kernel,
        [((2 * utt_rows * HALO, features), f32)] * 2,
        (),
        (before, behind, norm_gain, norm_bias, feed_in_bias, feed_out_bias),
        scratch=feed_scratch + [pltpu.SemaphoreType.DMA((2,))],
        cost=row_flops * 2 * hidden_units // 4,
        held=(feed_in, feed_out),
    )
    if head_attended.ndim == 2:
        placed = lax.dynamic_update_slice_in_dim(
            jnp.zeros((frames_all + 2 * HALO, lanes), bf16), head_attended, HALO + start_query, 0
        )
        main, before, behind = (
            placed[start : start + frames_all].reshape(seq_count, block_frames, lanes)
            for start in (HALO, 0, 2 * HALO)
        )
        head_attended = jnp.concatenate([main, before[:, :HALO], behind[:, -HALO:]], axis=1)
    attended_blocks = lax.all_to_all(head_attended, "seq", 0, 0, tiled=True)
    attended_blocks, after_sides, grad_sides = tie(attended_blocks, after_sides, grad_sides)
    if groups > 1:
        attended_blocks = jnp.sum(
            attended_blocks.reshape((groups, HEADS) + attended_blocks.shape[1:]), axis=0
        )
    taps = depthwise.T
    padded = pltpu.VMEM((utt_rows, block_frames + 2 * HALO + 16, features), f32)
    (
        after_attend,
        mixer_pack,
        linear_half,
        gate_half,
        gated,
        convolved,
        shared,
    ) = vmem_call(
        bind(mixer_kernel, utt_rows),
        [
            (extended, f32),
            ((rows, 2 * features), bf16),
            (square, f32),
            (square, f32),
            (extended, bf16),
            (extended, f32),
            ((8 * count, 128), f32),
        ],
        (info,),
        (
            attended_blocks,
            after_first,
            after_sides,
            norm_gain,
            norm_bias,
            attend_out,
            attend_vectors,
            mixer_in,
            mixer_in_bias.reshape(1, -1),
            taps,
            mixer_vectors,
        ),
        scratch=(padded,),
        cost=row_flops * 3 * features,
    )
    (
        layer_output,
        grad_mixer,
        grad_batch,
        normed_batch,
        second_pack,
        shared,
        batch_rows,
        middle_rows,
    ) = vmem_call(
        bind(middle_kernel, utt_rows, seq_count),
        [
            (square, f32),
            (square, f32),
            (extended, f32),
            (extended, f32),
            ((rows, 2 * hidden_units + 4 * features), bf16),
            ((8 * count, 128), f32),
            ((8, features), f32),
            ((16, features), f32),
        ],
        (all_limits, lax.axis_index("utt").reshape(1)),
        (
            convolved,
            all_shared(shared),
            after_attend,
            out_grad.reshape(rows, features),
            grad_sides,
            norm_gain,
            norm_bias,
            batch_gain.reshape(1, -1),
            batch_shift.reshape(1, -1),
            running_mean.reshape(1, -1),
            running_variance.reshape(1, -1),
            mixer_out,
            mixer_vectors,
            feed_in_bias,
            feed_out_bias,
        ),
        scratch=feed_scratch + [pltpu.SemaphoreType.DMA((2,))],
        cost=row_flops * (4 * hidden_units + 2 * features),
        held=(feed_in, feed_out),
    )
    phases = list(zip(*step_orders()))
    near = axis_bits("utt")[0]
    core = side(near).reshape(1)
    halves = jnp.stack([side(step) for step in phases[0]])
    places = jnp.concatenate([core, halves])
    half_units, half_features = hidden_units // 2, features // 2

    def with_pair(array):
        return [array, swap(array, near)]

    second_pair = with_pair(second_pack)
    second_sent, second_kept = block_sums(
        second_kernel,
        places,
        2,
        [
            columns(second_pair, features, 8),
            columns(second_pair, half_units, 0, True),
            columns(second_pair, half_units, 2, True),
            columns(second_pair, features, 9),
        ],
    )
    other_places = [
        jnp.concatenate([near_core, near_halves])
        for near_halves in (halves, 1 - halves)
        for near_core in (core, 1 - core)
    ][1:]
    second_pair, second_sent, second_kept, shared, other_places = tie(
        second_pair, second_sent, second_kept, all_shared(shared), other_places
    )
    (
        batch_grads,
        grad_attend,
        mixer_back_pack,
        grad_blocks,
        mixer_rows,
    ) = vmem_call(
        bind(mixer_back_kernel, utt_rows),
        [
            ((8, features), f32),
            (square, f32),
            ((rows, 3 * features), bf16),
            ((HEADS, block_frames, lanes), bf16),
            ((16, features), f32),
        ],
        (info,),
        (
            grad_batch,
            normed_batch,
            shared,
            batch_rows,
            batch_gain.reshape(1, -1),
            gated,
            linear_half,
            gate_half,
            grad_mixer,
            after_attend,
            norm_gain,
            taps,
            mixer_in,
            attend_out,
        ),
        scratch=(padded, padded),
        cost=row_flops * 4 * features,
    )
    mixer_pair, mixer_back_pair = with_pair(mixer_pack), with_pair(mixer_back_pack)
    third_sent, third_kept = block_sums(
        mixer_blocks_kernel,
        places,
        1,
        [
            columns(mixer_pair, features, 1),
            columns(mixer_back_pair, features, 0, True),
            columns(second_pair, half_features, 20, True),
            columns(second_pair, features, 11),
            columns(mixer_pair, half_features, 0, True),
            columns(mixer_back_pair, features, 2),
        ],
    )
    second_sent, third_sent = tie(second_sent, third_sent)
    early_sent, early_kept = second_sent + third_sent, second_kept + third_kept
    early_arrived = swap_all(early_sent, phases[0])
    head_grad = heads_out(grad_blocks, groups).reshape(frames_all, lanes)
    if groups > 1:
        head_grad = lax.dynamic_slice_in_dim(head_grad, start_query, query_frames, 0)
    head_grad, early_kept = tie(head_grad, early_kept)
    *head_grads, head_weight_grad, head_sums = attend_heads_back(
        weights,
        head_content,
        head_grad,
        arrived,
        head_shift,
        head_weight,
        query_sin,
        query_cos,
        key_table,
    )
    head_grads, head_weight_grad, head_sums, early_arrived = tie(
        head_grads, head_weight_grad, head_sums, early_arrived
    )
    grad_blocks = head_grads[-1].reshape(seq_count, block_frames, -1)
    returned = lax.all_to_all(grad_blocks, "seq", 0, 0, tiled=True)
    if groups > 1:
        returned = jnp.sum(
            returned.astype(f32).reshape(groups, HEADS, block_frames, 2 * lanes), axis=0
        ).astype(bf16)
        returned = jnp.concatenate([frames_back(head_grads[0]), returned], axis=2)
    head_vector_grads = lax.dynamic_update_slice_in_dim(
        jnp.zeros((8, features), f32),
        jnp.sum(head_sums.reshape(8, utt_rows, HEAD_DIM), axis=1),
        head * HEAD_DIM,
        1,
    )
    early_sent, early_kept = fold_rows([(early_kept, early_arrived)], phases[1], 1, VMEM_LIMIT)
    early_sent, head_weight_grad = tie(early_sent, head_weight_grad)
    early_arrived = swap_all(early_sent, phases[1])
    head_weight_grad = jnp.transpose(
        head_weight_grad.reshape(HEAD_DIM, 2, features // 2), (2, 1, 0)
    ).reshape(features, HEAD_DIM)
    position_weight_grad = lax.dynamic_update_slice_in_dim(
        jnp.zeros((features, features), f32), head_weight_grad, head * HEAD_DIM, 1
    )
    entry_pair = with_pair(entry_pack)
    position_pair = with_pair(position_weight_grad.astype(bf16))
    entry_cols = vmem_call(
        turn_kernel,
        [
            ((features, 2 * rows), bf16),
            ((half_units, 2 * rows), bf16),
            ((features, 2 * rows), bf16),
            ((features, features), bf16),
        ],
        (),
        columns(entry_pair, features, 4)
        + columns(entry_pair, half_units, 0, True)
        + columns(entry_pair, features, 5)
        + position_pair,
        numbers=(places,),
    )
    returned, early_arrived, entry_cols = tie(returned, early_arrived, entry_cols)
    (
        frames_grad,
        entry_back_pack,
        grad_pre_first,
        entry_rows,
    ) = vmem_call(
        entry_back_kernel,
        [
            (square, f32),
            ((rows, half_units + 4 * features), bf16),
            ((rows, half_units), bf16),
            ((16, features), f32),
        ],
        (core,),
        (
            returned,
            grad_attend,
            flat_frames,
            after_first,
            slope_first,
            norm_gain,
        ),
        scratch=feed_scratch + [attend_scratch, pltpu.SemaphoreType.DMA((3,))],
        cost=row_flops * (2 * hidden_units + 3 * features),
        held=(feed_in, feed_out, attend_in),
    )
    late_factors = (entry_cols, grad_pre_first, with_pair(entry_back_pack))
    late_sent = late_blocks(False, places, *late_factors)
    late_sent, late_factors, middle_rows = tie(late_sent, late_factors, middle_rows)
    late_arrived = swap_all(late_sent, phases[0])
    late_kept = late_blocks(True, places, *late_factors)
    flat = jnp.concatenate([middle_rows, mixer_rows, entry_rows, head_vector_grads], axis=0)
    flat_steps = [near] + [steps[0] for steps in phases]
    def in_turn(arrived_rows, steps, work):
        nonlocal flat
        flat_arrived = swap(flat, flat_steps.pop()) if flat_steps else jnp.zeros_like(flat)
        after, next_arrived = None, []
        for i, rows in enumerate(arrived_rows):
            if after is not None:
                rows, _ = tie(rows, after)
            if i == len(arrived_rows) - 1:
                rows, flat_arrived = tie(rows, flat_arrived)
            after = work(i, rows)
            next_arrived.append(swap(after, steps[i]) if steps else after)
        flat = flat + flat_arrived
        return next_arrived

    late_kept = list(late_kept)
    for steps in phases[1:]:

        def fold(i, rows):
            pairs = [([late_kept[i]], [rows])]
            if steps is phases[2]:
                pairs = [([early_kept[i]], [early_arrived[i]])] + pairs
            parts = 1 if steps in phases[1:3] else 2
            (sent_rows,), (late_kept[i],) = fold_rows(pairs, [steps[i]], parts)
            return sent_rows

        late_arrived = in_turn(late_arrived, steps, fold)
    sums = [None] * len(late_arrived)

    def add(i, rows):
        (sums[i],) = add_rows([late_kept[i]], [rows])
        return sums[i]

    arrived_rows = in_turn(late_arrived, phases[-1], add)
    for number in range(len(phases) - 1, 0, -1):

        def join(i, rows):
            (sums[i],) = join_rows([sums[i]], [rows], [phases[number][i]])
            return sums[i]

        arrived_rows = in_turn(arrived_rows, phases[number - 1], join)
    for step in flat_steps:
        flat = flat + swap(flat, step)
    vector_grads = vmem_call(
        vectors_kernel,
        [
            (norm_gain.shape, f32),
            (norm_bias.shape, f32),
            (feed_in_bias.shape, f32),
            (feed_out_bias.shape, f32),
            (attend_vectors.shape, f32),
            ((1, 2 * features), f32),
            (mixer_vectors.shape, f32),
            ((KERNEL, features), f32),
        ],
        (),
        (flat,),
    )
    vector_grads = list(vector_grads)
    vector_grads[5] = vector_grads[5].reshape(-1)
    vector_grads[7] = vector_grads[7].T
    vector_grads = [*vector_grads, batch_grads[1], batch_grads[0], batch_rows[2], batch_rows[3]]
    across_rows = swap_all(sums, [near] * 3)
    shapes = [feed_in.shape, feed_out.shape, mixer_in.shape, mixer_out.shape]
    shapes += [attend_out.shape, attend_in.shape]
    spread = spread_blocks(places, sums, shapes, [])
    spread = spread_blocks(other_places[0], across_rows, shapes, spread)
    spread, arrived_rows, vector_grads = tie(spread, arrived_rows, vector_grads)
    across_rows = swap_all(arrived_rows, [near] * 3)
    spread = spread_blocks(other_places[1], arrived_rows, shapes, spread)
    (
        feed_in_grad,
        feed_out_grad,
        mixer_in_grad,
        mixer_out_grad,
        attend_out_grad,
        attend_in_grad,
    ) = spread_blocks(other_places[2], across_rows, shapes, spread)
    (
        norm_gain_grad,
        norm_bias_grad,
        feed_in_bias_grad,
        feed_out_bias_grad,
        attend_vectors_grad,
        mixer_in_bias_grad,
        mixer_vectors_grad,
        taps_grad,
        batch_gain_grad,
        batch_shift_grad,
        new_mean,
        new_variance,
    ) = vector_grads
    return (
        layer_output.reshape(frames.shape),
        frames_grad.reshape(frames.shape),
        norm_gain_grad,
        norm_bias_grad,
        feed_in_grad,
        feed_in_bias_grad,
        feed_out_grad,
        feed_out_bias_grad,
        attend_in_grad,
        attend_vectors_grad,
        attend_out_grad,
        mixer_in_grad,
        mixer_in_bias_grad,
        taps_grad,
        mixer_vectors_grad,
        mixer_out_grad,
        batch_gain_grad,
        batch_shift_grad,
        new_mean,
        new_variance,
    )


def solution(mesh):
    return jax.shard_map(
        shards,
        mesh=mesh,
        in_specs=(
            P("utt", "seq", None),
            P("utt"),
            P("utt", "seq", None),
            P(),
            P(),
            P(),
            P(),
            P(),
            P(),
            P(),
            P(),
            P(),
            P(),
            P(),
            P(),
            P(),
            P(),
            P(),
            P(),
            P(),
            P(),
        ),
        out_specs=(
            P("utt", "seq", None),
            P("utt", "seq", None),
            P(),
            P(),
            P(),
            P(),
            P(),
            P(),
            P(),
            P(),
            P(),
            P(),
            P(),
            P(),
            P(),
            P(),
            P(),
            P(),
            P(),
            P(),
        ),
        check_vma=False,
    )
```
